32 devices in a mesh: dp: 16 (over z, y, x), fsdp: 2 (over core).
Axes of the slice: x: 2, y: 2, z: 4, core: 2. Of those that a mesh axis runs over, the one named last changes fastest.
Arguments:
- tokens: bfloat16 [8192, 1536], P(('dp', 'fsdp')), may hold values from -6 to 6
- cotangent: bfloat16 [8192, 1536], P(('dp', 'fsdp')), may hold values from -6 to 6
- deal: int32 [8192], P(('dp', 'fsdp')), may hold values from 0 to 8191, as said below
- first_len: int32 [2], replicated, may hold values from 1365 to 4096, as said below
- w_query: bfloat16 [1536, 1536], P('dp', 'fsdp'), may hold values from -0.15625 to 0.15625
- w_key: bfloat16 [1536, 128], P('dp', 'fsdp'), may hold values from -0.15625 to 0.15625
- w_value: bfloat16 [1536, 128], P('dp', 'fsdp'), may hold values from -0.15625 to 0.15625
- w_out: bfloat16 [1536, 1536], P('fsdp', 'dp'), may hold values from -3 to 3
- w_gate: bfloat16 [1536, 4608], P('dp', 'fsdp'), may hold values from -0.15625 to 0.15625
- w_up: bfloat16 [1536, 4608], P('dp', 'fsdp'), may hold values from -0.15625 to 0.15625
- w_down: bfloat16 [4608, 1536], P('fsdp', 'dp'), may hold values from -0.09375 to 0.09375
- norm_gains: bfloat16 [2, 1536], P('fsdp', 'dp'), may hold values from 0.25 to 1.75
Outputs:
- output: bfloat16 [8192, 1536], P(('dp', 'fsdp'))
- input_grad: bfloat16 [8192, 1536], P(('dp', 'fsdp'))
- grad_query: float32 [1536, 1536], P('dp', 'fsdp')
- grad_key: float32 [1536, 128], P('dp', 'fsdp')
- grad_value: float32 [1536, 128], P('dp', 'fsdp')
- grad_out: float32 [1536, 1536], P('fsdp', 'dp')
- grad_gate: float32 [1536, 4608], P('dp', 'fsdp')
- grad_up: float32 [1536, 4608], P('dp', 'fsdp')
- grad_down: float32 [4608, 1536], P('fsdp', 'dp')
- grad_gains: float32 [2, 1536], P('fsdp', 'dp')
The draws below stay inside these ranges and needn't reach their ends.
Inputs may be any that keep to these rules, and one draw needn't show every extreme that they name: deal is a permutation of 0 to 8191. The 256 packed positions of block b = d * 2 + f (blocks of 256 along the array) name exactly 16 rows of each block e * 2 + f, e < 16, and no other rows. In one stream, drawn from the seed, first_len is 4096: that stream holds a single sequence. In every other stream first_len is at most 2731, and its second sequence has 4096 - first_len rows.
All inputs are finite; a program needn't handle non-finite values.
Results may differ from the reference program's by a relative error of at most 0.017.
Values may be sent and summed in bfloat16 or wider, within the bound.
A program may use at most 320 MiB of HBM per device.

```python
import jax
import jax.numpy as jnp
from jax import lax

D = 1536
HEADS = 12
HEAD = 128
FF = 4608
WINDOW = 1024
MICRO = 2
TOK_DEV = 256
MB_TOK = 128
SPAN = 32
GROUP_TOK = 4096
MIN_LEN = 1365
GROUPS = 1
STREAMS = 2
TOKENS = 8192
N_DP = 16
N_FSDP = 2


def draw_deal(key, part):
    key = jax.random.fold_in(key, 11)
    stretch_rows = TOK_DEV // N_DP
    device_count = N_DP * N_FSDP
    first_keys = jax.random.split(jax.random.fold_in(key, 1), device_count)
    local_order = jax.vmap(lambda each_key: jax.random.permutation(each_key, TOK_DEV))(first_keys)
    sources = local_order + (jnp.arange(device_count, dtype=jnp.int32) * TOK_DEV)[:, None]
    sources = sources.reshape(N_DP, N_FSDP, N_DP, stretch_rows)
    collected = jnp.transpose(sources, (2, 1, 0, 3)).reshape(N_DP, N_FSDP, TOK_DEV)
    second_keys = jax.random.split(jax.random.fold_in(key, 2), device_count)
    shuffle = jax.vmap(lambda each_key: jax.random.permutation(each_key, TOK_DEV))(second_keys).reshape(N_DP, N_FSDP, TOK_DEV)
    dealt = jnp.take_along_axis(collected, shuffle, axis=2)
    return dealt.reshape(-1).astype(jnp.int32)


def draw_first_len(key, part):
    key = jax.random.fold_in(key, 23)
    drawn_lengths = jax.random.randint(jax.random.fold_in(key, 1), (STREAMS,), MIN_LEN, GROUP_TOK - MIN_LEN + 1)
    chosen = jax.random.randint(jax.random.fold_in(key, 2), (), 0, STREAMS)
    stream_ids = jnp.arange(STREAMS, dtype=jnp.int32)
    drawn_lengths = jnp.where(stream_ids == chosen, GROUP_TOK, drawn_lengths)
    return drawn_lengths.astype(jnp.int32)


def level_of(stream_key, shape, cuts, smallest, largest):
    def one(axis_at, blocks):
        heights = jax.random.uniform(jax.random.fold_in(jax.random.fold_in(stream_key, 6), axis_at), (blocks,), jnp.float32, smallest / len(cuts), largest / len(cuts))
        return jnp.repeat(jnp.exp(heights), shape[axis_at] // blocks).reshape((-1,) + (1,) * (len(shape) - axis_at - 1))

    loudness = one(*cuts[0])
    for cut in cuts[1:]:
        loudness = loudness * one(*cut)
    return loudness


def gaussian(key, dims, deviation, most, cuts=(), held_as=jnp.bfloat16):
    drawn = deviation * jax.random.normal(key, dims, jnp.float32)
    if cuts:
        drawn = drawn * level_of(key, dims, cuts, -0.22, 0.18)
    return jnp.clip(drawn, -most, most).astype(held_as)


def setup_inputs(seed: int = 0) -> dict:
    key_of = jax.random.split(jax.random.key(seed), 13)
    tokens = gaussian(key_of[0], (TOKENS, D), 1.0, 6.0, ((0, 32),))
    cotangent = gaussian(key_of[1], (TOKENS, D), 1.0, 6.0, ((0, 32),))
    deal = draw_deal(jax.random.fold_in(key_of[12], 71), 0)
    first_len = draw_first_len(jax.random.fold_in(key_of[12], 71), 0)
    w_query = gaussian(key_of[4], (D, HEADS * HEAD), D ** -0.5, 0.15625, ((0, 16), (1, 2)))
    w_key = gaussian(key_of[5], (D, HEAD), D ** -0.5, 0.15625, ((0, 16), (1, 2)))
    w_value = gaussian(key_of[6], (D, HEAD), D ** -0.5, 0.15625, ((0, 16), (1, 2)))
    w_out = gaussian(key_of[7], (HEADS * HEAD, D), (max(1, HEADS * HEAD // 384)) ** -0.5, 3.0, ((0, 2), (1, 16)))
    w_gate = gaussian(key_of[8], (D, FF), D ** -0.5, 0.15625, ((0, 16), (1, 2)))
    w_up = gaussian(key_of[9], (D, FF), D ** -0.5, 0.15625, ((0, 16), (1, 2)))
    w_down = gaussian(key_of[10], (FF, D), FF ** -0.5, 0.09375, ((0, 2), (1, 16)))
    norm_gains = jnp.clip(1.0 + 0.15 * jax.random.normal(key_of[11], (2, D), jnp.float32), 0.25, 1.75).astype(jnp.bfloat16)
    return dict(tokens=tokens, cotangent=cotangent, deal=deal, first_len=first_len, w_query=w_query, w_key=w_key, w_value=w_value, w_out=w_out, w_gate=w_gate, w_up=w_up, w_down=w_down, norm_gains=norm_gains)


@jax.custom_vjp
def low(v):
    return lax.optimization_barrier(v.astype(jnp.bfloat16)).astype(jnp.float32)

@jax.custom_vjp
def low_back(v):
    return v

def low_keep(v):
    return (low(v), None)

def low_pass(kept, grad):
    return (grad,)

def back_keep(v):
    return (v, None)

def back_low(kept, grad):
    return (low(grad),)
low.defvjp(low_keep, low_pass)
low_back.defvjp(back_keep, back_low)
HIGHEST_PRECISION = lax.Precision.HIGHEST
EPSILON = 1e-06
NEGATIVE = -1e+30

def normed(row_values, gain_row):
    return row_values * lax.rsqrt(lax.optimization_barrier(jnp.mean(row_values * row_values, axis=-1, keepdims=True)) + EPSILON) * gain_row

def rotate(values, cosine, sine_table):
    half_width = values.shape[-1] // 2
    front_half = values[..., :half_width]
    back_half = values[..., half_width:]
    return jnp.concatenate([front_half * cosine - back_half * sine_table, back_half * cosine + front_half * sine_table], axis=-1)

def angles(places):
    half_width = HEAD // 2
    frequency = 10000.0 ** (-jnp.arange(half_width, dtype=jnp.float32) * 2.0 / HEAD)
    angle_rows = places.astype(jnp.float32)[:, None] * frequency[None, :]
    return (jnp.cos(angle_rows), jnp.sin(angle_rows))

def windowed(query_rows, key_rows, value_rows, first_length):
    row_count = query_rows.shape[0]
    block_rows = min(512, row_count)
    block_count = row_count // block_rows
    key_span = block_rows + WINDOW
    front_pad = jnp.zeros((WINDOW, HEAD), jnp.float32)
    padded_keys = jnp.concatenate([front_pad, key_rows], axis=0)
    padded_values = jnp.concatenate([front_pad, value_rows], axis=0)
    score_scale = HEAD ** (-0.5)

    def one_block(pieces):
        query_block, start_row = pieces
        key_block = lax.dynamic_slice_in_dim(padded_keys, start_row, key_span, 0)
        value_block = lax.dynamic_slice_in_dim(padded_values, start_row, key_span, 0)
        query_place = start_row + jnp.arange(block_rows, dtype=jnp.int32)
        key_place = start_row - WINDOW + jnp.arange(key_span, dtype=jnp.int32)
        query_later = query_place >= first_length
        key_later = key_place >= first_length
        allowed = (query_later[:, None] == key_later[None, :]) & (key_place[None, :] >= 0) & (key_place[None, :] <= query_place[:, None]) & (query_place[:, None] - key_place[None, :] < WINDOW)
        scores = low_back(jnp.einsum('qhd,kd->hqk', query_block, key_block, precision=HIGHEST_PRECISION) * score_scale)
        scores = jnp.where(allowed[None], scores, NEGATIVE)
        row_top = lax.optimization_barrier(jnp.max(scores, axis=-1, keepdims=True))
        exp_scores = jnp.exp(scores - row_top)
        soft_weights = exp_scores / lax.optimization_barrier(jnp.sum(exp_scores, axis=-1, keepdims=True))
        return jnp.einsum('hqk,kd->qhd', low(soft_weights), value_block, precision=HIGHEST_PRECISION)
    start_rows = jnp.arange(block_count, dtype=jnp.int32) * block_rows
    attended = lax.map(jax.checkpoint(one_block), (query_rows.reshape(block_count, block_rows, HEADS, HEAD), start_rows))
    return attended.reshape(row_count, HEADS, HEAD)

def stream_layer(row_values, first_length, weights):
    w_query, w_key, w_value, w_out, w_gate, w_up, w_down, gains = weights
    row_count = row_values.shape[0]
    places = jnp.arange(row_count, dtype=jnp.int32)
    second_seq = places >= first_length
    within = places - jnp.where(second_seq, first_length, 0)
    cosine, sine_table = angles(within)
    normal_one = low(normed(row_values, gains[0]))
    query_raw = low_back(jnp.dot(normal_one, w_query, precision=HIGHEST_PRECISION)).reshape(row_count, HEADS, HEAD)
    query_rows = low(rotate(query_raw, cosine[:, None, :], sine_table[:, None, :]))
    key_rows = low(rotate(low_back(jnp.dot(normal_one, w_key, precision=HIGHEST_PRECISION)), cosine, sine_table))
    value_rows = low(low_back(jnp.dot(normal_one, w_value, precision=HIGHEST_PRECISION)))
    attended = windowed(query_rows, key_rows, value_rows, first_length)
    mixed_heads = low(low_back(attended.reshape(row_count, HEADS * HEAD)))
    branch = low_back(jnp.dot(mixed_heads, w_out, precision=HIGHEST_PRECISION))
    middle = row_values + branch
    normal_two = low(normed(middle, gains[1]))
    gate_rows = low_back(jnp.dot(normal_two, w_gate, precision=HIGHEST_PRECISION))
    upward = low_back(jnp.dot(normal_two, w_up, precision=HIGHEST_PRECISION))
    hidden = low(jax.nn.gelu(gate_rows, approximate=True) * upward)
    return middle + jnp.dot(hidden, w_down, precision=HIGHEST_PRECISION)

def reference(tokens, cotangent, deal, first_len, w_query, w_key, w_value, w_out, w_gate, w_up, w_down, norm_gains):
    order_back = jnp.argsort(deal).astype(jnp.int32)

    def forward(row_values, query_w, key_w, value_w, out_w, gate_w, up_w, down_w, gains):
        weights = (query_w, key_w, value_w, out_w, gate_w, up_w, down_w, gains)
        packed = row_values[deal].reshape(GROUPS, SPAN, MICRO, MB_TOK, D)
        streams = jnp.transpose(packed, (0, 2, 1, 3, 4)).reshape(STREAMS, GROUP_TOK, D)

        def one_stream(paired):
            return stream_layer(paired[0], paired[1], weights)
        finished = lax.map(jax.checkpoint(one_stream), (streams, first_len))
        finished = jnp.transpose(finished.reshape(GROUPS, MICRO, SPAN, MB_TOK, D), (0, 2, 1, 3, 4)).reshape(TOKENS, D)
        return finished[order_back]
    floats = (tokens.astype(jnp.float32), w_query.astype(jnp.float32), w_key.astype(jnp.float32), w_value.astype(jnp.float32), w_out.astype(jnp.float32), w_gate.astype(jnp.float32), w_up.astype(jnp.float32), w_down.astype(jnp.float32), norm_gains.astype(jnp.float32))
    result, pullback = jax.vjp(forward, *floats)
    grads = pullback(cotangent.astype(jnp.float32))
    return (result.astype(jnp.bfloat16), grads[0].astype(jnp.bfloat16), grads[1], grads[2], grads[3], grads[4], grads[5], grads[6], grads[7], grads[8])
```

```python
import functools

import jax
import jax.numpy as jnp
from jax import lax
from jax.experimental import pallas as pl
from jax.experimental.pallas import tpu as pltpu
from jax.sharding import PartitionSpec as P

HEADS = 12
HEAD = 128
WINDOW = 1024
MICRO = 2


EPSILON = 1e-06
NEGATIVE = -1e30
VMEM_ASK = 62 * 2**20


def passed_along(x, axis, by):
    count = lax.axis_size(axis)
    pairs = [(i, i + by) for i in range(count) if 0 <= i + by < count]
    return lax.ppermute(x, axis, pairs)


def normed(row_values, gain_row):
    return (
        row_values
        * lax.rsqrt(jnp.mean(row_values * row_values, axis=-1, keepdims=True) + EPSILON)
        * gain_row
    )


def rotate(values, cosine, sine_table):
    half_width = values.shape[-1] // 2
    front_half = values[..., :half_width]
    back_half = values[..., half_width:]
    return jnp.concatenate(
        [
            front_half * cosine - back_half * sine_table,
            back_half * cosine + front_half * sine_table,
        ],
        axis=-1,
    )


def angles(places):
    half_width = HEAD // 2
    frequency = 10000.0 ** (-jnp.arange(half_width, dtype=jnp.float32) * 2.0 / HEAD)
    angle_rows = places.astype(jnp.float32)[:, None] * frequency[None, :]
    return (jnp.cos(angle_rows), jnp.sin(angle_rows))


def contract_rows(left, right):
    return lax.dot_general(
        left, right, (((0,), (0,)), ((), ())), preferred_element_type=jnp.float32
    )


def against(left, right):
    return lax.dot_general(
        left, right, (((1,), (1,)), ((), ())), preferred_element_type=jnp.float32
    )


def gelu_tanh(inputs):
    return jax.nn.gelu(inputs, approximate=True)


def per_device(
    tokens,
    cotangent,
    deal,
    first_len,
    w_query,
    w_key,
    w_value,
    w_out,
    w_gate,
    w_up,
    w_down,
    norm_gains,
):
    peer_count = lax.axis_size("dp")
    core_count = lax.axis_size("fsdp")
    device_total = peer_count * core_count
    row_count = tokens.shape[0]
    model_width = tokens.shape[1]
    per_peer = row_count // peer_count
    micro_rows = row_count // MICRO
    reach_steps = min(device_total - 1, (WINDOW + micro_rows - 2) // micro_rows)
    linear = lax.axis_index("dp") * core_count + lax.axis_index("fsdp")
    source_peer = deal // (row_count * core_count)
    offsets = deal % row_count
    bucket_order = jnp.argsort(source_peer, stable=True)
    inverse = jnp.argsort(bucket_order)
    wanted = offsets[bucket_order].reshape(peer_count, per_peer)
    requested = lax.all_to_all(wanted, "dp", split_axis=0, concat_axis=0, tiled=True)
    picked = requested.reshape(-1)
    fetched = (
        lax.all_to_all(
            tokens[picked].reshape(peer_count, per_peer, model_width),
            "dp",
            split_axis=0,
            concat_axis=0,
            tiled=True,
        ),
        lax.all_to_all(
            cotangent[picked].reshape(peer_count, per_peer, model_width),
            "dp",
            split_axis=0,
            concat_axis=0,
            tiled=True,
        ),
    )
    rows_in = fetched[0].reshape(row_count, model_width)[inverse]
    grad_in = fetched[1].reshape(row_count, model_width)[inverse]
    halves = (
        lax.all_gather(w_query, "dp", axis=0, tiled=True),
        lax.all_gather(w_key, "dp", axis=0, tiled=True),
        lax.all_gather(w_value, "dp", axis=0, tiled=True),
        lax.all_gather(w_out, "dp", axis=1, tiled=True),
        lax.all_gather(w_gate, "dp", axis=0, tiled=True),
        lax.all_gather(w_up, "dp", axis=0, tiled=True),
        lax.all_gather(w_down, "dp", axis=1, tiled=True),
        lax.all_gather(norm_gains, "dp", axis=1, tiled=True),
    )
    gathered = (
        lax.all_gather(halves[0], "fsdp", axis=1, tiled=True),
        lax.all_gather(halves[1], "fsdp", axis=1, tiled=True),
        lax.all_gather(halves[2], "fsdp", axis=1, tiled=True),
        lax.all_gather(halves[3], "fsdp", axis=0, tiled=True),
        lax.all_gather(halves[4], "fsdp", axis=1, tiled=True),
        lax.all_gather(halves[5], "fsdp", axis=1, tiled=True),
        lax.all_gather(halves[6], "fsdp", axis=0, tiled=True),
        lax.all_gather(halves[7], "fsdp", axis=0, tiled=True),
    )
    full_query, full_key, full_value, full_out, full_gate, full_up, full_down, full_gains = gathered
    gain_one = full_gains[0].astype(jnp.float32)
    gain_two = full_gains[1].astype(jnp.float32)
    inside = jnp.arange(micro_rows, dtype=jnp.int32)
    query_place = linear * micro_rows + inside
    query_later = query_place[None, :] >= first_len[:, None]
    query_within = query_place[None, :] - jnp.where(query_later, first_len[:, None], 0)
    distance = jnp.arange(reach_steps, -1, -1, dtype=jnp.int32)
    key_place = ((linear - distance)[:, None] * micro_rows + inside[None, :]).reshape(-1)
    key_later = key_place[None, :] >= first_len[:, None]
    allowed = (
        (query_later[:, :, None] == key_later[:, None, :])
        & (key_place[None, None, :] >= 0)
        & (key_place[None, None, :] <= query_place[None, :, None])
        & (query_place[None, :, None] - key_place[None, None, :] < WINDOW)
    )
    rows_float = rows_in.astype(jnp.float32)
    cosine, sine_table = angles(query_within.reshape(-1))
    score_scale = HEAD ** (-0.5)
    normal_one = normed(rows_float, gain_one).astype(jnp.bfloat16)
    query_raw = jnp.dot(normal_one, full_query, preferred_element_type=jnp.float32).reshape(
        row_count, HEADS, HEAD
    )
    query_rows = rotate(query_raw, cosine[:, None, :], sine_table[:, None, :]).astype(jnp.bfloat16)
    key_rows = rotate(
        jnp.dot(normal_one, full_key, preferred_element_type=jnp.float32), cosine, sine_table
    ).astype(jnp.bfloat16)
    value_rows = jnp.dot(normal_one, full_value, preferred_element_type=jnp.float32).astype(
        jnp.bfloat16
    )
    earlier = []
    for distance_step in range(1, reach_steps + 1):
        earlier.append(passed_along((key_rows, value_rows), ("dp", "fsdp"), distance_step))
    ordered = earlier[::-1] + [(key_rows, value_rows)]
    all_keys = jnp.concatenate(
        [member[0].reshape(MICRO, micro_rows, HEAD) for member in ordered], axis=1
    )
    all_values = jnp.concatenate(
        [member[1].reshape(MICRO, micro_rows, HEAD) for member in ordered], axis=1
    )
    by_head = jnp.transpose(query_rows.reshape(MICRO, micro_rows, HEADS, HEAD), (2, 0, 1, 3))

    def attend(query_head):
        scores = jnp.where(
            allowed,
            jnp.einsum("mqd,mkd->mqk", query_head, all_keys, preferred_element_type=jnp.float32)
            * score_scale,
            NEGATIVE,
        )
        row_top = jnp.max(scores, axis=2, keepdims=True)
        exp_scores = jnp.exp(scores - row_top)
        row_total = jnp.sum(exp_scores, axis=2, keepdims=True)
        soft_weights = (exp_scores / row_total).astype(jnp.bfloat16)
        attended_head = jnp.einsum(
            "mqk,mkd->mqd", soft_weights, all_values, preferred_element_type=jnp.float32
        )
        return (attended_head, row_top[..., 0] + jnp.log(row_total[..., 0]))

    attended, log_total = lax.map(attend, by_head)
    mixed_heads = (
        jnp.transpose(attended, (1, 2, 0, 3)).reshape(row_count, HEADS * HEAD).astype(jnp.bfloat16)
    )
    middle = rows_float + jnp.dot(mixed_heads, full_out, preferred_element_type=jnp.float32)
    normal_two = normed(middle, gain_two).astype(jnp.bfloat16)
    gate_rows = jnp.dot(normal_two, full_gate, preferred_element_type=jnp.float32)
    upward = jnp.dot(normal_two, full_up, preferred_element_type=jnp.float32)
    activated = gelu_tanh(gate_rows)
    hidden = (activated * upward).astype(jnp.bfloat16)
    result = (middle + jnp.dot(hidden, full_down, preferred_element_type=jnp.float32)).astype(
        jnp.bfloat16
    )
    grad_float = grad_in.astype(jnp.float32)
    grad_down = contract_rows(hidden, grad_in)
    grad_hidden = against(grad_in, full_down)
    gelu_value, gelu_pull = jax.vjp(gelu_tanh, gate_rows)
    grad_gate_rows = gelu_pull(grad_hidden * upward)[0].astype(jnp.bfloat16)
    grad_up_rows = (grad_hidden * activated).astype(jnp.bfloat16)
    grad_gate = contract_rows(normal_two, grad_gate_rows)
    grad_up = contract_rows(normal_two, grad_up_rows)
    grad_two = against(grad_gate_rows, full_gate) + against(grad_up_rows, full_up)
    norm_value, norm_pull = jax.vjp(normed, middle, gain_two)
    grad_middle_norm, gain_two_grad = norm_pull(grad_two)
    grad_middle = grad_float + grad_middle_norm
    grad_middle_low = grad_middle.astype(jnp.bfloat16)
    grad_out = contract_rows(mixed_heads, grad_middle_low)
    grad_mixed = against(grad_middle_low, full_out).astype(jnp.bfloat16)
    grad_by_head = jnp.transpose(grad_mixed.reshape(MICRO, micro_rows, HEADS, HEAD), (2, 0, 1, 3))

    def attend_back(running, pieces):
        key_total, value_total = running
        query_head, grad_head, total_head = pieces
        scores = (
            jnp.einsum("mqd,mkd->mqk", query_head, all_keys, preferred_element_type=jnp.float32)
            * score_scale
        )
        soft_weights = jnp.where(allowed, jnp.exp(scores - total_head[..., None]), 0.0)
        value_total = value_total + jnp.einsum(
            "mqk,mqd->mkd",
            soft_weights.astype(jnp.bfloat16),
            grad_head,
            preferred_element_type=jnp.float32,
        )
        grad_soft = jnp.einsum(
            "mqd,mkd->mqk", grad_head, all_values, preferred_element_type=jnp.float32
        )
        row_delta = jnp.sum(grad_soft * soft_weights, axis=2, keepdims=True)
        grad_scores = (soft_weights * (grad_soft - row_delta)).astype(jnp.bfloat16)
        grad_query_head = (
            jnp.einsum("mqk,mkd->mqd", grad_scores, all_keys, preferred_element_type=jnp.float32)
            * score_scale
        )
        key_total = (
            key_total
            + jnp.einsum(
                "mqk,mqd->mkd", grad_scores, query_head, preferred_element_type=jnp.float32
            )
            * score_scale
        )
        return ((key_total, value_total), grad_query_head)

    zero_block = jnp.zeros((MICRO, (reach_steps + 1) * micro_rows, HEAD), jnp.float32)
    totals, grad_query_heads = lax.scan(
        attend_back, (zero_block, zero_block), (by_head, grad_by_head, log_total)
    )
    key_total, value_total = totals

    def piece_of(total, distance_step):
        begin_row = (reach_steps - distance_step) * micro_rows
        return total[:, begin_row : begin_row + micro_rows].reshape(row_count, HEAD)

    own_key = piece_of(key_total, 0)
    own_value = piece_of(value_total, 0)
    for distance_step in range(1, reach_steps + 1):
        returned_pair = (
            passed_along(
                piece_of(key_total, distance_step).astype(jnp.bfloat16),
                ("dp", "fsdp"),
                -distance_step,
            ).astype(jnp.float32),
            passed_along(
                piece_of(value_total, distance_step).astype(jnp.bfloat16),
                ("dp", "fsdp"),
                -distance_step,
            ).astype(jnp.float32),
        )
        own_key = own_key + returned_pair[0]
        own_value = own_value + returned_pair[1]
    grad_value_rows = own_value.astype(jnp.bfloat16)
    grad_query_rot = jnp.transpose(grad_query_heads, (1, 2, 0, 3)).reshape(row_count, HEADS, HEAD)
    grad_query_raw = (
        rotate(grad_query_rot, cosine[:, None, :], -sine_table[:, None, :])
        .reshape(row_count, HEADS * HEAD)
        .astype(jnp.bfloat16)
    )
    grad_key_raw = rotate(own_key, cosine, -sine_table).astype(jnp.bfloat16)
    grad_query = contract_rows(normal_one, grad_query_raw)
    grad_key = contract_rows(normal_one, grad_key_raw)
    grad_value = contract_rows(normal_one, grad_value_rows)
    grad_one = (
        against(grad_query_raw, full_query)
        + against(grad_key_raw, full_key)
        + against(grad_value_rows, full_value)
    )
    first_value, first_pull = jax.vjp(normed, rows_float, gain_one)
    grad_rows_norm, gain_one_grad = first_pull(grad_one)
    grad_rows = (grad_middle + grad_rows_norm).astype(jnp.bfloat16)
    grad_gains = jnp.stack([gain_one_grad, gain_two_grad])
    sectioned = (
        lax.psum_scatter(
            grad_query.astype(jnp.bfloat16), "fsdp", scatter_dimension=1, tiled=True
        ).astype(jnp.float32),
        lax.psum_scatter(
            grad_key.astype(jnp.bfloat16), "fsdp", scatter_dimension=1, tiled=True
        ).astype(jnp.float32),
        lax.psum_scatter(
            grad_value.astype(jnp.bfloat16), "fsdp", scatter_dimension=1, tiled=True
        ).astype(jnp.float32),
        lax.psum_scatter(
            grad_out.astype(jnp.bfloat16), "fsdp", scatter_dimension=0, tiled=True
        ).astype(jnp.float32),
        lax.psum_scatter(
            grad_gate.astype(jnp.bfloat16), "fsdp", scatter_dimension=1, tiled=True
        ).astype(jnp.float32),
        lax.psum_scatter(
            grad_up.astype(jnp.bfloat16), "fsdp", scatter_dimension=1, tiled=True
        ).astype(jnp.float32),
        lax.psum_scatter(
            grad_down.astype(jnp.bfloat16), "fsdp", scatter_dimension=0, tiled=True
        ).astype(jnp.float32),
        lax.psum_scatter(
            grad_gains.astype(jnp.bfloat16), "fsdp", scatter_dimension=0, tiled=True
        ).astype(jnp.float32),
    )
    reduced = (
        lax.psum_scatter(sectioned[0], "dp", scatter_dimension=0, tiled=True),
        lax.psum_scatter(sectioned[1], "dp", scatter_dimension=0, tiled=True),
        lax.psum_scatter(sectioned[2], "dp", scatter_dimension=0, tiled=True),
        lax.psum_scatter(sectioned[3], "dp", scatter_dimension=1, tiled=True),
        lax.psum_scatter(sectioned[4], "dp", scatter_dimension=0, tiled=True),
        lax.psum_scatter(sectioned[5], "dp", scatter_dimension=0, tiled=True),
        lax.psum_scatter(sectioned[6], "dp", scatter_dimension=1, tiled=True),
        lax.psum_scatter(sectioned[7], "dp", scatter_dimension=1, tiled=True),
    )
    returned = (
        lax.all_to_all(
            result[bucket_order].reshape(peer_count, per_peer, model_width),
            "dp",
            split_axis=0,
            concat_axis=0,
            tiled=True,
        ),
        lax.all_to_all(
            grad_rows[bucket_order].reshape(peer_count, per_peer, model_width),
            "dp",
            split_axis=0,
            concat_axis=0,
            tiled=True,
        ),
    )
    output = jnp.zeros_like(tokens).at[picked].set(returned[0].reshape(row_count, model_width))
    input_grad = jnp.zeros_like(tokens).at[picked].set(returned[1].reshape(row_count, model_width))
    return (
        output,
        input_grad,
        reduced[0],
        reduced[1],
        reduced[2],
        reduced[3],
        reduced[4],
        reduced[5],
        reduced[6],
        reduced[7],
    )


MESH = pl.DeviceIdType.MESH
BF16 = jnp.bfloat16
F32 = jnp.float32
PLANE = 4
ANY = pl.BlockSpec(memory_space=pl.ANY)
VM = pl.BlockSpec(memory_space=pltpu.VMEM)
SM = pl.BlockSpec(memory_space=pltpu.SMEM)


def mm(left, right):
    return jnp.dot(left, right, preferred_element_type=F32)


def mm_nt(left, right):
    return lax.dot_general(left, right, (((1,), (1,)), ((), ())), preferred_element_type=F32)


def mm_tn(left, right):
    return lax.dot_general(left, right, (((0,), (0,)), ((), ())), preferred_element_type=F32)


class Place:
    def __init__(self, chips):
        self.chips = chips
        self.groups = chips // PLANE
        self.d = lax.axis_index("dp")
        self.f = lax.axis_index("fsdp")
        self.other = 1 - self.f
        self.g = self.d // PLANE
        self.p = self.d % PLANE
        self.x = self.p % 2
        self.y = self.p // 2

    def plane_pos(self, j):
        return ((self.y + j // 2) % 2) * 2 + (self.x + j % 2) % 2

    def plane_chip(self, j):
        return self.g * PLANE + self.plane_pos(j)

    def column_chip(self, k):
        return ((self.g + k) % self.groups) * PLANE + self.p


def greet_all(place):
    barrier = pltpu.get_barrier_semaphore()
    total = place.chips * 2
    me = place.d * 2 + place.f

    def signal(k, carry):
        to = (me + k) % total
        pl.semaphore_signal(barrier, inc=1, device_id=(to // 2, to % 2), device_id_type=MESH)
        return carry

    lax.fori_loop(1, total, signal, 0)
    pl.semaphore_wait(barrier, total - 1)


class Sent:
    def __init__(self):
        self.copies = []

    def remote(self, src, dst, send_sem, recv_sem, device):
        copy = pltpu.make_async_remote_copy(
            src_ref=src,
            dst_ref=dst,
            send_sem=send_sem,
            recv_sem=recv_sem,
            device_id=device,
            device_id_type=MESH,
        )
        copy.start()
        self.copies.append(copy)

    def finish(self):
        for copy in self.copies:
            copy.wait_send()
        self.copies = []


def arrived(ref, sem):
    pltpu.make_async_copy(ref, ref, sem).wait()


def iota(shape, dim):
    return lax.broadcasted_iota(jnp.int32, shape, dim)


def gain_spread(width, share):
    column = iota((128, width), 1).astype(F32)
    inside = column - jnp.floor((column + 0.5) * (1.0 / share)) * share
    row = iota((128, width), 0).astype(F32)
    return (inside == row).astype(BF16)


def own_stretch(chips, width, share):
    row = iota((chips, width), 0)
    column = iota((chips, width), 1)
    return (column >= row * share) & (column < row * share + share)


def gain_row(kvg_ref, which, chips, width, share):
    block = kvg_ref[which, :, share : share + 16, :].astype(F32)[:, 0, :].astype(BF16)
    spread = mm(block, gain_spread(width, share))
    return jnp.sum(jnp.where(own_stretch(chips, width, share), spread, 0.0), axis=0, keepdims=True)


def gather_kernel(
    chips,
    deal_ref,
    deal_col_ref,
    tokens_ref,
    cot_ref,
    wq_ref,
    wot_ref,
    kvg_ref,
    gate_ref,
    up_ref,
    down_ref,
    full_q,
    full_ot,
    full_kvg,
    full_three,
    rows_out,
    pg_all,
    take_ref,
    place_ref,
    deal_all,
    give,
    got,
    deal_send,
    deal_recv,
    row_send,
    row_recv,
    attn_send,
    attn_recv,
    fan_send,
    kv_sems,
    three_send,
    three_recv,
    relay_send,
    relay_recv,
    own_sems,
    pg_send,
    pg_recv,
    local_sems,
):
    place = Place(chips)
    d, f, other = place.d, place.f, place.other
    rows, width = tokens_ref.shape
    share = wq_ref.shape[0]
    half = share // 2
    per = rows // chips
    part = gate_ref.shape[1] // 2
    sent = Sent()
    greet_all(place)

    deal_all[d] = deal_ref[...]
    for k in range(1, chips):
        to = (d + k) % chips
        sent.remote(
            deal_all.at[d], deal_all.at[d], deal_send.at[k], deal_recv.at[d], (to, f)
        )

    def attn_slices(s):
        band = pl.ds(pl.multiple_of(s * share, 16), share)
        return (full_q.at[band], full_ot.at[band], full_kvg.at[f, s])

    mine = attn_slices(d)
    sources = (wq_ref, wot_ref, kvg_ref)
    for a in range(3):
        for k in range(1, place.groups):
            sent.remote(
                sources[a], mine[a], attn_send.at[a, k], attn_recv.at[a, d], (place.column_chip(k), f)
            )
    locals_ = [pltpu.make_async_copy(sources[a], mine[a], local_sems.at[a]) for a in range(3)]
    for copy in locals_:
        copy.start()
    for a in range(3):
        for j in range(1, PLANE):
            sent.remote(
                sources[a],
                mine[a],
                fan_send.at[a, 0, j],
                attn_recv.at[a, d],
                (place.plane_chip(j), f),
            )

    mats = (gate_ref, up_ref, down_ref)

    three_copies = []
    for k in range(place.groups):
        for b in range(2):
            to_x = (place.x + b) % 2
            chip = ((place.g + k) % place.groups) * PLANE + 2 * f + to_x
            slot = 2 * k + b
            for core in range(2):
                for a in range(3):
                    src = mats[a].at[
                        pl.ds(half * core, half), pl.ds(pl.multiple_of(part * to_x, 128), part)
                    ]
                    dst = full_three.at[a, pl.ds(pl.multiple_of(d * share + half * core, 16), half)]
                    copy = pltpu.make_async_remote_copy(
                        src_ref=src,
                        dst_ref=dst,
                        send_sem=three_send.at[a, slot, core],
                        recv_sem=three_recv.at[a, d],
                        device_id=(chip, core),
                        device_id_type=MESH,
                    )
                    three_copies.append((slot, copy))
    for slot, copy in three_copies:
        if slot == 0:
            pl.when(place.y != f)(copy.start)
        else:
            copy.start()

    def own_parts():
        band = pl.ds(pl.multiple_of(d * share, 16), share)
        to = []
        for a in range(3):
            src = mats[a].at[:, pl.ds(pl.multiple_of(part * place.x, 128), part)]
            to.append((src, full_three.at[a, band]))
        return to

    def own_local():
        return [
            pltpu.make_async_copy(src, dst, local_sems.at[3 + a])
            for a, (src, dst) in enumerate(own_parts())
        ]

    def own_remote():
        return [
            pltpu.make_async_remote_copy(
                src_ref=src,
                dst_ref=dst,
                send_sem=own_sems.at[0, a],
                recv_sem=own_sems.at[1, a],
                device_id=(d, other),
                device_id_type=MESH,
            )
            for a, (src, dst) in enumerate(own_parts())
        ]

    @pl.when(place.y == f)
    def _():
        for copy in own_local() + own_remote():
            copy.start()

    for k in range(1, chips):
        arrived(deal_all.at[(d + k) % chips], deal_recv.at[(d + k) % chips])
    deals = deal_all[:, 0, :]
    chip_bits = (2 * rows).bit_length() - 1
    wants = lax.shift_right_logical(deals, chip_bits) == d
    offset = deals & (rows - 1)
    earlier = (iota((rows, rows), 0) < iota((rows, rows), 1)).astype(BF16)
    rank = mm(wants.astype(F32).astype(BF16), earlier)
    for j in range(chips):
        hit = wants[j : j + 1, :] & (rank[j : j + 1, :] == iota((per, rows), 0).astype(F32))
        index = jnp.sum(jnp.where(hit, offset[j : j + 1, :], 0), axis=1, keepdims=True)
        take_ref[j * per : (j + 1) * per, :] = (index == iota((per, rows), 1)).astype(F32).astype(BF16)
    give[:, :width] = mm(take_ref[...], tokens_ref[...]).astype(BF16)
    give[:, width:] = mm(take_ref[...], cot_ref[...]).astype(BF16)

    def block(k):
        return pl.ds(pl.multiple_of(k * per, per), per)

    for k in range(1, chips):
        to = (d + k) % chips
        sent.remote(give.at[block(to)], got.at[block(d)], row_send.at[k], row_recv.at[d], (to, f))
    got[block(d), :] = give[block(d), :]

    for k in range(1, place.groups):
        s = place.column_chip(k)
        piece = attn_slices(s)
        for a in range(3):
            arrived(piece[a], attn_recv.at[a, s])
            for j in range(1, PLANE):
                sent.remote(
                    piece[a],
                    piece[a],
                    fan_send.at[a, k, j],
                    attn_recv.at[a, s],
                    (place.plane_chip(j), f),
                )

    source_col = lax.shift_right_logical(deal_col_ref[...], chip_bits)
    source_row = lax.shift_right_logical(deal_ref[0:1, :], chip_bits)
    same = (source_col == source_row) & (iota((rows, rows), 1) < iota((rows, rows), 0))
    order = jnp.sum(same.astype(F32), axis=1, keepdims=True).astype(jnp.int32)
    where_from = source_col * per + order
    place_ref[...] = (where_from == iota((rows, rows), 1)).astype(F32).astype(BF16)
    for k in range(1, chips):
        s = (d + k) % chips
        arrived(got.at[block(s)], row_recv.at[s])
    rows_out[...] = mm(place_ref[...], got[:, :width]).astype(BF16)
    pg_all[place.p] = mm(place_ref[...], got[:, width:]).astype(BF16)
    for j in range(1, PLANE):
        sent.remote(
            pg_all.at[place.p],
            pg_all.at[place.p],
            pg_send.at[j],
            pg_recv.at[place.p],
            (place.plane_chip(j), f),
        )

    for k in range(place.groups):
        for j in range(PLANE):
            s = ((place.g + k) % place.groups) * PLANE + place.plane_pos(j)
            if k == 0 and j == 0:
                continue
            band = pl.ds(pl.multiple_of(s * share + half * f, 16), half)
            for a in range(3):
                piece = full_three.at[a, band]
                arrived(piece, three_recv.at[a, s])
                sent.remote(piece, piece, relay_send.at[a, s], relay_recv.at[a, s], (d, other))
    for k in range(place.groups):
        for j in range(1, PLANE):
            s = ((place.g + k) % place.groups) * PLANE + place.plane_pos(j)
            piece = attn_slices(s)
            for a in range(3):
                arrived(piece[a], attn_recv.at[a, s])
    for copy in locals_:
        copy.wait()
    sent.remote(full_kvg.at[f], full_kvg.at[f], kv_sems.at[0], kv_sems.at[1], (d, other))
    for j in range(1, PLANE):
        pos = place.plane_pos(j)
        arrived(pg_all.at[pos], pg_recv.at[pos])
    for k in range(place.groups):
        for j in range(PLANE):
            s = ((place.g + k) % place.groups) * PLANE + place.plane_pos(j)
            if k == 0 and j == 0:
                continue
            band = pl.ds(pl.multiple_of(s * share + half * other, 16), half)
            for a in range(3):
                arrived(full_three.at[a, band], relay_recv.at[a, s])

    @pl.when(place.y == f)
    def _():
        for copy in own_local():
            copy.wait()
        for copy in own_remote():
            copy.wait_send()

    @pl.when(place.y != f)
    def _():
        for copy in own_remote():
            copy.wait_recv()

    arrived(full_kvg.at[other], kv_sems.at[1])
    for slot, copy in three_copies:
        if slot == 0:
            pl.when(place.y != f)(copy.wait_send)
        else:
            copy.wait_send()
    sent.finish()


def gather(chips, deal, tokens, cotangent, wq, wot, kvg, gate, up, down):
    rows, width = tokens.shape
    share = wq.shape[0]
    groups = chips // PLANE
    part = gate.shape[1] // 2
    dma = pltpu.SemaphoreType.DMA
    deal_rows = jnp.broadcast_to(deal[None, :], (8, rows))
    deal_col = jnp.broadcast_to(deal[:, None], (rows, rows))
    return pl.pallas_call(
        functools.partial(gather_kernel, chips),
        out_shape=(
            jax.ShapeDtypeStruct((width, wq.shape[1]), BF16),
            jax.ShapeDtypeStruct((width, wq.shape[1]), BF16),
            jax.ShapeDtypeStruct((2, chips) + kvg.shape, BF16),
            jax.ShapeDtypeStruct((3, width, part), BF16),
            jax.ShapeDtypeStruct((rows, width), BF16),
            jax.ShapeDtypeStruct((PLANE, rows, width), BF16),
            jax.ShapeDtypeStruct((rows, rows), BF16),
            jax.ShapeDtypeStruct((rows, rows), BF16),
        ),
        in_specs=[VM] * 4 + [ANY] * 6,
        out_specs=(ANY, ANY, ANY, ANY, VM, VM, VM, VM),
        scratch_shapes=[
            pltpu.VMEM((chips, 8, rows), jnp.int32),
            pltpu.VMEM((rows, 2 * width), BF16),
            pltpu.VMEM((rows, 2 * width), BF16),
            dma((chips,)),
            dma((chips,)),
            dma((chips,)),
            dma((chips,)),
            dma((3, groups)),
            dma((3, chips)),
            dma((3, groups, PLANE)),
            dma((2,)),
            dma((3, 2 * groups, 2)),
            dma((3, chips)),
            dma((3, chips)),
            dma((3, chips)),
            dma((2, 3)),
            dma((PLANE,)),
            dma((PLANE,)),
            dma((6,)),
        ],
        compiler_params=pltpu.CompilerParams(
            collective_id=0, has_side_effects=True, vmem_limit_bytes=VMEM_ASK
        ),
        name="gather_weights_and_rows",
    )(deal_rows, deal_col, tokens, cotangent, wq, wot, kvg, gate, up, down)


def rms_scale(values):
    return lax.rsqrt(jnp.mean(values * values, axis=-1, keepdims=True) + EPSILON)


def turned(values, cosine, sine):
    return values * cosine + pltpu.roll(values, HEAD // 2, 1) * sine


def halves_in(first, second):
    front = iota(first.shape, 1) < HEAD // 2
    return (
        jnp.where(front, first, pltpu.roll(second, HEAD // 2, 1)),
        jnp.where(front, pltpu.roll(first, HEAD // 2, 1), second),
    )


def attention_kernel(
    chips,
    reach,
    first_ref,
    rows_ref,
    wq_ref,
    wot_ref,
    kvg_ref,
    cos_ref,
    sin_ref,
    n1_ref,
    qs_ref,
    kv_ref,
    probs_ref,
    mixed_ref,
    middle_ref,
    n2_ref,
    bias_ref,
    branch_out,
    branch_in,
    n1_sems,
    kv_send,
    kv_recv,
    branch_sems,
):
    place = Place(chips)
    d, f, other = place.d, place.f, place.other
    rows, width = rows_ref.shape
    micro = rows // MICRO
    heads = wq_ref.shape[1] // HEAD
    share = width // chips
    slots = 2 * reach + 2
    span = (2 * reach + 1) * micro
    sent = Sent()
    greet_all(place)

    row_values = rows_ref[...].astype(F32)
    gain_one = gain_row(kvg_ref, 0, chips, width, share)
    n1_ref[f] = (row_values * rms_scale(row_values) * gain_one).astype(BF16)
    sent.remote(n1_ref.at[f], n1_ref.at[f], n1_sems.at[0], n1_sems.at[1], (d, other))

    kvw = [kvg_ref[i, :, 0:share, :].reshape(width, HEAD) for i in range(2)]
    raw = [mm(n1_ref[f], kvw[i]) for i in range(2)]
    key_raw, value_raw = halves_in(raw[0], raw[1])
    for m in range(MICRO):
        hm = 2 * f + m
        band = slice(m * micro, (m + 1) * micro)
        key = turned(key_raw[band], cos_ref[hm], sin_ref[hm])
        kv_ref[m, 2 * reach + f, :, 0:HEAD] = key.astype(BF16)
        kv_ref[m, 2 * reach + f, :, HEAD:] = value_raw[band].astype(BF16)
    own_kv = kv_ref.at[:, 2 * reach + f]

    def kv_copy(j, core):
        slot = 2 * reach + f - 2 * j
        return pltpu.make_async_remote_copy(
            src_ref=own_kv,
            dst_ref=kv_ref.at[:, slot],
            send_sem=kv_send.at[j, core],
            recv_sem=kv_recv.at[slot],
            device_id=(d + j, core),
            device_id_type=MESH,
        )

    sent.remote(
        own_kv, own_kv, kv_send.at[0, 0], kv_recv.at[2 * reach + f], (d, other)
    )
    for j in range(1, reach + 1):

        @pl.when(d + j < chips)
        def _():
            for core in range(2):
                kv_copy(j, core).start()

        @pl.when(d - j < 0)
        def _():
            for core in range(2):
                kv_ref[:, 2 * reach - 2 * j + core] = jnp.zeros((MICRO, micro, 2 * HEAD), BF16)

    def project(h):
        raw_q = mm(n1_ref[h], wq_ref[...])
        for m in range(MICRO):
            hm = 2 * h + m
            cosine, sine = cos_ref[hm], sin_ref[hm]
            for i in range(heads):
                one = raw_q[m * micro : (m + 1) * micro, i * HEAD : (i + 1) * HEAD]
                qs_ref[hm, i * micro : (i + 1) * micro, :] = turned(one, cosine, sine).astype(BF16)

    project(f)
    arrived(n1_ref.at[other], n1_sems.at[1])
    project(other)

    def make_bias(hm, carry):
        h, m = hm // 2, hm % 2
        first = first_ref[m]
        query = (2 * d + h) * micro + iota((span, micro), 1)
        key = (2 * d + h - 2 * reach) * micro + iota((span, micro), 0)
        allowed = (
            (jnp.where(query >= first, 1, 0) == jnp.where(key >= first, 1, 0))
            & (key >= 0)
            & (key <= query)
            & (query - key < WINDOW)
        )
        bias_ref[hm] = jnp.where(allowed, 0.0, NEGATIVE)
        return carry

    lax.fori_loop(0, 4, make_bias, 0)
    arrived(kv_ref.at[:, 2 * reach + other], kv_recv.at[2 * reach + other])
    for j in range(1, reach + 1):

        @pl.when(d - j >= 0)
        def _():
            for core in range(2):
                slot = 2 * reach - 2 * j + core
                arrived(kv_ref.at[:, slot], kv_recv.at[slot])

    score_scale = HEAD ** (-0.5)

    def attend(hm, carry):
        h, m = hm // 2, hm % 2
        keys = kv_ref[m, pl.ds(h, 2 * reach + 1), :, 0:HEAD].reshape(span, HEAD)
        values_t = kv_ref[m, pl.ds(h, 2 * reach + 1), :, HEAD:].reshape(span, HEAD).T
        for pair in range(heads // 2):
            band = slice(pair * 2 * micro, (pair + 1) * 2 * micro)
            bias = bias_ref[hm]
            scores = mm_nt(keys, qs_ref[hm, band, :]) * score_scale + jnp.concatenate(
                [bias, bias], axis=1
            )
            exp_scores = jnp.exp(scores - jnp.max(scores, axis=0, keepdims=True))
            total = jnp.sum(exp_scores, axis=0, keepdims=True)
            probs = (exp_scores * (1.0 / total)).astype(BF16)
            probs_ref[hm, :, band] = probs
            out_t = mm(values_t, probs)
            for i in range(2):
                one = out_t[:, i * micro : (i + 1) * micro].T
                head = pair * 2 + i
                mixed_ref[hm, :, head * HEAD : (head + 1) * HEAD] = one.astype(BF16)
        return carry

    lax.fori_loop(0, 4, attend, 0)

    def branch(h):
        return mm_nt(mixed_ref[pl.ds(2 * h, 2)].reshape(rows, heads * HEAD), wot_ref[...])

    branch_out[...] = branch(other).astype(BF16)
    sent.remote(branch_out, branch_in, branch_sems.at[0], branch_sems.at[1], (d, other))
    own = branch(f)
    arrived(branch_in, branch_sems.at[1])
    middle = row_values + own + branch_in[...].astype(F32)
    middle_ref[...] = middle
    gain_two = gain_row(kvg_ref, 1, chips, width, share)
    n2_ref[...] = (middle * rms_scale(middle) * gain_two).astype(BF16)

    for j in range(1, reach + 1):

        @pl.when(d + j < chips)
        def _():
            for core in range(2):
                kv_copy(j, core).wait_send()

    sent.finish()


def attention(chips, reach, first_len, rows_in, wq, wot, kvg, cosine, sine):
    rows, width = rows_in.shape
    micro = rows // MICRO
    heads = wq.shape[1] // HEAD
    slots = 2 * reach + 2
    span = (2 * reach + 1) * micro
    dma = pltpu.SemaphoreType.DMA
    shape = jax.ShapeDtypeStruct
    return pl.pallas_call(
        functools.partial(attention_kernel, chips, reach),
        out_shape=(
            shape((2, rows, width), BF16),
            shape((4, heads * micro, HEAD), BF16),
            shape((MICRO, slots, micro, 2 * HEAD), BF16),
            shape((4, span, heads * micro), BF16),
            shape((4, micro, heads * HEAD), BF16),
            shape((rows, width), F32),
            shape((rows, width), BF16),
        ),
        in_specs=[SM] + [VM] * 6,
        out_specs=(VM,) * 7,
        scratch_shapes=[
            pltpu.VMEM((4, span, micro), F32),
            pltpu.VMEM((rows, width), BF16),
            pltpu.VMEM((rows, width), BF16),
            dma((2,)),
            dma((reach + 1, 2)),
            dma((slots,)),
            dma((2,)),
        ],
        compiler_params=pltpu.CompilerParams(
            collective_id=1, has_side_effects=True, vmem_limit_bytes=VMEM_ASK
        ),
        name="attention_forward",
    )(first_len, rows_in, wq, wot, kvg, cosine, sine)


def mlp_kernel(
    chips,
    n2_ref,
    middle_ref,
    pg_ref,
    three_ref,
    out_ref,
    two_ref,
    grads_ref,
    n2_all,
    turned_ref,
    hidden_ref,
    gate_rows_ref,
    up_rows_ref,
    two_give,
    two_got,
    out_give,
    out_got,
    n2_send,
    n2_recv,
    two_send,
    two_recv,
    out_send,
    out_recv,
):
    place = Place(chips)
    f, p = place.f, place.p
    rows, width = n2_ref.shape
    part = three_ref.shape[2]
    greet_all(place)
    sent = Sent()
    n2_all[p] = n2_ref[...]
    for j in range(1, PLANE):
        sent.remote(
            n2_all.at[p], n2_all.at[p], n2_send.at[j], n2_recv.at[p], (place.plane_chip(j), f)
        )

    def two_copy(j):
        return pltpu.make_async_remote_copy(
            src_ref=two_give.at[j - 1],
            dst_ref=two_got.at[j - 1],
            send_sem=two_send.at[j],
            recv_sem=two_recv.at[j],
            device_id=(place.plane_chip(j), f),
            device_id_type=MESH,
        )

    def out_copy(j):
        return pltpu.make_async_remote_copy(
            src_ref=out_give.at[j - 1],
            dst_ref=out_got.at[j - 1],
            send_sem=out_send.at[j],
            recv_sem=out_recv.at[j],
            device_id=(place.plane_chip(j), f),
            device_id_type=MESH,
        )

    curve = 0.7978845608028654
    cubic = 0.044715

    def one_block(j, carry):
        pos = place.plane_pos(j)

        @pl.when(j > 0)
        def _():
            arrived(n2_all.at[pos], n2_recv.at[pos])

        x = n2_all[pos]
        gate = mm(x, three_ref[0])
        upward = mm(x, three_ref[1])
        grad_hidden = mm(pg_ref[pos], three_ref[2])
        square = gate * gate
        tanh = jnp.tanh(curve * gate * (1.0 + cubic * square))
        activated = 0.5 * gate * (1.0 + tanh)
        slope = 0.5 * (1.0 + tanh) + (0.5 * curve) * gate * (1.0 - tanh * tanh) * (
            1.0 + (3.0 * cubic) * square
        )
        band = pl.ds(pl.multiple_of(pos * rows, rows), rows)
        hidden_ref[band, :] = (activated * upward).astype(BF16)
        gate_rows_ref[band, :] = (grad_hidden * upward * slope).astype(BF16)
        up_rows_ref[band, :] = (grad_hidden * activated).astype(BF16)
        back = mm_nt(gate_rows_ref[band, :], three_ref[0]) + mm_nt(up_rows_ref[band, :], three_ref[1])

        @pl.when(j > 0)
        def _():
            two_give[j - 1] = back.astype(BF16)
            two_copy(j).start()

        @pl.when(j == 0)
        def _():
            two_ref[...] = back

        return carry

    lax.fori_loop(0, PLANE, one_block, 0)

    def out_step(j):
        pos = place.plane_pos(j)
        band = pl.ds(pl.multiple_of(pos * rows, rows), rows)
        return pos, mm_nt(hidden_ref[band, :], three_ref[2])

    def send_out(j, carry):
        pos, piece = out_step(j)
        out_give[j - 1] = piece.astype(BF16)
        out_copy(j).start()
        return carry

    lax.fori_loop(1, PLANE, send_out, 0)
    own_out = middle_ref[...] + out_step(0)[1]

    tile = rows
    tiles = width // tile

    def turn(source, index):
        def step(i, carry):
            at = pl.ds(pl.multiple_of(i * rows, rows), rows)
            turned_ref[:, at] = source[i].T
            return carry

        lax.fori_loop(0, PLANE, step, 0)

    def weight_grad(index, right):
        def step(i, carry):
            at = pl.ds(pl.multiple_of(i * tile, tile), tile)
            grads_ref[index, at, :] = mm(turned_ref[at, :], right[...]).astype(BF16)
            return carry

        lax.fori_loop(0, tiles, step, 0)

    turn(pg_ref, 0)
    weight_grad(2, hidden_ref)
    turn(n2_all, 1)
    weight_grad(0, gate_rows_ref)
    weight_grad(1, up_rows_ref)

    for j in range(1, PLANE):
        arrived(two_got.at[j - 1], two_recv.at[j])
        two_ref[...] = two_ref[...] + two_got[j - 1].astype(F32)
    for j in range(1, PLANE):
        arrived(out_got.at[j - 1], out_recv.at[j])
        own_out = own_out + out_got[j - 1].astype(F32)
    out_ref[...] = own_out.astype(BF16)
    for j in range(1, PLANE):
        two_copy(j).wait_send()
        out_copy(j).wait_send()
    sent.finish()


def mlp(chips, n2, middle, pg_all, three):
    rows, width = n2.shape
    part = three.shape[2]
    dma = pltpu.SemaphoreType.DMA
    shape = jax.ShapeDtypeStruct
    wide = PLANE * rows
    return pl.pallas_call(
        functools.partial(mlp_kernel, chips),
        out_shape=(
            shape((rows, width), BF16),
            shape((rows, width), F32),
            shape((3, width, part), BF16),
        ),
        in_specs=[VM] * 4,
        out_specs=(VM,) * 3,
        scratch_shapes=[
            pltpu.VMEM((PLANE, rows, width), BF16),
            pltpu.VMEM((width, wide), BF16),
            pltpu.VMEM((wide, part), BF16),
            pltpu.VMEM((wide, part), BF16),
            pltpu.VMEM((wide, part), BF16),
        ]
        + [pltpu.VMEM((PLANE - 1, rows, width), BF16)] * 4
        + [dma((PLANE,))] * 6,
        compiler_params=pltpu.CompilerParams(
            collective_id=2, has_side_effects=True, vmem_limit_bytes=VMEM_ASK
        ),
        name="mlp_both_ways",
    )(n2, middle, pg_all, three)


def norm_back(values, gain, grad):
    scale = rms_scale(values)
    unit = values * scale
    lifted = grad * gain
    gain_grad = jnp.sum(grad * unit, axis=0, keepdims=True)
    back = scale * (lifted - unit * jnp.mean(lifted * unit, axis=-1, keepdims=True))
    return back, gain_grad


def attention_back_kernel(
    chips,
    reach,
    rows_ref,
    pg_ref,
    middle_ref,
    two_ref,
    n1_ref,
    qs_ref,
    kv_ref,
    probs_ref,
    mixed_ref,
    wq_ref,
    wot_ref,
    kvg_ref,
    cos_ref,
    sin_ref,
    grad_rows_ref,
    gq_ref,
    got_ref,
    gkvg_ref,
    low_ref,
    lows_t,
    mixed_rows,
    grad_mixed,
    grad_q,
    kv_total,
    kv_give,
    kv_got,
    one_out,
    one_in,
    low_sems,
    kv_send,
    kv_recv,
    one_sems,
):
    place = Place(chips)
    d, f, other = place.d, place.f, place.other
    rows, width = rows_ref.shape
    micro = rows // MICRO
    heads = wq_ref.shape[1] // HEAD
    share = width // chips
    slots = 2 * reach + 2
    span = (2 * reach + 1) * micro
    sent = Sent()
    greet_all(place)

    gain_two = gain_row(kvg_ref, 1, chips, width, share)
    back, gain_two_grad = norm_back(middle_ref[...], gain_two, two_ref[...])
    grad_middle = pg_ref[...].astype(F32) + back
    low_ref[f] = grad_middle.astype(BF16)
    sent.remote(low_ref.at[f], low_ref.at[f], low_sems.at[0], low_sems.at[1], (d, other))
    kv_total[...] = jnp.zeros_like(kv_total)

    def mix_back(h):
        grads = mm(low_ref[h], wot_ref[...])
        for m in range(MICRO):
            for i in range(heads):
                grad_mixed[2 * h + m, i * micro : (i + 1) * micro, :] = grads[
                    m * micro : (m + 1) * micro, i * HEAD : (i + 1) * HEAD
                ].astype(BF16)

    mix_back(f)
    arrived(low_ref.at[other], low_sems.at[1])
    mix_back(other)

    score_scale = HEAD ** (-0.5)

    def attend_back(hm, carry):
        h, m = hm // 2, hm % 2
        at = pl.ds(h, 2 * reach + 1)
        keys = kv_ref[m, at, :, 0:HEAD].reshape(span, HEAD)
        values = kv_ref[m, at, :, HEAD:].reshape(span, HEAD)
        keys_t = keys.T
        key_total = jnp.zeros((span, HEAD), F32)
        value_total = jnp.zeros((span, HEAD), F32)
        for pair in range(heads // 2):
            band = slice(pair * 2 * micro, (pair + 1) * 2 * micro)
            probs = probs_ref[hm, :, band]
            grads = grad_mixed[hm, band, :]
            queries = qs_ref[hm, band, :]
            value_total = value_total + mm(probs, grads)
            grad_probs = mm_nt(values, grads)
            wide = probs.astype(F32)
            delta = jnp.sum(grad_probs * wide, axis=0, keepdims=True)
            grad_scores = (wide * (grad_probs - delta)).astype(BF16)
            key_total = key_total + mm(grad_scores, queries)
            query_t = mm(keys_t, grad_scores) * score_scale
            for i in range(2):
                head = pair * 2 + i
                one = query_t[:, i * micro : (i + 1) * micro].T
                grad_q[hm, :, head * HEAD : (head + 1) * HEAD] = turned(
                    one, cos_ref[hm], -sin_ref[hm]
                ).astype(BF16)
        key_total = (key_total * score_scale).reshape(2 * reach + 1, micro, HEAD)
        kv_total[m, at, :, 0:HEAD] = kv_total[m, at, :, 0:HEAD] + key_total
        kv_total[m, at, :, HEAD:] = kv_total[m, at, :, HEAD:] + value_total.reshape(
            2 * reach + 1, micro, HEAD
        )
        return carry

    lax.fori_loop(0, 4, attend_back, 0)

    kv_give[...] = kv_total[...].astype(BF16)

    def kv_copy(j, core):
        return pltpu.make_async_remote_copy(
            src_ref=kv_give.at[:, 2 * reach - 2 * j + core],
            dst_ref=kv_got.at[2 * j + f],
            send_sem=kv_send.at[j, core],
            recv_sem=kv_recv.at[2 * j + f],
            device_id=(d - j, core),
            device_id_type=MESH,
        )

    sent.remote(
        kv_give.at[:, 2 * reach + other],
        kv_got.at[f],
        kv_send.at[0, 0],
        kv_recv.at[f],
        (d, other),
    )
    for j in range(1, reach + 1):

        @pl.when(d - j >= 0)
        def _():
            for core in range(2):
                kv_copy(j, core).start()

    lows_t[:, 0:rows] = low_ref[0].T
    lows_t[:, rows:] = low_ref[1].T
    tile = 2 * HEAD
    for hm in range(4):
        mixed_rows[hm * micro : (hm + 1) * micro, :] = mixed_ref[hm]

    def out_tile(i, carry):
        at = pl.ds(pl.multiple_of(i * tile, tile), tile)
        got_ref[at, :] = mm(lows_t[at, :], mixed_rows[...]).astype(BF16)
        return carry

    lax.fori_loop(0, width // tile, out_tile, 0)
    lows_t[:, 0:rows] = n1_ref[0].T
    lows_t[:, rows:] = n1_ref[1].T
    for hm in range(4):
        mixed_rows[hm * micro : (hm + 1) * micro, :] = grad_q[hm]

    def query_tile(i, carry):
        at = pl.ds(pl.multiple_of(i * tile, tile), tile)
        gq_ref[at, :] = mm(lows_t[at, :], mixed_rows[...]).astype(BF16)
        return carry

    lax.fori_loop(0, width // tile, query_tile, 0)

    def one_back(h):
        band = pl.ds(pl.multiple_of(h * rows, rows), rows)
        return mm_nt(mixed_rows[band, :], wq_ref[...])

    one_out[...] = one_back(other).astype(BF16)
    sent.remote(one_out, one_in, one_sems.at[0], one_sems.at[1], (d, other))
    grad_one = one_back(f)

    sums = [kv_total[m, 2 * reach + f] for m in range(MICRO)]
    arrived(kv_got.at[other], kv_recv.at[other])
    sums = [sums[m] + kv_got[other, m].astype(F32) for m in range(MICRO)]
    for j in range(1, reach + 1):
        for core in range(2):
            slot = 2 * j + core

            @pl.when(d + j < chips)
            def _():
                arrived(kv_got.at[slot], kv_recv.at[slot])

            @pl.when(d + j >= chips)
            def _():
                kv_got[slot] = jnp.zeros((MICRO, micro, 2 * HEAD), BF16)

            sums = [sums[m] + kv_got[slot, m].astype(F32) for m in range(MICRO)]
    key_rows = jnp.concatenate(
        [
            turned(sums[m][:, 0:HEAD], cos_ref[2 * f + m], -sin_ref[2 * f + m])
            for m in range(MICRO)
        ],
        axis=0,
    )
    value_rows = jnp.concatenate([sums[m][:, HEAD:] for m in range(MICRO)], axis=0)
    pieces = halves_in(key_rows, value_rows)
    n1_own_t = n1_ref[f].T
    row_values = rows_ref[...].astype(F32)
    for i in range(2):
        piece = pieces[i].astype(BF16)
        gkvg_ref[i, :, 0:share, :] = (
            mm(n1_own_t, piece).astype(BF16).reshape(chips, share, HEAD)
        )
        grad_one = grad_one + mm_nt(piece, kvg_ref[i, :, 0:share, :].reshape(width, HEAD))
    arrived(one_in, one_sems.at[1])
    grad_one = grad_one + one_in[...].astype(F32)
    gain_one = gain_row(kvg_ref, 0, chips, width, share)
    back_one, gain_one_grad = norm_back(row_values, gain_one, grad_one)
    grad_rows_ref[...] = (grad_middle + back_one).astype(BF16)
    spread = gain_spread(width, share)
    stretch = own_stretch(chips, width, share)
    for i, grad in enumerate((gain_one_grad, gain_two_grad)):
        piece = mm_nt(jnp.where(stretch, grad, 0.0).astype(BF16), spread)
        row = iota((chips, 16, HEAD), 1)
        gkvg_ref[i, :, share : share + 16, :] = jnp.where(
            row == 0, piece[:, None, :], 0.0
        ).astype(BF16)

    for j in range(1, reach + 1):

        @pl.when(d - j >= 0)
        def _():
            for core in range(2):
                kv_copy(j, core).wait_send()

    sent.finish()


def attention_back(chips, reach, rows_in, pg, middle, two, n1, qs, kv, probs, mixed, wq, wot, kvg, cosine, sine):
    rows, width = rows_in.shape
    micro = rows // MICRO
    heads = wq.shape[1] // HEAD
    slots = 2 * reach + 2
    dma = pltpu.SemaphoreType.DMA
    shape = jax.ShapeDtypeStruct
    return pl.pallas_call(
        functools.partial(attention_back_kernel, chips, reach),
        out_shape=(
            shape((rows, width), BF16),
            shape(wq.shape, BF16),
            shape(wot.shape, BF16),
            shape(kvg.shape, BF16),
        ),
        in_specs=[VM] * 14,
        out_specs=(VM,) * 4,
        scratch_shapes=[
            pltpu.VMEM((2, rows, width), BF16),
            pltpu.VMEM((width, 2 * rows), BF16),
            pltpu.VMEM((2 * rows, heads * HEAD), BF16),
            pltpu.VMEM((4, heads * micro, HEAD), BF16),
            pltpu.VMEM((4, micro, heads * HEAD), BF16),
            pltpu.VMEM((MICRO, slots, micro, 2 * HEAD), F32),
            pltpu.VMEM((MICRO, slots, micro, 2 * HEAD), BF16),
            pltpu.VMEM((slots, MICRO, micro, 2 * HEAD), BF16),
            pltpu.VMEM((rows, width), BF16),
            pltpu.VMEM((rows, width), BF16),
            dma((2,)),
            dma((reach + 1, 2)),
            dma((slots,)),
            dma((2,)),
        ],
        compiler_params=pltpu.CompilerParams(
            collective_id=3, has_side_effects=True, vmem_limit_bytes=VMEM_ASK
        ),
        name="attention_backward",
    )(rows_in, pg, middle, two, n1, qs, kv, probs, mixed, wq, wot, kvg, cosine, sine)


def scatter_kernel(
    chips,
    three_ref,
    gq_ref,
    got_ref,
    gkvg_ref,
    outs_ref,
    grad_rows_ref,
    take_ref,
    place_ref,
    three_out,
    q_out,
    ot_out,
    kvg_out,
    output_ref,
    input_grad_ref,
    pair_got,
    three_give,
    three_got,
    kvg_got,
    attn_got,
    attn_give,
    attn_last,
    kvg_fan,
    kvg_give,
    kvg_last,
    give,
    got,
    pair_send,
    pair_recv,
    three_send,
    three_recv,
    kvg_sems,
    fan_send,
    fan_recv,
    column_send,
    column_recv,
    row_send,
    row_recv,
):
    place = Place(chips)
    d, f, other = place.d, place.f, place.other
    groups = place.groups
    rows, width = outs_ref.shape
    share = width // chips
    half = share // 2
    part = three_ref.shape[2]
    per = rows // chips
    sent = Sent()
    greet_all(place)

    def order(k, j):
        return ((place.g + k) % groups) * PLANE + place.plane_pos(j)

    def band(s, core):
        return pl.ds(pl.multiple_of(s * share + half * core, 16), half)

    steps = [(k, j) for k in range(groups) for j in range(PLANE)]
    steps = steps[1:] + steps[:1]
    sent.remote(gkvg_ref.at[other], kvg_got, kvg_sems.at[0], kvg_sems.at[1], (d, other))
    for k, j in steps:
        s = order(k, j)
        sent.remote(
            three_ref.at[:, band(s, other)],
            pair_got.at[s],
            pair_send.at[s],
            pair_recv.at[s],
            (d, other),
        )

    def whole(s):
        return pl.ds(pl.multiple_of(s * share, 16), share)

    attn = (gq_ref, got_ref)
    for j in range(1, PLANE):
        to = place.plane_pos(j)
        for k in range(groups):
            s = ((place.g + k) % groups) * PLANE + to
            for a in range(2):
                sent.remote(
                    attn[a].at[whole(s)],
                    attn_got.at[a, j, s // PLANE],
                    fan_send.at[a, j, k],
                    fan_recv.at[a, j, s // PLANE],
                    (place.plane_chip(j), f),
                )

    def block(k):
        return pl.ds(pl.multiple_of(k * per, per), per)

    give[:, :width] = mm_tn(place_ref[...], outs_ref[...]).astype(BF16)
    give[:, width:] = mm_tn(place_ref[...], grad_rows_ref[...]).astype(BF16)
    for k in range(1, chips):
        to = (d + k) % chips
        sent.remote(give.at[block(to)], got.at[block(d)], row_send.at[k], row_recv.at[d], (to, f))
    got[block(d), :] = give[block(d), :]

    arrived(kvg_got, kvg_sems.at[1])
    for s in range(chips):
        kvg_give[s] = (gkvg_ref[f, s].astype(F32) + kvg_got[s].astype(F32)).astype(BF16)
    for j in range(1, PLANE):
        to = place.plane_pos(j)
        for k in range(groups):
            s = ((place.g + k) % groups) * PLANE + to
            sent.remote(
                kvg_give.at[s],
                kvg_fan.at[j, s // PLANE],
                fan_send.at[2, j, k],
                fan_recv.at[2, j, s // PLANE],
                (place.plane_chip(j), f),
            )

    def three_slot(j_x, k):
        return 2 * k + j_x

    for n, (k, j) in enumerate(steps):
        s = order(k, j)
        arrived(pair_got.at[s], pair_recv.at[s])
        for a in range(3):
            three_give[s, a] = (
                three_ref[a, band(s, f), :].astype(F32) + pair_got[s, a].astype(F32)
            ).astype(BF16)
        dst = three_got.at[2 * place.g + place.x, f]
        recv = three_recv.at[2 * place.g + place.x, f]
        if (k, j) == (0, 0):
            remote = pltpu.make_async_remote_copy(
                src_ref=three_give.at[s],
                dst_ref=dst,
                send_sem=three_send.at[s],
                recv_sem=recv,
                device_id=(d, other),
                device_id_type=MESH,
            )

            @pl.when(place.y != f)
            def _():
                remote.start()

            @pl.when(place.y == f)
            def _():
                three_got[2 * place.g + place.x, f] = three_give[s]

            own_remote = remote
        else:
            sent.remote(three_give.at[s], dst, three_send.at[s], recv, (s, place.y))

    for k in list(range(1, groups)) + [0]:
        g = (place.g + k) % groups
        s = g * PLANE + place.p
        for a in range(2):
            total = attn[a][whole(s), :].astype(F32)
            for j in range(1, PLANE):
                arrived(attn_got.at[a, j, g], fan_recv.at[a, j, g])
                total = total + attn_got[a, j, g].astype(F32)
            if k == 0:
                (q_out, ot_out)[a][...] = total
            else:
                attn_give[a, g] = total.astype(BF16)
                sent.remote(
                    attn_give.at[a, g],
                    attn_last.at[a, place.g],
                    column_send.at[a, k],
                    column_recv.at[a, place.g],
                    (s, f),
                )
        total = kvg_give[s].astype(F32)
        for j in range(1, PLANE):
            arrived(kvg_fan.at[j, g], fan_recv.at[2, j, g])
            total = total + kvg_fan[j, g].astype(F32)
        if k == 0:
            kvg_out[...] = total
        else:
            kvg_give[s] = total.astype(BF16)
            sent.remote(
                kvg_give.at[s],
                kvg_last.at[place.g],
                column_send.at[2, k],
                column_recv.at[2, place.g],
                (s, f),
            )

    for k in range(1, chips):
        s = (d + k) % chips
        arrived(got.at[block(s)], row_recv.at[s])
    output_ref[...] = mm_tn(take_ref[...], got[:, :width]).astype(BF16)
    input_grad_ref[...] = mm_tn(take_ref[...], got[:, width:]).astype(BF16)

    for k in range(1, groups):
        g = (place.g + k) % groups
        for a in range(2):
            arrived(attn_last.at[a, g], column_recv.at[a, g])
            out = (q_out, ot_out)[a]
            out[...] = out[...] + attn_last[a, g].astype(F32)
        arrived(kvg_last.at[g], column_recv.at[2, g])
        kvg_out[...] = kvg_out[...] + kvg_last[g].astype(F32)

    for cx in range(2):
        for core in range(2):
            for k in range(groups):
                g = (place.g + k) % groups
                slot = 2 * g + cx
                piece = three_got.at[slot, core]

                if k == 0:
                    @pl.when((place.y != f) | (place.x != cx) | (core != f))
                    def _():
                        arrived(piece, three_recv.at[slot, core])
                else:
                    arrived(piece, three_recv.at[slot, core])
            for a in range(3):
                total = three_got[cx, core, a].astype(F32)
                for g in range(1, groups):
                    total = total + three_got[2 * g + cx, core, a].astype(F32)
                three_out[a, half * core : half * (core + 1), cx * part : (cx + 1) * part] = total

    @pl.when(place.y != f)
    def _():
        own_remote.wait_send()

    sent.finish()


def scatter(chips, three, gq, got, gkvg, outs, grad_rows, take, placing):
    rows, width = outs.shape
    share = width // chips
    half = share // 2
    part = three.shape[2]
    groups = chips // PLANE
    heads_wide = gq.shape[1]
    small = gkvg.shape[2:]
    dma = pltpu.SemaphoreType.DMA
    shape = jax.ShapeDtypeStruct
    return pl.pallas_call(
        functools.partial(scatter_kernel, chips),
        out_shape=(
            shape((3, share, 2 * part), F32),
            shape((share, heads_wide), F32),
            shape((share, heads_wide), F32),
            shape(small, F32),
            shape((rows, width), BF16),
            shape((rows, width), BF16),
        ),
        in_specs=[VM] * 8,
        out_specs=(VM,) * 6,
        scratch_shapes=[
            pltpu.VMEM((chips, 3, half, part), BF16),
            pltpu.VMEM((chips, 3, half, part), BF16),
            pltpu.VMEM((2 * groups, 2, 3, half, part), BF16),
            pltpu.VMEM((chips,) + small, BF16),
            pltpu.VMEM((2, PLANE, groups, share, heads_wide), BF16),
            pltpu.VMEM((2, groups, share, heads_wide), BF16),
            pltpu.VMEM((2, groups, share, heads_wide), BF16),
            pltpu.VMEM((PLANE, groups) + small, BF16),
            pltpu.VMEM((chips,) + small, BF16),
            pltpu.VMEM((groups,) + small, BF16),
            pltpu.VMEM((rows, 2 * width), BF16),
            pltpu.VMEM((rows, 2 * width), BF16),
            dma((chips,)),
            dma((chips,)),
            dma((chips,)),
            dma((2 * groups, 2)),
            dma((2,)),
            dma((3, PLANE, groups)),
            dma((3, PLANE, groups)),
            dma((3, groups)),
            dma((3, groups)),
            dma((chips,)),
            dma((chips,)),
        ],
        compiler_params=pltpu.CompilerParams(
            collective_id=4, has_side_effects=True, vmem_limit_bytes=VMEM_ASK
        ),
        name="scatter_grads_and_rows",
    )(three, gq, got, gkvg, outs, grad_rows, take, placing)


def planned(
    tokens,
    cotangent,
    deal,
    first_len,
    w_query,
    w_key,
    w_value,
    w_out,
    w_gate,
    w_up,
    w_down,
    norm_gains,
):
    chips = lax.axis_size("dp")
    rows, width = tokens.shape
    micro = rows // MICRO
    share = w_query.shape[0]
    back_blocks = min(2 * chips - 1, (WINDOW + micro - 2) // micro)
    reach = (back_blocks + 1) // 2
    d = lax.axis_index("dp")
    inside = jnp.arange(micro, dtype=jnp.int32)
    positions = (2 * d + jnp.arange(2, dtype=jnp.int32))[:, None, None] * micro + inside
    second = positions >= first_len[None, :, None]
    within = positions - jnp.where(second, first_len[None, :, None], 0)
    cosine, sine = angles(within.reshape(-1))
    cosine = jnp.concatenate([cosine, cosine], axis=1).reshape(4, micro, HEAD)
    sine = jnp.concatenate([-sine, sine], axis=1).reshape(4, micro, HEAD)
    gain_rows = jnp.pad(norm_gains, ((0, 15), (0, HEAD - share)))
    kvg = jnp.concatenate([jnp.concatenate([w_key, w_value], axis=1), gain_rows], axis=0)
    wq, wot, kvg_all, three, rows_in, pg_all, take, placing = gather(
        chips, deal, tokens, cotangent, w_query, w_out.T, kvg, w_gate, w_up, w_down.T
    )
    n1, qs, kv, probs, mixed, middle, n2 = attention(
        chips, reach, first_len, rows_in, wq, wot, kvg_all, cosine, sine
    )
    outs, grad_two, three_grads = mlp(chips, n2, middle, pg_all, three)
    pg = lax.dynamic_index_in_dim(pg_all, d % PLANE, 0, keepdims=False)
    grad_rows, gq, got, gkvg = attention_back(
        chips, reach, rows_in, pg, middle, grad_two, n1, qs, kv, probs, mixed, wq, wot, kvg_all,
        cosine, sine,
    )
    three_out, q_out, ot_out, kvg_out, output, input_grad = scatter(
        chips, three_grads, gq, got, gkvg, outs, grad_rows, take, placing
    )
    key_cols = w_key.shape[1]
    return (
        output,
        input_grad,
        q_out,
        kvg_out[:share, :key_cols],
        kvg_out[:share, key_cols:],
        ot_out.T,
        three_out[0],
        three_out[1],
        three_out[2].T,
        kvg_out[share : share + 1, :share],
    )


def fits_plan(mesh, share):
    chips = mesh.shape["dp"]
    return mesh.shape["fsdp"] == 2 and chips % PLANE == 0 and share % 32 == 0 and share < HEAD


def solution(mesh):
    in_specs = (
        P(("dp", "fsdp"), None),
        P(("dp", "fsdp"), None),
        P(("dp", "fsdp")),
        P(),
        P("dp", "fsdp"),
        P("dp", "fsdp"),
        P("dp", "fsdp"),
        P("fsdp", "dp"),
        P("dp", "fsdp"),
        P("dp", "fsdp"),
        P("fsdp", "dp"),
        P("fsdp", "dp"),
    )
    out_specs = (
        P(("dp", "fsdp"), None),
        P(("dp", "fsdp"), None),
        P("dp", "fsdp"),
        P("dp", "fsdp"),
        P("dp", "fsdp"),
        P("fsdp", "dp"),
        P("dp", "fsdp"),
        P("dp", "fsdp"),
        P("fsdp", "dp"),
        P("fsdp", "dp"),
    )
    def placed(*arrays):
        share = arrays[4].shape[0] // mesh.shape["dp"]
        program = planned if fits_plan(mesh, share) else per_device
        return jax.shard_map(
            program, mesh=mesh, in_specs=in_specs, out_specs=out_specs, check_vma=False
        )(*arrays)

    return placed
```

```python
import functools

import jax
import jax.numpy as jnp
from jax import lax
from jax.experimental import pallas as pl
from jax.experimental.pallas import tpu as pltpu
from jax.sharding import PartitionSpec as P

HEADS = 12
HEAD = 128
WINDOW = 1024
MICRO = 2


EPSILON = 1e-06
NEGATIVE = -1e30
VMEM_ASK = 62 * 2**20


def passed_along(x, axis, by):
    count = lax.axis_size(axis)
    pairs = [(i, i + by) for i in range(count) if 0 <= i + by < count]
    return lax.ppermute(x, axis, pairs)


def normed(row_values, gain_row):
    return (
        row_values
        * lax.rsqrt(jnp.mean(row_values * row_values, axis=-1, keepdims=True) + EPSILON)
        * gain_row
    )


def rotate(values, cosine, sine_table):
    half_width = values.shape[-1] // 2
    front_half = values[..., :half_width]
    back_half = values[..., half_width:]
    return jnp.concatenate(
        [
            front_half * cosine - back_half * sine_table,
            back_half * cosine + front_half * sine_table,
        ],
        axis=-1,
    )


def angles(places):
    half_width = HEAD // 2
    frequency = 10000.0 ** (-jnp.arange(half_width, dtype=jnp.float32) * 2.0 / HEAD)
    angle_rows = places.astype(jnp.float32)[:, None] * frequency[None, :]
    return (jnp.cos(angle_rows), jnp.sin(angle_rows))


def contract_rows(left, right):
    return lax.dot_general(
        left, right, (((0,), (0,)), ((), ())), preferred_element_type=jnp.float32
    )


def against(left, right):
    return lax.dot_general(
        left, right, (((1,), (1,)), ((), ())), preferred_element_type=jnp.float32
    )


def gelu_tanh(inputs):
    return jax.nn.gelu(inputs, approximate=True)


def per_device(
    tokens,
    cotangent,
    deal,
    first_len,
    w_query,
    w_key,
    w_value,
    w_out,
    w_gate,
    w_up,
    w_down,
    norm_gains,
):
    peer_count = lax.axis_size("dp")
    core_count = lax.axis_size("fsdp")
    device_total = peer_count * core_count
    row_count = tokens.shape[0]
    model_width = tokens.shape[1]
    per_peer = row_count // peer_count
    micro_rows = row_count // MICRO
    reach_steps = min(device_total - 1, (WINDOW + micro_rows - 2) // micro_rows)
    linear = lax.axis_index("dp") * core_count + lax.axis_index("fsdp")
    source_peer = deal // (row_count * core_count)
    offsets = deal % row_count
    bucket_order = jnp.argsort(source_peer, stable=True)
    inverse = jnp.argsort(bucket_order)
    wanted = offsets[bucket_order].reshape(peer_count, per_peer)
    requested = lax.all_to_all(wanted, "dp", split_axis=0, concat_axis=0, tiled=True)
    picked = requested.reshape(-1)
    fetched = (
        lax.all_to_all(
            tokens[picked].reshape(peer_count, per_peer, model_width),
            "dp",
            split_axis=0,
            concat_axis=0,
            tiled=True,
        ),
        lax.all_to_all(
            cotangent[picked].reshape(peer_count, per_peer, model_width),
            "dp",
            split_axis=0,
            concat_axis=0,
            tiled=True,
        ),
    )
    rows_in = fetched[0].reshape(row_count, model_width)[inverse]
    grad_in = fetched[1].reshape(row_count, model_width)[inverse]
    halves = (
        lax.all_gather(w_query, "dp", axis=0, tiled=True),
        lax.all_gather(w_key, "dp", axis=0, tiled=True),
        lax.all_gather(w_value, "dp", axis=0, tiled=True),
        lax.all_gather(w_out, "dp", axis=1, tiled=True),
        lax.all_gather(w_gate, "dp", axis=0, tiled=True),
        lax.all_gather(w_up, "dp", axis=0, tiled=True),
        lax.all_gather(w_down, "dp", axis=1, tiled=True),
        lax.all_gather(norm_gains, "dp", axis=1, tiled=True),
    )
    gathered = (
        lax.all_gather(halves[0], "fsdp", axis=1, tiled=True),
        lax.all_gather(halves[1], "fsdp", axis=1, tiled=True),
        lax.all_gather(halves[2], "fsdp", axis=1, tiled=True),
        lax.all_gather(halves[3], "fsdp", axis=0, tiled=True),
        lax.all_gather(halves[4], "fsdp", axis=1, tiled=True),
        lax.all_gather(halves[5], "fsdp", axis=1, tiled=True),
        lax.all_gather(halves[6], "fsdp", axis=0, tiled=True),
        lax.all_gather(halves[7], "fsdp", axis=0, tiled=True),
    )
    full_query, full_key, full_value, full_out, full_gate, full_up, full_down, full_gains = gathered
    gain_one = full_gains[0].astype(jnp.float32)
    gain_two = full_gains[1].astype(jnp.float32)
    inside = jnp.arange(micro_rows, dtype=jnp.int32)
    query_place = linear * micro_rows + inside
    query_later = query_place[None, :] >= first_len[:, None]
    query_within = query_place[None, :] - jnp.where(query_later, first_len[:, None], 0)
    distance = jnp.arange(reach_steps, -1, -1, dtype=jnp.int32)
    key_place = ((linear - distance)[:, None] * micro_rows + inside[None, :]).reshape(-1)
    key_later = key_place[None, :] >= first_len[:, None]
    allowed = (
        (query_later[:, :, None] == key_later[:, None, :])
        & (key_place[None, None, :] >= 0)
        & (key_place[None, None, :] <= query_place[None, :, None])
        & (query_place[None, :, None] - key_place[None, None, :] < WINDOW)
    )
    rows_float = rows_in.astype(jnp.float32)
    cosine, sine_table = angles(query_within.reshape(-1))
    score_scale = HEAD ** (-0.5)
    normal_one = normed(rows_float, gain_one).astype(jnp.bfloat16)
    query_raw = jnp.dot(normal_one, full_query, preferred_element_type=jnp.float32).reshape(
        row_count, HEADS, HEAD
    )
    query_rows = rotate(query_raw, cosine[:, None, :], sine_table[:, None, :]).astype(jnp.bfloat16)
    key_rows = rotate(
        jnp.dot(normal_one, full_key, preferred_element_type=jnp.float32), cosine, sine_table
    ).astype(jnp.bfloat16)
    value_rows = jnp.dot(normal_one, full_value, preferred_element_type=jnp.float32).astype(
        jnp.bfloat16
    )
    earlier = []
    for distance_step in range(1, reach_steps + 1):
        earlier.append(passed_along((key_rows, value_rows), ("dp", "fsdp"), distance_step))
    ordered = earlier[::-1] + [(key_rows, value_rows)]
    all_keys = jnp.concatenate(
        [member[0].reshape(MICRO, micro_rows, HEAD) for member in ordered], axis=1
    )
    all_values = jnp.concatenate(
        [member[1].reshape(MICRO, micro_rows, HEAD) for member in ordered], axis=1
    )
    by_head = jnp.transpose(query_rows.reshape(MICRO, micro_rows, HEADS, HEAD), (2, 0, 1, 3))

    def attend(query_head):
        scores = jnp.where(
            allowed,
            jnp.einsum("mqd,mkd->mqk", query_head, all_keys, preferred_element_type=jnp.float32)
            * score_scale,
            NEGATIVE,
        )
        row_top = jnp.max(scores, axis=2, keepdims=True)
        exp_scores = jnp.exp(scores - row_top)
        row_total = jnp.sum(exp_scores, axis=2, keepdims=True)
        soft_weights = (exp_scores / row_total).astype(jnp.bfloat16)
        attended_head = jnp.einsum(
            "mqk,mkd->mqd", soft_weights, all_values, preferred_element_type=jnp.float32
        )
        return (attended_head, row_top[..., 0] + jnp.log(row_total[..., 0]))

    attended, log_total = lax.map(attend, by_head)
    mixed_heads = (
        jnp.transpose(attended, (1, 2, 0, 3)).reshape(row_count, HEADS * HEAD).astype(jnp.bfloat16)
    )
    middle = rows_float + jnp.dot(mixed_heads, full_out, preferred_element_type=jnp.float32)
    normal_two = normed(middle, gain_two).astype(jnp.bfloat16)
    gate_rows = jnp.dot(normal_two, full_gate, preferred_element_type=jnp.float32)
    upward = jnp.dot(normal_two, full_up, preferred_element_type=jnp.float32)
    activated = gelu_tanh(gate_rows)
    hidden = (activated * upward).astype(jnp.bfloat16)
    result = (middle + jnp.dot(hidden, full_down, preferred_element_type=jnp.float32)).astype(
        jnp.bfloat16
    )
    grad_float = grad_in.astype(jnp.float32)
    grad_down = contract_rows(hidden, grad_in)
    grad_hidden = against(grad_in, full_down)
    gelu_value, gelu_pull = jax.vjp(gelu_tanh, gate_rows)
    grad_gate_rows = gelu_pull(grad_hidden * upward)[0].astype(jnp.bfloat16)
    grad_up_rows = (grad_hidden * activated).astype(jnp.bfloat16)
    grad_gate = contract_rows(normal_two, grad_gate_rows)
    grad_up = contract_rows(normal_two, grad_up_rows)
    grad_two = against(grad_gate_rows, full_gate) + against(grad_up_rows, full_up)
    norm_value, norm_pull = jax.vjp(normed, middle, gain_two)
    grad_middle_norm, gain_two_grad = norm_pull(grad_two)
    grad_middle = grad_float + grad_middle_norm
    grad_middle_low = grad_middle.astype(jnp.bfloat16)
    grad_out = contract_rows(mixed_heads, grad_middle_low)
    grad_mixed = against(grad_middle_low, full_out).astype(jnp.bfloat16)
    grad_by_head = jnp.transpose(grad_mixed.reshape(MICRO, micro_rows, HEADS, HEAD), (2, 0, 1, 3))

    def attend_back(running, pieces):
        key_total, value_total = running
        query_head, grad_head, total_head = pieces
        scores = (
            jnp.einsum("mqd,mkd->mqk", query_head, all_keys, preferred_element_type=jnp.float32)
            * score_scale
        )
        soft_weights = jnp.where(allowed, jnp.exp(scores - total_head[..., None]), 0.0)
        value_total = value_total + jnp.einsum(
            "mqk,mqd->mkd",
            soft_weights.astype(jnp.bfloat16),
            grad_head,
            preferred_element_type=jnp.float32,
        )
        grad_soft = jnp.einsum(
            "mqd,mkd->mqk", grad_head, all_values, preferred_element_type=jnp.float32
        )
        row_delta = jnp.sum(grad_soft * soft_weights, axis=2, keepdims=True)
        grad_scores = (soft_weights * (grad_soft - row_delta)).astype(jnp.bfloat16)
        grad_query_head = (
            jnp.einsum("mqk,mkd->mqd", grad_scores, all_keys, preferred_element_type=jnp.float32)
            * score_scale
        )
        key_total = (
            key_total
            + jnp.einsum(
                "mqk,mqd->mkd", grad_scores, query_head, preferred_element_type=jnp.float32
            )
            * score_scale
        )
        return ((key_total, value_total), grad_query_head)

    zero_block = jnp.zeros((MICRO, (reach_steps + 1) * micro_rows, HEAD), jnp.float32)
    totals, grad_query_heads = lax.scan(
        attend_back, (zero_block, zero_block), (by_head, grad_by_head, log_total)
    )
    key_total, value_total = totals

    def piece_of(total, distance_step):
        begin_row = (reach_steps - distance_step) * micro_rows
        return total[:, begin_row : begin_row + micro_rows].reshape(row_count, HEAD)

    own_key = piece_of(key_total, 0)
    own_value = piece_of(value_total, 0)
    for distance_step in range(1, reach_steps + 1):
        returned_pair = (
            passed_along(
                piece_of(key_total, distance_step).astype(jnp.bfloat16),
                ("dp", "fsdp"),
                -distance_step,
            ).astype(jnp.float32),
            passed_along(
                piece_of(value_total, distance_step).astype(jnp.bfloat16),
                ("dp", "fsdp"),
                -distance_step,
            ).astype(jnp.float32),
        )
        own_key = own_key + returned_pair[0]
        own_value = own_value + returned_pair[1]
    grad_value_rows = own_value.astype(jnp.bfloat16)
    grad_query_rot = jnp.transpose(grad_query_heads, (1, 2, 0, 3)).reshape(row_count, HEADS, HEAD)
    grad_query_raw = (
        rotate(grad_query_rot, cosine[:, None, :], -sine_table[:, None, :])
        .reshape(row_count, HEADS * HEAD)
        .astype(jnp.bfloat16)
    )
    grad_key_raw = rotate(own_key, cosine, -sine_table).astype(jnp.bfloat16)
    grad_query = contract_rows(normal_one, grad_query_raw)
    grad_key = contract_rows(normal_one, grad_key_raw)
    grad_value = contract_rows(normal_one, grad_value_rows)
    grad_one = (
        against(grad_query_raw, full_query)
        + against(grad_key_raw, full_key)
        + against(grad_value_rows, full_value)
    )
    first_value, first_pull = jax.vjp(normed, rows_float, gain_one)
    grad_rows_norm, gain_one_grad = first_pull(grad_one)
    grad_rows = (grad_middle + grad_rows_norm).astype(jnp.bfloat16)
    grad_gains = jnp.stack([gain_one_grad, gain_two_grad])
    sectioned = (
        lax.psum_scatter(
            grad_query.astype(jnp.bfloat16), "fsdp", scatter_dimension=1, tiled=True
        ).astype(jnp.float32),
        lax.psum_scatter(
            grad_key.astype(jnp.bfloat16), "fsdp", scatter_dimension=1, tiled=True
        ).astype(jnp.float32),
        lax.psum_scatter(
            grad_value.astype(jnp.bfloat16), "fsdp", scatter_dimension=1, tiled=True
        ).astype(jnp.float32),
        lax.psum_scatter(
            grad_out.astype(jnp.bfloat16), "fsdp", scatter_dimension=0, tiled=True
        ).astype(jnp.float32),
        lax.psum_scatter(
            grad_gate.astype(jnp.bfloat16), "fsdp", scatter_dimension=1, tiled=True
        ).astype(jnp.float32),
        lax.psum_scatter(
            grad_up.astype(jnp.bfloat16), "fsdp", scatter_dimension=1, tiled=True
        ).astype(jnp.float32),
        lax.psum_scatter(
            grad_down.astype(jnp.bfloat16), "fsdp", scatter_dimension=0, tiled=True
        ).astype(jnp.float32),
        lax.psum_scatter(
            grad_gains.astype(jnp.bfloat16), "fsdp", scatter_dimension=0, tiled=True
        ).astype(jnp.float32),
    )
    reduced = (
        lax.psum_scatter(sectioned[0], "dp", scatter_dimension=0, tiled=True),
        lax.psum_scatter(sectioned[1], "dp", scatter_dimension=0, tiled=True),
        lax.psum_scatter(sectioned[2], "dp", scatter_dimension=0, tiled=True),
        lax.psum_scatter(sectioned[3], "dp", scatter_dimension=1, tiled=True),
        lax.psum_scatter(sectioned[4], "dp", scatter_dimension=0, tiled=True),
        lax.psum_scatter(sectioned[5], "dp", scatter_dimension=0, tiled=True),
        lax.psum_scatter(sectioned[6], "dp", scatter_dimension=1, tiled=True),
        lax.psum_scatter(sectioned[7], "dp", scatter_dimension=1, tiled=True),
    )
    returned = (
        lax.all_to_all(
            result[bucket_order].reshape(peer_count, per_peer, model_width),
            "dp",
            split_axis=0,
            concat_axis=0,
            tiled=True,
        ),
        lax.all_to_all(
            grad_rows[bucket_order].reshape(peer_count, per_peer, model_width),
            "dp",
            split_axis=0,
            concat_axis=0,
            tiled=True,
        ),
    )
    output = jnp.zeros_like(tokens).at[picked].set(returned[0].reshape(row_count, model_width))
    input_grad = jnp.zeros_like(tokens).at[picked].set(returned[1].reshape(row_count, model_width))
    return (
        output,
        input_grad,
        reduced[0],
        reduced[1],
        reduced[2],
        reduced[3],
        reduced[4],
        reduced[5],
        reduced[6],
        reduced[7],
    )


MESH = pl.DeviceIdType.MESH
BF16 = jnp.bfloat16
F32 = jnp.float32
PLANE = 4
ANY = pl.BlockSpec(memory_space=pl.ANY)
VM = pl.BlockSpec(memory_space=pltpu.VMEM)
SM = pl.BlockSpec(memory_space=pltpu.SMEM)


def mm(left, right):
    return jnp.dot(left, right, preferred_element_type=F32)


def mm_nt(left, right):
    return lax.dot_general(left, right, (((1,), (1,)), ((), ())), preferred_element_type=F32)


def mm_tn(left, right):
    return lax.dot_general(left, right, (((0,), (0,)), ((), ())), preferred_element_type=F32)


class Place:
    def __init__(self, chips):
        self.chips = chips
        self.groups = chips // PLANE
        self.d = lax.axis_index("dp")
        self.f = lax.axis_index("fsdp")
        self.other = 1 - self.f
        self.g = self.d // PLANE
        self.p = self.d % PLANE
        self.x = self.p % 2
        self.y = self.p // 2

    def plane_pos(self, j):
        return ((self.y + j // 2) % 2) * 2 + (self.x + j % 2) % 2

    def plane_chip(self, j):
        return self.g * PLANE + self.plane_pos(j)

    def column_chip(self, k):
        return ((self.g + k) % self.groups) * PLANE + self.p


def greet_all(place):
    barrier = pltpu.get_barrier_semaphore()
    total = place.chips * 2
    me = place.d * 2 + place.f

    def signal(k, carry):
        to = (me + k) % total
        pl.semaphore_signal(barrier, inc=1, device_id=(to // 2, to % 2), device_id_type=MESH)
        return carry

    lax.fori_loop(1, total, signal, 0)
    pl.semaphore_wait(barrier, total - 1)


class Sent:
    def __init__(self):
        self.copies = []

    def remote(self, src, dst, send_sem, recv_sem, device):
        copy = pltpu.make_async_remote_copy(
            src_ref=src,
            dst_ref=dst,
            send_sem=send_sem,
            recv_sem=recv_sem,
            device_id=device,
            device_id_type=MESH,
        )
        copy.start()
        self.copies.append(copy)

    def finish(self):
        for copy in self.copies:
            copy.wait_send()
        self.copies = []


def arrived(ref, sem):
    pltpu.make_async_copy(ref, ref, sem).wait()


def iota(shape, dim):
    return lax.broadcasted_iota(jnp.int32, shape, dim)


def gain_spread(width, share):
    column = iota((128, width), 1).astype(F32)
    inside = column - jnp.floor((column + 0.5) * (1.0 / share)) * share
    row = iota((128, width), 0).astype(F32)
    return (inside == row).astype(BF16)


def own_stretch(chips, width, share):
    row = iota((chips, width), 0)
    column = iota((chips, width), 1)
    return (column >= row * share) & (column < row * share + share)


def gain_row(kvg_ref, which, chips, width, share):
    block = kvg_ref[which, :, share : share + 16, :].astype(F32)[:, 0, :].astype(BF16)
    spread = mm(block, gain_spread(width, share))
    return jnp.sum(jnp.where(own_stretch(chips, width, share), spread, 0.0), axis=0, keepdims=True)


def rms_scale(values):
    return lax.rsqrt(jnp.mean(values * values, axis=-1, keepdims=True) + EPSILON)


def turned(values, cosine, sine):
    return values * cosine + pltpu.roll(values, HEAD // 2, 1) * sine


def halves_in(first, second):
    front = iota(first.shape, 1) < HEAD // 2
    return (
        jnp.where(front, first, pltpu.roll(second, HEAD // 2, 1)),
        jnp.where(front, pltpu.roll(first, HEAD // 2, 1), second),
    )


class Chain:
    def __init__(self, place, piece, count, up_sems, down_sems, recv_sems):
        self.place, self.piece, self.count = place, piece, count
        self.up_sems, self.down_sems, self.recv_sems = up_sems, down_sems, recv_sems
        self.has_up = place.g + 1 < place.groups
        self.has_down = place.g >= 1

    def hop(self, a, origin, up):
        place = self.place
        ref = self.piece(a, origin)
        to = place.d + PLANE if up else place.d - PLANE
        sems = self.up_sems if up else self.down_sems
        return pltpu.make_async_remote_copy(
            src_ref=ref,
            dst_ref=ref,
            send_sem=sems.at[a, origin],
            recv_sem=self.recv_sems.at[a, origin],
            device_id=(to, place.f),
            device_id_type=MESH,
        )

    def start(self, a):
        def one(up):
            self.hop(a, self.place.g, up).start()

        pl.when(self.has_up)(functools.partial(one, True))
        pl.when(self.has_down)(functools.partial(one, False))

    def step(self, k, arrays, then):
        place = self.place

        def from_below():
            origin = place.g - k
            for a in arrays:
                arrived(self.piece(a, origin), self.recv_sems.at[a, origin])

                @pl.when(self.has_up)
                def _():
                    self.hop(a, origin, True).start()

                then(a, origin)

        def from_above():
            origin = place.g + k
            for a in arrays:
                arrived(self.piece(a, origin), self.recv_sems.at[a, origin])

                @pl.when(self.has_down)
                def _():
                    self.hop(a, origin, False).start()

                then(a, origin)

        pl.when(place.g >= k)(from_below)
        pl.when(place.g + k < place.groups)(from_above)

    def finish(self):
        place = self.place
        for k in range(place.groups):
            for a in range(self.count):

                @pl.when((place.g >= k) & self.has_up)
                def _():
                    self.hop(a, place.g - k, True).wait_send()

                @pl.when((place.g + k < place.groups) & self.has_down)
                def _():
                    self.hop(a, place.g + k, False).wait_send()


def forward_kernel(
    chips,
    reach,
    first_ref,
    deal_ref,
    deal_col_ref,
    cos_ref,
    sin_ref,
    tokens_ref,
    cot_ref,
    wq_ref,
    wot_ref,
    kvg_ref,
    gate_ref,
    up_ref,
    down_ref,
    full_three,
    full_q,
    full_ot,
    full_kvg,
    rows_out,
    pg_all,
    take_ref,
    place_ref,
    n1_ref,
    qs_ref,
    kv_ref,
    probs_ref,
    mixed_ref,
    middle_ref,
    n2_all,
    deal_all,
    give,
    got,
    bias_ref,
    branch_out,
    branch_in,
    deal_send,
    deal_recv,
    row_send,
    row_recv,
    attn_up,
    attn_down,
    attn_recv,
    fan_send,
    fan_recv,
    kvg_sems,
    stage_send,
    stage_recv,
    three_up,
    three_down,
    three_recv,
    relay_send,
    relay_recv,
    plane_send,
    plane_recv,
    n1_sems,
    kv_send,
    kv_recv,
    branch_sems,
    local_sems,
):
    place = Place(chips)
    d, f, other = place.d, place.f, place.other
    groups = place.groups
    rows, width = tokens_ref.shape
    share = wq_ref.shape[0]
    half = share // 2
    per = rows // chips
    part = gate_ref.shape[1] // 2
    micro = rows // MICRO
    heads = wq_ref.shape[1] // HEAD
    span = (2 * reach + 1) * micro
    sent = Sent()
    greet_all(place)

    deal_all[d] = deal_ref[...]
    for k in range(1, chips):
        to = (d + k) % chips
        sent.remote(deal_all.at[d], deal_all.at[d], deal_send.at[k], deal_recv.at[d], (to, f))

    def attn_piece(a, s):
        if a == 0:
            return full_kvg.at[f, s]
        band = pl.ds(pl.multiple_of(s * share, 16), share)
        return (full_q if a == 1 else full_ot).at[band]

    own_attn = (kvg_ref, wq_ref, wot_ref)
    copies = [
        pltpu.make_async_copy(own_attn[a], attn_piece(a, d), local_sems.at[a]) for a in range(3)
    ]
    for copy in copies:
        copy.start()
    for copy in copies:
        copy.wait()
    attn = Chain(
        place, lambda a, g: attn_piece(a, g * PLANE + place.p), 3, attn_up, attn_down, attn_recv
    )

    def fan(a, g):
        for j in range(1, PLANE if a == 0 else PLANE - 1):
            fan_copy(a, g, j).start()

    def fan_copy(a, g, j):
        s = g * PLANE + place.p
        return pltpu.make_async_remote_copy(
            src_ref=attn_piece(a, s),
            dst_ref=attn_piece(a, s),
            send_sem=fan_send.at[a, g, j],
            recv_sem=fan_recv.at[a, s],
            device_id=(place.plane_chip(j), f),
            device_id_type=MESH,
        )

    def pass_copy(a, g):
        by_x = place.plane_pos(1)
        by_y = place.plane_pos(2)
        even = g % 2 == 0
        s = g * PLANE + jnp.where(even, by_x, by_y)
        to = jnp.where(even, place.plane_chip(2), place.plane_chip(1))
        return pltpu.make_async_remote_copy(
            src_ref=attn_piece(a, s),
            dst_ref=attn_piece(a, s),
            send_sem=fan_send.at[a, g, PLANE - 1],
            recv_sem=fan_recv.at[a, s],
            device_id=(to, f),
            device_id_type=MESH,
        )

    def pass_on(a, g):
        s = g * PLANE + jnp.where(g % 2 == 0, place.plane_pos(1), place.plane_pos(2))
        arrived(attn_piece(a, s), fan_recv.at[a, s])
        pass_copy(a, g).start()

    def pass_all(a):
        pass_on(a, place.g)
        for k in range(1, groups):
            pl.when(place.g >= k)(functools.partial(pass_on, a, place.g - k))
            pl.when(place.g + k < groups)(functools.partial(pass_on, a, place.g + k))

    for a in range(2):
        attn.start(a)
        fan(a, place.g)
    attn.start(2)

    mats = (gate_ref, up_ref, down_ref)

    def stage_src(a, to_x, core):
        return mats[a].at[pl.ds(half * core, half), pl.ds(pl.multiple_of(part * to_x, 128), part)]

    def stage_copy(a, b, core):
        to_x = (place.x + b) % 2
        return pltpu.make_async_remote_copy(
            src_ref=stage_src(a, to_x, core),
            dst_ref=full_three.at[a, d, core],
            send_sem=stage_send.at[a, b, core],
            recv_sem=stage_recv.at[a, place.p],
            device_id=(place.g * PLANE + 2 * f + to_x, core),
            device_id_type=MESH,
        )

    def own_copy(a):
        return pltpu.make_async_copy(
            mats[a].at[pl.ds(pl.multiple_of(half * f, 16), half), pl.ds(pl.multiple_of(part * place.x, 128), part)],
            full_three.at[a, d, f],
            local_sems.at[a],
        )

    def pair_copy(a):
        return pltpu.make_async_remote_copy(
            src_ref=mats[a].at[
                pl.ds(pl.multiple_of(half * other, 16), half),
                pl.ds(pl.multiple_of(part * place.x, 128), part),
            ],
            dst_ref=full_three.at[a, d, other],
            send_sem=stage_send.at[a, 0, 0],
            recv_sem=stage_recv.at[a, place.p],
            device_id=(d, other),
            device_id_type=MESH,
        )

    for a in range(3):
        for core in range(2):
            stage_copy(a, 1, core).start()

        @pl.when(place.y != f)
        def _():
            for core in range(2):
                stage_copy(a, 0, core).start()

        @pl.when(place.y == f)
        def _():
            own_copy(a).start()
            pair_copy(a).start()

    for k in range(1, chips):
        s = (d + k) % chips
        arrived(deal_all.at[s], deal_recv.at[s])
    chip_bits = (2 * rows).bit_length() - 1
    deals = deal_all[:, 0, :]
    wants = lax.shift_right_logical(deals, chip_bits) == d
    offset = deals & (rows - 1)
    earlier = (iota((rows, rows), 0) < iota((rows, rows), 1)).astype(BF16)
    rank = mm(wants.astype(F32).astype(BF16), earlier)
    for j in range(chips):
        hit = wants[j : j + 1, :] & (rank[j : j + 1, :] == iota((per, rows), 0).astype(F32))
        index = jnp.sum(jnp.where(hit, offset[j : j + 1, :], 0), axis=1, keepdims=True)
        take_ref[j * per : (j + 1) * per, :] = (
            (index == iota((per, rows), 1)).astype(F32).astype(BF16)
        )

    def block(k):
        return pl.ds(pl.multiple_of(k * per, per), per)

    def give_rows(i, source_ref):
        give[i] = mm(take_ref[...], source_ref[...]).astype(BF16)
        for k in range(1, chips):
            to = (d + k) % chips
            sent.remote(
                give.at[i, block(to)],
                got.at[i, block(d)],
                row_send.at[i, k],
                row_recv.at[i, d],
                (to, f),
            )
        got[i, block(d), :] = give[i, block(d), :]

    def take_rows(i):
        for k in range(1, chips):
            s = (d + k) % chips
            arrived(got.at[i, block(s)], row_recv.at[i, s])
        return mm(place_ref[...], got[i])

    give_rows(0, tokens_ref)
    def soon(a, g):
        if a < 2:
            fan(a, g)

    def column_pass(k, a):
        pl.when(place.g >= k)(functools.partial(pass_on, a, place.g - k))
        pl.when(place.g + k < groups)(functools.partial(pass_on, a, place.g + k))

    def make_bias(hm, carry):
        h, m = hm // 2, hm % 2
        first = first_ref[m]
        query = (2 * d + h) * micro + iota((span, micro), 1)
        key = (2 * d + h - 2 * reach) * micro + iota((span, micro), 0)
        allowed = (
            (jnp.where(query >= first, 1, 0) == jnp.where(key >= first, 1, 0))
            & (key >= 0)
            & (key <= query)
            & (query - key < WINDOW)
        )
        bias_ref[hm] = jnp.where(allowed, 0.0, NEGATIVE)
        return carry

    lax.fori_loop(0, 4, make_bias, 0)

    attn.step(1, (0, 1, 2), soon)
    pass_on(1, place.g)
    source_col = lax.shift_right_logical(deal_col_ref[...], chip_bits)
    source_row = lax.shift_right_logical(deal_ref[0:1, :], chip_bits)
    same = (source_col == source_row) & (iota((rows, rows), 1) < iota((rows, rows), 0))
    order = jnp.sum(same.astype(F32), axis=1, keepdims=True).astype(jnp.int32)
    where_from = source_col * per + order
    place_ref[...] = (where_from == iota((rows, rows), 1)).astype(F32).astype(BF16)
    three = Chain(
        place,
        lambda a, g: full_three.at[a, pl.ds(g * PLANE, PLANE), f],
        3,
        three_up,
        three_down,
        three_recv,
    )

    def relay_copy(a, g):
        ref = full_three.at[a, pl.ds(g * PLANE, PLANE), f]
        return pltpu.make_async_remote_copy(
            src_ref=ref,
            dst_ref=ref,
            send_sem=relay_send.at[a, g],
            recv_sem=relay_recv.at[a, g],
            device_id=(d, other),
            device_id_type=MESH,
        )

    def relay(a, g):
        relay_copy(a, g).start()

    def three_start(a):
        for j in range(1, PLANE):
            pos = place.plane_pos(j)
            arrived(full_three.at[a, place.g * PLANE + pos, f], stage_recv.at[a, pos])

        @pl.when(place.y == f)
        def _():
            own_copy(a).wait()

        @pl.when(place.y != f)
        def _():
            arrived(full_three.at[a, d, f], stage_recv.at[a, place.p])

        three.start(a)
        relay(a, place.g)

    for k in range(2, groups):
        attn.step(k, (0, 1, 2), soon)
        column_pass(k - 1, 1)
        if k == groups - 2:
            three_start(0)
            give_rows(1, cot_ref)
    row_values = take_rows(0)
    column_pass(groups - 1, 1)

    for g in range(groups):
        fan(2, g)
    rows_out[...] = row_values.astype(BF16)

    def attn_wait(a):
        for g in range(groups):
            if a == 0:
                left = range(1, PLANE)
            else:
                left = (2 - g % 2, 3)
            for j in left:
                s = g * PLANE + place.plane_pos(j)
                arrived(attn_piece(a, s), fan_recv.at[a, s])

    def spread_copy(i, block_ref, pos, side, to, slot):
        piece = block_ref.at[pos, pl.ds(side * micro, micro)]
        return pltpu.make_async_remote_copy(
            src_ref=piece,
            dst_ref=piece,
            send_sem=plane_send.at[i, slot],
            recv_sem=plane_recv.at[i, pos, side],
            device_id=(to, f),
            device_id_type=MESH,
        )

    by_x, by_y, far = (place.plane_pos(j) for j in range(1, PLANE))
    to_x, to_y = place.plane_chip(1), place.plane_chip(2)

    def spread(i, block_ref):
        sends = ((0, to_x), (1, to_y), (1, to_x), (0, to_y))
        for slot, (side, to) in enumerate(sends):
            copy = spread_copy(i, block_ref, place.p, side, to, slot)
            copy.start()
            sent.copies.append(copy)

    def spread_on(i, block_ref):
        for slot, pos, side, to in ((4, by_x, 0, to_y), (5, by_y, 1, to_x)):
            arrived(block_ref.at[pos, pl.ds(side * micro, micro)], plane_recv.at[i, pos, side])
            copy = spread_copy(i, block_ref, pos, side, to, slot)
            copy.start()
            sent.copies.append(copy)

    def spread_wait(i, block_ref):
        for pos, side in ((by_x, 1), (by_y, 0), (far, 0), (far, 1)):
            arrived(block_ref.at[pos, pl.ds(side * micro, micro)], plane_recv.at[i, pos, side])

    attn_wait(0)
    sent.remote(full_kvg.at[f], full_kvg.at[f], kvg_sems.at[0], kvg_sems.at[1], (d, other))
    arrived(full_kvg.at[other], kvg_sems.at[1])

    gain_one = gain_row(full_kvg, 0, chips, width, share)
    n1_ref[f] = (row_values * rms_scale(row_values) * gain_one).astype(BF16)
    sent.remote(n1_ref.at[f], n1_ref.at[f], n1_sems.at[0], n1_sems.at[1], (d, other))

    kvw = [full_kvg[i, :, 0:share, :].reshape(width, HEAD) for i in range(2)]
    raw = [mm(n1_ref[f], kvw[i]) for i in range(2)]
    key_raw, value_raw = halves_in(raw[0], raw[1])
    for m in range(MICRO):
        hm = 2 * f + m
        band = slice(m * micro, (m + 1) * micro)
        key = turned(key_raw[band], cos_ref[hm], sin_ref[hm])
        kv_ref[m, 2 * reach + f, :, 0:HEAD] = key.astype(BF16)
        kv_ref[m, 2 * reach + f, :, HEAD:] = value_raw[band].astype(BF16)
    own_kv = kv_ref.at[:, 2 * reach + f]

    def kv_copy(j, core):
        slot = 2 * reach + f - 2 * j
        return pltpu.make_async_remote_copy(
            src_ref=own_kv,
            dst_ref=kv_ref.at[:, slot],
            send_sem=kv_send.at[j, core],
            recv_sem=kv_recv.at[slot],
            device_id=(d + j, core),
            device_id_type=MESH,
        )

    sent.remote(own_kv, own_kv, kv_send.at[0, 0], kv_recv.at[2 * reach + f], (d, other))
    for j in range(1, reach + 1):

        @pl.when(d + j < chips)
        def _():
            for core in range(2):
                kv_copy(j, core).start()

        @pl.when(d - j < 0)
        def _():
            for core in range(2):
                kv_ref[:, 2 * reach - 2 * j + core] = jnp.zeros((MICRO, micro, 2 * HEAD), BF16)

    three_start(1)
    three_start(2)

    def project(h):
        raw_q = mm(n1_ref[h], full_q[...])
        for m in range(MICRO):
            hm = 2 * h + m
            cosine, sine = cos_ref[hm], sin_ref[hm]
            for i in range(heads):
                one = raw_q[m * micro : (m + 1) * micro, i * HEAD : (i + 1) * HEAD]
                qs_ref[hm, i * micro : (i + 1) * micro, :] = turned(one, cosine, sine).astype(BF16)

    attn_wait(1)
    project(f)
    arrived(n1_ref.at[other], n1_sems.at[1])
    project(other)
    three.step(1, (0,), relay)

    arrived(kv_ref.at[:, 2 * reach + other], kv_recv.at[2 * reach + other])
    for j in range(1, reach + 1):

        @pl.when(d - j >= 0)
        def _():
            for core in range(2):
                slot = 2 * reach - 2 * j + core
                arrived(kv_ref.at[:, slot], kv_recv.at[slot])

    score_scale = HEAD ** (-0.5)

    def attend(hm):
        h, m = hm // 2, hm % 2
        keys = kv_ref[m, h : h + 2 * reach + 1, :, 0:HEAD].reshape(span, HEAD)
        values_t = kv_ref[m, h : h + 2 * reach + 1, :, HEAD:].reshape(span, HEAD).T

        def pair_step(pair, carry):
            start = pl.multiple_of(pair * 2 * micro, 2 * micro)
            band = pl.ds(start, 2 * micro)
            bias = bias_ref[hm]
            scores = mm_nt(keys, qs_ref[hm, band, :]) * score_scale + jnp.concatenate(
                [bias, bias], axis=1
            )
            exp_scores = jnp.exp(scores - jnp.max(scores, axis=0, keepdims=True))
            total = jnp.sum(exp_scores, axis=0, keepdims=True)
            probs = (exp_scores * (1.0 / total)).astype(BF16)
            probs_ref[hm, :, band] = probs
            out_t = mm(values_t, probs)
            mixed_ref[hm, :, band] = jnp.concatenate(
                [out_t[:, i * micro : (i + 1) * micro].T for i in range(2)], axis=1
            ).astype(BF16)
            return carry

        lax.fori_loop(0, heads // 2, pair_step, 0)

    attend(0)
    three.step(1, (1,), relay)
    pass_all(2)
    pg_all[place.p] = take_rows(1).astype(BF16)
    spread(0, pg_all)
    attend(1)
    three.step(1, (2,), relay)
    attend(2)
    three.step(2, (0,), relay)
    attend(3)

    def branch(h):
        return mm_nt(mixed_ref[pl.ds(2 * h, 2)].reshape(rows, heads * HEAD), full_ot[...])

    attn_wait(2)
    spread_on(0, pg_all)
    branch_out[...] = branch(other).astype(BF16)
    sent.remote(branch_out, branch_in, branch_sems.at[0], branch_sems.at[1], (d, other))
    own = branch(f)
    arrived(branch_in, branch_sems.at[1])
    middle = rows_out[...].astype(F32) + own + branch_in[...].astype(F32)
    middle_ref[...] = middle
    gain_two = gain_row(full_kvg, 1, chips, width, share)
    n2_all[place.p] = (middle * rms_scale(middle) * gain_two).astype(BF16)
    spread(1, n2_all)
    three.step(2, (1,), relay)
    spread_on(1, n2_all)
    three.step(2, (2,), relay)
    for k in range(3, groups):
        three.step(k, (0, 1, 2), relay)

    for g in range(groups):
        for a in range(3):
            arrived(full_three.at[a, pl.ds(g * PLANE, PLANE), other], relay_recv.at[a, g])
    spread_wait(0, pg_all)
    spread_wait(1, n2_all)

    attn.finish()
    three.finish()
    for g in range(groups):
        for a in range(3):
            relay_copy(a, g).wait_send()
            for j in range(1, PLANE if a == 0 else PLANE - 1):
                fan_copy(a, g, j).wait_send()
            if a > 0:
                pass_copy(a, g).wait_send()
    for a in range(3):
        for core in range(2):
            stage_copy(a, 1, core).wait_send()

        @pl.when(place.y != f)
        def _():
            for core in range(2):
                stage_copy(a, 0, core).wait_send()

        @pl.when(place.y == f)
        def _():
            pair_copy(a).wait_send()

    for j in range(1, reach + 1):

        @pl.when(d + j < chips)
        def _():
            for core in range(2):
                kv_copy(j, core).wait_send()

    sent.finish()


def forward(chips, reach, first_len, deal, cosine, sine, tokens, cotangent, wq, wot, kvg, gate, up, down):
    rows, width = tokens.shape
    share = wq.shape[0]
    groups = chips // PLANE
    part = gate.shape[1] // 2
    micro = rows // MICRO
    heads = wq.shape[1] // HEAD
    slots = 2 * reach + 2
    span = (2 * reach + 1) * micro
    dma = pltpu.SemaphoreType.DMA
    shape = jax.ShapeDtypeStruct
    deal_rows = jnp.broadcast_to(deal[None, :], (8, rows))
    deal_col = jnp.broadcast_to(deal[:, None], (rows, rows))
    return pl.pallas_call(
        functools.partial(forward_kernel, chips, reach),
        out_shape=(
            shape((3, chips, 2, share // 2, part), BF16),
            shape((width, wq.shape[1]), BF16),
            shape((width, wq.shape[1]), BF16),
            shape((2, chips) + kvg.shape, BF16),
            shape((rows, width), BF16),
            shape((PLANE, rows, width), BF16),
            shape((rows, rows), BF16),
            shape((rows, rows), BF16),
            shape((2, rows, width), BF16),
            shape((4, heads * micro, HEAD), BF16),
            shape((MICRO, slots, micro, 2 * HEAD), BF16),
            shape((4, span, heads * micro), BF16),
            shape((4, micro, heads * HEAD), BF16),
            shape((rows, width), F32),
            shape((PLANE, rows, width), BF16),
        ),
        in_specs=[SM] + [VM] * 6 + [ANY] * 6,
        out_specs=(ANY,) + (VM,) * 14,
        scratch_shapes=[
            pltpu.VMEM((chips, 8, rows), jnp.int32),
            pltpu.VMEM((2, rows, width), BF16),
            pltpu.VMEM((2, rows, width), BF16),
            pltpu.VMEM((4, span, micro), F32),
            pltpu.VMEM((rows, width), BF16),
            pltpu.VMEM((rows, width), BF16),
            dma((chips,)),
            dma((chips,)),
            dma((2, chips)),
            dma((2, chips)),
            dma((3, groups)),
            dma((3, groups)),
            dma((3, groups)),
            dma((3, groups, PLANE)),
            dma((3, chips)),
            dma((2,)),
            dma((3, 2, 2)),
            dma((3, PLANE)),
            dma((3, groups)),
            dma((3, groups)),
            dma((3, groups)),
            dma((3, groups)),
            dma((3, groups)),
            dma((2, 6)),
            dma((2, PLANE, 2)),
            dma((2,)),
            dma((reach + 1, 2)),
            dma((slots,)),
            dma((2,)),
            dma((3,)),
        ],
        compiler_params=pltpu.CompilerParams(
            collective_id=0, has_side_effects=True, vmem_limit_bytes=VMEM_ASK
        ),
        name="gather_and_attention",
    )(first_len, deal_rows, deal_col, cosine, sine, tokens, cotangent, wq, wot, kvg, gate, up, down)


def mlp_kernel(
    chips,
    n2_all,
    middle_ref,
    pg_ref,
    three_ref,
    out_ref,
    two_ref,
    grads_ref,
    turned_ref,
    hidden_ref,
    gate_rows_ref,
    up_rows_ref,
    two_give,
    two_got,
    out_give,
    out_got,
    two_send,
    two_recv,
    out_send,
    out_recv,
):
    place = Place(chips)
    f, p = place.f, place.p
    rows, width = middle_ref.shape
    greet_all(place)
    def two_copy(j):
        return pltpu.make_async_remote_copy(
            src_ref=two_give.at[j - 1],
            dst_ref=two_got.at[j - 1],
            send_sem=two_send.at[j],
            recv_sem=two_recv.at[j],
            device_id=(place.plane_chip(j), f),
            device_id_type=MESH,
        )

    def out_copy(j):
        return pltpu.make_async_remote_copy(
            src_ref=out_give.at[j - 1],
            dst_ref=out_got.at[j - 1],
            send_sem=out_send.at[j],
            recv_sem=out_recv.at[j],
            device_id=(place.plane_chip(j), f),
            device_id_type=MESH,
        )

    curve = 0.7978845608028654
    cubic = 0.044715

    def one_block(j, carry):
        pos = place.plane_pos(j)
        x = n2_all[pos]
        gate = mm(x, three_ref[0])
        upward = mm(x, three_ref[1])
        grad_hidden = mm(pg_ref[pos], three_ref[2])
        square = gate * gate
        tanh = jnp.tanh(curve * gate * (1.0 + cubic * square))
        activated = 0.5 * gate * (1.0 + tanh)
        slope = 0.5 * (1.0 + tanh) + (0.5 * curve) * gate * (1.0 - tanh * tanh) * (
            1.0 + (3.0 * cubic) * square
        )
        band = pl.ds(pl.multiple_of(pos * rows, rows), rows)
        hidden_ref[band, :] = (activated * upward).astype(BF16)
        gate_rows_ref[band, :] = (grad_hidden * upward * slope).astype(BF16)
        up_rows_ref[band, :] = (grad_hidden * activated).astype(BF16)
        back = mm_nt(gate_rows_ref[band, :], three_ref[0]) + mm_nt(up_rows_ref[band, :], three_ref[1])

        @pl.when(j > 0)
        def _():
            two_give[j - 1] = back.astype(BF16)
            two_copy(j).start()

        @pl.when(j == 0)
        def _():
            two_ref[...] = back

        return carry

    lax.fori_loop(0, PLANE, one_block, 0)

    def out_step(j):
        pos = place.plane_pos(j)
        band = pl.ds(pl.multiple_of(pos * rows, rows), rows)
        return pos, mm_nt(hidden_ref[band, :], three_ref[2])

    def send_out(j, carry):
        pos, piece = out_step(j)
        out_give[j - 1] = piece.astype(BF16)
        out_copy(j).start()
        return carry

    lax.fori_loop(1, PLANE, send_out, 0)
    own_out = middle_ref[...] + out_step(0)[1]

    tile = rows
    tiles = width // tile

    def turn(source, index):
        def step(i, carry):
            at = pl.ds(pl.multiple_of(i * rows, rows), rows)
            turned_ref[:, at] = source[i].T
            return carry

        lax.fori_loop(0, PLANE, step, 0)

    def weight_grad(index, right):
        def step(i, carry):
            at = pl.ds(pl.multiple_of(i * tile, tile), tile)
            grads_ref[index, at, :] = mm(turned_ref[at, :], right[...]).astype(BF16)
            return carry

        lax.fori_loop(0, tiles, step, 0)

    turn(pg_ref, 0)
    weight_grad(2, hidden_ref)
    turn(n2_all, 1)
    weight_grad(0, gate_rows_ref)
    weight_grad(1, up_rows_ref)

    for j in range(1, PLANE):
        arrived(two_got.at[j - 1], two_recv.at[j])
        two_ref[...] = two_ref[...] + two_got[j - 1].astype(F32)
    for j in range(1, PLANE):
        arrived(out_got.at[j - 1], out_recv.at[j])
        own_out = own_out + out_got[j - 1].astype(F32)
    out_ref[...] = own_out.astype(BF16)
    for j in range(1, PLANE):
        two_copy(j).wait_send()
        out_copy(j).wait_send()


def mlp(chips, n2, middle, pg_all, three):
    rows, width = middle.shape
    part = three.shape[2]
    dma = pltpu.SemaphoreType.DMA
    shape = jax.ShapeDtypeStruct
    wide = PLANE * rows
    return pl.pallas_call(
        functools.partial(mlp_kernel, chips),
        out_shape=(
            shape((rows, width), BF16),
            shape((rows, width), F32),
            shape((3, width, part), BF16),
        ),
        in_specs=[VM] * 4,
        out_specs=(VM,) * 3,
        scratch_shapes=[
            pltpu.VMEM((width, wide), BF16),
            pltpu.VMEM((wide, part), BF16),
            pltpu.VMEM((wide, part), BF16),
            pltpu.VMEM((wide, part), BF16),
        ]
        + [pltpu.VMEM((PLANE - 1, rows, width), BF16)] * 4
        + [dma((PLANE,))] * 4,
        compiler_params=pltpu.CompilerParams(
            collective_id=2, has_side_effects=True, vmem_limit_bytes=VMEM_ASK
        ),
        name="mlp_both_ways",
    )(n2, middle, pg_all, three)


def norm_back(values, gain, grad):
    scale = rms_scale(values)
    unit = values * scale
    lifted = grad * gain
    gain_grad = jnp.sum(grad * unit, axis=0, keepdims=True)
    back = scale * (lifted - unit * jnp.mean(lifted * unit, axis=-1, keepdims=True))
    return back, gain_grad


def attention_back_kernel(
    chips,
    reach,
    rows_ref,
    pg_ref,
    middle_ref,
    two_ref,
    n1_ref,
    qs_ref,
    kv_ref,
    probs_ref,
    mixed_ref,
    wq_ref,
    wot_ref,
    kvg_ref,
    cos_ref,
    sin_ref,
    grad_rows_ref,
    gq_ref,
    got_ref,
    gkvg_ref,
    low_ref,
    lows_t,
    mixed_rows,
    grad_mixed,
    grad_q,
    kv_total,
    kv_give,
    kv_got,
    one_out,
    one_in,
    low_sems,
    kv_send,
    kv_recv,
    one_sems,
):
    place = Place(chips)
    d, f, other = place.d, place.f, place.other
    rows, width = rows_ref.shape
    micro = rows // MICRO
    heads = wq_ref.shape[1] // HEAD
    share = width // chips
    slots = 2 * reach + 2
    span = (2 * reach + 1) * micro
    sent = Sent()
    greet_all(place)

    gain_two = gain_row(kvg_ref, 1, chips, width, share)
    back, gain_two_grad = norm_back(middle_ref[...], gain_two, two_ref[...])
    grad_middle = pg_ref[...].astype(F32) + back
    low_ref[f] = grad_middle.astype(BF16)
    sent.remote(low_ref.at[f], low_ref.at[f], low_sems.at[0], low_sems.at[1], (d, other))
    kv_total[...] = jnp.zeros_like(kv_total)

    def mix_back(h):
        grads = mm(low_ref[h], wot_ref[...])
        for m in range(MICRO):
            for i in range(heads):
                grad_mixed[2 * h + m, i * micro : (i + 1) * micro, :] = grads[
                    m * micro : (m + 1) * micro, i * HEAD : (i + 1) * HEAD
                ].astype(BF16)

    mix_back(f)
    arrived(low_ref.at[other], low_sems.at[1])
    mix_back(other)

    score_scale = HEAD ** (-0.5)

    def attend_back(hm, carry):
        h, m = hm // 2, hm % 2
        at = pl.ds(h, 2 * reach + 1)
        keys = kv_ref[m, at, :, 0:HEAD].reshape(span, HEAD)
        values = kv_ref[m, at, :, HEAD:].reshape(span, HEAD)
        keys_t = keys.T
        key_total = jnp.zeros((span, HEAD), F32)
        value_total = jnp.zeros((span, HEAD), F32)
        for pair in range(heads // 2):
            band = slice(pair * 2 * micro, (pair + 1) * 2 * micro)
            probs = probs_ref[hm, :, band]
            grads = grad_mixed[hm, band, :]
            queries = qs_ref[hm, band, :]
            value_total = value_total + mm(probs, grads)
            grad_probs = mm_nt(values, grads)
            wide = probs.astype(F32)
            delta = jnp.sum(grad_probs * wide, axis=0, keepdims=True)
            grad_scores = (wide * (grad_probs - delta)).astype(BF16)
            key_total = key_total + mm(grad_scores, queries)
            query_t = mm(keys_t, grad_scores) * score_scale
            for i in range(2):
                head = pair * 2 + i
                one = query_t[:, i * micro : (i + 1) * micro].T
                grad_q[hm, :, head * HEAD : (head + 1) * HEAD] = turned(
                    one, cos_ref[hm], -sin_ref[hm]
                ).astype(BF16)
        key_total = (key_total * score_scale).reshape(2 * reach + 1, micro, HEAD)
        kv_total[m, at, :, 0:HEAD] = kv_total[m, at, :, 0:HEAD] + key_total
        kv_total[m, at, :, HEAD:] = kv_total[m, at, :, HEAD:] + value_total.reshape(
            2 * reach + 1, micro, HEAD
        )
        return carry

    lax.fori_loop(0, 4, attend_back, 0)

    kv_give[...] = kv_total[...].astype(BF16)

    def kv_copy(j, core):
        return pltpu.make_async_remote_copy(
            src_ref=kv_give.at[:, 2 * reach - 2 * j + core],
            dst_ref=kv_got.at[2 * j + f],
            send_sem=kv_send.at[j, core],
            recv_sem=kv_recv.at[2 * j + f],
            device_id=(d - j, core),
            device_id_type=MESH,
        )

    sent.remote(
        kv_give.at[:, 2 * reach + other],
        kv_got.at[f],
        kv_send.at[0, 0],
        kv_recv.at[f],
        (d, other),
    )
    for j in range(1, reach + 1):

        @pl.when(d - j >= 0)
        def _():
            for core in range(2):
                kv_copy(j, core).start()

    lows_t[:, 0:rows] = low_ref[0].T
    lows_t[:, rows:] = low_ref[1].T
    tile = 2 * HEAD
    for hm in range(4):
        mixed_rows[hm * micro : (hm + 1) * micro, :] = mixed_ref[hm]

    def out_tile(i, carry):
        at = pl.ds(pl.multiple_of(i * tile, tile), tile)
        got_ref[at, :] = mm(lows_t[at, :], mixed_rows[...]).astype(BF16)
        return carry

    lax.fori_loop(0, width // tile, out_tile, 0)
    lows_t[:, 0:rows] = n1_ref[0].T
    lows_t[:, rows:] = n1_ref[1].T
    for hm in range(4):
        mixed_rows[hm * micro : (hm + 1) * micro, :] = grad_q[hm]

    def query_tile(i, carry):
        at = pl.ds(pl.multiple_of(i * tile, tile), tile)
        gq_ref[at, :] = mm(lows_t[at, :], mixed_rows[...]).astype(BF16)
        return carry

    lax.fori_loop(0, width // tile, query_tile, 0)

    def one_back(h):
        band = pl.ds(pl.multiple_of(h * rows, rows), rows)
        return mm_nt(mixed_rows[band, :], wq_ref[...])

    one_out[...] = one_back(other).astype(BF16)
    sent.remote(one_out, one_in, one_sems.at[0], one_sems.at[1], (d, other))
    grad_one = one_back(f)

    sums = [kv_total[m, 2 * reach + f] for m in range(MICRO)]
    arrived(kv_got.at[other], kv_recv.at[other])
    sums = [sums[m] + kv_got[other, m].astype(F32) for m in range(MICRO)]
    for j in range(1, reach + 1):
        for core in range(2):
            slot = 2 * j + core

            @pl.when(d + j < chips)
            def _():
                arrived(kv_got.at[slot], kv_recv.at[slot])

            @pl.when(d + j >= chips)
            def _():
                kv_got[slot] = jnp.zeros((MICRO, micro, 2 * HEAD), BF16)

            sums = [sums[m] + kv_got[slot, m].astype(F32) for m in range(MICRO)]
    key_rows = jnp.concatenate(
        [
            turned(sums[m][:, 0:HEAD], cos_ref[2 * f + m], -sin_ref[2 * f + m])
            for m in range(MICRO)
        ],
        axis=0,
    )
    value_rows = jnp.concatenate([sums[m][:, HEAD:] for m in range(MICRO)], axis=0)
    pieces = halves_in(key_rows, value_rows)
    n1_own_t = n1_ref[f].T
    row_values = rows_ref[...].astype(F32)
    for i in range(2):
        piece = pieces[i].astype(BF16)
        gkvg_ref[i, :, 0:share, :] = (
            mm(n1_own_t, piece).astype(BF16).reshape(chips, share, HEAD)
        )
        grad_one = grad_one + mm_nt(piece, kvg_ref[i, :, 0:share, :].reshape(width, HEAD))
    arrived(one_in, one_sems.at[1])
    grad_one = grad_one + one_in[...].astype(F32)
    gain_one = gain_row(kvg_ref, 0, chips, width, share)
    back_one, gain_one_grad = norm_back(row_values, gain_one, grad_one)
    grad_rows_ref[...] = (grad_middle + back_one).astype(BF16)
    spread = gain_spread(width, share)
    stretch = own_stretch(chips, width, share)
    for i, grad in enumerate((gain_one_grad, gain_two_grad)):
        piece = mm_nt(jnp.where(stretch, grad, 0.0).astype(BF16), spread)
        row = iota((chips, 16, HEAD), 1)
        gkvg_ref[i, :, share : share + 16, :] = jnp.where(
            row == 0, piece[:, None, :], 0.0
        ).astype(BF16)

    for j in range(1, reach + 1):

        @pl.when(d - j >= 0)
        def _():
            for core in range(2):
                kv_copy(j, core).wait_send()

    sent.finish()


def attention_back(chips, reach, rows_in, pg, middle, two, n1, qs, kv, probs, mixed, wq, wot, kvg, cosine, sine):
    rows, width = rows_in.shape
    micro = rows // MICRO
    heads = wq.shape[1] // HEAD
    slots = 2 * reach + 2
    dma = pltpu.SemaphoreType.DMA
    shape = jax.ShapeDtypeStruct
    return pl.pallas_call(
        functools.partial(attention_back_kernel, chips, reach),
        out_shape=(
            shape((rows, width), BF16),
            shape(wq.shape, BF16),
            shape(wot.shape, BF16),
            shape(kvg.shape, BF16),
        ),
        in_specs=[VM] * 14,
        out_specs=(VM,) * 4,
        scratch_shapes=[
            pltpu.VMEM((2, rows, width), BF16),
            pltpu.VMEM((width, 2 * rows), BF16),
            pltpu.VMEM((2 * rows, heads * HEAD), BF16),
            pltpu.VMEM((4, heads * micro, HEAD), BF16),
            pltpu.VMEM((4, micro, heads * HEAD), BF16),
            pltpu.VMEM((MICRO, slots, micro, 2 * HEAD), F32),
            pltpu.VMEM((MICRO, slots, micro, 2 * HEAD), BF16),
            pltpu.VMEM((slots, MICRO, micro, 2 * HEAD), BF16),
            pltpu.VMEM((rows, width), BF16),
            pltpu.VMEM((rows, width), BF16),
            dma((2,)),
            dma((reach + 1, 2)),
            dma((slots,)),
            dma((2,)),
        ],
        compiler_params=pltpu.CompilerParams(
            collective_id=3, has_side_effects=True, vmem_limit_bytes=VMEM_ASK
        ),
        name="attention_backward",
    )(rows_in, pg, middle, two, n1, qs, kv, probs, mixed, wq, wot, kvg, cosine, sine)


def scatter_kernel(
    chips,
    three_ref,
    gq_ref,
    got_ref,
    gkvg_ref,
    outs_ref,
    grad_rows_ref,
    take_ref,
    place_ref,
    three_out,
    q_out,
    ot_out,
    kvg_out,
    output_ref,
    input_grad_ref,
    pair_got,
    three_give,
    three_got,
    kvg_got,
    attn_got,
    attn_give,
    attn_last,
    kvg_fan,
    kvg_give,
    kvg_last,
    give,
    got,
    pair_send,
    pair_recv,
    three_send,
    three_recv,
    kvg_sems,
    fan_send,
    fan_recv,
    column_send,
    column_recv,
    row_send,
    row_recv,
):
    place = Place(chips)
    d, f, other = place.d, place.f, place.other
    groups = place.groups
    rows, width = outs_ref.shape
    share = width // chips
    half = share // 2
    part = three_ref.shape[2]
    per = rows // chips
    sent = Sent()
    greet_all(place)

    def order(k, j):
        return ((place.g + k) % groups) * PLANE + place.plane_pos(j)

    def band(s, core):
        return pl.ds(pl.multiple_of(s * share + half * core, 16), half)

    steps = [(k, j) for k in range(groups) for j in range(PLANE)]
    steps = steps[1:] + steps[:1]
    sent.remote(gkvg_ref.at[other], kvg_got, kvg_sems.at[0], kvg_sems.at[1], (d, other))
    for k, j in steps:
        s = order(k, j)
        sent.remote(
            three_ref.at[:, band(s, other)],
            pair_got.at[s],
            pair_send.at[s],
            pair_recv.at[s],
            (d, other),
        )

    def whole(s):
        return pl.ds(pl.multiple_of(s * share, 16), share)

    attn = (gq_ref, got_ref)
    for j in range(1, PLANE):
        to = place.plane_pos(j)
        for k in range(groups):
            s = ((place.g + k) % groups) * PLANE + to
            for a in range(2):
                sent.remote(
                    attn[a].at[whole(s)],
                    attn_got.at[a, j, s // PLANE],
                    fan_send.at[a, j, k],
                    fan_recv.at[a, j, s // PLANE],
                    (place.plane_chip(j), f),
                )

    def block(k):
        return pl.ds(pl.multiple_of(k * per, per), per)

    give[:, :width] = mm_tn(place_ref[...], outs_ref[...]).astype(BF16)
    give[:, width:] = mm_tn(place_ref[...], grad_rows_ref[...]).astype(BF16)
    for k in range(1, chips):
        to = (d + k) % chips
        sent.remote(give.at[block(to)], got.at[block(d)], row_send.at[k], row_recv.at[d], (to, f))
    got[block(d), :] = give[block(d), :]

    arrived(kvg_got, kvg_sems.at[1])
    for s in range(chips):
        kvg_give[s] = (gkvg_ref[f, s].astype(F32) + kvg_got[s].astype(F32)).astype(BF16)
    for j in range(1, PLANE):
        to = place.plane_pos(j)
        for k in range(groups):
            s = ((place.g + k) % groups) * PLANE + to
            sent.remote(
                kvg_give.at[s],
                kvg_fan.at[j, s // PLANE],
                fan_send.at[2, j, k],
                fan_recv.at[2, j, s // PLANE],
                (place.plane_chip(j), f),
            )

    def three_slot(j_x, k):
        return 2 * k + j_x

    for n, (k, j) in enumerate(steps):
        s = order(k, j)
        arrived(pair_got.at[s], pair_recv.at[s])
        for a in range(3):
            three_give[s, a] = (
                three_ref[a, band(s, f), :].astype(F32) + pair_got[s, a].astype(F32)
            ).astype(BF16)
        dst = three_got.at[2 * place.g + place.x, f]
        recv = three_recv.at[2 * place.g + place.x, f]
        if (k, j) == (0, 0):
            remote = pltpu.make_async_remote_copy(
                src_ref=three_give.at[s],
                dst_ref=dst,
                send_sem=three_send.at[s],
                recv_sem=recv,
                device_id=(d, other),
                device_id_type=MESH,
            )

            @pl.when(place.y != f)
            def _():
                remote.start()

            @pl.when(place.y == f)
            def _():
                three_got[2 * place.g + place.x, f] = three_give[s]

            own_remote = remote
        else:
            sent.remote(three_give.at[s], dst, three_send.at[s], recv, (s, place.y))

    for k in list(range(1, groups)) + [0]:
        g = (place.g + k) % groups
        s = g * PLANE + place.p
        for a in range(2):
            total = attn[a][whole(s), :].astype(F32)
            for j in range(1, PLANE):
                arrived(attn_got.at[a, j, g], fan_recv.at[a, j, g])
                total = total + attn_got[a, j, g].astype(F32)
            if k == 0:
                (q_out, ot_out)[a][...] = total
            else:
                attn_give[a, g] = total.astype(BF16)
                sent.remote(
                    attn_give.at[a, g],
                    attn_last.at[a, place.g],
                    column_send.at[a, k],
                    column_recv.at[a, place.g],
                    (s, f),
                )
        total = kvg_give[s].astype(F32)
        for j in range(1, PLANE):
            arrived(kvg_fan.at[j, g], fan_recv.at[2, j, g])
            total = total + kvg_fan[j, g].astype(F32)
        if k == 0:
            kvg_out[...] = total
        else:
            kvg_give[s] = total.astype(BF16)
            sent.remote(
                kvg_give.at[s],
                kvg_last.at[place.g],
                column_send.at[2, k],
                column_recv.at[2, place.g],
                (s, f),
            )

    for k in range(1, chips):
        s = (d + k) % chips
        arrived(got.at[block(s)], row_recv.at[s])
    output_ref[...] = mm_tn(take_ref[...], got[:, :width]).astype(BF16)
    input_grad_ref[...] = mm_tn(take_ref[...], got[:, width:]).astype(BF16)

    for k in range(1, groups):
        g = (place.g + k) % groups
        for a in range(2):
            arrived(attn_last.at[a, g], column_recv.at[a, g])
            out = (q_out, ot_out)[a]
            out[...] = out[...] + attn_last[a, g].astype(F32)
        arrived(kvg_last.at[g], column_recv.at[2, g])
        kvg_out[...] = kvg_out[...] + kvg_last[g].astype(F32)

    for cx in range(2):
        for core in range(2):
            for k in range(groups):
                g = (place.g + k) % groups
                slot = 2 * g + cx
                piece = three_got.at[slot, core]

                if k == 0:
                    @pl.when((place.y != f) | (place.x != cx) | (core != f))
                    def _():
                        arrived(piece, three_recv.at[slot, core])
                else:
                    arrived(piece, three_recv.at[slot, core])
            for a in range(3):
                total = three_got[cx, core, a].astype(F32)
                for g in range(1, groups):
                    total = total + three_got[2 * g + cx, core, a].astype(F32)
                three_out[a, half * core : half * (core + 1), cx * part : (cx + 1) * part] = total

    @pl.when(place.y != f)
    def _():
        own_remote.wait_send()

    sent.finish()


def scatter(chips, three, gq, got, gkvg, outs, grad_rows, take, placing):
    rows, width = outs.shape
    share = width // chips
    half = share // 2
    part = three.shape[2]
    groups = chips // PLANE
    heads_wide = gq.shape[1]
    small = gkvg.shape[2:]
    dma = pltpu.SemaphoreType.DMA
    shape = jax.ShapeDtypeStruct
    return pl.pallas_call(
        functools.partial(scatter_kernel, chips),
        out_shape=(
            shape((3, share, 2 * part), F32),
            shape((share, heads_wide), F32),
            shape((share, heads_wide), F32),
            shape(small, F32),
            shape((rows, width), BF16),
            shape((rows, width), BF16),
        ),
        in_specs=[VM] * 8,
        out_specs=(VM,) * 6,
        scratch_shapes=[
            pltpu.VMEM((chips, 3, half, part), BF16),
            pltpu.VMEM((chips, 3, half, part), BF16),
            pltpu.VMEM((2 * groups, 2, 3, half, part), BF16),
            pltpu.VMEM((chips,) + small, BF16),
            pltpu.VMEM((2, PLANE, groups, share, heads_wide), BF16),
            pltpu.VMEM((2, groups, share, heads_wide), BF16),
            pltpu.VMEM((2, groups, share, heads_wide), BF16),
            pltpu.VMEM((PLANE, groups) + small, BF16),
            pltpu.VMEM((chips,) + small, BF16),
            pltpu.VMEM((groups,) + small, BF16),
            pltpu.VMEM((rows, 2 * width), BF16),
            pltpu.VMEM((rows, 2 * width), BF16),
            dma((chips,)),
            dma((chips,)),
            dma((chips,)),
            dma((2 * groups, 2)),
            dma((2,)),
            dma((3, PLANE, groups)),
            dma((3, PLANE, groups)),
            dma((3, groups)),
            dma((3, groups)),
            dma((chips,)),
            dma((chips,)),
        ],
        compiler_params=pltpu.CompilerParams(
            collective_id=4, has_side_effects=True, vmem_limit_bytes=VMEM_ASK
        ),
        name="scatter_grads_and_rows",
    )(three, gq, got, gkvg, outs, grad_rows, take, placing)


def planned(
    tokens,
    cotangent,
    deal,
    first_len,
    w_query,
    w_key,
    w_value,
    w_out,
    w_gate,
    w_up,
    w_down,
    norm_gains,
):
    chips = lax.axis_size("dp")
    rows, width = tokens.shape
    micro = rows // MICRO
    share = w_query.shape[0]
    back_blocks = min(2 * chips - 1, (WINDOW + micro - 2) // micro)
    reach = (back_blocks + 1) // 2
    d = lax.axis_index("dp")
    inside = jnp.arange(micro, dtype=jnp.int32)
    positions = (2 * d + jnp.arange(2, dtype=jnp.int32))[:, None, None] * micro + inside
    second = positions >= first_len[None, :, None]
    within = positions - jnp.where(second, first_len[None, :, None], 0)
    cosine, sine = angles(within.reshape(-1))
    cosine = jnp.concatenate([cosine, cosine], axis=1).reshape(4, micro, HEAD)
    sine = jnp.concatenate([-sine, sine], axis=1).reshape(4, micro, HEAD)
    gain_rows = jnp.pad(norm_gains, ((0, 15), (0, HEAD - share)))
    kvg = jnp.concatenate([jnp.concatenate([w_key, w_value], axis=1), gain_rows], axis=0)
    (
        three, wq, wot, kvg_all, rows_in, pg_all, take, placing, n1, qs, kv, probs, mixed, middle, n2
    ) = forward(
        chips, reach, first_len, deal, cosine, sine, tokens, cotangent, w_query, w_out.T, kvg,
        w_gate, w_up, w_down.T,
    )
    three = three.reshape(3, width, three.shape[-1])
    outs, grad_two, three_grads = mlp(chips, n2, middle, pg_all, three)
    pg = lax.dynamic_index_in_dim(pg_all, d % PLANE, 0, keepdims=False)
    grad_rows, gq, got, gkvg = attention_back(
        chips, reach, rows_in, pg, middle, grad_two, n1, qs, kv, probs, mixed, wq, wot, kvg_all,
        cosine, sine,
    )
    three_out, q_out, ot_out, kvg_out, output, input_grad = scatter(
        chips, three_grads, gq, got, gkvg, outs, grad_rows, take, placing
    )
    key_cols = w_key.shape[1]
    return (
        output,
        input_grad,
        q_out,
        kvg_out[:share, :key_cols],
        kvg_out[:share, key_cols:],
        ot_out.T,
        three_out[0],
        three_out[1],
        three_out[2].T,
        kvg_out[share : share + 1, :share],
    )


def fits_plan(mesh, share):
    chips = mesh.shape["dp"]
    return mesh.shape["fsdp"] == 2 and chips % PLANE == 0 and share % 32 == 0 and share < HEAD


def solution(mesh):
    in_specs = (
        P(("dp", "fsdp"), None),
        P(("dp", "fsdp"), None),
        P(("dp", "fsdp")),
        P(),
        P("dp", "fsdp"),
        P("dp", "fsdp"),
        P("dp", "fsdp"),
        P("fsdp", "dp"),
        P("dp", "fsdp"),
        P("dp", "fsdp"),
        P("fsdp", "dp"),
        P("fsdp", "dp"),
    )
    out_specs = (
        P(("dp", "fsdp"), None),
        P(("dp", "fsdp"), None),
        P("dp", "fsdp"),
        P("dp", "fsdp"),
        P("dp", "fsdp"),
        P("fsdp", "dp"),
        P("dp", "fsdp"),
        P("dp", "fsdp"),
        P("fsdp", "dp"),
        P("fsdp", "dp"),
    )
    def placed(*arrays):
        share = arrays[4].shape[0] // mesh.shape["dp"]
        program = planned if fits_plan(mesh, share) else per_device
        return jax.shard_map(
            program, mesh=mesh, in_specs=in_specs, out_specs=out_specs, check_vma=False
        )(*arrays)

    return placed
```

```python
import functools

import jax
import jax.numpy as jnp
from jax import lax
from jax.experimental import pallas as pl
from jax.experimental.pallas import tpu as pltpu
from jax.sharding import PartitionSpec as P

HEADS = 12
HEAD = 128
WINDOW = 1024
MICRO = 2


EPSILON = 1e-06
NEGATIVE = -1e30
VMEM_ASK = 62 * 2**20


def passed_along(x, axis, by):
    count = lax.axis_size(axis)
    pairs = [(i, i + by) for i in range(count) if 0 <= i + by < count]
    return lax.ppermute(x, axis, pairs)


def normed(row_values, gain_row):
    return (
        row_values
        * lax.rsqrt(jnp.mean(row_values * row_values, axis=-1, keepdims=True) + EPSILON)
        * gain_row
    )


def rotate(values, cosine, sine_table):
    half_width = values.shape[-1] // 2
    front_half = values[..., :half_width]
    back_half = values[..., half_width:]
    return jnp.concatenate(
        [
            front_half * cosine - back_half * sine_table,
            back_half * cosine + front_half * sine_table,
        ],
        axis=-1,
    )


def angles(places):
    half_width = HEAD // 2
    frequency = 10000.0 ** (-jnp.arange(half_width, dtype=jnp.float32) * 2.0 / HEAD)
    angle_rows = places.astype(jnp.float32)[:, None] * frequency[None, :]
    return (jnp.cos(angle_rows), jnp.sin(angle_rows))


def contract_rows(left, right):
    return lax.dot_general(
        left, right, (((0,), (0,)), ((), ())), preferred_element_type=jnp.float32
    )


def against(left, right):
    return lax.dot_general(
        left, right, (((1,), (1,)), ((), ())), preferred_element_type=jnp.float32
    )


def gelu_tanh(inputs):
    return jax.nn.gelu(inputs, approximate=True)


def per_device(
    tokens,
    cotangent,
    deal,
    first_len,
    w_query,
    w_key,
    w_value,
    w_out,
    w_gate,
    w_up,
    w_down,
    norm_gains,
):
    peer_count = lax.axis_size("dp")
    core_count = lax.axis_size("fsdp")
    device_total = peer_count * core_count
    row_count = tokens.shape[0]
    model_width = tokens.shape[1]
    per_peer = row_count // peer_count
    micro_rows = row_count // MICRO
    reach_steps = min(device_total - 1, (WINDOW + micro_rows - 2) // micro_rows)
    linear = lax.axis_index("dp") * core_count + lax.axis_index("fsdp")
    source_peer = deal // (row_count * core_count)
    offsets = deal % row_count
    bucket_order = jnp.argsort(source_peer, stable=True)
    inverse = jnp.argsort(bucket_order)
    wanted = offsets[bucket_order].reshape(peer_count, per_peer)
    requested = lax.all_to_all(wanted, "dp", split_axis=0, concat_axis=0, tiled=True)
    picked = requested.reshape(-1)
    fetched = (
        lax.all_to_all(
            tokens[picked].reshape(peer_count, per_peer, model_width),
            "dp",
            split_axis=0,
            concat_axis=0,
            tiled=True,
        ),
        lax.all_to_all(
            cotangent[picked].reshape(peer_count, per_peer, model_width),
            "dp",
            split_axis=0,
            concat_axis=0,
            tiled=True,
        ),
    )
    rows_in = fetched[0].reshape(row_count, model_width)[inverse]
    grad_in = fetched[1].reshape(row_count, model_width)[inverse]
    halves = (
        lax.all_gather(w_query, "dp", axis=0, tiled=True),
        lax.all_gather(w_key, "dp", axis=0, tiled=True),
        lax.all_gather(w_value, "dp", axis=0, tiled=True),
        lax.all_gather(w_out, "dp", axis=1, tiled=True),
        lax.all_gather(w_gate, "dp", axis=0, tiled=True),
        lax.all_gather(w_up, "dp", axis=0, tiled=True),
        lax.all_gather(w_down, "dp", axis=1, tiled=True),
        lax.all_gather(norm_gains, "dp", axis=1, tiled=True),
    )
    gathered = (
        lax.all_gather(halves[0], "fsdp", axis=1, tiled=True),
        lax.all_gather(halves[1], "fsdp", axis=1, tiled=True),
        lax.all_gather(halves[2], "fsdp", axis=1, tiled=True),
        lax.all_gather(halves[3], "fsdp", axis=0, tiled=True),
        lax.all_gather(halves[4], "fsdp", axis=1, tiled=True),
        lax.all_gather(halves[5], "fsdp", axis=1, tiled=True),
        lax.all_gather(halves[6], "fsdp", axis=0, tiled=True),
        lax.all_gather(halves[7], "fsdp", axis=0, tiled=True),
    )
    full_query, full_key, full_value, full_out, full_gate, full_up, full_down, full_gains = gathered
    gain_one = full_gains[0].astype(jnp.float32)
    gain_two = full_gains[1].astype(jnp.float32)
    inside = jnp.arange(micro_rows, dtype=jnp.int32)
    query_place = linear * micro_rows + inside
    query_later = query_place[None, :] >= first_len[:, None]
    query_within = query_place[None, :] - jnp.where(query_later, first_len[:, None], 0)
    distance = jnp.arange(reach_steps, -1, -1, dtype=jnp.int32)
    key_place = ((linear - distance)[:, None] * micro_rows + inside[None, :]).reshape(-1)
    key_later = key_place[None, :] >= first_len[:, None]
    allowed = (
        (query_later[:, :, None] == key_later[:, None, :])
        & (key_place[None, None, :] >= 0)
        & (key_place[None, None, :] <= query_place[None, :, None])
        & (query_place[None, :, None] - key_place[None, None, :] < WINDOW)
    )
    rows_float = rows_in.astype(jnp.float32)
    cosine, sine_table = angles(query_within.reshape(-1))
    score_scale = HEAD ** (-0.5)
    normal_one = normed(rows_float, gain_one).astype(jnp.bfloat16)
    query_raw = jnp.dot(normal_one, full_query, preferred_element_type=jnp.float32).reshape(
        row_count, HEADS, HEAD
    )
    query_rows = rotate(query_raw, cosine[:, None, :], sine_table[:, None, :]).astype(jnp.bfloat16)
    key_rows = rotate(
        jnp.dot(normal_one, full_key, preferred_element_type=jnp.float32), cosine, sine_table
    ).astype(jnp.bfloat16)
    value_rows = jnp.dot(normal_one, full_value, preferred_element_type=jnp.float32).astype(
        jnp.bfloat16
    )
    earlier = []
    for distance_step in range(1, reach_steps + 1):
        earlier.append(passed_along((key_rows, value_rows), ("dp", "fsdp"), distance_step))
    ordered = earlier[::-1] + [(key_rows, value_rows)]
    all_keys = jnp.concatenate(
        [member[0].reshape(MICRO, micro_rows, HEAD) for member in ordered], axis=1
    )
    all_values = jnp.concatenate(
        [member[1].reshape(MICRO, micro_rows, HEAD) for member in ordered], axis=1
    )
    by_head = jnp.transpose(query_rows.reshape(MICRO, micro_rows, HEADS, HEAD), (2, 0, 1, 3))

    def attend(query_head):
        scores = jnp.where(
            allowed,
            jnp.einsum("mqd,mkd->mqk", query_head, all_keys, preferred_element_type=jnp.float32)
            * score_scale,
            NEGATIVE,
        )
        row_top = jnp.max(scores, axis=2, keepdims=True)
        exp_scores = jnp.exp(scores - row_top)
        row_total = jnp.sum(exp_scores, axis=2, keepdims=True)
        soft_weights = (exp_scores / row_total).astype(jnp.bfloat16)
        attended_head = jnp.einsum(
            "mqk,mkd->mqd", soft_weights, all_values, preferred_element_type=jnp.float32
        )
        return (attended_head, row_top[..., 0] + jnp.log(row_total[..., 0]))

    attended, log_total = lax.map(attend, by_head)
    mixed_heads = (
        jnp.transpose(attended, (1, 2, 0, 3)).reshape(row_count, HEADS * HEAD).astype(jnp.bfloat16)
    )
    middle = rows_float + jnp.dot(mixed_heads, full_out, preferred_element_type=jnp.float32)
    normal_two = normed(middle, gain_two).astype(jnp.bfloat16)
    gate_rows = jnp.dot(normal_two, full_gate, preferred_element_type=jnp.float32)
    upward = jnp.dot(normal_two, full_up, preferred_element_type=jnp.float32)
    activated = gelu_tanh(gate_rows)
    hidden = (activated * upward).astype(jnp.bfloat16)
    result = (middle + jnp.dot(hidden, full_down, preferred_element_type=jnp.float32)).astype(
        jnp.bfloat16
    )
    grad_float = grad_in.astype(jnp.float32)
    grad_down = contract_rows(hidden, grad_in)
    grad_hidden = against(grad_in, full_down)
    gelu_value, gelu_pull = jax.vjp(gelu_tanh, gate_rows)
    grad_gate_rows = gelu_pull(grad_hidden * upward)[0].astype(jnp.bfloat16)
    grad_up_rows = (grad_hidden * activated).astype(jnp.bfloat16)
    grad_gate = contract_rows(normal_two, grad_gate_rows)
    grad_up = contract_rows(normal_two, grad_up_rows)
    grad_two = against(grad_gate_rows, full_gate) + against(grad_up_rows, full_up)
    norm_value, norm_pull = jax.vjp(normed, middle, gain_two)
    grad_middle_norm, gain_two_grad = norm_pull(grad_two)
    grad_middle = grad_float + grad_middle_norm
    grad_middle_low = grad_middle.astype(jnp.bfloat16)
    grad_out = contract_rows(mixed_heads, grad_middle_low)
    grad_mixed = against(grad_middle_low, full_out).astype(jnp.bfloat16)
    grad_by_head = jnp.transpose(grad_mixed.reshape(MICRO, micro_rows, HEADS, HEAD), (2, 0, 1, 3))

    def attend_back(running, pieces):
        key_total, value_total = running
        query_head, grad_head, total_head = pieces
        scores = (
            jnp.einsum("mqd,mkd->mqk", query_head, all_keys, preferred_element_type=jnp.float32)
            * score_scale
        )
        soft_weights = jnp.where(allowed, jnp.exp(scores - total_head[..., None]), 0.0)
        value_total = value_total + jnp.einsum(
            "mqk,mqd->mkd",
            soft_weights.astype(jnp.bfloat16),
            grad_head,
            preferred_element_type=jnp.float32,
        )
        grad_soft = jnp.einsum(
            "mqd,mkd->mqk", grad_head, all_values, preferred_element_type=jnp.float32
        )
        row_delta = jnp.sum(grad_soft * soft_weights, axis=2, keepdims=True)
        grad_scores = (soft_weights * (grad_soft - row_delta)).astype(jnp.bfloat16)
        grad_query_head = (
            jnp.einsum("mqk,mkd->mqd", grad_scores, all_keys, preferred_element_type=jnp.float32)
            * score_scale
        )
        key_total = (
            key_total
            + jnp.einsum(
                "mqk,mqd->mkd", grad_scores, query_head, preferred_element_type=jnp.float32
            )
            * score_scale
        )
        return ((key_total, value_total), grad_query_head)

    zero_block = jnp.zeros((MICRO, (reach_steps + 1) * micro_rows, HEAD), jnp.float32)
    totals, grad_query_heads = lax.scan(
        attend_back, (zero_block, zero_block), (by_head, grad_by_head, log_total)
    )
    key_total, value_total = totals

    def piece_of(total, distance_step):
        begin_row = (reach_steps - distance_step) * micro_rows
        return total[:, begin_row : begin_row + micro_rows].reshape(row_count, HEAD)

    own_key = piece_of(key_total, 0)
    own_value = piece_of(value_total, 0)
    for distance_step in range(1, reach_steps + 1):
        returned_pair = (
            passed_along(
                piece_of(key_total, distance_step).astype(jnp.bfloat16),
                ("dp", "fsdp"),
                -distance_step,
            ).astype(jnp.float32),
            passed_along(
                piece_of(value_total, distance_step).astype(jnp.bfloat16),
                ("dp", "fsdp"),
                -distance_step,
            ).astype(jnp.float32),
        )
        own_key = own_key + returned_pair[0]
        own_value = own_value + returned_pair[1]
    grad_value_rows = own_value.astype(jnp.bfloat16)
    grad_query_rot = jnp.transpose(grad_query_heads, (1, 2, 0, 3)).reshape(row_count, HEADS, HEAD)
    grad_query_raw = (
        rotate(grad_query_rot, cosine[:, None, :], -sine_table[:, None, :])
        .reshape(row_count, HEADS * HEAD)
        .astype(jnp.bfloat16)
    )
    grad_key_raw = rotate(own_key, cosine, -sine_table).astype(jnp.bfloat16)
    grad_query = contract_rows(normal_one, grad_query_raw)
    grad_key = contract_rows(normal_one, grad_key_raw)
    grad_value = contract_rows(normal_one, grad_value_rows)
    grad_one = (
        against(grad_query_raw, full_query)
        + against(grad_key_raw, full_key)
        + against(grad_value_rows, full_value)
    )
    first_value, first_pull = jax.vjp(normed, rows_float, gain_one)
    grad_rows_norm, gain_one_grad = first_pull(grad_one)
    grad_rows = (grad_middle + grad_rows_norm).astype(jnp.bfloat16)
    grad_gains = jnp.stack([gain_one_grad, gain_two_grad])
    sectioned = (
        lax.psum_scatter(
            grad_query.astype(jnp.bfloat16), "fsdp", scatter_dimension=1, tiled=True
        ).astype(jnp.float32),
        lax.psum_scatter(
            grad_key.astype(jnp.bfloat16), "fsdp", scatter_dimension=1, tiled=True
        ).astype(jnp.float32),
        lax.psum_scatter(
            grad_value.astype(jnp.bfloat16), "fsdp", scatter_dimension=1, tiled=True
        ).astype(jnp.float32),
        lax.psum_scatter(
            grad_out.astype(jnp.bfloat16), "fsdp", scatter_dimension=0, tiled=True
        ).astype(jnp.float32),
        lax.psum_scatter(
            grad_gate.astype(jnp.bfloat16), "fsdp", scatter_dimension=1, tiled=True
        ).astype(jnp.float32),
        lax.psum_scatter(
            grad_up.astype(jnp.bfloat16), "fsdp", scatter_dimension=1, tiled=True
        ).astype(jnp.float32),
        lax.psum_scatter(
            grad_down.astype(jnp.bfloat16), "fsdp", scatter_dimension=0, tiled=True
        ).astype(jnp.float32),
        lax.psum_scatter(
            grad_gains.astype(jnp.bfloat16), "fsdp", scatter_dimension=0, tiled=True
        ).astype(jnp.float32),
    )
    reduced = (
        lax.psum_scatter(sectioned[0], "dp", scatter_dimension=0, tiled=True),
        lax.psum_scatter(sectioned[1], "dp", scatter_dimension=0, tiled=True),
        lax.psum_scatter(sectioned[2], "dp", scatter_dimension=0, tiled=True),
        lax.psum_scatter(sectioned[3], "dp", scatter_dimension=1, tiled=True),
        lax.psum_scatter(sectioned[4], "dp", scatter_dimension=0, tiled=True),
        lax.psum_scatter(sectioned[5], "dp", scatter_dimension=0, tiled=True),
        lax.psum_scatter(sectioned[6], "dp", scatter_dimension=1, tiled=True),
        lax.psum_scatter(sectioned[7], "dp", scatter_dimension=1, tiled=True),
    )
    returned = (
        lax.all_to_all(
            result[bucket_order].reshape(peer_count, per_peer, model_width),
            "dp",
            split_axis=0,
            concat_axis=0,
            tiled=True,
        ),
        lax.all_to_all(
            grad_rows[bucket_order].reshape(peer_count, per_peer, model_width),
            "dp",
            split_axis=0,
            concat_axis=0,
            tiled=True,
        ),
    )
    output = jnp.zeros_like(tokens).at[picked].set(returned[0].reshape(row_count, model_width))
    input_grad = jnp.zeros_like(tokens).at[picked].set(returned[1].reshape(row_count, model_width))
    return (
        output,
        input_grad,
        reduced[0],
        reduced[1],
        reduced[2],
        reduced[3],
        reduced[4],
        reduced[5],
        reduced[6],
        reduced[7],
    )


MESH = pl.DeviceIdType.MESH
BF16 = jnp.bfloat16
F32 = jnp.float32
PLANE = 4
ANY = pl.BlockSpec(memory_space=pl.ANY)
VM = pl.BlockSpec(memory_space=pltpu.VMEM)
SM = pl.BlockSpec(memory_space=pltpu.SMEM)


def mm(left, right):
    return jnp.dot(left, right, preferred_element_type=F32)


def mm_nt(left, right):
    return lax.dot_general(left, right, (((1,), (1,)), ((), ())), preferred_element_type=F32)


def mm_tn(left, right):
    return lax.dot_general(left, right, (((0,), (0,)), ((), ())), preferred_element_type=F32)


class Place:
    def __init__(self, chips):
        self.chips = chips
        self.groups = chips // PLANE
        self.d = lax.axis_index("dp")
        self.f = lax.axis_index("fsdp")
        self.other = 1 - self.f
        self.g = self.d // PLANE
        self.p = self.d % PLANE
        self.x = self.p % 2
        self.y = self.p // 2

    def plane_pos(self, j):
        return ((self.y + j // 2) % 2) * 2 + (self.x + j % 2) % 2

    def plane_chip(self, j):
        return self.g * PLANE + self.plane_pos(j)

    def column_chip(self, k):
        return ((self.g + k) % self.groups) * PLANE + self.p


def greet_all(place):
    barrier = pltpu.get_barrier_semaphore()
    total = place.chips * 2
    me = place.d * 2 + place.f

    def signal(k, carry):
        to = (me + k) % total
        pl.semaphore_signal(barrier, inc=1, device_id=(to // 2, to % 2), device_id_type=MESH)
        return carry

    lax.fori_loop(1, total, signal, 0)
    pl.semaphore_wait(barrier, total - 1)


class Sent:
    def __init__(self):
        self.copies = []

    def remote(self, src, dst, send_sem, recv_sem, device):
        copy = pltpu.make_async_remote_copy(
            src_ref=src,
            dst_ref=dst,
            send_sem=send_sem,
            recv_sem=recv_sem,
            device_id=device,
            device_id_type=MESH,
        )
        copy.start()
        self.copies.append(copy)

    def finish(self):
        for copy in self.copies:
            copy.wait_send()
        self.copies = []


def arrived(ref, sem):
    pltpu.make_async_copy(ref, ref, sem).wait()


def iota(shape, dim):
    return lax.broadcasted_iota(jnp.int32, shape, dim)


def gain_spread(width, share):
    column = iota((128, width), 1).astype(F32)
    inside = column - jnp.floor((column + 0.5) * (1.0 / share)) * share
    row = iota((128, width), 0).astype(F32)
    return (inside == row).astype(BF16)


def own_stretch(chips, width, share):
    row = iota((chips, width), 0)
    column = iota((chips, width), 1)
    return (column >= row * share) & (column < row * share + share)


def gain_row(kvg_ref, which, chips, width, share):
    block = kvg_ref[which, :, share : share + 16, :].astype(F32)[:, 0, :].astype(BF16)
    spread = mm(block, gain_spread(width, share))
    return jnp.sum(jnp.where(own_stretch(chips, width, share), spread, 0.0), axis=0, keepdims=True)


def rms_scale(values):
    return lax.rsqrt(jnp.mean(values * values, axis=-1, keepdims=True) + EPSILON)


def turned(values, cosine, sine):
    return values * cosine + pltpu.roll(values, HEAD // 2, 1) * sine


def halves_in(first, second):
    front = iota(first.shape, 1) < HEAD // 2
    return (
        jnp.where(front, first, pltpu.roll(second, HEAD // 2, 1)),
        jnp.where(front, pltpu.roll(first, HEAD // 2, 1), second),
    )


class Chain:
    def __init__(self, place, piece, count, up_sems, down_sems, recv_sems):
        self.place, self.piece, self.count = place, piece, count
        self.up_sems, self.down_sems, self.recv_sems = up_sems, down_sems, recv_sems
        self.has_up = place.g + 1 < place.groups
        self.has_down = place.g >= 1

    def hop(self, a, origin, up):
        place = self.place
        ref = self.piece(a, origin)
        to = place.d + PLANE if up else place.d - PLANE
        sems = self.up_sems if up else self.down_sems
        return pltpu.make_async_remote_copy(
            src_ref=ref,
            dst_ref=ref,
            send_sem=sems.at[a, origin],
            recv_sem=self.recv_sems.at[a, origin],
            device_id=(to, place.f),
            device_id_type=MESH,
        )

    def start(self, a):
        def one(up):
            self.hop(a, self.place.g, up).start()

        pl.when(self.has_up)(functools.partial(one, True))
        pl.when(self.has_down)(functools.partial(one, False))

    def step(self, k, arrays, then):
        place = self.place

        def from_below():
            origin = place.g - k
            for a in arrays:
                arrived(self.piece(a, origin), self.recv_sems.at[a, origin])

                @pl.when(self.has_up)
                def _():
                    self.hop(a, origin, True).start()

                then(a, origin)

        def from_above():
            origin = place.g + k
            for a in arrays:
                arrived(self.piece(a, origin), self.recv_sems.at[a, origin])

                @pl.when(self.has_down)
                def _():
                    self.hop(a, origin, False).start()

                then(a, origin)

        pl.when(place.g >= k)(from_below)
        pl.when(place.g + k < place.groups)(from_above)

    def finish(self):
        place = self.place
        for k in range(place.groups):
            for a in range(self.count):

                @pl.when((place.g >= k) & self.has_up)
                def _():
                    self.hop(a, place.g - k, True).wait_send()

                @pl.when((place.g + k < place.groups) & self.has_down)
                def _():
                    self.hop(a, place.g + k, False).wait_send()


def forward_kernel(
    chips,
    reach,
    first_ref,
    deal_ref,
    deal_col_ref,
    cos_ref,
    sin_ref,
    tokens_ref,
    cot_ref,
    wq_ref,
    wot_ref,
    kvg_ref,
    gate_ref,
    up_ref,
    down_ref,
    full_three,
    full_q,
    full_ot,
    full_kvg,
    rows_out,
    pg_all,
    take_ref,
    place_ref,
    n1_ref,
    qs_ref,
    kv_ref,
    probs_ref,
    mixed_ref,
    middle_ref,
    n2_all,
    gain_two_ref,
    deal_all,
    give,
    got,
    bias_ref,
    branch_out,
    branch_in,
    deal_send,
    deal_recv,
    row_send,
    row_recv,
    attn_up,
    attn_down,
    attn_recv,
    fan_send,
    fan_recv,
    kvg_sems,
    stage_send,
    stage_recv,
    three_up,
    three_down,
    three_recv,
    relay_send,
    relay_recv,
    plane_send,
    plane_recv,
    n1_sems,
    kv_send,
    kv_recv,
    branch_sems,
    local_sems,
):
    place = Place(chips)
    d, f, other = place.d, place.f, place.other
    groups = place.groups
    rows, width = tokens_ref.shape
    share = wq_ref.shape[0]
    half = share // 2
    per = rows // chips
    part = gate_ref.shape[1] // 2
    micro = rows // MICRO
    heads = wq_ref.shape[1] // HEAD
    span = (2 * reach + 1) * micro
    sent = Sent()
    greet_all(place)

    deal_all[d] = deal_ref[...]
    for k in range(1, chips):
        to = (d + k) % chips
        sent.remote(deal_all.at[d], deal_all.at[d], deal_send.at[k], deal_recv.at[d], (to, f))

    def attn_piece(a, s):
        if a == 0:
            return full_kvg.at[f, s]
        band = pl.ds(pl.multiple_of(s * share, 16), share)
        return (full_q if a == 1 else full_ot).at[band]

    own_attn = (kvg_ref, wq_ref, wot_ref)
    copies = [
        pltpu.make_async_copy(own_attn[a], attn_piece(a, d), local_sems.at[a]) for a in range(3)
    ]
    for copy in copies:
        copy.start()
    for copy in copies:
        copy.wait()
    attn = Chain(
        place, lambda a, g: attn_piece(a, g * PLANE + place.p), 3, attn_up, attn_down, attn_recv
    )

    def fan(a, g):
        for j in range(1, PLANE if a == 0 else PLANE - 1):
            fan_copy(a, g, j).start()

    def fan_copy(a, g, j):
        s = g * PLANE + place.p
        return pltpu.make_async_remote_copy(
            src_ref=attn_piece(a, s),
            dst_ref=attn_piece(a, s),
            send_sem=fan_send.at[a, g, j],
            recv_sem=fan_recv.at[a, s],
            device_id=(place.plane_chip(j), f),
            device_id_type=MESH,
        )

    def pass_copy(a, g):
        by_x = place.plane_pos(1)
        by_y = place.plane_pos(2)
        even = g % 2 == 0
        s = g * PLANE + jnp.where(even, by_x, by_y)
        to = jnp.where(even, place.plane_chip(2), place.plane_chip(1))
        return pltpu.make_async_remote_copy(
            src_ref=attn_piece(a, s),
            dst_ref=attn_piece(a, s),
            send_sem=fan_send.at[a, g, PLANE - 1],
            recv_sem=fan_recv.at[a, s],
            device_id=(to, f),
            device_id_type=MESH,
        )

    def pass_on(a, g):
        s = g * PLANE + jnp.where(g % 2 == 0, place.plane_pos(1), place.plane_pos(2))
        arrived(attn_piece(a, s), fan_recv.at[a, s])
        pass_copy(a, g).start()

    def pass_all(a):
        pass_on(a, place.g)
        for k in range(1, groups):
            pl.when(place.g >= k)(functools.partial(pass_on, a, place.g - k))
            pl.when(place.g + k < groups)(functools.partial(pass_on, a, place.g + k))

    for a in range(2):
        attn.start(a)
        fan(a, place.g)
    attn.start(2)

    mats = (gate_ref, up_ref, down_ref)

    def stage_src(a, to_x, core):
        return mats[a].at[pl.ds(half * core, half), pl.ds(pl.multiple_of(part * to_x, 128), part)]

    def stage_copy(a, b, core):
        to_x = (place.x + b) % 2
        return pltpu.make_async_remote_copy(
            src_ref=stage_src(a, to_x, core),
            dst_ref=full_three.at[a, d, core],
            send_sem=stage_send.at[a, b, core],
            recv_sem=stage_recv.at[a, place.p],
            device_id=(place.g * PLANE + 2 * f + to_x, core),
            device_id_type=MESH,
        )

    def own_copy(a):
        return pltpu.make_async_copy(
            mats[a].at[pl.ds(pl.multiple_of(half * f, 16), half), pl.ds(pl.multiple_of(part * place.x, 128), part)],
            full_three.at[a, d, f],
            local_sems.at[a],
        )

    def pair_copy(a):
        return pltpu.make_async_remote_copy(
            src_ref=mats[a].at[
                pl.ds(pl.multiple_of(half * other, 16), half),
                pl.ds(pl.multiple_of(part * place.x, 128), part),
            ],
            dst_ref=full_three.at[a, d, other],
            send_sem=stage_send.at[a, 0, 0],
            recv_sem=stage_recv.at[a, place.p],
            device_id=(d, other),
            device_id_type=MESH,
        )

    for a in range(3):
        for core in range(2):
            stage_copy(a, 1, core).start()

        @pl.when(place.y != f)
        def _():
            for core in range(2):
                stage_copy(a, 0, core).start()

        @pl.when(place.y == f)
        def _():
            own_copy(a).start()
            pair_copy(a).start()

    for k in range(1, chips):
        s = (d + k) % chips
        arrived(deal_all.at[s], deal_recv.at[s])
    chip_bits = (2 * rows).bit_length() - 1
    deals = deal_all[:, 0, :]
    wants = lax.shift_right_logical(deals, chip_bits) == d
    offset = deals & (rows - 1)
    earlier = (iota((rows, rows), 0) < iota((rows, rows), 1)).astype(BF16)
    rank = mm(wants.astype(F32).astype(BF16), earlier)
    for j in range(chips):
        hit = wants[j : j + 1, :] & (rank[j : j + 1, :] == iota((per, rows), 0).astype(F32))
        index = jnp.sum(jnp.where(hit, offset[j : j + 1, :], 0), axis=1, keepdims=True)
        take_ref[j * per : (j + 1) * per, :] = (
            (index == iota((per, rows), 1)).astype(F32).astype(BF16)
        )

    def block(k):
        return pl.ds(pl.multiple_of(k * per, per), per)

    def give_rows(i, source_ref):
        give[i] = mm(take_ref[...], source_ref[...]).astype(BF16)
        for k in range(1, chips):
            to = (d + k) % chips
            sent.remote(
                give.at[i, block(to)],
                got.at[i, block(d)],
                row_send.at[i, k],
                row_recv.at[i, d],
                (to, f),
            )
        got[i, block(d), :] = give[i, block(d), :]

    def take_rows(i):
        for k in range(1, chips):
            s = (d + k) % chips
            arrived(got.at[i, block(s)], row_recv.at[i, s])
        return mm(place_ref[...], got[i])

    give_rows(0, tokens_ref)
    def soon(a, g):
        if a < 2:
            fan(a, g)

    def column_pass(k, a):
        pl.when(place.g >= k)(functools.partial(pass_on, a, place.g - k))
        pl.when(place.g + k < groups)(functools.partial(pass_on, a, place.g + k))

    def make_bias(hm, carry):
        h, m = hm // 2, hm % 2
        first = first_ref[m]
        query = (2 * d + h) * micro + iota((span, micro), 1)
        key = (2 * d + h - 2 * reach) * micro + iota((span, micro), 0)
        allowed = (
            (jnp.where(query >= first, 1, 0) == jnp.where(key >= first, 1, 0))
            & (key >= 0)
            & (key <= query)
            & (query - key < WINDOW)
        )
        bias_ref[hm] = jnp.where(allowed, 0.0, NEGATIVE)
        return carry

    lax.fori_loop(0, 4, make_bias, 0)

    attn.step(1, (0, 1, 2), soon)
    pass_on(1, place.g)
    source_col = lax.shift_right_logical(deal_col_ref[...], chip_bits)
    source_row = lax.shift_right_logical(deal_ref[0:1, :], chip_bits)
    same = (source_col == source_row) & (iota((rows, rows), 1) < iota((rows, rows), 0))
    order = jnp.sum(same.astype(F32), axis=1, keepdims=True).astype(jnp.int32)
    where_from = source_col * per + order
    place_ref[...] = (where_from == iota((rows, rows), 1)).astype(F32).astype(BF16)
    three = Chain(
        place,
        lambda a, g: full_three.at[a, pl.ds(g * PLANE, PLANE), f],
        3,
        three_up,
        three_down,
        three_recv,
    )

    def relay_copy(a, g):
        ref = full_three.at[a, pl.ds(g * PLANE, PLANE), f]
        return pltpu.make_async_remote_copy(
            src_ref=ref,
            dst_ref=ref,
            send_sem=relay_send.at[a, g],
            recv_sem=relay_recv.at[a, g],
            device_id=(d, other),
            device_id_type=MESH,
        )

    def relay(a, g):
        relay_copy(a, g).start()

    def three_start(a):
        for j in range(1, PLANE):
            pos = place.plane_pos(j)
            arrived(full_three.at[a, place.g * PLANE + pos, f], stage_recv.at[a, pos])

        @pl.when(place.y == f)
        def _():
            own_copy(a).wait()

        @pl.when(place.y != f)
        def _():
            arrived(full_three.at[a, d, f], stage_recv.at[a, place.p])

        three.start(a)
        relay(a, place.g)

    for k in range(2, groups):
        attn.step(k, (0, 1, 2), soon)
        column_pass(k - 1, 1)
        if k == groups - 2:
            three_start(0)
            give_rows(1, cot_ref)
    row_values = take_rows(0)
    column_pass(groups - 1, 1)

    for g in range(groups):
        fan(2, g)
    rows_out[...] = row_values.astype(BF16)

    def attn_wait(a):
        for g in range(groups):
            if a == 0:
                left = range(1, PLANE)
            else:
                left = (2 - g % 2, 3)
            for j in left:
                s = g * PLANE + place.plane_pos(j)
                arrived(attn_piece(a, s), fan_recv.at[a, s])

    def spread_copy(i, block_ref, pos, side, to, slot):
        piece = block_ref.at[pos, pl.ds(side * micro, micro)]
        return pltpu.make_async_remote_copy(
            src_ref=piece,
            dst_ref=piece,
            send_sem=plane_send.at[i, slot],
            recv_sem=plane_recv.at[i, pos, side],
            device_id=(to, f),
            device_id_type=MESH,
        )

    by_x, by_y, far = (place.plane_pos(j) for j in range(1, PLANE))
    to_x, to_y = place.plane_chip(1), place.plane_chip(2)

    def spread(i, block_ref):
        sends = ((0, to_x), (1, to_y), (1, to_x), (0, to_y))
        for slot, (side, to) in enumerate(sends):
            copy = spread_copy(i, block_ref, place.p, side, to, slot)
            copy.start()
            sent.copies.append(copy)

    def spread_on(i, block_ref):
        for slot, pos, side, to in ((4, by_x, 0, to_y), (5, by_y, 1, to_x)):
            arrived(block_ref.at[pos, pl.ds(side * micro, micro)], plane_recv.at[i, pos, side])
            copy = spread_copy(i, block_ref, pos, side, to, slot)
            copy.start()
            sent.copies.append(copy)

    def spread_wait(i, block_ref):
        for pos, side in ((by_x, 1), (by_y, 0), (far, 0), (far, 1)):
            arrived(block_ref.at[pos, pl.ds(side * micro, micro)], plane_recv.at[i, pos, side])

    attn_wait(0)
    sent.remote(full_kvg.at[f], full_kvg.at[f], kvg_sems.at[0], kvg_sems.at[1], (d, other))
    arrived(full_kvg.at[other], kvg_sems.at[1])

    gain_one = gain_row(full_kvg, 0, chips, width, share)
    n1_ref[f] = (row_values * rms_scale(row_values) * gain_one).astype(BF16)
    sent.remote(n1_ref.at[f], n1_ref.at[f], n1_sems.at[0], n1_sems.at[1], (d, other))

    kvw = [full_kvg[i, :, 0:share, :].reshape(width, HEAD) for i in range(2)]
    raw = [mm(n1_ref[f], kvw[i]) for i in range(2)]
    key_raw, value_raw = halves_in(raw[0], raw[1])
    for m in range(MICRO):
        hm = 2 * f + m
        band = slice(m * micro, (m + 1) * micro)
        key = turned(key_raw[band], cos_ref[hm], sin_ref[hm])
        kv_ref[m, 2 * reach + f, :, 0:HEAD] = key.astype(BF16)
        kv_ref[m, 2 * reach + f, :, HEAD:] = value_raw[band].astype(BF16)
    own_kv = kv_ref.at[:, 2 * reach + f]

    def kv_copy(j, core):
        slot = 2 * reach + f - 2 * j
        return pltpu.make_async_remote_copy(
            src_ref=own_kv,
            dst_ref=kv_ref.at[:, slot],
            send_sem=kv_send.at[j, core],
            recv_sem=kv_recv.at[slot],
            device_id=(d + j, core),
            device_id_type=MESH,
        )

    sent.remote(own_kv, own_kv, kv_send.at[0, 0], kv_recv.at[2 * reach + f], (d, other))
    for j in range(1, reach + 1):

        @pl.when(d + j < chips)
        def _():
            for core in range(2):
                kv_copy(j, core).start()

        @pl.when(d - j < 0)
        def _():
            for core in range(2):
                kv_ref[:, 2 * reach - 2 * j + core] = jnp.zeros((MICRO, micro, 2 * HEAD), BF16)

    three_start(1)
    three_start(2)

    def project(h):
        raw_q = mm(n1_ref[h], full_q[...])
        for m in range(MICRO):
            hm = 2 * h + m
            cosine, sine = cos_ref[hm], sin_ref[hm]
            for i in range(heads):
                one = raw_q[m * micro : (m + 1) * micro, i * HEAD : (i + 1) * HEAD]
                qs_ref[hm, i * micro : (i + 1) * micro, :] = turned(one, cosine, sine).astype(BF16)

    attn_wait(1)
    project(f)
    arrived(n1_ref.at[other], n1_sems.at[1])
    project(other)
    three.step(1, (0,), relay)

    arrived(kv_ref.at[:, 2 * reach + other], kv_recv.at[2 * reach + other])
    for j in range(1, reach + 1):

        @pl.when(d - j >= 0)
        def _():
            for core in range(2):
                slot = 2 * reach - 2 * j + core
                arrived(kv_ref.at[:, slot], kv_recv.at[slot])

    score_scale = HEAD ** (-0.5)

    def attend(hm):
        h, m = hm // 2, hm % 2
        keys = kv_ref[m, h : h + 2 * reach + 1, :, 0:HEAD].reshape(span, HEAD)
        values_t = kv_ref[m, h : h + 2 * reach + 1, :, HEAD:].reshape(span, HEAD).T

        def pair_step(pair, carry):
            start = pl.multiple_of(pair * 2 * micro, 2 * micro)
            band = pl.ds(start, 2 * micro)
            bias = bias_ref[hm]
            scores = mm_nt(keys, qs_ref[hm, band, :]) * score_scale + jnp.concatenate(
                [bias, bias], axis=1
            )
            exp_scores = jnp.exp(scores - jnp.max(scores, axis=0, keepdims=True))
            total = jnp.sum(exp_scores, axis=0, keepdims=True)
            probs = (exp_scores * (1.0 / total)).astype(BF16)
            probs_ref[hm, :, band] = probs
            out_t = mm(values_t, probs)
            mixed_ref[hm, :, band] = jnp.concatenate(
                [out_t[:, i * micro : (i + 1) * micro].T for i in range(2)], axis=1
            ).astype(BF16)
            return carry

        lax.fori_loop(0, heads // 2, pair_step, 0)

    attend(0)
    three.step(1, (1,), relay)
    pass_all(2)
    pg_all[place.p] = take_rows(1).astype(BF16)
    spread(0, pg_all)
    attend(1)
    three.step(1, (2,), relay)
    attend(2)
    three.step(2, (0,), relay)
    attend(3)

    def branch(h):
        return mm_nt(mixed_ref[pl.ds(2 * h, 2)].reshape(rows, heads * HEAD), full_ot[...])

    attn_wait(2)
    spread_on(0, pg_all)
    branch_out[...] = branch(other).astype(BF16)
    sent.remote(branch_out, branch_in, branch_sems.at[0], branch_sems.at[1], (d, other))
    own = branch(f)
    arrived(branch_in, branch_sems.at[1])
    middle = rows_out[...].astype(F32) + own + branch_in[...].astype(F32)
    middle_ref[...] = middle
    gain_two = gain_row(full_kvg, 1, chips, width, share)
    gain_two_ref[...] = gain_two
    n2_all[place.p] = (middle * rms_scale(middle) * gain_two).astype(BF16)
    spread(1, n2_all)
    three.step(2, (1,), relay)
    spread_on(1, n2_all)
    three.step(2, (2,), relay)
    for k in range(3, groups):
        three.step(k, (0, 1, 2), relay)

    for g in range(groups):
        for a in range(3):
            arrived(full_three.at[a, pl.ds(g * PLANE, PLANE), other], relay_recv.at[a, g])
    spread_wait(0, pg_all)
    spread_wait(1, n2_all)

    attn.finish()
    three.finish()
    for g in range(groups):
        for a in range(3):
            relay_copy(a, g).wait_send()
            for j in range(1, PLANE if a == 0 else PLANE - 1):
                fan_copy(a, g, j).wait_send()
            if a > 0:
                pass_copy(a, g).wait_send()
    for a in range(3):
        for core in range(2):
            stage_copy(a, 1, core).wait_send()

        @pl.when(place.y != f)
        def _():
            for core in range(2):
                stage_copy(a, 0, core).wait_send()

        @pl.when(place.y == f)
        def _():
            pair_copy(a).wait_send()

    for j in range(1, reach + 1):

        @pl.when(d + j < chips)
        def _():
            for core in range(2):
                kv_copy(j, core).wait_send()

    sent.finish()


def forward(chips, reach, first_len, deal, cosine, sine, tokens, cotangent, wq, wot, kvg, gate, up, down):
    rows, width = tokens.shape
    share = wq.shape[0]
    groups = chips // PLANE
    part = gate.shape[1] // 2
    micro = rows // MICRO
    heads = wq.shape[1] // HEAD
    slots = 2 * reach + 2
    span = (2 * reach + 1) * micro
    dma = pltpu.SemaphoreType.DMA
    shape = jax.ShapeDtypeStruct
    deal_rows = jnp.broadcast_to(deal[None, :], (8, rows))
    deal_col = jnp.broadcast_to(deal[:, None], (rows, rows))
    return pl.pallas_call(
        functools.partial(forward_kernel, chips, reach),
        out_shape=(
            shape((3, chips, 2, share // 2, part), BF16),
            shape((width, wq.shape[1]), BF16),
            shape((width, wq.shape[1]), BF16),
            shape((2, chips) + kvg.shape, BF16),
            shape((rows, width), BF16),
            shape((PLANE, rows, width), BF16),
            shape((rows, rows), BF16),
            shape((rows, rows), BF16),
            shape((2, rows, width), BF16),
            shape((4, heads * micro, HEAD), BF16),
            shape((MICRO, slots, micro, 2 * HEAD), BF16),
            shape((4, span, heads * micro), BF16),
            shape((4, micro, heads * HEAD), BF16),
            shape((rows, width), F32),
            shape((PLANE, rows, width), BF16),
            shape((1, width), F32),
        ),
        in_specs=[SM] + [VM] * 6 + [ANY] * 6,
        out_specs=(ANY,) + (VM,) * 15,
        scratch_shapes=[
            pltpu.VMEM((chips, 8, rows), jnp.int32),
            pltpu.VMEM((2, rows, width), BF16),
            pltpu.VMEM((2, rows, width), BF16),
            pltpu.VMEM((4, span, micro), F32),
            pltpu.VMEM((rows, width), BF16),
            pltpu.VMEM((rows, width), BF16),
            dma((chips,)),
            dma((chips,)),
            dma((2, chips)),
            dma((2, chips)),
            dma((3, groups)),
            dma((3, groups)),
            dma((3, groups)),
            dma((3, groups, PLANE)),
            dma((3, chips)),
            dma((2,)),
            dma((3, 2, 2)),
            dma((3, PLANE)),
            dma((3, groups)),
            dma((3, groups)),
            dma((3, groups)),
            dma((3, groups)),
            dma((3, groups)),
            dma((2, 6)),
            dma((2, PLANE, 2)),
            dma((2,)),
            dma((reach + 1, 2)),
            dma((slots,)),
            dma((2,)),
            dma((3,)),
        ],
        compiler_params=pltpu.CompilerParams(
            collective_id=0, has_side_effects=True, vmem_limit_bytes=VMEM_ASK
        ),
        name="gather_and_attention",
    )(first_len, deal_rows, deal_col, cosine, sine, tokens, cotangent, wq, wot, kvg, gate, up, down)


def norm_back(values, gain, grad):
    scale = rms_scale(values)
    unit = values * scale
    lifted = grad * gain
    gain_grad = jnp.sum(grad * unit, axis=0, keepdims=True)
    back = scale * (lifted - unit * jnp.mean(lifted * unit, axis=-1, keepdims=True))
    return back, gain_grad


def mlp_kernel(
    chips,
    n2_all,
    middle_ref,
    pg_ref,
    gain_ref,
    three_hbm,
    out_ref,
    two_ref,
    gain_grad_ref,
    half_ref,
    three_ref,
    turned_ref,
    hidden_ref,
    gate_rows_ref,
    up_rows_ref,
    two_give,
    two_got,
    out_give,
    out_got,
    out_total,
    pair_got,
    load_sems,
    two_send,
    two_recv,
    out_send,
    out_recv,
    pair_send,
    pair_recv,
):
    place = Place(chips)
    d, f, other = place.d, place.f, place.other
    groups = place.groups
    rows, width = middle_ref.shape
    part = three_ref.shape[-1]
    plane_width = width // groups
    loads = [
        pltpu.make_async_copy(three_hbm.at[a], three_ref.at[a], load_sems.at[a]) for a in range(3)
    ]
    for load in loads:
        load.start()
    greet_all(place)

    def weight(a):
        return three_ref[a].reshape(width, part)

    def two_copy(j):
        return pltpu.make_async_remote_copy(
            src_ref=two_give.at[j - 1],
            dst_ref=two_got.at[j - 1],
            send_sem=two_send.at[j],
            recv_sem=two_recv.at[j],
            device_id=(place.plane_chip(j), f),
            device_id_type=MESH,
        )

    def out_copy(j):
        return pltpu.make_async_remote_copy(
            src_ref=out_give.at[j - 1],
            dst_ref=out_got.at[j - 1],
            send_sem=out_send.at[j],
            recv_sem=out_recv.at[j],
            device_id=(place.plane_chip(j), f),
            device_id_type=MESH,
        )

    curve = 0.7978845608028654
    cubic = 0.044715
    for load in loads:
        load.wait()

    def at_turn(i):
        return ((i + 2) % 3 + 1) * (1 - i // 3)

    def band_of(pos):
        return pl.ds(pl.multiple_of(pos * rows, rows), rows)

    def one_block(i, carry):
        j = at_turn(i)
        pos = place.plane_pos(j)
        x = n2_all[pos]
        gate = mm(x, weight(0))
        upward = mm(x, weight(1))
        grad_hidden = mm(pg_ref[pos], weight(2))
        square = gate * gate
        tanh = jnp.tanh(curve * gate * (1.0 + cubic * square))
        activated = 0.5 * gate * (1.0 + tanh)
        slope = 0.5 * (1.0 + tanh) + (0.5 * curve) * gate * (1.0 - tanh * tanh) * (
            1.0 + (3.0 * cubic) * square
        )
        band = band_of(pos)
        hidden_ref[band, :] = (activated * upward).astype(BF16)
        gate_rows_ref[band, :] = (grad_hidden * upward * slope).astype(BF16)
        up_rows_ref[band, :] = (grad_hidden * activated).astype(BF16)
        back = mm_nt(gate_rows_ref[band, :], weight(0)) + mm_nt(up_rows_ref[band, :], weight(1))

        @pl.when(j > 0)
        def _():
            two_give[j - 1] = back.astype(BF16)
            two_copy(j).start()

        @pl.when(j == 0)
        def _():
            two_ref[...] = back

        return carry

    lax.fori_loop(0, PLANE, one_block, 0)

    def out_block(i, carry):
        j = at_turn(i)
        piece = mm_nt(hidden_ref[band_of(place.plane_pos(j)), :], weight(2))

        @pl.when(j > 0)
        def _():
            out_give[j - 1] = piece.astype(BF16)
            out_copy(j).start()

        @pl.when(j == 0)
        def _():
            out_total[...] = middle_ref[...] + piece

        return carry

    lax.fori_loop(0, PLANE, out_block, 0)

    def turn(source):
        def step(i, carry):
            turned_ref[:, band_of(i)] = source[i].T
            return carry

        lax.fori_loop(0, PLANE, step, 0)

    def pair_copy(a, g):
        return pltpu.make_async_remote_copy(
            src_ref=three_ref.at[a, pl.ds(g * PLANE, PLANE), other],
            dst_ref=pair_got.at[a, g],
            send_sem=pair_send.at[a, g],
            recv_sem=pair_recv.at[a, g],
            device_id=(d, other),
            device_id_type=MESH,
        )

    def weight_grad(a, right):
        def step(g, carry):
            at = pl.ds(pl.multiple_of(g * plane_width, 128), plane_width)
            piece = mm(turned_ref[at, :], right[...]).astype(BF16)
            three_ref[a, pl.ds(g * PLANE, PLANE)] = piece.reshape(
                PLANE, 2, plane_width // (2 * PLANE), part
            )
            pair_copy(a, g).start()
            return carry

        lax.fori_loop(0, groups, step, 0)

    def pair_sum(a):
        def step(g, carry):
            arrived(pair_got.at[a, g], pair_recv.at[a, g])
            half_ref[a, g] = (
                three_ref[a, pl.ds(g * PLANE, PLANE), f].astype(F32) + pair_got[a, g].astype(F32)
            ).astype(BF16)
            return carry

        lax.fori_loop(0, groups, step, 0)

    turn(pg_ref)
    weight_grad(2, hidden_ref)
    turn(n2_all)
    weight_grad(0, gate_rows_ref)
    pair_sum(2)
    weight_grad(1, up_rows_ref)
    pair_sum(0)
    for j in (1, 2, 3):
        arrived(two_got.at[j - 1], two_recv.at[j])
        two_ref[...] = two_ref[...] + two_got[j - 1].astype(F32)
    back, gain_grad_ref[...] = norm_back(middle_ref[...], gain_ref[...], two_ref[...])
    two_ref[...] = pg_ref[place.p].astype(F32) + back
    pair_sum(1)
    for j in (1, 2, 3):
        arrived(out_got.at[j - 1], out_recv.at[j])
        out_total[...] = out_total[...] + out_got[j - 1].astype(F32)
    out_ref[...] = out_total[...].astype(BF16)
    for j in range(1, PLANE):
        two_copy(j).wait_send()
        out_copy(j).wait_send()
    for a in range(3):
        for g in range(groups):
            pair_copy(a, g).wait_send()


def mlp(chips, n2, middle, pg_all, gain_two, three):
    rows, width = middle.shape
    part = three.shape[-1]
    groups = chips // PLANE
    dma = pltpu.SemaphoreType.DMA
    shape = jax.ShapeDtypeStruct
    wide = PLANE * rows
    halves = (3, groups, PLANE) + three.shape[3:]
    return pl.pallas_call(
        functools.partial(mlp_kernel, chips),
        out_shape=(
            shape((rows, width), BF16),
            shape((rows, width), F32),
            shape((1, width), F32),
            shape(halves, BF16),
        ),
        in_specs=[VM] * 4 + [ANY],
        out_specs=(VM,) * 4,
        scratch_shapes=[
            pltpu.VMEM(three.shape, BF16),
            pltpu.VMEM((width, wide), BF16),
            pltpu.VMEM((wide, part), BF16),
            pltpu.VMEM((wide, part), BF16),
            pltpu.VMEM((wide, part), BF16),
        ]
        + [pltpu.VMEM((PLANE - 1, rows, width), BF16)] * 4
        + [pltpu.VMEM((rows, width), F32), pltpu.VMEM(halves, BF16), dma((3,))]
        + [dma((PLANE,))] * 4
        + [dma((3, groups))] * 2,
        compiler_params=pltpu.CompilerParams(
            collective_id=1, has_side_effects=True, vmem_limit_bytes=VMEM_ASK
        ),
        name="mlp_both_ways",
    )(n2, middle, pg_all, gain_two, three)


class ChainSum:
    def __init__(self, place, value, got, last, give, up_sems, down_sems, recv_sems, last_sems):
        self.place, self.value, self.got, self.last, self.give = place, value, got, last, give
        self.up_sems, self.down_sems = up_sems, down_sems
        self.recv_sems, self.last_sems = recv_sems, last_sems
        self.has_up = place.g + 1 < place.groups
        self.has_down = place.g >= 1

    def hop(self, a, g, k, up):
        to_last = k == 1 and not up
        place = self.place
        return pltpu.make_async_remote_copy(
            src_ref=self.give(a, g),
            dst_ref=self.last(a) if to_last else self.got(a, g),
            send_sem=(self.up_sems if up else self.down_sems).at[a, g],
            recv_sem=self.last_sems.at[a] if to_last else self.recv_sems.at[a, g],
            device_id=(place.d + PLANE if up else place.d - PLANE, place.f),
            device_id_type=MESH,
        )

    def step(self, a, k):
        place = self.place

        def toward(up):
            g = place.g + k if up else place.g - k
            total = self.value(a, k, up)
            from_behind = self.has_down if up else self.has_up

            @pl.when(from_behind)
            def _():
                arrived(self.got(a, g), self.recv_sems.at[a, g])
                self.give(a, g)[...] = (total + self.got(a, g)[...].astype(F32)).astype(BF16)

            @pl.when(jnp.logical_not(from_behind))
            def _():
                self.give(a, g)[...] = total.astype(BF16)

            self.hop(a, g, k, up).start()

        pl.when(place.g + k < place.groups)(functools.partial(toward, True))
        pl.when(place.g >= k)(functools.partial(toward, False))

    def final(self, a):
        place = self.place
        got, last = self.got(a, place.g), self.last(a)

        @pl.when(self.has_down)
        def _():
            arrived(got, self.recv_sems.at[a, place.g])

        @pl.when(jnp.logical_not(self.has_down))
        def _():
            got[...] = jnp.zeros(got.shape, BF16)

        @pl.when(self.has_up)
        def _():
            arrived(last, self.last_sems.at[a])

        @pl.when(jnp.logical_not(self.has_up))
        def _():
            last[...] = jnp.zeros(last.shape, BF16)

        return self.value(a, 0, True) + got[...].astype(F32) + last[...].astype(F32)

    def finish(self, count):
        place = self.place
        for a in range(count):
            for k in range(1, place.groups):

                @pl.when(place.g + k < place.groups)
                def _():
                    self.hop(a, place.g + k, k, True).wait_send()

                @pl.when(place.g >= k)
                def _():
                    self.hop(a, place.g - k, k, False).wait_send()


def backward_kernel(
    chips,
    reach,
    outs_ref,
    rows_ref,
    grad_middle_ref,
    gain_two_grad_ref,
    n1_ref,
    qs_ref,
    kv_ref,
    mixed_ref,
    wq_ref,
    wot_ref,
    kvg_ref,
    cos_ref,
    sin_ref,
    take_ref,
    place_ref,
    probs_hbm,
    half_hbm,
    three_end,
    q_out,
    ot_out,
    kvg_out,
    output_ref,
    input_grad_ref,
    probs_ref,
    low_ref,
    lows_t,
    mixed_rows,
    grad_mixed,
    grad_q,
    kv_total,
    kv_give,
    kv_pair,
    kv_got,
    one_out,
    one_in,
    three_got,
    three_last,
    three_stage,
    heads_ref,
    plane_relay,
    plane_got,
    column_got,
    column_last,
    column_give,
    gkvg_ref,
    gkvg_pair,
    small_got,
    small_give,
    small_column,
    give,
    got,
    probs_sems,
    stage_sems,
    low_sems,
    kv_send,
    kv_recv,
    one_sems,
    three_up,
    three_down,
    three_recv,
    three_last_sems,
    end_send,
    end_recv,
    direct_send,
    relay_send,
    relay_recv,
    plane_recv,
    small_send,
    small_recv,
    column_up,
    column_down,
    column_recv,
    column_last_sems,
    row_send,
    row_recv,
):
    place = Place(chips)
    d, f, other = place.d, place.f, place.other
    groups = place.groups
    rows, width = rows_ref.shape
    micro = rows // MICRO
    heads = wq_ref.shape[1] // HEAD
    share = width // chips
    half = share // 2
    part = half_hbm.shape[-1]
    per = rows // chips
    span = (2 * reach + 1) * micro
    by_x, by_y, far = (place.plane_pos(j) for j in range(1, PLANE))
    to_x, to_y = place.plane_chip(1), place.plane_chip(2)
    sent = Sent()

    pairs = heads // 2

    def probs_copy(n):
        band = pl.ds(pl.multiple_of((n % pairs) * 2 * micro, 2 * micro), 2 * micro)
        return pltpu.make_async_copy(
            probs_hbm.at[n // pairs, :, band], probs_ref.at[n % 2], probs_sems.at[n % 2]
        )

    probs_copy(0).start()
    greet_all(place)

    events = [(a, k) for k in range(groups - 1, -1, -1) for a in (2, 0, 1)]

    def stage_copy(n, up):
        a, k = events[n]
        slot = 0 if up else 1
        return pltpu.make_async_copy(
            half_hbm.at[a, place.g + k if up else place.g - k],
            three_stage.at[n % 2, slot],
            stage_sems.at[n % 2, slot],
        )

    def fetch(n):
        k = events[n][1]
        pl.when(place.g + k < groups)(stage_copy(n, True).start)
        if k > 0:
            pl.when(place.g >= k)(stage_copy(n, False).start)

    def three_value(a, k, up):
        n = events.index((a, k))
        stage_copy(n, up).wait()
        return three_stage[n % 2, 0 if up else 1].astype(F32)

    fetch(0)
    three = ChainSum(
        place,
        three_value,
        lambda a, g: three_got.at[a, g],
        lambda a: three_last.at[a],
        lambda a, g: three_got.at[a, g],
        three_up,
        three_down,
        three_recv,
        three_last_sems,
    )

    def three_steps(k, arrays=(2, 0, 1)):
        for a in arrays:
            fetch(events.index((a, k)) + 1)
            three.step(a, k)

    for k in range(groups - 1, 2, -1):
        three_steps(k)

    low_ref[f] = grad_middle_ref[...].astype(BF16)
    sent.remote(low_ref.at[f], low_ref.at[f], low_sems.at[0], low_sems.at[1], (d, other))
    kv_total[...] = jnp.zeros_like(kv_total)

    def block(k):
        return pl.ds(pl.multiple_of(k * per, per), per)

    def rows_home(i, source_ref):
        give[i] = mm_tn(place_ref[...], source_ref[...]).astype(BF16)
        for k in range(1, chips):
            to = (d + k) % chips
            sent.remote(
                give.at[i, block(to)],
                got.at[i, block(d)],
                row_send.at[i, k],
                row_recv.at[i, d],
                (to, f),
            )
        got[i, block(d), :] = give[i, block(d), :]

    def rows_back(i):
        for k in range(1, chips):
            s = (d + k) % chips
            arrived(got.at[i, block(s)], row_recv.at[i, s])
        return mm_tn(take_ref[...], got[i]).astype(BF16)

    def mix_back(h):
        grads = mm(low_ref[h], wot_ref[...])
        for m in range(MICRO):
            for i in range(heads):
                grad_mixed[2 * h + m, i * micro : (i + 1) * micro, :] = grads[
                    m * micro : (m + 1) * micro, i * HEAD : (i + 1) * HEAD
                ].astype(BF16)

    mix_back(f)
    arrived(low_ref.at[other], low_sems.at[1])
    mix_back(other)

    def whole(g, pos):
        return pl.ds(pl.multiple_of((g * PLANE + pos) * share, 16), share)

    def term(a, g, pos):
        return heads_ref.at[a, whole(g, pos)]

    def plane_copy(kind, a, g):
        even = g % 2 == 0
        near_pos, near_to, near_side = (by_x, to_x, 0) if even else (by_y, to_y, 1)
        if kind == 0:
            src, dst, to = term(a, g, near_pos), plane_got.at[a, near_side, g], near_to
            send, recv = direct_send.at[a, 0, g], plane_recv.at[a, near_side, g]
        elif kind == 1:
            src, dst, to = term(a, g, far), plane_relay.at[a, g], near_to
            send, recv = direct_send.at[a, 1, g], relay_recv.at[a, g]
        else:
            side = 1 - near_side
            src, dst, to = plane_relay.at[a, g], plane_got.at[a, side, g], to_y if even else to_x
            send, recv = relay_send.at[a, g], plane_recv.at[a, side, g]
        return pltpu.make_async_remote_copy(
            src_ref=src,
            dst_ref=dst,
            send_sem=send,
            recv_sem=recv,
            device_id=(to, f),
            device_id_type=MESH,
        )

    def plane_start(a):
        for g in range(groups):
            plane_copy(1, a, g).start()
            plane_copy(0, a, g).start()

    def plane_pass(a):
        for g in range(groups):
            arrived(plane_relay.at[a, g], relay_recv.at[a, g])
            mine = term(a, g, by_y if g % 2 == 0 else by_x)
            plane_relay[a, g] = (plane_relay[a, g].astype(F32) + mine[...].astype(F32)).astype(BF16)
            plane_copy(2, a, g).start()

    def plane_total(a, k, up):
        g = place.g + k if up else place.g - k
        total = term(a, g, place.p)[...].astype(F32)
        for side in range(2):
            arrived(plane_got.at[a, side, g], plane_recv.at[a, side, g])
            total = total + plane_got[a, side, g].astype(F32)
        return total

    column = ChainSum(
        place,
        plane_total,
        lambda a, g: column_got.at[a, g],
        lambda a: column_last.at[a],
        lambda a, g: column_give.at[a, g],
        column_up,
        column_down,
        column_recv,
        column_last_sems,
    )

    tile = 2 * HEAD

    def head_grads(a, left_ref):
        lows_t[:, 0:rows] = left_ref[0].T
        lows_t[:, rows:] = left_ref[1].T

        def step(i, carry):
            at = pl.ds(pl.multiple_of(i * tile, tile), tile)
            heads_ref[a, at, :] = mm(lows_t[at, :], mixed_rows[...]).astype(BF16)
            return carry

        lax.fori_loop(0, width // tile, step, 0)

    for hm in range(4):
        mixed_rows[hm * micro : (hm + 1) * micro, :] = mixed_ref[hm]
    head_grads(0, low_ref)
    plane_start(0)
    rows_home(0, outs_ref)
    for k in range(min(2, groups - 1), 1, -1):
        three_steps(k, (2,))

    score_scale = HEAD ** (-0.5)

    def attend_back(hm):
        h, m = hm // 2, hm % 2
        at = slice(h, h + 2 * reach + 1)
        keys = kv_ref[m, at, :, 0:HEAD].reshape(span, HEAD)
        values = kv_ref[m, at, :, HEAD:].reshape(span, HEAD)
        keys_t = keys.T

        def pair_step(pair, carry):
            key_total, value_total = carry
            band = pl.ds(pl.multiple_of(pair * 2 * micro, 2 * micro), 2 * micro)
            n = hm * pairs + pair
            probs_copy(n).wait()
            pl.when(n + 1 < 4 * pairs)(lambda: probs_copy(n + 1).start())
            probs = probs_ref[n % 2]
            grads = grad_mixed[hm, band, :]
            queries = qs_ref[hm, band, :]
            value_total = value_total + mm(probs, grads)
            grad_probs = mm_nt(values, grads)
            wide = probs.astype(F32)
            delta = jnp.sum(grad_probs * wide, axis=0, keepdims=True)
            grad_scores = (wide * (grad_probs - delta)).astype(BF16)
            key_total = key_total + mm(grad_scores, queries)
            query_t = mm(keys_t, grad_scores) * score_scale
            grad_q[hm, :, band] = jnp.concatenate(
                [
                    turned(
                        query_t[:, i * micro : (i + 1) * micro].T, cos_ref[hm], -sin_ref[hm]
                    )
                    for i in range(2)
                ],
                axis=1,
            ).astype(BF16)
            return key_total, value_total

        zero = jnp.zeros((span, HEAD), F32)
        key_total, value_total = lax.fori_loop(0, heads // 2, pair_step, (zero, zero))
        key_total = (key_total * score_scale).reshape(2 * reach + 1, micro, HEAD)
        kv_total[m, at, :, 0:HEAD] = kv_total[m, at, :, 0:HEAD] + key_total
        kv_total[m, at, :, HEAD:] = kv_total[m, at, :, HEAD:] + value_total.reshape(
            2 * reach + 1, micro, HEAD
        )

    attend_back(0)
    plane_pass(0)
    for k in range(min(2, groups - 1), 1, -1):
        three_steps(k, (0,))
    attend_back(1)
    for k in range(min(2, groups - 1), 1, -1):
        three_steps(k, (1,))
    attend_back(2)
    three_steps(1, (2,))
    attend_back(3)

    kv_give[...] = kv_total[...].astype(BF16)
    own_slots = [2 * j + f for j in range(reach + 1)]
    other_slots = [2 * j + other for j in range(reach + 1)]
    for j in range(reach + 1):
        sent.remote(
            kv_give.at[:, other_slots[j]],
            kv_pair.at[:, j],
            kv_send.at[0, j],
            kv_recv.at[0, j],
            (d, other),
        )

    def kv_copy(j):
        return pltpu.make_async_remote_copy(
            src_ref=kv_give.at[:, own_slots[reach - j]],
            dst_ref=kv_got.at[j],
            send_sem=kv_send.at[1, j],
            recv_sem=kv_recv.at[1, j],
            device_id=(d - j, f),
            device_id_type=MESH,
        )

    for hm in range(4):
        mixed_rows[hm * micro : (hm + 1) * micro, :] = grad_q[hm]
    for j in range(reach, -1, -1):
        s = reach - j
        arrived(kv_pair.at[:, s], kv_recv.at[0, s])
        total = kv_total[:, own_slots[s]] + kv_pair[:, s].astype(F32)
        kv_total[:, own_slots[s]] = total
        if j > 0:
            kv_give[:, own_slots[s]] = total.astype(BF16)

            @pl.when(d - j >= 0)
            def _():
                kv_copy(j).start()

    def one_back(h):
        at = pl.ds(pl.multiple_of(h * rows, rows), rows)
        return mm_nt(mixed_rows[at, :], wq_ref[...])

    one_out[...] = one_back(other).astype(BF16)
    sent.remote(one_out, one_in, one_sems.at[0], one_sems.at[1], (d, other))
    head_grads(1, n1_ref)
    plane_start(1)
    grad_one = one_back(f)
    plane_pass(1)

    sums = [kv_total[m, 2 * reach + f] for m in range(MICRO)]
    for j in range(1, reach + 1):

        @pl.when(d + j < chips)
        def _():
            arrived(kv_got.at[j], kv_recv.at[1, j])

        @pl.when(d + j >= chips)
        def _():
            kv_got[j] = jnp.zeros((MICRO, micro, 2 * HEAD), BF16)

        sums = [sums[m] + kv_got[j, m].astype(F32) for m in range(MICRO)]
    key_rows = jnp.concatenate(
        [
            turned(sums[m][:, 0:HEAD], cos_ref[2 * f + m], -sin_ref[2 * f + m])
            for m in range(MICRO)
        ],
        axis=0,
    )
    value_rows = jnp.concatenate([sums[m][:, HEAD:] for m in range(MICRO)], axis=0)
    pieces = halves_in(key_rows, value_rows)
    n1_own_t = n1_ref[f].T
    row_values = rows_ref[...].astype(F32)
    for i in range(2):
        piece = pieces[i].astype(BF16)
        gkvg_ref[i, :, 0:share, :] = mm(n1_own_t, piece).astype(BF16).reshape(chips, share, HEAD)
        grad_one = grad_one + mm_nt(piece, kvg_ref[i, :, 0:share, :].reshape(width, HEAD))
    arrived(one_in, one_sems.at[1])
    grad_one = grad_one + one_in[...].astype(F32)
    gain_one = gain_row(kvg_ref, 0, chips, width, share)
    back_one, gain_one_grad = norm_back(row_values, gain_one, grad_one)
    one_in[...] = (grad_middle_ref[...] + back_one).astype(BF16)
    rows_home(1, one_in)
    spread = gain_spread(width, share)
    stretch = own_stretch(chips, width, share)
    for i, grad in enumerate((gain_one_grad, gain_two_grad_ref[...])):
        piece = mm_nt(jnp.where(stretch, grad, 0.0).astype(BF16), spread)
        row = iota((chips, 16, HEAD), 1)
        gkvg_ref[i, :, share : share + 16, :] = jnp.where(
            row == 0, piece[:, None, :], 0.0
        ).astype(BF16)
    sent.remote(gkvg_ref.at[other], gkvg_pair, small_send.at[0], small_recv.at[0], (d, other))
    arrived(gkvg_pair, small_recv.at[0])

    def small_sum(s):
        return gkvg_ref[f, s].astype(F32) + gkvg_pair[s].astype(F32)

    for j in range(1, PLANE):
        pos = place.plane_pos(j)
        for g in range(groups):
            small_give[j, g] = small_sum(g * PLANE + pos).astype(BF16)
        sent.remote(
            small_give.at[j],
            small_got.at[j],
            small_send.at[j],
            small_recv.at[j],
            (place.plane_chip(j), f),
        )

    three_steps(1, (0, 1))
    for k in range(groups - 1, 0, -1):
        for a in range(2):
            column.step(a, k)
    for j in range(1, PLANE):
        arrived(small_got.at[j], small_recv.at[j])
    for k in range(1, groups):
        g = (place.g + k) % groups
        s = g * PLANE + place.p
        total = small_sum(s)
        for j in range(1, PLANE):
            total = total + small_got[j, g].astype(F32)
        small_give[0, g] = total.astype(BF16)
        sent.remote(
            small_give.at[0, g],
            small_column.at[place.g],
            small_send.at[PLANE + k],
            small_recv.at[PLANE + place.g],
            (s, f),
        )
    total = small_sum(d)
    for j in range(1, PLANE):
        total = total + small_got[j, place.g].astype(F32)
    kvg_out[...] = total

    def end_copy(a, j):
        pos = place.plane_pos(j)
        return pltpu.make_async_remote_copy(
            src_ref=three_got.at[a, place.g, pos],
            dst_ref=three_end.at[a, place.x, f],
            send_sem=end_send.at[a, j],
            recv_sem=end_recv.at[a, place.x, f],
            device_id=(place.plane_chip(j), place.y),
            device_id_type=MESH,
        )

    def end_local(a):
        return pltpu.make_async_copy(
            three_got.at[a, place.g, place.p], three_end.at[a, place.x, f], end_send.at[a, 0]
        )

    for a in (2, 0, 1):
        if a != 1:
            fetch(events.index((a, 0)) + 1)
        three_got[a, place.g] = three.final(a).astype(BF16)
        for j in range(1, PLANE):
            end_copy(a, j).start()
        pl.when(place.y == f)(end_local(a).start)
        pl.when(place.y != f)(end_copy(a, 0).start)

    output_ref[...] = rows_back(0)
    for a in range(2):
        (ot_out, q_out)[a][...] = column.final(a)
    for k in range(1, groups):
        g = (place.g + k) % groups
        arrived(small_column.at[g], small_recv.at[PLANE + g])
        kvg_out[...] = kvg_out[...] + small_column[g].astype(F32)
    input_grad_ref[...] = rows_back(1)
    for a in (2, 0, 1):
        for cx in range(2):
            for core in range(2):
                own = (place.y == f) & (place.x == cx) & (core == f)

                @pl.when(own)
                def _():
                    end_local(a).wait()

                @pl.when(jnp.logical_not(own))
                def _():
                    arrived(three_end.at[a, cx, core], end_recv.at[a, cx, core])

    three.finish(3)
    column.finish(2)
    for a in range(3):
        for j in range(1, PLANE):
            end_copy(a, j).wait_send()
        pl.when(place.y != f)(end_copy(a, 0).wait_send)
    for a in range(2):
        for g in range(groups):
            for kind in range(3):
                plane_copy(kind, a, g).wait_send()
    for j in range(1, reach + 1):

        @pl.when(d - j >= 0)
        def _():
            kv_copy(j).wait_send()

    sent.finish()


def backward(chips, reach, outs, rows_in, grad_middle, gain_two_grad, n1, qs, kv, mixed, wq, wot, kvg, cosine, sine, take, placing, probs, halves):
    rows, width = rows_in.shape
    micro = rows // MICRO
    heads_wide = wq.shape[1]
    heads = heads_wide // HEAD
    groups = chips // PLANE
    share = width // chips
    half, part = halves.shape[3:]
    slots = 2 * reach + 2
    small = kvg.shape[2:]
    dma = pltpu.SemaphoreType.DMA
    shape = jax.ShapeDtypeStruct
    vm = pltpu.VMEM
    kv_shape = (MICRO, slots, micro, 2 * HEAD)
    return pl.pallas_call(
        functools.partial(backward_kernel, chips, reach),
        out_shape=(
            shape((3, 2, 2, half, part), BF16),
            shape((share, heads_wide), F32),
            shape((share, heads_wide), F32),
            shape(small, F32),
            shape((rows, width), BF16),
            shape((rows, width), BF16),
        ),
        in_specs=[VM] * 15 + [ANY] * 2,
        out_specs=(ANY,) + (VM,) * 5,
        scratch_shapes=[
            vm((2, probs.shape[1], 2 * micro), BF16),
            vm((2, rows, width), BF16),
            vm((width, 2 * rows), BF16),
            vm((2 * rows, heads_wide), BF16),
            vm((4, heads * micro, HEAD), BF16),
            vm((4, micro, heads_wide), BF16),
            vm(kv_shape, F32),
            vm(kv_shape, BF16),
            vm((MICRO, reach + 1, micro, 2 * HEAD), BF16),
            vm((reach + 1, MICRO, micro, 2 * HEAD), BF16),
            vm((rows, width), BF16),
            vm((rows, width), BF16),
            vm((3, groups, PLANE, half, part), BF16),
            vm((3, PLANE, half, part), BF16),
            vm((2, 2, PLANE, half, part), BF16),
            vm((2, width, heads_wide), BF16),
            vm((2, groups, share, heads_wide), BF16),
            vm((2, 2, groups, share, heads_wide), BF16),
            vm((2, groups, share, heads_wide), BF16),
            vm((2, share, heads_wide), BF16),
            vm((2, groups, share, heads_wide), BF16),
            vm((2, chips) + small, BF16),
            vm((chips,) + small, BF16),
            vm((PLANE, groups) + small, BF16),
            vm((PLANE, groups) + small, BF16),
            vm((groups,) + small, BF16),
            vm((2, rows, width), BF16),
            vm((2, rows, width), BF16),
            dma((2,)),
            dma((2, 2)),
            dma((2,)),
            dma((2, reach + 1)),
            dma((2, reach + 1)),
            dma((2,)),
            dma((3, groups)),
            dma((3, groups)),
            dma((3, groups)),
            dma((3,)),
            dma((3, PLANE)),
            dma((3, 2, 2)),
            dma((2, 2, groups)),
            dma((2, groups)),
            dma((2, groups)),
            dma((2, 2, groups)),
            dma((PLANE + groups,)),
            dma((PLANE + groups,)),
            dma((2, groups)),
            dma((2, groups)),
            dma((2, groups)),
            dma((2,)),
            dma((2, chips)),
            dma((2, chips)),
        ],
        compiler_params=pltpu.CompilerParams(
            collective_id=2, has_side_effects=True, vmem_limit_bytes=VMEM_ASK
        ),
        name="attention_backward_and_scatter",
    )(outs, rows_in, grad_middle, gain_two_grad, n1, qs, kv, mixed, wq, wot, kvg, cosine, sine, take, placing, probs, halves)


def planned(
    tokens,
    cotangent,
    deal,
    first_len,
    w_query,
    w_key,
    w_value,
    w_out,
    w_gate,
    w_up,
    w_down,
    norm_gains,
):
    chips = lax.axis_size("dp")
    rows, width = tokens.shape
    micro = rows // MICRO
    share = w_query.shape[0]
    back_blocks = min(2 * chips - 1, (WINDOW + micro - 2) // micro)
    reach = (back_blocks + 1) // 2
    d = lax.axis_index("dp")
    inside = jnp.arange(micro, dtype=jnp.int32)
    positions = (2 * d + jnp.arange(2, dtype=jnp.int32))[:, None, None] * micro + inside
    second = positions >= first_len[None, :, None]
    within = positions - jnp.where(second, first_len[None, :, None], 0)
    cosine, sine = angles(within.reshape(-1))
    cosine = jnp.concatenate([cosine, cosine], axis=1).reshape(4, micro, HEAD)
    sine = jnp.concatenate([-sine, sine], axis=1).reshape(4, micro, HEAD)
    gain_rows = jnp.pad(norm_gains, ((0, 15), (0, HEAD - share)))
    kvg = jnp.concatenate([jnp.concatenate([w_key, w_value], axis=1), gain_rows], axis=0)
    (
        three, wq, wot, kvg_all, rows_in, pg_all, take, placing, n1, qs, kv, probs, mixed, middle, n2, gain_two
    ) = forward(
        chips, reach, first_len, deal, cosine, sine, tokens, cotangent, w_query, w_out.T, kvg,
        w_gate, w_up, w_down.T,
    )
    outs, grad_middle, gain_two_grad, halves = mlp(chips, n2, middle, pg_all, gain_two, three)
    three_out, q_out, ot_out, kvg_out, output, input_grad = backward(
        chips, reach, outs, rows_in, grad_middle, gain_two_grad, n1, qs, kv, mixed, wq, wot,
        kvg_all, cosine, sine, take, placing, probs, halves,
    )
    units = w_gate.shape[1]
    three_out = jnp.transpose(three_out, (0, 2, 3, 1, 4)).reshape(3, share, units).astype(F32)
    key_cols = w_key.shape[1]
    return (
        output,
        input_grad,
        q_out,
        kvg_out[:share, :key_cols],
        kvg_out[:share, key_cols:],
        ot_out.T,
        three_out[0],
        three_out[1],
        three_out[2].T,
        kvg_out[share : share + 1, :share],
    )


def fits_plan(mesh, share):
    chips = mesh.shape["dp"]
    return mesh.shape["fsdp"] == 2 and chips % PLANE == 0 and share % 32 == 0 and share < HEAD


def solution(mesh):
    in_specs = (
        P(("dp", "fsdp"), None),
        P(("dp", "fsdp"), None),
        P(("dp", "fsdp")),
        P(),
        P("dp", "fsdp"),
        P("dp", "fsdp"),
        P("dp", "fsdp"),
        P("fsdp", "dp"),
        P("dp", "fsdp"),
        P("dp", "fsdp"),
        P("fsdp", "dp"),
        P("fsdp", "dp"),
    )
    out_specs = (
        P(("dp", "fsdp"), None),
        P(("dp", "fsdp"), None),
        P("dp", "fsdp"),
        P("dp", "fsdp"),
        P("dp", "fsdp"),
        P("fsdp", "dp"),
        P("dp", "fsdp"),
        P("dp", "fsdp"),
        P("fsdp", "dp"),
        P("fsdp", "dp"),
    )
    def placed(*arrays):
        share = arrays[4].shape[0] // mesh.shape["dp"]
        program = planned if fits_plan(mesh, share) else per_device
        return jax.shard_map(
            program, mesh=mesh, in_specs=in_specs, out_specs=out_specs, check_vma=False
        )(*arrays)

    return placed
```

```python
import functools

import jax
import jax.numpy as jnp
from jax import lax
from jax.experimental import pallas as pl
from jax.experimental.pallas import tpu as pltpu
from jax.sharding import PartitionSpec as P

HEADS = 12
HEAD = 128
WINDOW = 1024
MICRO = 2


EPSILON = 1e-06
NEGATIVE = -1e30
VMEM_ASK = 62 * 2**20


def passed_along(x, axis, by):
    count = lax.axis_size(axis)
    pairs = [(i, i + by) for i in range(count) if 0 <= i + by < count]
    return lax.ppermute(x, axis, pairs)


def normed(row_values, gain_row):
    return (
        row_values
        * lax.rsqrt(jnp.mean(row_values * row_values, axis=-1, keepdims=True) + EPSILON)
        * gain_row
    )


def rotate(values, cosine, sine_table):
    half_width = values.shape[-1] // 2
    front_half = values[..., :half_width]
    back_half = values[..., half_width:]
    return jnp.concatenate(
        [
            front_half * cosine - back_half * sine_table,
            back_half * cosine + front_half * sine_table,
        ],
        axis=-1,
    )


def angles(places):
    half_width = HEAD // 2
    frequency = 10000.0 ** (-jnp.arange(half_width, dtype=jnp.float32) * 2.0 / HEAD)
    angle_rows = places.astype(jnp.float32)[:, None] * frequency[None, :]
    return (jnp.cos(angle_rows), jnp.sin(angle_rows))


def contract_rows(left, right):
    return lax.dot_general(
        left, right, (((0,), (0,)), ((), ())), preferred_element_type=jnp.float32
    )


def against(left, right):
    return lax.dot_general(
        left, right, (((1,), (1,)), ((), ())), preferred_element_type=jnp.float32
    )


def gelu_tanh(inputs):
    return jax.nn.gelu(inputs, approximate=True)


def per_device(
    tokens,
    cotangent,
    deal,
    first_len,
    w_query,
    w_key,
    w_value,
    w_out,
    w_gate,
    w_up,
    w_down,
    norm_gains,
):
    peer_count = lax.axis_size("dp")
    core_count = lax.axis_size("fsdp")
    device_total = peer_count * core_count
    row_count = tokens.shape[0]
    model_width = tokens.shape[1]
    per_peer = row_count // peer_count
    micro_rows = row_count // MICRO
    reach_steps = min(device_total - 1, (WINDOW + micro_rows - 2) // micro_rows)
    linear = lax.axis_index("dp") * core_count + lax.axis_index("fsdp")
    source_peer = deal // (row_count * core_count)
    offsets = deal % row_count
    bucket_order = jnp.argsort(source_peer, stable=True)
    inverse = jnp.argsort(bucket_order)
    wanted = offsets[bucket_order].reshape(peer_count, per_peer)
    requested = lax.all_to_all(wanted, "dp", split_axis=0, concat_axis=0, tiled=True)
    picked = requested.reshape(-1)
    fetched = (
        lax.all_to_all(
            tokens[picked].reshape(peer_count, per_peer, model_width),
            "dp",
            split_axis=0,
            concat_axis=0,
            tiled=True,
        ),
        lax.all_to_all(
            cotangent[picked].reshape(peer_count, per_peer, model_width),
            "dp",
            split_axis=0,
            concat_axis=0,
            tiled=True,
        ),
    )
    rows_in = fetched[0].reshape(row_count, model_width)[inverse]
    grad_in = fetched[1].reshape(row_count, model_width)[inverse]
    halves = (
        lax.all_gather(w_query, "dp", axis=0, tiled=True),
        lax.all_gather(w_key, "dp", axis=0, tiled=True),
        lax.all_gather(w_value, "dp", axis=0, tiled=True),
        lax.all_gather(w_out, "dp", axis=1, tiled=True),
        lax.all_gather(w_gate, "dp", axis=0, tiled=True),
        lax.all_gather(w_up, "dp", axis=0, tiled=True),
        lax.all_gather(w_down, "dp", axis=1, tiled=True),
        lax.all_gather(norm_gains, "dp", axis=1, tiled=True),
    )
    gathered = (
        lax.all_gather(halves[0], "fsdp", axis=1, tiled=True),
        lax.all_gather(halves[1], "fsdp", axis=1, tiled=True),
        lax.all_gather(halves[2], "fsdp", axis=1, tiled=True),
        lax.all_gather(halves[3], "fsdp", axis=0, tiled=True),
        lax.all_gather(halves[4], "fsdp", axis=1, tiled=True),
        lax.all_gather(halves[5], "fsdp", axis=1, tiled=True),
        lax.all_gather(halves[6], "fsdp", axis=0, tiled=True),
        lax.all_gather(halves[7], "fsdp", axis=0, tiled=True),
    )
    full_query, full_key, full_value, full_out, full_gate, full_up, full_down, full_gains = gathered
    gain_one = full_gains[0].astype(jnp.float32)
    gain_two = full_gains[1].astype(jnp.float32)
    inside = jnp.arange(micro_rows, dtype=jnp.int32)
    query_place = linear * micro_rows + inside
    query_later = query_place[None, :] >= first_len[:, None]
    query_within = query_place[None, :] - jnp.where(query_later, first_len[:, None], 0)
    distance = jnp.arange(reach_steps, -1, -1, dtype=jnp.int32)
    key_place = ((linear - distance)[:, None] * micro_rows + inside[None, :]).reshape(-1)
    key_later = key_place[None, :] >= first_len[:, None]
    allowed = (
        (query_later[:, :, None] == key_later[:, None, :])
        & (key_place[None, None, :] >= 0)
        & (key_place[None, None, :] <= query_place[None, :, None])
        & (query_place[None, :, None] - key_place[None, None, :] < WINDOW)
    )
    rows_float = rows_in.astype(jnp.float32)
    cosine, sine_table = angles(query_within.reshape(-1))
    score_scale = HEAD ** (-0.5)
    normal_one = normed(rows_float, gain_one).astype(jnp.bfloat16)
    query_raw = jnp.dot(normal_one, full_query, preferred_element_type=jnp.float32).reshape(
        row_count, HEADS, HEAD
    )
    query_rows = rotate(query_raw, cosine[:, None, :], sine_table[:, None, :]).astype(jnp.bfloat16)
    key_rows = rotate(
        jnp.dot(normal_one, full_key, preferred_element_type=jnp.float32), cosine, sine_table
    ).astype(jnp.bfloat16)
    value_rows = jnp.dot(normal_one, full_value, preferred_element_type=jnp.float32).astype(
        jnp.bfloat16
    )
    earlier = []
    for distance_step in range(1, reach_steps + 1):
        earlier.append(passed_along((key_rows, value_rows), ("dp", "fsdp"), distance_step))
    ordered = earlier[::-1] + [(key_rows, value_rows)]
    all_keys = jnp.concatenate(
        [member[0].reshape(MICRO, micro_rows, HEAD) for member in ordered], axis=1
    )
    all_values = jnp.concatenate(
        [member[1].reshape(MICRO, micro_rows, HEAD) for member in ordered], axis=1
    )
    by_head = jnp.transpose(query_rows.reshape(MICRO, micro_rows, HEADS, HEAD), (2, 0, 1, 3))

    def attend(query_head):
        scores = jnp.where(
            allowed,
            jnp.einsum("mqd,mkd->mqk", query_head, all_keys, preferred_element_type=jnp.float32)
            * score_scale,
            NEGATIVE,
        )
        row_top = jnp.max(scores, axis=2, keepdims=True)
        exp_scores = jnp.exp(scores - row_top)
        row_total = jnp.sum(exp_scores, axis=2, keepdims=True)
        soft_weights = (exp_scores / row_total).astype(jnp.bfloat16)
        attended_head = jnp.einsum(
            "mqk,mkd->mqd", soft_weights, all_values, preferred_element_type=jnp.float32
        )
        return (attended_head, row_top[..., 0] + jnp.log(row_total[..., 0]))

    attended, log_total = lax.map(attend, by_head)
    mixed_heads = (
        jnp.transpose(attended, (1, 2, 0, 3)).reshape(row_count, HEADS * HEAD).astype(jnp.bfloat16)
    )
    middle = rows_float + jnp.dot(mixed_heads, full_out, preferred_element_type=jnp.float32)
    normal_two = normed(middle, gain_two).astype(jnp.bfloat16)
    gate_rows = jnp.dot(normal_two, full_gate, preferred_element_type=jnp.float32)
    upward = jnp.dot(normal_two, full_up, preferred_element_type=jnp.float32)
    activated = gelu_tanh(gate_rows)
    hidden = (activated * upward).astype(jnp.bfloat16)
    result = (middle + jnp.dot(hidden, full_down, preferred_element_type=jnp.float32)).astype(
        jnp.bfloat16
    )
    grad_float = grad_in.astype(jnp.float32)
    grad_down = contract_rows(hidden, grad_in)
    grad_hidden = against(grad_in, full_down)
    gelu_value, gelu_pull = jax.vjp(gelu_tanh, gate_rows)
    grad_gate_rows = gelu_pull(grad_hidden * upward)[0].astype(jnp.bfloat16)
    grad_up_rows = (grad_hidden * activated).astype(jnp.bfloat16)
    grad_gate = contract_rows(normal_two, grad_gate_rows)
    grad_up = contract_rows(normal_two, grad_up_rows)
    grad_two = against(grad_gate_rows, full_gate) + against(grad_up_rows, full_up)
    norm_value, norm_pull = jax.vjp(normed, middle, gain_two)
    grad_middle_norm, gain_two_grad = norm_pull(grad_two)
    grad_middle = grad_float + grad_middle_norm
    grad_middle_low = grad_middle.astype(jnp.bfloat16)
    grad_out = contract_rows(mixed_heads, grad_middle_low)
    grad_mixed = against(grad_middle_low, full_out).astype(jnp.bfloat16)
    grad_by_head = jnp.transpose(grad_mixed.reshape(MICRO, micro_rows, HEADS, HEAD), (2, 0, 1, 3))

    def attend_back(running, pieces):
        key_total, value_total = running
        query_head, grad_head, total_head = pieces
        scores = (
            jnp.einsum("mqd,mkd->mqk", query_head, all_keys, preferred_element_type=jnp.float32)
            * score_scale
        )
        soft_weights = jnp.where(allowed, jnp.exp(scores - total_head[..., None]), 0.0)
        value_total = value_total + jnp.einsum(
            "mqk,mqd->mkd",
            soft_weights.astype(jnp.bfloat16),
            grad_head,
            preferred_element_type=jnp.float32,
        )
        grad_soft = jnp.einsum(
            "mqd,mkd->mqk", grad_head, all_values, preferred_element_type=jnp.float32
        )
        row_delta = jnp.sum(grad_soft * soft_weights, axis=2, keepdims=True)
        grad_scores = (soft_weights * (grad_soft - row_delta)).astype(jnp.bfloat16)
        grad_query_head = (
            jnp.einsum("mqk,mkd->mqd", grad_scores, all_keys, preferred_element_type=jnp.float32)
            * score_scale
        )
        key_total = (
            key_total
            + jnp.einsum(
                "mqk,mqd->mkd", grad_scores, query_head, preferred_element_type=jnp.float32
            )
            * score_scale
        )
        return ((key_total, value_total), grad_query_head)

    zero_block = jnp.zeros((MICRO, (reach_steps + 1) * micro_rows, HEAD), jnp.float32)
    totals, grad_query_heads = lax.scan(
        attend_back, (zero_block, zero_block), (by_head, grad_by_head, log_total)
    )
    key_total, value_total = totals

    def piece_of(total, distance_step):
        begin_row = (reach_steps - distance_step) * micro_rows
        return total[:, begin_row : begin_row + micro_rows].reshape(row_count, HEAD)

    own_key = piece_of(key_total, 0)
    own_value = piece_of(value_total, 0)
    for distance_step in range(1, reach_steps + 1):
        returned_pair = (
            passed_along(
                piece_of(key_total, distance_step).astype(jnp.bfloat16),
                ("dp", "fsdp"),
                -distance_step,
            ).astype(jnp.float32),
            passed_along(
                piece_of(value_total, distance_step).astype(jnp.bfloat16),
                ("dp", "fsdp"),
                -distance_step,
            ).astype(jnp.float32),
        )
        own_key = own_key + returned_pair[0]
        own_value = own_value + returned_pair[1]
    grad_value_rows = own_value.astype(jnp.bfloat16)
    grad_query_rot = jnp.transpose(grad_query_heads, (1, 2, 0, 3)).reshape(row_count, HEADS, HEAD)
    grad_query_raw = (
        rotate(grad_query_rot, cosine[:, None, :], -sine_table[:, None, :])
        .reshape(row_count, HEADS * HEAD)
        .astype(jnp.bfloat16)
    )
    grad_key_raw = rotate(own_key, cosine, -sine_table).astype(jnp.bfloat16)
    grad_query = contract_rows(normal_one, grad_query_raw)
    grad_key = contract_rows(normal_one, grad_key_raw)
    grad_value = contract_rows(normal_one, grad_value_rows)
    grad_one = (
        against(grad_query_raw, full_query)
        + against(grad_key_raw, full_key)
        + against(grad_value_rows, full_value)
    )
    first_value, first_pull = jax.vjp(normed, rows_float, gain_one)
    grad_rows_norm, gain_one_grad = first_pull(grad_one)
    grad_rows = (grad_middle + grad_rows_norm).astype(jnp.bfloat16)
    grad_gains = jnp.stack([gain_one_grad, gain_two_grad])
    sectioned = (
        lax.psum_scatter(
            grad_query.astype(jnp.bfloat16), "fsdp", scatter_dimension=1, tiled=True
        ).astype(jnp.float32),
        lax.psum_scatter(
            grad_key.astype(jnp.bfloat16), "fsdp", scatter_dimension=1, tiled=True
        ).astype(jnp.float32),
        lax.psum_scatter(
            grad_value.astype(jnp.bfloat16), "fsdp", scatter_dimension=1, tiled=True
        ).astype(jnp.float32),
        lax.psum_scatter(
            grad_out.astype(jnp.bfloat16), "fsdp", scatter_dimension=0, tiled=True
        ).astype(jnp.float32),
        lax.psum_scatter(
            grad_gate.astype(jnp.bfloat16), "fsdp", scatter_dimension=1, tiled=True
        ).astype(jnp.float32),
        lax.psum_scatter(
            grad_up.astype(jnp.bfloat16), "fsdp", scatter_dimension=1, tiled=True
        ).astype(jnp.float32),
        lax.psum_scatter(
            grad_down.astype(jnp.bfloat16), "fsdp", scatter_dimension=0, tiled=True
        ).astype(jnp.float32),
        lax.psum_scatter(
            grad_gains.astype(jnp.bfloat16), "fsdp", scatter_dimension=0, tiled=True
        ).astype(jnp.float32),
    )
    reduced = (
        lax.psum_scatter(sectioned[0], "dp", scatter_dimension=0, tiled=True),
        lax.psum_scatter(sectioned[1], "dp", scatter_dimension=0, tiled=True),
        lax.psum_scatter(sectioned[2], "dp", scatter_dimension=0, tiled=True),
        lax.psum_scatter(sectioned[3], "dp", scatter_dimension=1, tiled=True),
        lax.psum_scatter(sectioned[4], "dp", scatter_dimension=0, tiled=True),
        lax.psum_scatter(sectioned[5], "dp", scatter_dimension=0, tiled=True),
        lax.psum_scatter(sectioned[6], "dp", scatter_dimension=1, tiled=True),
        lax.psum_scatter(sectioned[7], "dp", scatter_dimension=1, tiled=True),
    )
    returned = (
        lax.all_to_all(
            result[bucket_order].reshape(peer_count, per_peer, model_width),
            "dp",
            split_axis=0,
            concat_axis=0,
            tiled=True,
        ),
        lax.all_to_all(
            grad_rows[bucket_order].reshape(peer_count, per_peer, model_width),
            "dp",
            split_axis=0,
            concat_axis=0,
            tiled=True,
        ),
    )
    output = jnp.zeros_like(tokens).at[picked].set(returned[0].reshape(row_count, model_width))
    input_grad = jnp.zeros_like(tokens).at[picked].set(returned[1].reshape(row_count, model_width))
    return (
        output,
        input_grad,
        reduced[0],
        reduced[1],
        reduced[2],
        reduced[3],
        reduced[4],
        reduced[5],
        reduced[6],
        reduced[7],
    )


MESH = pl.DeviceIdType.MESH
BF16 = jnp.bfloat16
F32 = jnp.float32
PLANE = 4
ANY = pl.BlockSpec(memory_space=pl.ANY)
VM = pl.BlockSpec(memory_space=pltpu.VMEM)
SM = pl.BlockSpec(memory_space=pltpu.SMEM)


def mm(left, right):
    return jnp.dot(left, right, preferred_element_type=F32)


def mm_nt(left, right):
    return lax.dot_general(left, right, (((1,), (1,)), ((), ())), preferred_element_type=F32)


def mm_tn(left, right):
    return lax.dot_general(left, right, (((0,), (0,)), ((), ())), preferred_element_type=F32)


class Place:
    def __init__(self, chips):
        self.chips = chips
        self.groups = chips // PLANE
        self.d = lax.axis_index("dp")
        self.f = lax.axis_index("fsdp")
        self.other = 1 - self.f
        self.g = self.d // PLANE
        self.p = self.d % PLANE
        self.x = self.p % 2
        self.y = self.p // 2

    def plane_pos(self, j):
        return ((self.y + j // 2) % 2) * 2 + (self.x + j % 2) % 2

    def plane_chip(self, j):
        return self.g * PLANE + self.plane_pos(j)

    def column_chip(self, k):
        return ((self.g + k) % self.groups) * PLANE + self.p


def greet_all(place):
    barrier = pltpu.get_barrier_semaphore()
    total = place.chips * 2
    me = place.d * 2 + place.f

    def signal(k, carry):
        to = (me + k) % total
        pl.semaphore_signal(barrier, inc=1, device_id=(to // 2, to % 2), device_id_type=MESH)
        return carry

    lax.fori_loop(1, total, signal, 0)
    pl.semaphore_wait(barrier, total - 1)


class Sent:
    def __init__(self):
        self.copies = []

    def remote(self, src, dst, send_sem, recv_sem, device):
        copy = pltpu.make_async_remote_copy(
            src_ref=src,
            dst_ref=dst,
            send_sem=send_sem,
            recv_sem=recv_sem,
            device_id=device,
            device_id_type=MESH,
        )
        copy.start()
        self.copies.append(copy)

    def finish(self):
        for copy in self.copies:
            copy.wait_send()
        self.copies = []


def arrived(ref, sem):
    pltpu.make_async_copy(ref, ref, sem).wait()


def iota(shape, dim):
    return lax.broadcasted_iota(jnp.int32, shape, dim)


def fold(values, combine):
    parts = values.reshape(values.shape[0] // 8, 8, values.shape[1])
    total = parts[0]
    for i in range(1, parts.shape[0]):
        total = combine(total, parts[i])
    return total


def gain_spread(width, share):
    column = iota((128, width), 1).astype(F32)
    inside = column - jnp.floor((column + 0.5) * (1.0 / share)) * share
    row = iota((128, width), 0).astype(F32)
    return (inside == row).astype(BF16)


def own_stretch(chips, width, share):
    row = iota((chips, width), 0)
    column = iota((chips, width), 1)
    return (column >= row * share) & (column < row * share + share)


def gain_row(kvg_ref, which, chips, width, share):
    block = kvg_ref[which, :, share : share + 16, :].astype(F32)[:, 0, :].astype(BF16)
    spread = mm(block, gain_spread(width, share))
    return jnp.sum(jnp.where(own_stretch(chips, width, share), spread, 0.0), axis=0, keepdims=True)


def rms_scale(values):
    return lax.rsqrt(jnp.mean(values * values, axis=-1, keepdims=True) + EPSILON)


def turned(values, cosine, sine):
    return values * cosine + pltpu.roll(values, HEAD // 2, 1) * sine


def halves_in(first, second):
    front = iota(first.shape, 1) < HEAD // 2
    return (
        jnp.where(front, first, pltpu.roll(second, HEAD // 2, 1)),
        jnp.where(front, pltpu.roll(first, HEAD // 2, 1), second),
    )


class PlaneSpread:
    def __init__(self, place, blocks, send_sems, recv_sems):
        self.place, self.blocks, self.send_sems, self.recv_sems = place, blocks, send_sems, recv_sems
        self.half = blocks.shape[1] // 2
        self.by_x, self.by_y, self.far = (place.plane_pos(j) for j in range(1, PLANE))

    def piece(self, pos, side):
        return self.blocks.at[pos, pl.ds(side * self.half, self.half)]

    def copy(self, slot):
        place = self.place
        pos, side, over_x = (
            (place.p, 0, 1),
            (place.p, 1, 0),
            (place.p, 1, 1),
            (place.p, 0, 0),
            (self.by_x, 0, 0),
            (self.by_y, 1, 1),
        )[slot]
        return pltpu.make_async_remote_copy(
            src_ref=self.piece(pos, side),
            dst_ref=self.piece(pos, side),
            send_sem=self.send_sems.at[slot],
            recv_sem=self.recv_sems.at[pos, side],
            device_id=(place.plane_chip(1 if over_x else 2), place.f),
            device_id_type=MESH,
        )

    def start(self):
        for slot in range(4):
            self.copy(slot).start()

    def pass_on(self):
        for slot, pos, side in ((4, self.by_x, 0), (5, self.by_y, 1)):
            arrived(self.piece(pos, side), self.recv_sems.at[pos, side])
            self.copy(slot).start()

    def wait(self):
        for pos, side in ((self.by_x, 1), (self.by_y, 0), (self.far, 0), (self.far, 1)):
            arrived(self.piece(pos, side), self.recv_sems.at[pos, side])

    def finish(self):
        for slot in range(6):
            self.copy(slot).wait_send()


class Chain:
    def __init__(self, place, piece, hops, up_sems, down_sems, recv_sems):
        self.place, self.piece, self.hops = place, piece, hops
        self.up_sems, self.down_sems, self.recv_sems = up_sems, down_sems, recv_sems
        self.has_up = place.g + 1 < place.groups
        self.has_down = place.g >= 1

    def hop(self, a, origin, up):
        place = self.place
        ref = self.piece(a, origin)
        to = place.d + PLANE if up else place.d - PLANE
        sems = self.up_sems if up else self.down_sems
        return pltpu.make_async_remote_copy(
            src_ref=ref,
            dst_ref=ref,
            send_sem=sems.at[a, origin],
            recv_sem=self.recv_sems.at[a, origin],
            device_id=(to, place.f),
            device_id_type=MESH,
        )

    def start(self, a):
        def one(up):
            self.hop(a, self.place.g, up).start()

        pl.when(self.has_up)(functools.partial(one, True))
        pl.when(self.has_down)(functools.partial(one, False))

    def step(self, k, arrays, then):
        place = self.place

        def from_below():
            origin = place.g - k
            for a in arrays:
                arrived(self.piece(a, origin), self.recv_sems.at[a, origin])

                if k < self.hops[a]:
                    pl.when(self.has_up)(self.hop(a, origin, True).start)
                then(a, origin)

        def from_above():
            origin = place.g + k
            for a in arrays:
                arrived(self.piece(a, origin), self.recv_sems.at[a, origin])

                if k < self.hops[a]:
                    pl.when(self.has_down)(self.hop(a, origin, False).start)
                then(a, origin)

        pl.when(place.g >= k)(from_below)
        pl.when(place.g + k < place.groups)(from_above)

    def finish(self):
        place = self.place
        for a, hops in enumerate(self.hops):
            for k in range(hops):

                @pl.when((place.g >= k) & self.has_up)
                def _():
                    self.hop(a, place.g - k, True).wait_send()

                @pl.when((place.g + k < place.groups) & self.has_down)
                def _():
                    self.hop(a, place.g + k, False).wait_send()


def forward_kernel(
    chips,
    reach,
    first_ref,
    deal_ref,
    deal_col_ref,
    cos_ref,
    sin_ref,
    tokens_ref,
    cot_ref,
    wq_ref,
    wot_ref,
    kvg_ref,
    gate_ref,
    up_ref,
    down_ref,
    full_three,
    full_q,
    full_ot,
    full_kvg,
    rows_out,
    pg_ref,
    take_ref,
    place_ref,
    n1_ref,
    qs_ref,
    kv_ref,
    probs_ref,
    mixed_ref,
    middle_ref,
    n2_all,
    gain_two_ref,
    deal_all,
    give,
    got,
    bias_ref,
    branch_out,
    branch_in,
    scores_ref,
    deal_send,
    deal_recv,
    row_send,
    row_recv,
    attn_up,
    attn_down,
    attn_recv,
    fan_send,
    fan_recv,
    kvg_sems,
    stage_send,
    stage_recv,
    three_up,
    three_down,
    three_recv,
    relay_send,
    relay_recv,
    plane_send,
    plane_recv,
    n1_sems,
    kv_send,
    kv_recv,
    branch_sems,
    local_sems,
):
    place = Place(chips)
    d, f, other = place.d, place.f, place.other
    groups = place.groups
    rows, width = tokens_ref.shape
    share = wq_ref.shape[0]
    half = share // 2
    per = rows // chips
    part = gate_ref.shape[1] // 2
    micro = rows // MICRO
    heads = wq_ref.shape[1] // HEAD
    span = (2 * reach + 1) * micro
    sent = Sent()
    greet_all(place)

    deal_all[d] = deal_ref[...]
    for k in range(1, chips):
        to = (d + k) % chips
        sent.remote(deal_all.at[d], deal_all.at[d], deal_send.at[k], deal_recv.at[d], (to, f))

    def attn_piece(a, s):
        if a == 0:
            return full_kvg.at[f, s]
        band = pl.ds(pl.multiple_of(s * share, 16), share)
        return (full_q if a == 1 else full_ot).at[band]

    own_attn = (kvg_ref, wq_ref, wot_ref)
    copies = [
        pltpu.make_async_copy(own_attn[a], attn_piece(a, d), local_sems.at[a]) for a in range(3)
    ]
    for copy in copies:
        copy.start()
    for copy in copies:
        copy.wait()
    attn = Chain(
        place,
        lambda a, g: attn_piece(a, g * PLANE + place.p),
        (groups - 1,) * 3,
        attn_up,
        attn_down,
        attn_recv,
    )

    def fan(a, g):
        for j in range(1, PLANE if a == 0 else PLANE - 1):
            fan_copy(a, g, j).start()

    def fan_copy(a, g, j):
        s = g * PLANE + place.p
        return pltpu.make_async_remote_copy(
            src_ref=attn_piece(a, s),
            dst_ref=attn_piece(a, s),
            send_sem=fan_send.at[a, g, j],
            recv_sem=fan_recv.at[a, s],
            device_id=(place.plane_chip(j), f),
            device_id_type=MESH,
        )

    def pass_copy(a, g):
        by_x = place.plane_pos(1)
        by_y = place.plane_pos(2)
        even = g % 2 == 0
        s = g * PLANE + jnp.where(even, by_x, by_y)
        to = jnp.where(even, place.plane_chip(2), place.plane_chip(1))
        return pltpu.make_async_remote_copy(
            src_ref=attn_piece(a, s),
            dst_ref=attn_piece(a, s),
            send_sem=fan_send.at[a, g, PLANE - 1],
            recv_sem=fan_recv.at[a, s],
            device_id=(to, f),
            device_id_type=MESH,
        )

    def pass_on(a, g):
        s = g * PLANE + jnp.where(g % 2 == 0, place.plane_pos(1), place.plane_pos(2))
        arrived(attn_piece(a, s), fan_recv.at[a, s])
        pass_copy(a, g).start()

    def pass_all(a):
        pass_on(a, place.g)
        for k in range(1, groups):
            pl.when(place.g >= k)(functools.partial(pass_on, a, place.g - k))
            pl.when(place.g + k < groups)(functools.partial(pass_on, a, place.g + k))

    for a in range(2):
        attn.start(a)
        fan(a, place.g)
    attn.start(2)

    def soon(a, g):
        if a < 2:
            fan(a, g)

    mats = (gate_ref, up_ref, down_ref)

    def stage_src(a, to_x, core):
        return mats[a].at[pl.ds(half * core, half), pl.ds(pl.multiple_of(part * to_x, 128), part)]

    def stage_copy(a, b, core):
        to_x = (place.x + b) % 2
        return pltpu.make_async_remote_copy(
            src_ref=stage_src(a, to_x, core),
            dst_ref=full_three.at[a, d, core],
            send_sem=stage_send.at[a, b, core],
            recv_sem=stage_recv.at[a, place.p],
            device_id=(place.g * PLANE + 2 * f + to_x, core),
            device_id_type=MESH,
        )

    def own_copy(a):
        return pltpu.make_async_copy(
            mats[a].at[pl.ds(pl.multiple_of(half * f, 16), half), pl.ds(pl.multiple_of(part * place.x, 128), part)],
            full_three.at[a, d, f],
            local_sems.at[a],
        )

    def pair_copy(a):
        return pltpu.make_async_remote_copy(
            src_ref=mats[a].at[
                pl.ds(pl.multiple_of(half * other, 16), half),
                pl.ds(pl.multiple_of(part * place.x, 128), part),
            ],
            dst_ref=full_three.at[a, d, other],
            send_sem=stage_send.at[a, 0, 0],
            recv_sem=stage_recv.at[a, place.p],
            device_id=(d, other),
            device_id_type=MESH,
        )

    def stage_start(a):
        for core in range(2):
            stage_copy(a, 1, core).start()

        @pl.when(place.y != f)
        def _():
            for core in range(2):
                stage_copy(a, 0, core).start()

        @pl.when(place.y == f)
        def _():
            own_copy(a).start()
            pair_copy(a).start()

    stage_start(0)

    for k in range(1, chips):
        s = (d + k) % chips
        arrived(deal_all.at[s], deal_recv.at[s])
    chip_bits = (2 * rows).bit_length() - 1
    deals = deal_all[:, 0, :]
    wants = lax.shift_right_logical(deals, chip_bits) == d
    offset = deals & (rows - 1)
    earlier = (iota((rows, rows), 0) < iota((rows, rows), 1)).astype(BF16)
    rank = mm(wants.astype(F32).astype(BF16), earlier)
    for j in range(chips):
        hit = wants[j : j + 1, :] & (rank[j : j + 1, :] == iota((per, rows), 0).astype(F32))
        index = jnp.sum(jnp.where(hit, offset[j : j + 1, :], 0), axis=1, keepdims=True)
        take_ref[j * per : (j + 1) * per, :] = (
            (index == iota((per, rows), 1)).astype(F32).astype(BF16)
        )

    def block(k):
        return pl.ds(pl.multiple_of(k * per, per), per)

    def give_rows(i, source_ref):
        give[i] = mm(take_ref[...], source_ref[...]).astype(BF16)
        got[i, block(d), :] = give[i, block(d), :]

    def send_rows(i):
        for k in range(1, chips):
            to = (d + k) % chips
            sent.remote(
                give.at[i, block(to)],
                got.at[i, block(d)],
                row_send.at[i, k],
                row_recv.at[i, d],
                (to, f),
            )

    def take_rows(i):
        for k in range(1, chips):
            s = (d + k) % chips
            arrived(got.at[i, block(s)], row_recv.at[i, s])
        return mm(place_ref[...], got[i])

    give_rows(0, tokens_ref)
    def column_pass(k, a):
        pl.when(place.g >= k)(functools.partial(pass_on, a, place.g - k))
        pl.when(place.g + k < groups)(functools.partial(pass_on, a, place.g + k))

    attn.step(1, (0, 1, 2), soon)
    pass_on(1, place.g)
    three = Chain(
        place,
        lambda a, g: full_three.at[a, pl.ds(g * PLANE, PLANE), f],
        (groups - 1, groups - 1, 1),
        three_up,
        three_down,
        three_recv,
    )

    def relay_copy(a, g):
        ref = full_three.at[a, pl.ds(g * PLANE, PLANE), f]
        return pltpu.make_async_remote_copy(
            src_ref=ref,
            dst_ref=ref,
            send_sem=relay_send.at[a, g],
            recv_sem=relay_recv.at[a, g],
            device_id=(d, other),
            device_id_type=MESH,
        )

    def relay(a, g):
        relay_copy(a, g).start()

    def three_start(a):
        for j in range(1, PLANE):
            pos = place.plane_pos(j)
            arrived(full_three.at[a, place.g * PLANE + pos, f], stage_recv.at[a, pos])

        @pl.when(place.y == f)
        def _():
            own_copy(a).wait()

        @pl.when(place.y != f)
        def _():
            arrived(full_three.at[a, d, f], stage_recv.at[a, place.p])

        three.start(a)
        relay(a, place.g)

    def meanwhile():
        source_col = lax.shift_right_logical(deal_col_ref[...], chip_bits)
        source_row = lax.shift_right_logical(deal_ref[0:1, :], chip_bits)
        same = (source_col == source_row) & (iota((rows, rows), 1) < iota((rows, rows), 0))
        order = jnp.sum(same.astype(F32), axis=1, keepdims=True).astype(jnp.int32)
        where_from = source_col * per + order
        place_ref[...] = (where_from == iota((rows, rows), 1)).astype(F32).astype(BF16)

        def make_bias(hm, carry):
            h, m = hm // 2, hm % 2
            first = first_ref[m]
            query = (2 * d + h) * micro + iota((span, micro), 1)
            key = (2 * d + h - 2 * reach) * micro + iota((span, micro), 0)
            allowed = (
                (jnp.where(query >= first, 1, 0) == jnp.where(key >= first, 1, 0))
                & (key >= 0)
                & (key <= query)
                & (query - key < WINDOW)
            )
            bias_ref[hm] = jnp.where(allowed, 0.0, NEGATIVE)
            return carry

        lax.fori_loop(0, 4, make_bias, 0)

    for k in range(2, groups):
        attn.step(k, (0, 1, 2), soon)
        column_pass(k - 1, 1)
        if k == 2:
            send_rows(0)
            three_start(0)
            stage_start(1)
            stage_start(2)
            meanwhile()
    row_values = take_rows(0)
    column_pass(groups - 1, 1)
    rows_out[...] = row_values.astype(BF16)

    def attn_wait(a):
        for g in range(groups):
            if a == 0:
                left = range(1, PLANE)
            else:
                left = (2 - g % 2, 3)
            for j in left:
                s = g * PLANE + place.plane_pos(j)
                arrived(attn_piece(a, s), fan_recv.at[a, s])

    n2 = PlaneSpread(place, n2_all, plane_send, plane_recv)

    attn_wait(0)
    sent.remote(full_kvg.at[f], full_kvg.at[f], kvg_sems.at[0], kvg_sems.at[1], (d, other))
    arrived(full_kvg.at[other], kvg_sems.at[1])

    gain_one = gain_row(full_kvg, 0, chips, width, share)
    n1_ref[f] = (row_values * rms_scale(row_values) * gain_one).astype(BF16)
    sent.remote(n1_ref.at[f], n1_ref.at[f], n1_sems.at[0], n1_sems.at[1], (d, other))

    kvw = [full_kvg[i, :, 0:share, :].reshape(width, HEAD) for i in range(2)]
    raw = [mm(n1_ref[f], kvw[i]) for i in range(2)]
    key_raw, value_raw = halves_in(raw[0], raw[1])
    for m in range(MICRO):
        hm = 2 * f + m
        band = slice(m * micro, (m + 1) * micro)
        key = turned(key_raw[band], cos_ref[hm], sin_ref[hm])
        kv_ref[m, 2 * reach + f, :, 0:HEAD] = key.astype(BF16)
        kv_ref[m, 2 * reach + f, :, HEAD:] = value_raw[band].astype(BF16)
    own_kv = kv_ref.at[:, 2 * reach + f]

    def kv_copy(j):
        return pltpu.make_async_remote_copy(
            src_ref=own_kv,
            dst_ref=kv_ref.at[:, 2 * reach + f - 2 * j],
            send_sem=kv_send.at[j, 0],
            recv_sem=kv_recv.at[2 * reach + f - 2 * j],
            device_id=(d + j, f),
            device_id_type=MESH,
        )

    def kv_pass(j):
        slot = 2 * reach + f - 2 * j
        return pltpu.make_async_remote_copy(
            src_ref=kv_ref.at[:, slot],
            dst_ref=kv_ref.at[:, slot],
            send_sem=kv_send.at[j, 1],
            recv_sem=kv_recv.at[slot],
            device_id=(d, other),
            device_id_type=MESH,
        )

    sent.remote(own_kv, own_kv, kv_send.at[0, 0], kv_recv.at[2 * reach + f], (d, other))
    for j in range(reach, 0, -1):
        pl.when(d + j < chips)(kv_copy(j).start)
    for j in range(1, reach + 1):

        @pl.when(d - j < 0)
        def _():
            for core in range(2):
                kv_ref[:, 2 * reach - 2 * j + core] = jnp.zeros((MICRO, micro, 2 * HEAD), BF16)

    give_rows(1, cot_ref)
    send_rows(1)
    for g in range(groups):
        fan(2, g)
    three_start(1)

    def project(h):
        raw_q = mm(n1_ref[h], full_q[...])
        for m in range(MICRO):
            hm = 2 * h + m
            cosine, sine = cos_ref[hm], sin_ref[hm]
            for i in range(heads):
                one = raw_q[m * micro : (m + 1) * micro, i * HEAD : (i + 1) * HEAD]
                qs_ref[hm, i * micro : (i + 1) * micro, :] = turned(one, cosine, sine).astype(BF16)

    attn_wait(1)
    project(f)
    arrived(n1_ref.at[other], n1_sems.at[1])
    project(other)
    three.step(1, (0,), relay)

    for j in range(1, reach + 1):

        @pl.when(d - j >= 0)
        def _():
            slot = 2 * reach - 2 * j + f
            arrived(kv_ref.at[:, slot], kv_recv.at[slot])
            kv_pass(j).start()

    arrived(kv_ref.at[:, 2 * reach + other], kv_recv.at[2 * reach + other])
    for j in range(1, reach + 1):

        @pl.when(d - j >= 0)
        def _():
            slot = 2 * reach - 2 * j + other
            arrived(kv_ref.at[:, slot], kv_recv.at[slot])

    score_scale = HEAD ** (-0.5)
    chunks = [slice(i, i + 64) for i in range(0, span, 64)]

    def attend(hm):
        h, m = hm // 2, hm % 2
        keys = kv_ref[m, h : h + 2 * reach + 1, :, 0:HEAD].reshape(span, HEAD)
        values_t = kv_ref[m, h : h + 2 * reach + 1, :, HEAD:].reshape(span, HEAD).T

        def pair_step(pair, carry):
            start = pl.multiple_of(pair * 2 * micro, 2 * micro)
            band = pl.ds(start, 2 * micro)
            scores_ref[...] = mm_nt(keys, qs_ref[hm, band, :])
            top = jnp.full((8, 2 * micro), NEGATIVE, F32)
            for at in chunks:
                bias = bias_ref[hm, at, :]
                scores = scores_ref[at, :] * score_scale + jnp.concatenate([bias, bias], axis=1)
                scores_ref[at, :] = scores
                top = jnp.maximum(top, fold(scores, jnp.maximum))
            top = jnp.max(top, axis=0, keepdims=True)
            total = jnp.zeros((8, 2 * micro), F32)
            for at in chunks:
                exp_scores = jnp.exp(scores_ref[at, :] - top)
                scores_ref[at, :] = exp_scores
                total = total + fold(exp_scores, jnp.add)
            share_of = 1.0 / jnp.sum(total, axis=0, keepdims=True)
            for at in chunks:
                probs_ref[hm, at, band] = (scores_ref[at, :] * share_of).astype(BF16)
            out_t = mm(values_t, probs_ref[hm, :, band])
            mixed_ref[hm, :, band] = jnp.concatenate(
                [out_t[:, i * micro : (i + 1) * micro].T for i in range(2)], axis=1
            ).astype(BF16)
            return carry

        lax.fori_loop(0, heads // 2, pair_step, 0)

    attend(0)
    pass_all(2)
    three.step(1, (1,), relay)
    attend(1)
    attend(2)
    three.step(2, (0,), relay)
    attend(3)

    def branch(h):
        return mm_nt(mixed_ref[pl.ds(2 * h, 2)].reshape(rows, heads * HEAD), full_ot[...])

    attn_wait(2)
    branch_out[...] = branch(other).astype(BF16)
    sent.remote(branch_out, branch_in, branch_sems.at[0], branch_sems.at[1], (d, other))
    own = branch(f)
    arrived(branch_in, branch_sems.at[1])
    middle = rows_out[...].astype(F32) + own + branch_in[...].astype(F32)
    middle_ref[...] = middle
    gain_two = gain_row(full_kvg, 1, chips, width, share)
    gain_two_ref[...] = gain_two
    n2_all[place.p] = (middle * rms_scale(middle) * gain_two).astype(BF16)
    n2.start()
    three.step(2, (1,), relay)
    three_start(2)
    n2.pass_on()
    for k in range(3, groups):
        three.step(k, (0, 1), relay)
    three.step(1, (2,), relay)
    pg_ref[...] = take_rows(1).astype(BF16)

    def relayed(a, k, use):
        pl.when(place.g >= k)(functools.partial(use, a, place.g - k))
        if k > 0:
            pl.when(place.g + k < groups)(functools.partial(use, a, place.g + k))

    def relay_wait(a, g):
        arrived(full_three.at[a, pl.ds(g * PLANE, PLANE), other], relay_recv.at[a, g])

    def relay_sent(a, g):
        relay_copy(a, g).wait_send()

    for a in range(3):
        for k in range(groups if a < 2 else min(2, groups)):
            relayed(a, k, relay_wait)
            relayed(a, k, relay_sent)
    n2.wait()
    n2.finish()

    attn.finish()
    three.finish()
    for g in range(groups):
        for a in range(3):
            for j in range(1, PLANE if a == 0 else PLANE - 1):
                fan_copy(a, g, j).wait_send()
            if a > 0:
                pass_copy(a, g).wait_send()
    for a in range(3):
        for core in range(2):
            stage_copy(a, 1, core).wait_send()

        @pl.when(place.y != f)
        def _():
            for core in range(2):
                stage_copy(a, 0, core).wait_send()

        @pl.when(place.y == f)
        def _():
            pair_copy(a).wait_send()

    for j in range(1, reach + 1):
        pl.when(d + j < chips)(kv_copy(j).wait_send)
        pl.when(d - j >= 0)(kv_pass(j).wait_send)

    sent.finish()


def forward(chips, reach, first_len, deal, cosine, sine, tokens, cotangent, wq, wot, kvg, gate, up, down):
    rows, width = tokens.shape
    share = wq.shape[0]
    groups = chips // PLANE
    part = gate.shape[1] // 2
    micro = rows // MICRO
    heads = wq.shape[1] // HEAD
    slots = 2 * reach + 2
    span = (2 * reach + 1) * micro
    dma = pltpu.SemaphoreType.DMA
    shape = jax.ShapeDtypeStruct
    deal_rows = jnp.broadcast_to(deal[None, :], (8, rows))
    deal_col = jnp.broadcast_to(deal[:, None], (rows, rows))
    return pl.pallas_call(
        functools.partial(forward_kernel, chips, reach),
        out_shape=(
            shape((3, chips, 2, share // 2, part), BF16),
            shape((width, wq.shape[1]), BF16),
            shape((width, wq.shape[1]), BF16),
            shape((2, chips) + kvg.shape, BF16),
            shape((rows, width), BF16),
            shape((rows, width), BF16),
            shape((rows, rows), BF16),
            shape((rows, rows), BF16),
            shape((2, rows, width), BF16),
            shape((4, heads * micro, HEAD), BF16),
            shape((MICRO, slots, micro, 2 * HEAD), BF16),
            shape((4, span, heads * micro), BF16),
            shape((4, micro, heads * HEAD), BF16),
            shape((rows, width), F32),
            shape((PLANE, rows, width), BF16),
            shape((1, width), F32),
        ),
        in_specs=[SM] + [VM] * 6 + [ANY] * 6,
        out_specs=(ANY,) + (VM,) * 15,
        scratch_shapes=[
            pltpu.VMEM((chips, 8, rows), jnp.int32),
            pltpu.VMEM((2, rows, width), BF16),
            pltpu.VMEM((2, rows, width), BF16),
            pltpu.VMEM((4, span, micro), F32),
            pltpu.VMEM((rows, width), BF16),
            pltpu.VMEM((rows, width), BF16),
            pltpu.VMEM((span, 2 * micro), F32),
            dma((chips,)),
            dma((chips,)),
            dma((2, chips)),
            dma((2, chips)),
            dma((3, groups)),
            dma((3, groups)),
            dma((3, groups)),
            dma((3, groups, PLANE)),
            dma((3, chips)),
            dma((2,)),
            dma((3, 2, 2)),
            dma((3, PLANE)),
            dma((3, groups)),
            dma((3, groups)),
            dma((3, groups)),
            dma((3, groups)),
            dma((3, groups)),
            dma((6,)),
            dma((PLANE, 2)),
            dma((2,)),
            dma((reach + 1, 2)),
            dma((slots,)),
            dma((2,)),
            dma((3,)),
        ],
        compiler_params=pltpu.CompilerParams(
            collective_id=0, has_side_effects=True, vmem_limit_bytes=VMEM_ASK
        ),
        name="gather_and_attention",
    )(first_len, deal_rows, deal_col, cosine, sine, tokens, cotangent, wq, wot, kvg, gate, up, down)


def norm_back(values, gain, grad):
    scale = rms_scale(values)
    unit = values * scale
    lifted = grad * gain
    gain_grad = jnp.sum(grad * unit, axis=0, keepdims=True)
    back = scale * (lifted - unit * jnp.mean(lifted * unit, axis=-1, keepdims=True))
    return back, gain_grad


class ChainSum:
    def __init__(self, place, value, got, last, give, up_sems, down_sems, recv_sems, last_sems):
        self.place, self.value, self.got, self.last, self.give = place, value, got, last, give
        self.up_sems, self.down_sems = up_sems, down_sems
        self.recv_sems, self.last_sems = recv_sems, last_sems
        self.has_up = place.g + 1 < place.groups
        self.has_down = place.g >= 1

    def hop(self, a, g, k, up):
        to_last = k == 1 and not up
        place = self.place
        return pltpu.make_async_remote_copy(
            src_ref=self.give(a, g),
            dst_ref=self.last(a) if to_last else self.got(a, g),
            send_sem=(self.up_sems if up else self.down_sems).at[a, g],
            recv_sem=self.last_sems.at[a] if to_last else self.recv_sems.at[a, g],
            device_id=(place.d + PLANE if up else place.d - PLANE, place.f),
            device_id_type=MESH,
        )

    def step(self, a, k):
        place = self.place

        def toward(up):
            g = place.g + k if up else place.g - k
            total = self.value(a, k, up)
            from_behind = self.has_down if up else self.has_up

            @pl.when(from_behind)
            def _():
                arrived(self.got(a, g), self.recv_sems.at[a, g])
                self.give(a, g)[...] = (total + self.got(a, g)[...].astype(F32)).astype(BF16)

            @pl.when(jnp.logical_not(from_behind))
            def _():
                self.give(a, g)[...] = total.astype(BF16)

            self.hop(a, g, k, up).start()

        pl.when(place.g + k < place.groups)(functools.partial(toward, True))
        pl.when(place.g >= k)(functools.partial(toward, False))

    def final(self, a):
        place = self.place
        got, last = self.got(a, place.g), self.last(a)

        @pl.when(self.has_down)
        def _():
            arrived(got, self.recv_sems.at[a, place.g])

        @pl.when(jnp.logical_not(self.has_down))
        def _():
            got[...] = jnp.zeros(got.shape, BF16)

        @pl.when(self.has_up)
        def _():
            arrived(last, self.last_sems.at[a])

        @pl.when(jnp.logical_not(self.has_up))
        def _():
            last[...] = jnp.zeros(last.shape, BF16)

        return self.value(a, 0, True) + got[...].astype(F32) + last[...].astype(F32)

    def finish(self, count):
        place = self.place
        for a in range(count):
            for k in range(1, place.groups):

                @pl.when(place.g + k < place.groups)
                def _():
                    self.hop(a, place.g + k, k, True).wait_send()

                @pl.when(place.g >= k)
                def _():
                    self.hop(a, place.g - k, k, False).wait_send()


class PlaneReduce:
    def __init__(self, place, give, got, relay, send_sems, recv_sems, relay_sems):
        self.place, self.give, self.got, self.relay = place, give, got, relay
        self.send_sems, self.recv_sems, self.relay_sems = send_sems, recv_sems, relay_sems
        self.half = give.shape[1] // 2

    def copy(self, which):
        place = self.place
        slot, side, over_x = ((2, 0, 1), (2, 1, 0), (0, 0, 1), (1, 1, 0), (0, 1, 1), (1, 0, 0))[which]
        band = pl.ds(side * self.half, self.half)
        if which < 2:
            dst, recv = self.relay.at[side], self.relay_sems.at[side]
        else:
            dst, recv = self.got.at[slot, band], self.recv_sems.at[slot, side]
        return pltpu.make_async_remote_copy(
            src_ref=self.give.at[slot, band] if which < 4 else self.relay.at[side],
            dst_ref=dst,
            send_sem=self.send_sems.at[which],
            recv_sem=recv,
            device_id=(place.plane_chip(1 if over_x else 2), place.f),
            device_id_type=MESH,
        )

    def start(self, turn):
        @pl.when(turn == 0)
        def _():
            self.copy(0).start()
            self.copy(1).start()

        @pl.when(turn == 1)
        def _():
            self.copy(2).start()

        @pl.when(turn == 2)
        def _():
            self.copy(3).start()

    def pass_on(self):
        for side, slot, which in ((0, 1, 5), (1, 0, 4)):
            arrived(self.relay.at[side], self.relay_sems.at[side])
            mine = self.give[slot, side * self.half : (side + 1) * self.half]
            self.relay[side] = (mine.astype(F32) + self.relay[side].astype(F32)).astype(BF16)
            self.copy(which).start()

    def total(self):
        for slot in range(2):
            for side in range(2):
                band = pl.ds(side * self.half, self.half)
                arrived(self.got.at[slot, band], self.recv_sems.at[slot, side])
        return self.got[0].astype(F32) + self.got[1].astype(F32)

    def finish(self):
        for which in range(6):
            self.copy(which).wait_send()


def mlp_kernel(
    chips,
    n2_all,
    middle_ref,
    pg_own,
    gain_ref,
    three_hbm,
    out_total,
    out_give,
    two_ref,
    gain_grad_ref,
    half_ref,
    down_sum,
    three_ref,
    hidden_ref,
    gate_rows_ref,
    up_rows_ref,
    two_give,
    two_got,
    two_relay,
    pair_got,
    down_grad,
    down_half,
    down_got,
    down_last,
    gate_ref,
    upward_ref,
    pg_ref,
    pg_send,
    pg_recv,
    load_sems,
    rest_up,
    rest_down,
    rest_recv,
    rest_relay,
    rest_relayed,
    two_send,
    two_recv,
    two_relays,
    pair_send,
    pair_recv,
    down_up,
    down_down,
    down_recv,
    down_last_sems,
):
    place = Place(chips)
    d, f, other = place.d, place.f, place.other
    groups = place.groups
    rows, width = middle_ref.shape
    wide = PLANE * rows
    part = three_ref.shape[-1]
    plane_width = width // groups
    loads = [
        pltpu.make_async_copy(three_hbm.at[a], three_ref.at[a], load_sems.at[0, a])
        for a in range(2)
    ]
    for load in loads:
        load.start()

    def planes(ref, g):
        return ref.at[2, pl.ds(g * PLANE, PLANE)]

    def down_load(g):
        return pltpu.make_async_copy(
            planes(three_hbm, g), planes(three_ref, g), load_sems.at[1, g]
        )

    def near(use):
        use(place.g)
        if groups > 1:
            pl.when(place.g >= 1)(lambda: use(place.g - 1))
            pl.when(place.g + 1 < groups)(lambda: use(place.g + 1))

    near(lambda g: down_load(g).start())
    greet_all(place)

    def rest_hop(g, up, k):
        src = three_hbm if k == 1 else three_ref
        return pltpu.make_async_remote_copy(
            src_ref=src.at[2, pl.ds(g * PLANE, PLANE), f],
            dst_ref=three_ref.at[2, pl.ds(g * PLANE, PLANE), f],
            send_sem=(rest_up if up else rest_down).at[g],
            recv_sem=rest_recv.at[g],
            device_id=(d + PLANE if up else d - PLANE, f),
            device_id_type=MESH,
        )

    def rest_pass(g):
        ref = three_ref.at[2, pl.ds(g * PLANE, PLANE), f]
        return pltpu.make_async_remote_copy(
            src_ref=ref,
            dst_ref=ref,
            send_sem=rest_relay.at[g],
            recv_sem=rest_relayed.at[g],
            device_id=(d, other),
            device_id_type=MESH,
        )

    has_up, has_down = place.g + 1 < groups, place.g >= 1

    def rest_each(k, use):
        pl.when(place.g >= k)(lambda: use(place.g - k, True, has_up))
        pl.when(place.g + k < groups)(lambda: use(place.g + k, False, has_down))

    def rest_step(k):
        def use(g, up, more):
            arrived(three_ref.at[2, pl.ds(g * PLANE, PLANE), f], rest_recv.at[g])
            if k + 1 < groups:
                pl.when(more)(rest_hop(g, up, k).start)
            rest_pass(g).start()

        rest_each(k, use)

    def rest_hops(k, act):
        if k + 1 < groups:
            up, down = (rest_hop(place.g - k, True, k), rest_hop(place.g + k, False, k))
            pl.when((place.g >= k) & (place.g < groups - 1))(getattr(up, act))
            pl.when((place.g < groups - k) & (place.g >= 1))(getattr(down, act))

    def rest_finish(k):
        def use(g, up, more):
            rest_pass(g).wait_send()
            arrived(three_ref.at[2, pl.ds(g * PLANE, PLANE), other], rest_relayed.at[g])

        rest_hops(k, "wait_send")
        if k > 1:
            rest_each(k, use)

    rest_hops(1, "start")
    cotangents = PlaneSpread(place, pg_ref, pg_send, pg_recv)
    pg_ref[place.p] = pg_own[...]
    cotangents.start()

    two = PlaneReduce(place, two_give, two_got, two_relay, two_send, two_recv, two_relays)
    curve = 0.7978845608028654
    cubic = 0.044715
    step_width = 2 * HEAD

    def weight(a, band):
        return three_ref[a, :, :, :, band].reshape(width, -1)

    chunks = [slice(i, i + 32) for i in range(0, wide, 32)]

    def forward_units(band, size):
        x = n2_all[...].reshape(wide, width)
        gate_ref[:, :size] = mm(x, weight(0, band))
        upward_ref[:, :size] = mm(x, weight(1, band))
        for at in chunks:
            gate = gate_ref[at, :size]
            upward = upward_ref[at, :size]
            square = gate * gate
            tanh = jnp.tanh(gate * (curve + (curve * cubic) * square))
            above = 0.5 * (1.0 + tanh)
            activated = gate * above
            slope = above + activated * (1.0 - tanh) * (curve + (3.0 * curve * cubic) * square)
            hidden_ref[at, band] = (activated * upward).astype(BF16)
            gate_rows_ref[at, band] = (upward * slope).astype(BF16)
            up_rows_ref[at, band] = activated.astype(BF16)

    def backward_units(band, size):
        gate_ref[:, :size] = mm(pg_ref[...].reshape(wide, width), weight(2, band))
        for at in chunks:
            grad_hidden = gate_ref[at, :size]
            gate_rows_ref[at, band] = (
                grad_hidden * gate_rows_ref[at, band].astype(F32)
            ).astype(BF16)
            up_rows_ref[at, band] = (grad_hidden * up_rows_ref[at, band].astype(F32)).astype(BF16)

    def over_units(body):
        full = part // step_width

        def step(i, carry):
            body(pl.ds(pl.multiple_of(i * step_width, step_width), step_width), step_width)
            return carry

        lax.fori_loop(0, full, step, 0)
        if part % step_width:
            body(pl.ds(full * step_width, part % step_width), part % step_width)

    def at_turn(i):
        return ((i + 2) % 3 + 1) * (1 - i // 3)

    def band_of(pos):
        return pl.ds(pl.multiple_of(pos * rows, rows), rows)

    def whole(a):
        return three_ref[a].reshape(width, part)

    def back_block(i, carry):
        band = band_of(place.plane_pos(at_turn(i)))
        back = mm_nt(gate_rows_ref[band, :], whole(0)) + mm_nt(up_rows_ref[band, :], whole(1))

        @pl.when(i < PLANE - 1)
        def _():
            two_give[(i + 2) % 3] = back.astype(BF16)

        @pl.when(i == PLANE - 1)
        def _():
            two_ref[...] = back

        two.start(i)
        return carry

    def out_block(i, carry):
        piece = mm_nt(hidden_ref[band_of(place.plane_pos(at_turn(i))), :], whole(2))

        @pl.when(i < PLANE - 1)
        def _():
            out_give[(i + 2) % 3] = piece.astype(BF16)

        @pl.when(i == PLANE - 1)
        def _():
            out_total[...] = (middle_ref[...] + piece).astype(BF16)

        return carry

    def grad_at(a, g, core):
        if a == 2:
            return down_grad.at[pl.ds(g * PLANE, PLANE), core]
        return three_ref.at[a, pl.ds(g * PLANE, PLANE), core]

    def pair_copy(a, g):
        return pltpu.make_async_remote_copy(
            src_ref=grad_at(a, g, other),
            dst_ref=pair_got.at[a, g],
            send_sem=pair_send.at[a, g],
            recv_sem=pair_recv.at[a, g],
            device_id=(d, other),
            device_id_type=MESH,
        )

    def weight_grad(a, left, right):
        def step(g, carry):
            at = pl.ds(pl.multiple_of(g * plane_width, 128), plane_width)
            piece = mm_tn(left[:, :, at].reshape(wide, plane_width), right[...]).astype(BF16)
            pieces = piece.reshape(PLANE, 2, plane_width // (2 * PLANE), part)
            for core in range(2):
                grad_at(a, g, core)[...] = pieces[:, core]
            pair_copy(a, g).start()
            return carry

        lax.fori_loop(0, groups, step, 0)

    def pair_sum(a, into):
        def step(g, carry):
            arrived(pair_got.at[a, g], pair_recv.at[a, g])
            into[g] = (grad_at(a, g, f)[...].astype(F32) + pair_got[a, g].astype(F32)).astype(BF16)
            return carry

        lax.fori_loop(0, groups, step, 0)

    down = ChainSum(
        place,
        lambda a, k, up: down_half[place.g + k if up else place.g - k].astype(F32),
        lambda a, g: down_got.at[g],
        lambda a: down_last.at[0],
        lambda a, g: down_got.at[g],
        down_up,
        down_down,
        down_recv,
        down_last_sems,
    )
    loads[0].wait()
    loads[1].wait()
    over_units(forward_units)
    cotangents.pass_on()
    near(lambda g: down_load(g).wait())
    for k in range(2, groups):
        rest_step(k)
    cotangents.wait()
    weight_grad(2, pg_ref, hidden_ref)
    for k in range(1, groups):
        rest_finish(k)
    over_units(backward_units)
    pair_sum(2, down_half)
    for k in range(groups - 1, 2, -1):
        down.step(0, k)
    lax.fori_loop(0, PLANE, back_block, 0)
    for k in range(min(2, groups - 1), 1, -1):
        down.step(0, k)
    lax.fori_loop(0, PLANE, out_block, 0)
    two.pass_on()
    weight_grad(0, n2_all, gate_rows_ref)
    down.step(0, 1)
    weight_grad(1, n2_all, up_rows_ref)
    pair_sum(0, half_ref.at[0])
    pair_sum(1, half_ref.at[1])
    grad_two = two_ref[...] + two.total()
    back, gain_grad_ref[...] = norm_back(middle_ref[...], gain_ref[...], grad_two)
    two_ref[...] = pg_ref[place.p].astype(F32) + back
    down_sum[...] = down.final(0).astype(BF16)
    two.finish()
    cotangents.finish()
    for a in range(3):
        for g in range(groups):
            pair_copy(a, g).wait_send()
    down.finish(1)


def mlp(chips, n2, middle, pg, gain_two, three):
    rows, width = middle.shape
    part = three.shape[-1]
    groups = chips // PLANE
    dma = pltpu.SemaphoreType.DMA
    shape = jax.ShapeDtypeStruct
    wide = PLANE * rows
    column = (groups, PLANE) + three.shape[3:]
    return pl.pallas_call(
        functools.partial(mlp_kernel, chips),
        out_shape=(
            shape((rows, width), BF16),
            shape((PLANE - 1, rows, width), BF16),
            shape((rows, width), F32),
            shape((1, width), F32),
            shape((2,) + column, BF16),
            shape(column[1:], BF16),
        ),
        in_specs=[VM] * 4 + [ANY],
        out_specs=(VM,) * 6,
        scratch_shapes=[
            pltpu.VMEM(three.shape, BF16),
            pltpu.VMEM((wide, part), BF16),
            pltpu.VMEM((wide, part), BF16),
            pltpu.VMEM((wide, part), BF16),
        ]
        + [
            pltpu.VMEM((PLANE - 1, rows, width), BF16),
            pltpu.VMEM((2, rows, width), BF16),
            pltpu.VMEM((2, rows // 2, width), BF16),
            pltpu.VMEM((3,) + column, BF16),
            pltpu.VMEM(three.shape[1:], BF16),
            pltpu.VMEM(column, BF16),
            pltpu.VMEM(column, BF16),
            pltpu.VMEM((1,) + column[1:], BF16),
            pltpu.VMEM((wide, 2 * HEAD), F32),
            pltpu.VMEM((wide, 2 * HEAD), F32),
            pltpu.VMEM((PLANE, rows, width), BF16),
            dma((6,)),
            dma((PLANE, 2)),
            dma((2, max(3, groups))),
        ]
        + [dma((groups,))] * 5
        + [
            dma((6,)),
            dma((2, 2)),
            dma((2,)),
            dma((3, groups)),
            dma((3, groups)),
            dma((1, groups)),
            dma((1, groups)),
            dma((1, groups)),
            dma((1,)),
        ],
        compiler_params=pltpu.CompilerParams(
            collective_id=1, has_side_effects=True, vmem_limit_bytes=VMEM_ASK
        ),
        name="mlp_both_ways",
    )(n2, middle, pg, gain_two, three)


def backward_kernel(
    chips,
    reach,
    out_own,
    out_give,
    down_sum,
    rows_ref,
    grad_middle_ref,
    gain_two_grad_ref,
    n1_ref,
    qs_ref,
    kv_ref,
    mixed_ref,
    wq_ref,
    wot_ref,
    kvg_ref,
    cos_ref,
    sin_ref,
    take_ref,
    place_ref,
    probs_hbm,
    half_hbm,
    three_end,
    q_out,
    ot_out,
    kvg_out,
    output_ref,
    input_grad_ref,
    probs_ref,
    low_ref,
    mixed_rows,
    grad_mixed,
    grad_q,
    kv_total,
    kv_give,
    kv_pair,
    kv_got,
    one_out,
    one_in,
    three_got,
    three_last,
    three_stage,
    heads_ref,
    plane_relay,
    plane_got,
    column_got,
    column_last,
    column_give,
    gkvg_ref,
    gkvg_pair,
    small_got,
    small_give,
    small_column,
    give,
    got,
    probs_sems,
    stage_sems,
    low_sems,
    kv_send,
    kv_recv,
    one_sems,
    three_up,
    three_down,
    three_recv,
    three_last_sems,
    end_send,
    end_recv,
    direct_send,
    relay_send,
    relay_recv,
    plane_recv,
    small_send,
    small_recv,
    column_up,
    column_down,
    column_recv,
    column_last_sems,
    row_send,
    row_recv,
    grad_probs_ref,
    grad_scores_ref,
    out_got,
    out_relay,
    out_send,
    out_recv,
    out_relays,
):
    place = Place(chips)
    d, f, other = place.d, place.f, place.other
    groups = place.groups
    rows, width = rows_ref.shape
    micro = rows // MICRO
    heads = wq_ref.shape[1] // HEAD
    share = width // chips
    half = share // 2
    part = half_hbm.shape[-1]
    per = rows // chips
    span = (2 * reach + 1) * micro
    by_x, by_y, far = (place.plane_pos(j) for j in range(1, PLANE))
    to_x, to_y = place.plane_chip(1), place.plane_chip(2)
    sent = Sent()

    pairs = heads // 2

    def probs_copy(n):
        band = pl.ds(pl.multiple_of((n % pairs) * 2 * micro, 2 * micro), 2 * micro)
        return pltpu.make_async_copy(
            probs_hbm.at[n // pairs, :, band], probs_ref.at[n % 2], probs_sems.at[n % 2]
        )

    probs_copy(0).start()
    greet_all(place)

    events = [(a, k) for k in range(groups - 1, -1, -1) for a in range(2)]

    def stage_copy(n, up):
        a, k = events[n]
        slot = 0 if up else 1
        return pltpu.make_async_copy(
            half_hbm.at[a, place.g + k if up else place.g - k],
            three_stage.at[n % 2, slot],
            stage_sems.at[n % 2, slot],
        )

    def fetch(n):
        k = events[n][1]
        pl.when(place.g + k < groups)(stage_copy(n, True).start)
        if k > 0:
            pl.when(place.g >= k)(stage_copy(n, False).start)

    def three_value(a, k, up):
        n = events.index((a, k))
        stage_copy(n, up).wait()
        return three_stage[n % 2, 0 if up else 1].astype(F32)

    out = PlaneReduce(place, out_give, out_got, out_relay, out_send, out_recv, out_relays)
    for which in range(4):
        out.copy(which).start()
    fetch(0)
    three = ChainSum(
        place,
        three_value,
        lambda a, g: three_got.at[a, g],
        lambda a: three_last.at[a],
        lambda a, g: three_got.at[a, g],
        three_up,
        three_down,
        three_recv,
        three_last_sems,
    )

    def three_steps(k, arrays=(0, 1)):
        for a in arrays:
            fetch(events.index((a, k)) + 1)
            three.step(a, k)

    for k in range(groups - 1, 2, -1):
        three_steps(k)

    low_ref[f] = grad_middle_ref[...].astype(BF16)
    sent.remote(low_ref.at[f], low_ref.at[f], low_sems.at[0], low_sems.at[1], (d, other))
    kv_total[...] = jnp.zeros_like(kv_total)

    def block(k):
        return pl.ds(pl.multiple_of(k * per, per), per)

    home = (Sent(), Sent())

    def rows_home(i, source_ref):
        if i > 0:
            home[i - 1].finish()
        give[...] = mm_tn(place_ref[...], source_ref[...]).astype(BF16)
        for k in range(1, chips):
            to = (d + k) % chips
            home[i].remote(
                give.at[block(to)],
                got.at[i, block(d)],
                row_send.at[i, k],
                row_recv.at[i, d],
                (to, f),
            )
        got[i, block(d), :] = give[block(d), :]

    def rows_back(i):
        for k in range(1, chips):
            s = (d + k) % chips
            arrived(got.at[i, block(s)], row_recv.at[i, s])
        return mm_tn(take_ref[...], got[i]).astype(BF16)

    def mix_back(h):
        grads = mm(low_ref[h], wot_ref[...])
        for m in range(MICRO):
            for i in range(heads):
                grad_mixed[2 * h + m, i * micro : (i + 1) * micro, :] = grads[
                    m * micro : (m + 1) * micro, i * HEAD : (i + 1) * HEAD
                ].astype(BF16)

    mix_back(f)
    arrived(low_ref.at[other], low_sems.at[1])
    mix_back(other)

    def whole(g, pos):
        return pl.ds(pl.multiple_of((g * PLANE + pos) * share, 16), share)

    def term(a, g, pos):
        return heads_ref.at[a, whole(g, pos)]

    def plane_copy(kind, a, g):
        even = g % 2 == 0
        near_pos, near_to, near_side = (by_x, to_x, 0) if even else (by_y, to_y, 1)
        if kind == 0:
            src, dst, to = term(a, g, near_pos), plane_got.at[a, near_side, g], near_to
            send, recv = direct_send.at[a, 0, g], plane_recv.at[a, near_side, g]
        elif kind == 1:
            src, dst, to = term(a, g, far), plane_relay.at[a, g], near_to
            send, recv = direct_send.at[a, 1, g], relay_recv.at[a, g]
        else:
            side = 1 - near_side
            src, dst, to = plane_relay.at[a, g], plane_got.at[a, side, g], to_y if even else to_x
            send, recv = relay_send.at[a, g], plane_recv.at[a, side, g]
        return pltpu.make_async_remote_copy(
            src_ref=src,
            dst_ref=dst,
            send_sem=send,
            recv_sem=recv,
            device_id=(to, f),
            device_id_type=MESH,
        )

    def plane_start(a):
        for g in range(groups):
            plane_copy(1, a, g).start()
            plane_copy(0, a, g).start()

    def plane_pass(a):
        for g in range(groups):
            arrived(plane_relay.at[a, g], relay_recv.at[a, g])
            mine = term(a, g, by_y if g % 2 == 0 else by_x)
            plane_relay[a, g] = (plane_relay[a, g].astype(F32) + mine[...].astype(F32)).astype(BF16)
            plane_copy(2, a, g).start()

    def plane_total(a, k, up):
        g = place.g + k if up else place.g - k
        total = term(a, g, place.p)[...].astype(F32)
        for side in range(2):
            arrived(plane_got.at[a, side, g], plane_recv.at[a, side, g])
            total = total + plane_got[a, side, g].astype(F32)
        return total

    column = ChainSum(
        place,
        plane_total,
        lambda a, g: column_got.at[a, g],
        lambda a: column_last.at[a],
        lambda a, g: column_give.at[a, g],
        column_up,
        column_down,
        column_recv,
        column_last_sems,
    )

    tile = 2 * HEAD

    def head_grads(a, left_ref):
        def step(i, carry):
            at = pl.ds(pl.multiple_of(i * tile, tile), tile)
            left = left_ref[:, :, at].reshape(2 * rows, tile)
            heads_ref[a, at, :] = mm_tn(left, mixed_rows[...]).astype(BF16)
            return carry

        lax.fori_loop(0, width // tile, step, 0)

    for hm in range(4):
        mixed_rows[hm * micro : (hm + 1) * micro, :] = mixed_ref[hm]
    head_grads(0, low_ref)
    plane_start(0)
    out.pass_on()

    score_scale = HEAD ** (-0.5)
    chunks = [slice(i, i + 64) for i in range(0, span, 64)]

    def attend_back(hm):
        h, m = hm // 2, hm % 2
        at = slice(h, h + 2 * reach + 1)
        keys = kv_ref[m, at, :, 0:HEAD].reshape(span, HEAD)
        values = kv_ref[m, at, :, HEAD:].reshape(span, HEAD)
        keys_t = keys.T

        def pair_step(pair, carry):
            band = pl.ds(pl.multiple_of(pair * 2 * micro, 2 * micro), 2 * micro)
            n = hm * pairs + pair
            probs_copy(n).wait()
            pl.when(n + 1 < 4 * pairs)(lambda: probs_copy(n + 1).start())
            grads = grad_mixed[hm, band, :]
            queries = qs_ref[hm, band, :]
            grad_probs_ref[...] = mm_nt(values, grads)
            delta = jnp.zeros((8, 2 * micro), F32)
            for part_at in chunks:
                wide = probs_ref[n % 2, part_at, :].astype(F32)
                delta = delta + fold(grad_probs_ref[part_at, :] * wide, jnp.add)
            delta = jnp.sum(delta, axis=0, keepdims=True)
            for part_at in chunks:
                wide = probs_ref[n % 2, part_at, :].astype(F32)
                grad_scores_ref[part_at, :] = (
                    wide * (grad_probs_ref[part_at, :] - delta)
                ).astype(BF16)
            grad_scores = grad_scores_ref[...]
            value_total = mm(probs_ref[n % 2], grads).reshape(2 * reach + 1, micro, HEAD)
            kv_total[m, at, :, HEAD:] = kv_total[m, at, :, HEAD:] + value_total
            key_total = mm(grad_scores, queries).reshape(2 * reach + 1, micro, HEAD)
            kv_total[m, at, :, 0:HEAD] = kv_total[m, at, :, 0:HEAD] + key_total
            query_t = mm(keys_t, grad_scores) * score_scale
            grad_q[hm, :, band] = jnp.concatenate(
                [
                    turned(
                        query_t[:, i * micro : (i + 1) * micro].T, cos_ref[hm], -sin_ref[hm]
                    )
                    for i in range(2)
                ],
                axis=1,
            ).astype(BF16)
            return carry

        lax.fori_loop(0, heads // 2, pair_step, 0)

    middle_steps = [(k, (a,)) for k in range(min(2, groups - 1), 0, -1) for a in range(2)]
    turns = iter(middle_steps)

    def next_step():
        for step in turns:
            three_steps(*step)
            break

    next_step()
    attend_back(0)
    next_step()
    attend_back(1)
    plane_pass(0)
    next_step()
    attend_back(2)
    one_out[...] = (out_own[...].astype(F32) + out.total()).astype(BF16)
    rows_home(0, one_out)
    next_step()
    attend_back(3)

    for m in range(MICRO):
        for slot in range(2 * reach + 2):
            kv_total[m, slot, :, 0:HEAD] = kv_total[m, slot, :, 0:HEAD] * score_scale
            kv_give[m, slot] = kv_total[m, slot].astype(BF16)
    own_slots = [2 * j + f for j in range(reach + 1)]
    other_slots = [2 * j + other for j in range(reach + 1)]
    for j in range(reach + 1):
        sent.remote(
            kv_give.at[:, other_slots[j]],
            kv_pair.at[:, j],
            kv_send.at[0, j],
            kv_recv.at[0, j],
            (d, other),
        )

    def kv_copy(j):
        return pltpu.make_async_remote_copy(
            src_ref=kv_give.at[:, own_slots[reach - j]],
            dst_ref=kv_got.at[j],
            send_sem=kv_send.at[1, j],
            recv_sem=kv_recv.at[1, j],
            device_id=(d - j, f),
            device_id_type=MESH,
        )

    for hm in range(4):
        mixed_rows[hm * micro : (hm + 1) * micro, :] = grad_q[hm]
    head_grads(1, n1_ref)
    plane_start(1)
    for j in range(reach, -1, -1):
        s = reach - j
        arrived(kv_pair.at[:, s], kv_recv.at[0, s])
        total = kv_total[:, own_slots[s]] + kv_pair[:, s].astype(F32)
        kv_total[:, own_slots[s]] = total
        if j > 0:
            kv_give[:, own_slots[s]] = total.astype(BF16)

            @pl.when(d - j >= 0)
            def _():
                kv_copy(j).start()

    def one_back(h):
        at = pl.ds(pl.multiple_of(h * rows, rows), rows)
        return mm_nt(mixed_rows[at, :], wq_ref[...])

    column_steps = [k for k in range(groups - 1, 0, -1)]
    column.step(0, column_steps[0])
    one_out[...] = one_back(other).astype(BF16)
    sent.remote(one_out, one_in, one_sems.at[0], one_sems.at[1], (d, other))
    grad_one = one_back(f)
    for k in column_steps[1:2]:
        column.step(0, k)
    plane_pass(1)
    for k in column_steps[2:]:
        column.step(0, k)

    sums = [kv_total[m, 2 * reach + f] for m in range(MICRO)]
    for j in range(1, reach + 1):

        @pl.when(d + j < chips)
        def _():
            arrived(kv_got.at[j], kv_recv.at[1, j])

        @pl.when(d + j >= chips)
        def _():
            kv_got[j] = jnp.zeros((MICRO, micro, 2 * HEAD), BF16)

        sums = [sums[m] + kv_got[j, m].astype(F32) for m in range(MICRO)]
    key_rows = jnp.concatenate(
        [
            turned(sums[m][:, 0:HEAD], cos_ref[2 * f + m], -sin_ref[2 * f + m])
            for m in range(MICRO)
        ],
        axis=0,
    )
    value_rows = jnp.concatenate([sums[m][:, HEAD:] for m in range(MICRO)], axis=0)
    pieces = halves_in(key_rows, value_rows)
    row_values = rows_ref[...].astype(F32)
    for i in range(2):
        piece = pieces[i].astype(BF16)
        gkvg_ref[i, :, 0:share, :] = mm_tn(n1_ref[f], piece).astype(BF16).reshape(chips, share, HEAD)
        grad_one = grad_one + mm_nt(piece, kvg_ref[i, :, 0:share, :].reshape(width, HEAD))
    arrived(one_in, one_sems.at[1])
    grad_one = grad_one + one_in[...].astype(F32)
    gain_one = gain_row(kvg_ref, 0, chips, width, share)
    back_one, gain_one_grad = norm_back(row_values, gain_one, grad_one)
    one_in[...] = (grad_middle_ref[...] + back_one).astype(BF16)
    column.step(1, column_steps[0])
    rows_home(1, one_in)
    spread = gain_spread(width, share)
    stretch = own_stretch(chips, width, share)
    for i, grad in enumerate((gain_one_grad, gain_two_grad_ref[...])):
        piece = mm_nt(jnp.where(stretch, grad, 0.0).astype(BF16), spread)
        row = iota((chips, 16, HEAD), 1)
        gkvg_ref[i, :, share : share + 16, :] = jnp.where(
            row == 0, piece[:, None, :], 0.0
        ).astype(BF16)
    sent.remote(gkvg_ref.at[other], gkvg_pair, small_send.at[0], small_recv.at[0], (d, other))
    arrived(gkvg_pair, small_recv.at[0])

    def small_sum(s):
        return gkvg_ref[f, s].astype(F32) + gkvg_pair[s].astype(F32)

    for j in range(1, PLANE):
        pos = place.plane_pos(j)
        for g in range(groups):
            small_give[j, g] = small_sum(g * PLANE + pos).astype(BF16)
        sent.remote(
            small_give.at[j],
            small_got.at[j],
            small_send.at[j],
            small_recv.at[j],
            (place.plane_chip(j), f),
        )

    for k in column_steps[1:]:
        column.step(1, k)
    for j in range(1, PLANE):
        arrived(small_got.at[j], small_recv.at[j])
    for k in range(1, groups):
        g = (place.g + k) % groups
        s = g * PLANE + place.p
        total = small_sum(s)
        for j in range(1, PLANE):
            total = total + small_got[j, g].astype(F32)
        small_give[0, g] = total.astype(BF16)
        sent.remote(
            small_give.at[0, g],
            small_column.at[place.g],
            small_send.at[PLANE + k],
            small_recv.at[PLANE + place.g],
            (s, f),
        )
    total = small_sum(d)
    for j in range(1, PLANE):
        total = total + small_got[j, place.g].astype(F32)
    kvg_out[...] = total

    def end_copy(a, j):
        pos = place.plane_pos(j)
        src = down_sum.at[pos] if a == 2 else three_got.at[a, place.g, pos]
        return pltpu.make_async_remote_copy(
            src_ref=src,
            dst_ref=three_end.at[a, place.x, f],
            send_sem=end_send.at[a, j],
            recv_sem=end_recv.at[a, place.x, f],
            device_id=(place.plane_chip(j), place.y),
            device_id_type=MESH,
        )

    def end_local(a):
        src = down_sum.at[place.p] if a == 2 else three_got.at[a, place.g, place.p]
        return pltpu.make_async_copy(src, three_end.at[a, place.x, f], end_send.at[a, 0])

    for a in (2, 0, 1):
        if a == 0:
            fetch(events.index((1, 0)))
        if a < 2:
            three_got[a, place.g] = three.final(a).astype(BF16)
        for j in range(1, PLANE):
            end_copy(a, j).start()
        pl.when(place.y == f)(end_local(a).start)
        pl.when(place.y != f)(end_copy(a, 0).start)

    output_ref[...] = rows_back(0)
    for a in range(2):
        (ot_out, q_out)[a][...] = column.final(a)
    for k in range(1, groups):
        g = (place.g + k) % groups
        arrived(small_column.at[g], small_recv.at[PLANE + g])
        kvg_out[...] = kvg_out[...] + small_column[g].astype(F32)
    input_grad_ref[...] = rows_back(1)
    for a in (2, 0, 1):
        for cx in range(2):
            for core in range(2):
                own = (place.y == f) & (place.x == cx) & (core == f)

                @pl.when(own)
                def _():
                    end_local(a).wait()

                @pl.when(jnp.logical_not(own))
                def _():
                    arrived(three_end.at[a, cx, core], end_recv.at[a, cx, core])

    out.finish()
    three.finish(2)
    column.finish(2)
    for a in range(3):
        for j in range(1, PLANE):
            end_copy(a, j).wait_send()
        pl.when(place.y != f)(end_copy(a, 0).wait_send)
    for a in range(2):
        for g in range(groups):
            for kind in range(3):
                plane_copy(kind, a, g).wait_send()
    for j in range(1, reach + 1):

        @pl.when(d - j >= 0)
        def _():
            kv_copy(j).wait_send()

    home[1].finish()
    sent.finish()


def backward(chips, reach, out_own, out_give, down_sum, rows_in, grad_middle, gain_two_grad, n1, qs, kv, mixed, wq, wot, kvg, cosine, sine, take, placing, probs, halves):
    rows, width = rows_in.shape
    micro = rows // MICRO
    heads_wide = wq.shape[1]
    heads = heads_wide // HEAD
    groups = chips // PLANE
    share = width // chips
    half, part = halves.shape[3:]
    slots = 2 * reach + 2
    small = kvg.shape[2:]
    dma = pltpu.SemaphoreType.DMA
    shape = jax.ShapeDtypeStruct
    vm = pltpu.VMEM
    kv_shape = (MICRO, slots, micro, 2 * HEAD)
    return pl.pallas_call(
        functools.partial(backward_kernel, chips, reach),
        out_shape=(
            shape((3, 2, 2, half, part), BF16),
            shape((share, heads_wide), F32),
            shape((share, heads_wide), F32),
            shape(small, F32),
            shape((rows, width), BF16),
            shape((rows, width), BF16),
        ),
        in_specs=[VM] * 17 + [ANY] * 2,
        out_specs=(ANY,) + (VM,) * 5,
        scratch_shapes=[
            vm((2, probs.shape[1], 2 * micro), BF16),
            vm((2, rows, width), BF16),
            vm((2 * rows, heads_wide), BF16),
            vm((4, heads * micro, HEAD), BF16),
            vm((4, micro, heads_wide), BF16),
            vm(kv_shape, F32),
            vm(kv_shape, BF16),
            vm((MICRO, reach + 1, micro, 2 * HEAD), BF16),
            vm((reach + 1, MICRO, micro, 2 * HEAD), BF16),
            vm((rows, width), BF16),
            vm((rows, width), BF16),
            vm((2, groups, PLANE, half, part), BF16),
            vm((2, PLANE, half, part), BF16),
            vm((2, 2, PLANE, half, part), BF16),
            vm((2, width, heads_wide), BF16),
            vm((2, groups, share, heads_wide), BF16),
            vm((2, 2, groups, share, heads_wide), BF16),
            vm((2, groups, share, heads_wide), BF16),
            vm((2, share, heads_wide), BF16),
            vm((2, groups, share, heads_wide), BF16),
            vm((2, chips) + small, BF16),
            vm((chips,) + small, BF16),
            vm((PLANE, groups) + small, BF16),
            vm((PLANE, groups) + small, BF16),
            vm((groups,) + small, BF16),
            vm((rows, width), BF16),
            vm((2, rows, width), BF16),
            dma((2,)),
            dma((2, 2)),
            dma((2,)),
            dma((2, reach + 1)),
            dma((2, reach + 1)),
            dma((2,)),
            dma((2, groups)),
            dma((2, groups)),
            dma((2, groups)),
            dma((2,)),
            dma((3, PLANE)),
            dma((3, 2, 2)),
            dma((2, 2, groups)),
            dma((2, groups)),
            dma((2, groups)),
            dma((2, 2, groups)),
            dma((PLANE + groups,)),
            dma((PLANE + groups,)),
            dma((2, groups)),
            dma((2, groups)),
            dma((2, groups)),
            dma((2,)),
            dma((2, chips)),
            dma((2, chips)),
            vm((probs.shape[1], 2 * micro), F32),
            vm((probs.shape[1], 2 * micro), BF16),
            vm((2, rows, width), BF16),
            vm((2, rows // 2, width), BF16),
            dma((6,)),
            dma((2, 2)),
            dma((2,)),
        ],
        compiler_params=pltpu.CompilerParams(
            collective_id=2, has_side_effects=True, vmem_limit_bytes=VMEM_ASK
        ),
        name="attention_backward_and_scatter",
    )(out_own, out_give, down_sum, rows_in, grad_middle, gain_two_grad, n1, qs, kv, mixed, wq, wot, kvg, cosine, sine, take, placing, probs, halves)


def planned(
    tokens,
    cotangent,
    deal,
    first_len,
    w_query,
    w_key,
    w_value,
    w_out,
    w_gate,
    w_up,
    w_down,
    norm_gains,
):
    chips = lax.axis_size("dp")
    rows, width = tokens.shape
    micro = rows // MICRO
    share = w_query.shape[0]
    back_blocks = min(2 * chips - 1, (WINDOW + micro - 2) // micro)
    reach = (back_blocks + 1) // 2
    d = lax.axis_index("dp")
    inside = jnp.arange(micro, dtype=jnp.int32)
    positions = (2 * d + jnp.arange(2, dtype=jnp.int32))[:, None, None] * micro + inside
    second = positions >= first_len[None, :, None]
    within = positions - jnp.where(second, first_len[None, :, None], 0)
    cosine, sine = angles(within.reshape(-1))
    cosine = jnp.concatenate([cosine, cosine], axis=1).reshape(4, micro, HEAD)
    sine = jnp.concatenate([-sine, sine], axis=1).reshape(4, micro, HEAD)
    gain_rows = jnp.pad(norm_gains, ((0, 15), (0, HEAD - share)))
    kvg = jnp.concatenate([jnp.concatenate([w_key, w_value], axis=1), gain_rows], axis=0)
    (
        three, wq, wot, kvg_all, rows_in, pg, take, placing, n1, qs, kv, probs, mixed, middle, n2, gain_two
    ) = forward(
        chips, reach, first_len, deal, cosine, sine, tokens, cotangent, w_query, w_out.T, kvg,
        w_gate, w_up, w_down.T,
    )
    out_own, out_give, grad_middle, gain_two_grad, halves, down_sum = mlp(
        chips, n2, middle, pg, gain_two, three
    )
    three_out, q_out, ot_out, kvg_out, output, input_grad = backward(
        chips, reach, out_own, out_give, down_sum, rows_in, grad_middle, gain_two_grad, n1, qs, kv, mixed, wq, wot,
        kvg_all, cosine, sine, take, placing, probs, halves,
    )
    units = w_gate.shape[1]
    three_out = jnp.transpose(three_out, (0, 2, 3, 1, 4)).reshape(3, share, units).astype(F32)
    key_cols = w_key.shape[1]
    return (
        output,
        input_grad,
        q_out,
        kvg_out[:share, :key_cols],
        kvg_out[:share, key_cols:],
        ot_out.T,
        three_out[0],
        three_out[1],
        three_out[2].T,
        kvg_out[share : share + 1, :share],
    )


def fits_plan(mesh, share):
    chips = mesh.shape["dp"]
    return mesh.shape["fsdp"] == 2 and chips % PLANE == 0 and share % 32 == 0 and share < HEAD


def solution(mesh):
    in_specs = (
        P(("dp", "fsdp"), None),
        P(("dp", "fsdp"), None),
        P(("dp", "fsdp")),
        P(),
        P("dp", "fsdp"),
        P("dp", "fsdp"),
        P("dp", "fsdp"),
        P("fsdp", "dp"),
        P("dp", "fsdp"),
        P("dp", "fsdp"),
        P("fsdp", "dp"),
        P("fsdp", "dp"),
    )
    out_specs = (
        P(("dp", "fsdp"), None),
        P(("dp", "fsdp"), None),
        P("dp", "fsdp"),
        P("dp", "fsdp"),
        P("dp", "fsdp"),
        P("fsdp", "dp"),
        P("dp", "fsdp"),
        P("dp", "fsdp"),
        P("fsdp", "dp"),
        P("fsdp", "dp"),
    )
    def placed(*arrays):
        share = arrays[4].shape[0] // mesh.shape["dp"]
        program = planned if fits_plan(mesh, share) else per_device
        return jax.shard_map(
            program, mesh=mesh, in_specs=in_specs, out_specs=out_specs, check_vma=False
        )(*arrays)

    return placed
```

```python
import functools

import jax
import jax.numpy as jnp
from jax import lax
from jax.experimental import pallas as pl
from jax.experimental.pallas import tpu as pltpu
from jax.sharding import PartitionSpec as P

HEADS = 12
HEAD = 128
WINDOW = 1024
MICRO = 2


EPSILON = 1e-06
NEGATIVE = -1e30
VMEM_ASK = 62 * 2**20


def passed_along(x, axis, by):
    count = lax.axis_size(axis)
    pairs = [(i, i + by) for i in range(count) if 0 <= i + by < count]
    return lax.ppermute(x, axis, pairs)


def normed(row_values, gain_row):
    return (
        row_values
        * lax.rsqrt(jnp.mean(row_values * row_values, axis=-1, keepdims=True) + EPSILON)
        * gain_row
    )


def rotate(values, cosine, sine_table):
    half_width = values.shape[-1] // 2
    front_half = values[..., :half_width]
    back_half = values[..., half_width:]
    return jnp.concatenate(
        [
            front_half * cosine - back_half * sine_table,
            back_half * cosine + front_half * sine_table,
        ],
        axis=-1,
    )


def angles(places):
    half_width = HEAD // 2
    frequency = 10000.0 ** (-jnp.arange(half_width, dtype=jnp.float32) * 2.0 / HEAD)
    angle_rows = places.astype(jnp.float32)[:, None] * frequency[None, :]
    return (jnp.cos(angle_rows), jnp.sin(angle_rows))


def contract_rows(left, right):
    return lax.dot_general(
        left, right, (((0,), (0,)), ((), ())), preferred_element_type=jnp.float32
    )


def against(left, right):
    return lax.dot_general(
        left, right, (((1,), (1,)), ((), ())), preferred_element_type=jnp.float32
    )


def gelu_tanh(inputs):
    return jax.nn.gelu(inputs, approximate=True)


def per_device(
    tokens,
    cotangent,
    deal,
    first_len,
    w_query,
    w_key,
    w_value,
    w_out,
    w_gate,
    w_up,
    w_down,
    norm_gains,
):
    peer_count = lax.axis_size("dp")
    core_count = lax.axis_size("fsdp")
    device_total = peer_count * core_count
    row_count = tokens.shape[0]
    model_width = tokens.shape[1]
    per_peer = row_count // peer_count
    micro_rows = row_count // MICRO
    reach_steps = min(device_total - 1, (WINDOW + micro_rows - 2) // micro_rows)
    linear = lax.axis_index("dp") * core_count + lax.axis_index("fsdp")
    source_peer = deal // (row_count * core_count)
    offsets = deal % row_count
    bucket_order = jnp.argsort(source_peer, stable=True)
    inverse = jnp.argsort(bucket_order)
    wanted = offsets[bucket_order].reshape(peer_count, per_peer)
    requested = lax.all_to_all(wanted, "dp", split_axis=0, concat_axis=0, tiled=True)
    picked = requested.reshape(-1)
    fetched = (
        lax.all_to_all(
            tokens[picked].reshape(peer_count, per_peer, model_width),
            "dp",
            split_axis=0,
            concat_axis=0,
            tiled=True,
        ),
        lax.all_to_all(
            cotangent[picked].reshape(peer_count, per_peer, model_width),
            "dp",
            split_axis=0,
            concat_axis=0,
            tiled=True,
        ),
    )
    rows_in = fetched[0].reshape(row_count, model_width)[inverse]
    grad_in = fetched[1].reshape(row_count, model_width)[inverse]
    halves = (
        lax.all_gather(w_query, "dp", axis=0, tiled=True),
        lax.all_gather(w_key, "dp", axis=0, tiled=True),
        lax.all_gather(w_value, "dp", axis=0, tiled=True),
        lax.all_gather(w_out, "dp", axis=1, tiled=True),
        lax.all_gather(w_gate, "dp", axis=0, tiled=True),
        lax.all_gather(w_up, "dp", axis=0, tiled=True),
        lax.all_gather(w_down, "dp", axis=1, tiled=True),
        lax.all_gather(norm_gains, "dp", axis=1, tiled=True),
    )
    gathered = (
        lax.all_gather(halves[0], "fsdp", axis=1, tiled=True),
        lax.all_gather(halves[1], "fsdp", axis=1, tiled=True),
        lax.all_gather(halves[2], "fsdp", axis=1, tiled=True),
        lax.all_gather(halves[3], "fsdp", axis=0, tiled=True),
        lax.all_gather(halves[4], "fsdp", axis=1, tiled=True),
        lax.all_gather(halves[5], "fsdp", axis=1, tiled=True),
        lax.all_gather(halves[6], "fsdp", axis=0, tiled=True),
        lax.all_gather(halves[7], "fsdp", axis=0, tiled=True),
    )
    full_query, full_key, full_value, full_out, full_gate, full_up, full_down, full_gains = gathered
    gain_one = full_gains[0].astype(jnp.float32)
    gain_two = full_gains[1].astype(jnp.float32)
    inside = jnp.arange(micro_rows, dtype=jnp.int32)
    query_place = linear * micro_rows + inside
    query_later = query_place[None, :] >= first_len[:, None]
    query_within = query_place[None, :] - jnp.where(query_later, first_len[:, None], 0)
    distance = jnp.arange(reach_steps, -1, -1, dtype=jnp.int32)
    key_place = ((linear - distance)[:, None] * micro_rows + inside[None, :]).reshape(-1)
    key_later = key_place[None, :] >= first_len[:, None]
    allowed = (
        (query_later[:, :, None] == key_later[:, None, :])
        & (key_place[None, None, :] >= 0)
        & (key_place[None, None, :] <= query_place[None, :, None])
        & (query_place[None, :, None] - key_place[None, None, :] < WINDOW)
    )
    rows_float = rows_in.astype(jnp.float32)
    cosine, sine_table = angles(query_within.reshape(-1))
    score_scale = HEAD ** (-0.5)
    normal_one = normed(rows_float, gain_one).astype(jnp.bfloat16)
    query_raw = jnp.dot(normal_one, full_query, preferred_element_type=jnp.float32).reshape(
        row_count, HEADS, HEAD
    )
    query_rows = rotate(query_raw, cosine[:, None, :], sine_table[:, None, :]).astype(jnp.bfloat16)
    key_rows = rotate(
        jnp.dot(normal_one, full_key, preferred_element_type=jnp.float32), cosine, sine_table
    ).astype(jnp.bfloat16)
    value_rows = jnp.dot(normal_one, full_value, preferred_element_type=jnp.float32).astype(
        jnp.bfloat16
    )
    earlier = []
    for distance_step in range(1, reach_steps + 1):
        earlier.append(passed_along((key_rows, value_rows), ("dp", "fsdp"), distance_step))
    ordered = earlier[::-1] + [(key_rows, value_rows)]
    all_keys = jnp.concatenate(
        [member[0].reshape(MICRO, micro_rows, HEAD) for member in ordered], axis=1
    )
    all_values = jnp.concatenate(
        [member[1].reshape(MICRO, micro_rows, HEAD) for member in ordered], axis=1
    )
    by_head = jnp.transpose(query_rows.reshape(MICRO, micro_rows, HEADS, HEAD), (2, 0, 1, 3))

    def attend(query_head):
        scores = jnp.where(
            allowed,
            jnp.einsum("mqd,mkd->mqk", query_head, all_keys, preferred_element_type=jnp.float32)
            * score_scale,
            NEGATIVE,
        )
        row_top = jnp.max(scores, axis=2, keepdims=True)
        exp_scores = jnp.exp(scores - row_top)
        row_total = jnp.sum(exp_scores, axis=2, keepdims=True)
        soft_weights = (exp_scores / row_total).astype(jnp.bfloat16)
        attended_head = jnp.einsum(
            "mqk,mkd->mqd", soft_weights, all_values, preferred_element_type=jnp.float32
        )
        return (attended_head, row_top[..., 0] + jnp.log(row_total[..., 0]))

    attended, log_total = lax.map(attend, by_head)
    mixed_heads = (
        jnp.transpose(attended, (1, 2, 0, 3)).reshape(row_count, HEADS * HEAD).astype(jnp.bfloat16)
    )
    middle = rows_float + jnp.dot(mixed_heads, full_out, preferred_element_type=jnp.float32)
    normal_two = normed(middle, gain_two).astype(jnp.bfloat16)
    gate_rows = jnp.dot(normal_two, full_gate, preferred_element_type=jnp.float32)
    upward = jnp.dot(normal_two, full_up, preferred_element_type=jnp.float32)
    activated = gelu_tanh(gate_rows)
    hidden = (activated * upward).astype(jnp.bfloat16)
    result = (middle + jnp.dot(hidden, full_down, preferred_element_type=jnp.float32)).astype(
        jnp.bfloat16
    )
    grad_float = grad_in.astype(jnp.float32)
    grad_down = contract_rows(hidden, grad_in)
    grad_hidden = against(grad_in, full_down)
    gelu_value, gelu_pull = jax.vjp(gelu_tanh, gate_rows)
    grad_gate_rows = gelu_pull(grad_hidden * upward)[0].astype(jnp.bfloat16)
    grad_up_rows = (grad_hidden * activated).astype(jnp.bfloat16)
    grad_gate = contract_rows(normal_two, grad_gate_rows)
    grad_up = contract_rows(normal_two, grad_up_rows)
    grad_two = against(grad_gate_rows, full_gate) + against(grad_up_rows, full_up)
    norm_value, norm_pull = jax.vjp(normed, middle, gain_two)
    grad_middle_norm, gain_two_grad = norm_pull(grad_two)
    grad_middle = grad_float + grad_middle_norm
    grad_middle_low = grad_middle.astype(jnp.bfloat16)
    grad_out = contract_rows(mixed_heads, grad_middle_low)
    grad_mixed = against(grad_middle_low, full_out).astype(jnp.bfloat16)
    grad_by_head = jnp.transpose(grad_mixed.reshape(MICRO, micro_rows, HEADS, HEAD), (2, 0, 1, 3))

    def attend_back(running, pieces):
        key_total, value_total = running
        query_head, grad_head, total_head = pieces
        scores = (
            jnp.einsum("mqd,mkd->mqk", query_head, all_keys, preferred_element_type=jnp.float32)
            * score_scale
        )
        soft_weights = jnp.where(allowed, jnp.exp(scores - total_head[..., None]), 0.0)
        value_total = value_total + jnp.einsum(
            "mqk,mqd->mkd",
            soft_weights.astype(jnp.bfloat16),
            grad_head,
            preferred_element_type=jnp.float32,
        )
        grad_soft = jnp.einsum(
            "mqd,mkd->mqk", grad_head, all_values, preferred_element_type=jnp.float32
        )
        row_delta = jnp.sum(grad_soft * soft_weights, axis=2, keepdims=True)
        grad_scores = (soft_weights * (grad_soft - row_delta)).astype(jnp.bfloat16)
        grad_query_head = (
            jnp.einsum("mqk,mkd->mqd", grad_scores, all_keys, preferred_element_type=jnp.float32)
            * score_scale
        )
        key_total = (
            key_total
            + jnp.einsum(
                "mqk,mqd->mkd", grad_scores, query_head, preferred_element_type=jnp.float32
            )
            * score_scale
        )
        return ((key_total, value_total), grad_query_head)

    zero_block = jnp.zeros((MICRO, (reach_steps + 1) * micro_rows, HEAD), jnp.float32)
    totals, grad_query_heads = lax.scan(
        attend_back, (zero_block, zero_block), (by_head, grad_by_head, log_total)
    )
    key_total, value_total = totals

    def piece_of(total, distance_step):
        begin_row = (reach_steps - distance_step) * micro_rows
        return total[:, begin_row : begin_row + micro_rows].reshape(row_count, HEAD)

    own_key = piece_of(key_total, 0)
    own_value = piece_of(value_total, 0)
    for distance_step in range(1, reach_steps + 1):
        returned_pair = (
            passed_along(
                piece_of(key_total, distance_step).astype(jnp.bfloat16),
                ("dp", "fsdp"),
                -distance_step,
            ).astype(jnp.float32),
            passed_along(
                piece_of(value_total, distance_step).astype(jnp.bfloat16),
                ("dp", "fsdp"),
                -distance_step,
            ).astype(jnp.float32),
        )
        own_key = own_key + returned_pair[0]
        own_value = own_value + returned_pair[1]
    grad_value_rows = own_value.astype(jnp.bfloat16)
    grad_query_rot = jnp.transpose(grad_query_heads, (1, 2, 0, 3)).reshape(row_count, HEADS, HEAD)
    grad_query_raw = (
        rotate(grad_query_rot, cosine[:, None, :], -sine_table[:, None, :])
        .reshape(row_count, HEADS * HEAD)
        .astype(jnp.bfloat16)
    )
    grad_key_raw = rotate(own_key, cosine, -sine_table).astype(jnp.bfloat16)
    grad_query = contract_rows(normal_one, grad_query_raw)
    grad_key = contract_rows(normal_one, grad_key_raw)
    grad_value = contract_rows(normal_one, grad_value_rows)
    grad_one = (
        against(grad_query_raw, full_query)
        + against(grad_key_raw, full_key)
        + against(grad_value_rows, full_value)
    )
    first_value, first_pull = jax.vjp(normed, rows_float, gain_one)
    grad_rows_norm, gain_one_grad = first_pull(grad_one)
    grad_rows = (grad_middle + grad_rows_norm).astype(jnp.bfloat16)
    grad_gains = jnp.stack([gain_one_grad, gain_two_grad])
    sectioned = (
        lax.psum_scatter(
            grad_query.astype(jnp.bfloat16), "fsdp", scatter_dimension=1, tiled=True
        ).astype(jnp.float32),
        lax.psum_scatter(
            grad_key.astype(jnp.bfloat16), "fsdp", scatter_dimension=1, tiled=True
        ).astype(jnp.float32),
        lax.psum_scatter(
            grad_value.astype(jnp.bfloat16), "fsdp", scatter_dimension=1, tiled=True
        ).astype(jnp.float32),
        lax.psum_scatter(
            grad_out.astype(jnp.bfloat16), "fsdp", scatter_dimension=0, tiled=True
        ).astype(jnp.float32),
        lax.psum_scatter(
            grad_gate.astype(jnp.bfloat16), "fsdp", scatter_dimension=1, tiled=True
        ).astype(jnp.float32),
        lax.psum_scatter(
            grad_up.astype(jnp.bfloat16), "fsdp", scatter_dimension=1, tiled=True
        ).astype(jnp.float32),
        lax.psum_scatter(
            grad_down.astype(jnp.bfloat16), "fsdp", scatter_dimension=0, tiled=True
        ).astype(jnp.float32),
        lax.psum_scatter(
            grad_gains.astype(jnp.bfloat16), "fsdp", scatter_dimension=0, tiled=True
        ).astype(jnp.float32),
    )
    reduced = (
        lax.psum_scatter(sectioned[0], "dp", scatter_dimension=0, tiled=True),
        lax.psum_scatter(sectioned[1], "dp", scatter_dimension=0, tiled=True),
        lax.psum_scatter(sectioned[2], "dp", scatter_dimension=0, tiled=True),
        lax.psum_scatter(sectioned[3], "dp", scatter_dimension=1, tiled=True),
        lax.psum_scatter(sectioned[4], "dp", scatter_dimension=0, tiled=True),
        lax.psum_scatter(sectioned[5], "dp", scatter_dimension=0, tiled=True),
        lax.psum_scatter(sectioned[6], "dp", scatter_dimension=1, tiled=True),
        lax.psum_scatter(sectioned[7], "dp", scatter_dimension=1, tiled=True),
    )
    returned = (
        lax.all_to_all(
            result[bucket_order].reshape(peer_count, per_peer, model_width),
            "dp",
            split_axis=0,
            concat_axis=0,
            tiled=True,
        ),
        lax.all_to_all(
            grad_rows[bucket_order].reshape(peer_count, per_peer, model_width),
            "dp",
            split_axis=0,
            concat_axis=0,
            tiled=True,
        ),
    )
    output = jnp.zeros_like(tokens).at[picked].set(returned[0].reshape(row_count, model_width))
    input_grad = jnp.zeros_like(tokens).at[picked].set(returned[1].reshape(row_count, model_width))
    return (
        output,
        input_grad,
        reduced[0],
        reduced[1],
        reduced[2],
        reduced[3],
        reduced[4],
        reduced[5],
        reduced[6],
        reduced[7],
    )


MESH = pl.DeviceIdType.MESH
BF16 = jnp.bfloat16
F32 = jnp.float32
PLANE = 4
ANY = pl.BlockSpec(memory_space=pl.ANY)
VM = pl.BlockSpec(memory_space=pltpu.VMEM)
SM = pl.BlockSpec(memory_space=pltpu.SMEM)


def mm(left, right):
    return jnp.dot(left, right, preferred_element_type=F32)


def mm_nt(left, right):
    return lax.dot_general(left, right, (((1,), (1,)), ((), ())), preferred_element_type=F32)


def mm_tn(left, right):
    return lax.dot_general(left, right, (((0,), (0,)), ((), ())), preferred_element_type=F32)


class Place:
    def __init__(self, chips):
        self.chips = chips
        self.groups = chips // PLANE
        self.d = lax.axis_index("dp")
        self.f = lax.axis_index("fsdp")
        self.other = 1 - self.f
        self.g = self.d // PLANE
        self.p = self.d % PLANE
        self.x = self.p % 2
        self.y = self.p // 2

    def plane_pos(self, j):
        return ((self.y + j // 2) % 2) * 2 + (self.x + j % 2) % 2

    def plane_chip(self, j):
        return self.g * PLANE + self.plane_pos(j)

    def column_chip(self, k):
        return ((self.g + k) % self.groups) * PLANE + self.p


def greet_all(place):
    barrier = pltpu.get_barrier_semaphore()
    total = place.chips * 2
    me = place.d * 2 + place.f

    def signal(k, carry):
        to = (me + k) % total
        pl.semaphore_signal(barrier, inc=1, device_id=(to // 2, to % 2), device_id_type=MESH)
        return carry

    lax.fori_loop(1, total, signal, 0)
    pl.semaphore_wait(barrier, total - 1)


class Sent:
    def __init__(self):
        self.copies = []

    def remote(self, src, dst, send_sem, recv_sem, device):
        copy = pltpu.make_async_remote_copy(
            src_ref=src,
            dst_ref=dst,
            send_sem=send_sem,
            recv_sem=recv_sem,
            device_id=device,
            device_id_type=MESH,
        )
        copy.start()
        self.copies.append(copy)

    def finish(self):
        for copy in self.copies:
            copy.wait_send()
        self.copies = []


def arrived(ref, sem):
    pltpu.make_async_copy(ref, ref, sem).wait()


def iota(shape, dim):
    return lax.broadcasted_iota(jnp.int32, shape, dim)


def fold(values, combine):
    parts = values.reshape(values.shape[0] // 8, 8, values.shape[1])
    total = parts[0]
    for i in range(1, parts.shape[0]):
        total = combine(total, parts[i])
    return total


def gain_spread(width, share):
    column = iota((128, width), 1).astype(F32)
    inside = column - jnp.floor((column + 0.5) * (1.0 / share)) * share
    row = iota((128, width), 0).astype(F32)
    return (inside == row).astype(BF16)


def own_stretch(chips, width, share):
    row = iota((chips, width), 0)
    column = iota((chips, width), 1)
    return (column >= row * share) & (column < row * share + share)


def gain_row(kvg_ref, which, chips, width, share):
    block = kvg_ref[which, :, share : share + 16, :].astype(F32)[:, 0, :].astype(BF16)
    spread = mm(block, gain_spread(width, share))
    return jnp.sum(jnp.where(own_stretch(chips, width, share), spread, 0.0), axis=0, keepdims=True)


def rms_scale(values):
    return lax.rsqrt(jnp.mean(values * values, axis=-1, keepdims=True) + EPSILON)


def turned(values, cosine, sine):
    return values * cosine + pltpu.roll(values, HEAD // 2, 1) * sine


def halves_in(first, second):
    front = iota(first.shape, 1) < HEAD // 2
    return (
        jnp.where(front, first, pltpu.roll(second, HEAD // 2, 1)),
        jnp.where(front, pltpu.roll(first, HEAD // 2, 1), second),
    )


class PlaneSpread:
    def __init__(self, place, blocks, send_sems, recv_sems):
        self.place, self.blocks, self.send_sems, self.recv_sems = place, blocks, send_sems, recv_sems
        self.half = blocks.shape[1] // 2
        self.by_x, self.by_y, self.far = (place.plane_pos(j) for j in range(1, PLANE))

    def piece(self, pos, side):
        return self.blocks.at[pos, pl.ds(side * self.half, self.half)]

    def copy(self, slot):
        place = self.place
        pos, side, over_x = (
            (place.p, 0, 1),
            (place.p, 1, 0),
            (place.p, 1, 1),
            (place.p, 0, 0),
            (self.by_x, 0, 0),
            (self.by_y, 1, 1),
        )[slot]
        return pltpu.make_async_remote_copy(
            src_ref=self.piece(pos, side),
            dst_ref=self.piece(pos, side),
            send_sem=self.send_sems.at[slot],
            recv_sem=self.recv_sems.at[pos, side],
            device_id=(place.plane_chip(1 if over_x else 2), place.f),
            device_id_type=MESH,
        )

    def start(self):
        for slot in range(4):
            self.copy(slot).start()

    def pass_on(self):
        for slot, pos, side in ((4, self.by_x, 0), (5, self.by_y, 1)):
            arrived(self.piece(pos, side), self.recv_sems.at[pos, side])
            self.copy(slot).start()

    def wait(self, blocks=(1, 2, 3)):
        left = ((1, self.by_x, 1), (2, self.by_y, 0), (3, self.far, 0), (3, self.far, 1))
        for block, pos, side in left:
            if block in blocks:
                arrived(self.piece(pos, side), self.recv_sems.at[pos, side])

    def finish(self):
        for slot in range(6):
            self.copy(slot).wait_send()


class Chain:
    def __init__(self, place, piece, hops, up_sems, down_sems, recv_sems):
        self.place, self.piece, self.hops = place, piece, hops
        self.up_sems, self.down_sems, self.recv_sems = up_sems, down_sems, recv_sems
        self.has_up = place.g + 1 < place.groups
        self.has_down = place.g >= 1

    def hop(self, a, origin, up):
        place = self.place
        ref = self.piece(a, origin)
        to = place.d + PLANE if up else place.d - PLANE
        sems = self.up_sems if up else self.down_sems
        return pltpu.make_async_remote_copy(
            src_ref=ref,
            dst_ref=ref,
            send_sem=sems.at[a, origin],
            recv_sem=self.recv_sems.at[a, origin],
            device_id=(to, place.f),
            device_id_type=MESH,
        )

    def start(self, a):
        def one(up):
            self.hop(a, self.place.g, up).start()

        pl.when(self.has_up)(functools.partial(one, True))
        pl.when(self.has_down)(functools.partial(one, False))

    def step(self, k, arrays, then):
        place = self.place

        def from_below():
            origin = place.g - k
            for a in arrays:
                arrived(self.piece(a, origin), self.recv_sems.at[a, origin])

                if k < self.hops[a]:
                    pl.when(self.has_up)(self.hop(a, origin, True).start)
                then(a, origin)

        def from_above():
            origin = place.g + k
            for a in arrays:
                arrived(self.piece(a, origin), self.recv_sems.at[a, origin])

                if k < self.hops[a]:
                    pl.when(self.has_down)(self.hop(a, origin, False).start)
                then(a, origin)

        pl.when(place.g >= k)(from_below)
        pl.when(place.g + k < place.groups)(from_above)

    def finish(self):
        place = self.place
        for a, hops in enumerate(self.hops):
            for k in range(hops):

                @pl.when((place.g >= k) & self.has_up)
                def _():
                    self.hop(a, place.g - k, True).wait_send()

                @pl.when((place.g + k < place.groups) & self.has_down)
                def _():
                    self.hop(a, place.g + k, False).wait_send()


def forward_kernel(
    chips,
    reach,
    first_ref,
    deal_ref,
    key_ref,
    value_ref,
    gains_ref,
    cos_ref,
    sin_ref,
    tokens_ref,
    cot_ref,
    wq_ref,
    wot_ref,
    gate_ref,
    up_ref,
    down_ref,
    full_three,
    out_full_q,
    out_full_ot,
    out_full_kvg,
    rows_out,
    pg_all,
    take_ref,
    place_ref,
    out_n1_ref,
    out_qs_ref,
    out_kv_ref,
    out_probs_ref,
    out_mixed_ref,
    middle_ref,
    n2_ref,
    gain_two_ref,
    square_ref,
    kvg_ref,
    deal_all,
    give,
    got,
    bias_ref,
    branch_out,
    branch_in,
    scores_ref,
    deal_send,
    deal_recv,
    row_send,
    row_recv,
    attn_up,
    attn_down,
    attn_recv,
    fan_send,
    fan_recv,
    kvg_sems,
    stage_send,
    stage_recv,
    three_up,
    three_down,
    three_recv,
    relay_send,
    relay_recv,
    plane_send,
    plane_recv,
    n1_sems,
    kv_send,
    kv_recv,
    branch_sems,
    local_sems,
    full_q,
    full_ot,
    full_kvg,
    n1_ref,
    qs_ref,
    kv_ref,
    probs_ref,
    mixed_ref,
    save_sems,
):
    place = Place(chips)
    d, f, other = place.d, place.f, place.other
    groups = place.groups
    rows, width = tokens_ref.shape
    share = wq_ref.shape[0]
    half = share // 2
    per = rows // chips
    part = gate_ref.shape[1] // 2
    micro = rows // MICRO
    heads = wq_ref.shape[1] // HEAD
    span = (2 * reach + 1) * micro
    sent = Sent()
    greet_all(place)
    saves = []

    def save(src, dst):
        copy = pltpu.make_async_copy(src, dst, save_sems.at[len(saves)])
        copy.start()
        saves.append(copy)


    deal_all[d] = jnp.broadcast_to(deal_ref[...], (8, rows))
    for k in range(1, chips):
        to = (d + k) % chips
        sent.remote(deal_all.at[d], deal_all.at[d], deal_send.at[k], deal_recv.at[d], (to, f))

    key_columns = key_ref.shape[0]
    square_ref[...] = jnp.zeros_like(square_ref)
    square_ref[0:key_columns, 0:share] = key_ref[...].astype(F32)
    square_ref[key_columns : 2 * key_columns, 0:share] = value_ref[...].astype(F32)
    kvg_ref[0:share] = square_ref[...].T[0:share].astype(BF16)
    square_ref[0:1, 0:share] = gains_ref[...].astype(F32)
    kvg_ref[share : share + 16] = jnp.where(
        iota((16, HEAD), 0) + iota((16, HEAD), 1) // share == 0, square_ref[0:16], 0.0
    ).astype(BF16)

    def attn_piece(a, s):
        if a == 0:
            return full_kvg.at[f, s]
        band = pl.ds(pl.multiple_of(s * share, 16), share)
        return (full_q if a == 1 else full_ot).at[band]

    own_attn = (kvg_ref, wq_ref, wot_ref)
    copies = [
        pltpu.make_async_copy(own_attn[a], attn_piece(a, d), local_sems.at[a]) for a in range(3)
    ]
    for copy in copies:
        copy.start()
    for copy in copies:
        copy.wait()
    attn = Chain(
        place,
        lambda a, g: attn_piece(a, g * PLANE + place.p),
        (groups - 1,) * 3,
        attn_up,
        attn_down,
        attn_recv,
    )

    def fan(a, g):
        for j in range(1, PLANE if a == 0 else PLANE - 1):
            fan_copy(a, g, j).start()

    def fan_copy(a, g, j):
        s = g * PLANE + place.p
        return pltpu.make_async_remote_copy(
            src_ref=attn_piece(a, s),
            dst_ref=attn_piece(a, s),
            send_sem=fan_send.at[a, g, j],
            recv_sem=fan_recv.at[a, s],
            device_id=(place.plane_chip(j), f),
            device_id_type=MESH,
        )

    def pass_copy(a, g):
        by_x = place.plane_pos(1)
        by_y = place.plane_pos(2)
        even = g % 2 == 0
        s = g * PLANE + jnp.where(even, by_x, by_y)
        to = jnp.where(even, place.plane_chip(2), place.plane_chip(1))
        return pltpu.make_async_remote_copy(
            src_ref=attn_piece(a, s),
            dst_ref=attn_piece(a, s),
            send_sem=fan_send.at[a, g, PLANE - 1],
            recv_sem=fan_recv.at[a, s],
            device_id=(to, f),
            device_id_type=MESH,
        )

    def pass_on(a, g):
        s = g * PLANE + jnp.where(g % 2 == 0, place.plane_pos(1), place.plane_pos(2))
        arrived(attn_piece(a, s), fan_recv.at[a, s])
        pass_copy(a, g).start()

    def pass_all(a):
        pass_on(a, place.g)
        for k in range(1, groups):
            pl.when(place.g >= k)(functools.partial(pass_on, a, place.g - k))
            pl.when(place.g + k < groups)(functools.partial(pass_on, a, place.g + k))

    for a in range(2):
        attn.start(a)
        fan(a, place.g)
    attn.start(2)

    def soon(a, g):
        if a < 2:
            fan(a, g)

    mats = (gate_ref, up_ref, down_ref)

    def stage_src(a, to_x, core):
        return mats[a].at[pl.ds(half * core, half), pl.ds(pl.multiple_of(part * to_x, 128), part)]

    def stage_copy(a, b, core):
        to_x = (place.x + b) % 2
        return pltpu.make_async_remote_copy(
            src_ref=stage_src(a, to_x, core),
            dst_ref=full_three.at[a, d, core],
            send_sem=stage_send.at[a, b, core],
            recv_sem=stage_recv.at[a, place.p],
            device_id=(place.g * PLANE + 2 * f + to_x, core),
            device_id_type=MESH,
        )

    def own_copy(a):
        return pltpu.make_async_copy(
            mats[a].at[pl.ds(pl.multiple_of(half * f, 16), half), pl.ds(pl.multiple_of(part * place.x, 128), part)],
            full_three.at[a, d, f],
            local_sems.at[a],
        )

    def pair_copy(a):
        return pltpu.make_async_remote_copy(
            src_ref=mats[a].at[
                pl.ds(pl.multiple_of(half * other, 16), half),
                pl.ds(pl.multiple_of(part * place.x, 128), part),
            ],
            dst_ref=full_three.at[a, d, other],
            send_sem=stage_send.at[a, 0, 0],
            recv_sem=stage_recv.at[a, place.p],
            device_id=(d, other),
            device_id_type=MESH,
        )

    def stage_start(a):
        for core in range(2):
            stage_copy(a, 1, core).start()

        @pl.when(place.y != f)
        def _():
            for core in range(2):
                stage_copy(a, 0, core).start()

        @pl.when(place.y == f)
        def _():
            own_copy(a).start()
            pair_copy(a).start()

    stage_start(0)

    for k in range(1, chips):
        s = (d + k) % chips
        arrived(deal_all.at[s], deal_recv.at[s])
    chip_bits = (2 * rows).bit_length() - 1
    deals = deal_all[:, 0, :]
    wants = lax.shift_right_logical(deals, chip_bits) == d
    offset = deals & (rows - 1)
    earlier = (iota((rows, rows), 0) < iota((rows, rows), 1)).astype(BF16)
    rank = mm(wants.astype(F32).astype(BF16), earlier)
    for j in range(chips):
        hit = wants[j : j + 1, :] & (rank[j : j + 1, :] == iota((per, rows), 0).astype(F32))
        index = jnp.sum(jnp.where(hit, offset[j : j + 1, :], 0), axis=1, keepdims=True)
        take_ref[j * per : (j + 1) * per, :] = (
            (index == iota((per, rows), 1)).astype(F32).astype(BF16)
        )

    def block(k):
        return pl.ds(pl.multiple_of(k * per, per), per)

    def give_rows(i, source_ref):
        give[i] = mm(take_ref[...], source_ref[...]).astype(BF16)
        got[i, block(d), :] = give[i, block(d), :]

    def send_rows(i):
        for k in range(1, chips):
            to = (d + k) % chips
            sent.remote(
                give.at[i, block(to)],
                got.at[i, block(d)],
                row_send.at[i, k],
                row_recv.at[i, d],
                (to, f),
            )

    def take_rows(i):
        for k in range(1, chips):
            s = (d + k) % chips
            arrived(got.at[i, block(s)], row_recv.at[i, s])
        return mm(place_ref[...], got[i])

    give_rows(0, tokens_ref)
    def column_pass(k, a):
        pl.when(place.g >= k)(functools.partial(pass_on, a, place.g - k))
        pl.when(place.g + k < groups)(functools.partial(pass_on, a, place.g + k))

    attn.step(1, (0, 1, 2), soon)
    pass_on(1, place.g)
    three = Chain(
        place,
        lambda a, g: full_three.at[a, pl.ds(g * PLANE, PLANE), f],
        (groups - 1, groups - 1, 0),
        three_up,
        three_down,
        three_recv,
    )

    def relay_copy(a, g):
        ref = full_three.at[a, pl.ds(g * PLANE, PLANE), f]
        return pltpu.make_async_remote_copy(
            src_ref=ref,
            dst_ref=ref,
            send_sem=relay_send.at[a, g],
            recv_sem=relay_recv.at[a, g],
            device_id=(d, other),
            device_id_type=MESH,
        )

    def relay(a, g):
        relay_copy(a, g).start()

    def three_start(a):
        for j in range(1, PLANE):
            pos = place.plane_pos(j)
            arrived(full_three.at[a, place.g * PLANE + pos, f], stage_recv.at[a, pos])

        @pl.when(place.y == f)
        def _():
            own_copy(a).wait()

        @pl.when(place.y != f)
        def _():
            arrived(full_three.at[a, d, f], stage_recv.at[a, place.p])

        if a < 2:
            three.start(a)
        relay(a, place.g)

    def meanwhile():
        source_row = lax.shift_right_logical(deal_ref[...], chip_bits)
        source_wide = jnp.broadcast_to(source_row.astype(F32), (rows, rows))
        source_col = source_wide.T.astype(jnp.int32)
        same = (source_col == source_row) & (iota((rows, rows), 1) < iota((rows, rows), 0))
        order = jnp.sum(same.astype(F32), axis=1, keepdims=True).astype(jnp.int32)
        where_from = source_col * per + order
        place_ref[...] = (where_from == iota((rows, rows), 1)).astype(F32).astype(BF16)

        def make_bias(hm, carry):
            h, m = hm // 2, hm % 2
            first = first_ref[m]
            query = (2 * d + h) * micro + iota((span, micro), 1)
            key = (2 * d + h - 2 * reach) * micro + iota((span, micro), 0)
            allowed = (
                (jnp.where(query >= first, 1, 0) == jnp.where(key >= first, 1, 0))
                & (key >= 0)
                & (key <= query)
                & (query - key < WINDOW)
            )
            bias_ref[hm] = jnp.where(allowed, 0.0, NEGATIVE)
            return carry

        lax.fori_loop(0, 4, make_bias, 0)

    for k in range(2, groups):
        attn.step(k, (0, 1, 2), soon)
        column_pass(k - 1, 1)
        if k == 2:
            send_rows(0)
            three_start(0)
            stage_start(1)
            stage_start(2)
            meanwhile()
    row_values = take_rows(0)
    column_pass(groups - 1, 1)
    rows_out[...] = row_values.astype(BF16)

    def attn_wait(a):
        for g in range(groups):
            if a == 0:
                left = range(1, PLANE)
            else:
                left = (2 - g % 2, 3)
            for j in left:
                s = g * PLANE + place.plane_pos(j)
                arrived(attn_piece(a, s), fan_recv.at[a, s])

    cotangents = PlaneSpread(place, pg_all, plane_send, plane_recv)

    attn_wait(0)
    sent.remote(full_kvg.at[f], full_kvg.at[f], kvg_sems.at[0], kvg_sems.at[1], (d, other))
    arrived(full_kvg.at[other], kvg_sems.at[1])
    save(full_kvg, out_full_kvg)

    gain_one = gain_row(full_kvg, 0, chips, width, share)
    n1_ref[f] = (row_values * rms_scale(row_values) * gain_one).astype(BF16)
    sent.remote(n1_ref.at[f], n1_ref.at[f], n1_sems.at[0], n1_sems.at[1], (d, other))

    kvw = [full_kvg[i, :, 0:share, :].reshape(width, HEAD) for i in range(2)]
    raw = [mm(n1_ref[f], kvw[i]) for i in range(2)]
    key_raw, value_raw = halves_in(raw[0], raw[1])
    for m in range(MICRO):
        hm = 2 * f + m
        band = slice(m * micro, (m + 1) * micro)
        key = turned(key_raw[band], cos_ref[hm], sin_ref[hm])
        kv_ref[m, 2 * reach + f, :, 0:HEAD] = key.astype(BF16)
        kv_ref[m, 2 * reach + f, :, HEAD:] = value_raw[band].astype(BF16)
    own_kv = kv_ref.at[:, 2 * reach + f]

    def kv_copy(j):
        return pltpu.make_async_remote_copy(
            src_ref=own_kv,
            dst_ref=kv_ref.at[:, 2 * reach + f - 2 * j],
            send_sem=kv_send.at[j, 0],
            recv_sem=kv_recv.at[2 * reach + f - 2 * j],
            device_id=(d + j, f),
            device_id_type=MESH,
        )

    def kv_pass(j):
        slot = 2 * reach + f - 2 * j
        return pltpu.make_async_remote_copy(
            src_ref=kv_ref.at[:, slot],
            dst_ref=kv_ref.at[:, slot],
            send_sem=kv_send.at[j, 1],
            recv_sem=kv_recv.at[slot],
            device_id=(d, other),
            device_id_type=MESH,
        )

    sent.remote(own_kv, own_kv, kv_send.at[0, 0], kv_recv.at[2 * reach + f], (d, other))
    for j in range(reach, 0, -1):
        pl.when(d + j < chips)(kv_copy(j).start)
    for j in range(1, reach + 1):

        @pl.when(d - j < 0)
        def _():
            for core in range(2):
                kv_ref[:, 2 * reach - 2 * j + core] = jnp.zeros((MICRO, micro, 2 * HEAD), BF16)

    give_rows(1, cot_ref)
    send_rows(1)
    for g in range(groups):
        fan(2, g)
    three_start(1)

    def project(h):
        raw_q = mm(n1_ref[h], full_q[...])
        for m in range(MICRO):
            hm = 2 * h + m
            cosine, sine = cos_ref[hm], sin_ref[hm]
            for i in range(heads):
                one = raw_q[m * micro : (m + 1) * micro, i * HEAD : (i + 1) * HEAD]
                qs_ref[hm, i * micro : (i + 1) * micro, :] = turned(one, cosine, sine).astype(BF16)

    attn_wait(1)
    save(full_q, out_full_q)
    project(f)
    arrived(n1_ref.at[other], n1_sems.at[1])
    project(other)
    save(n1_ref, out_n1_ref)
    save(qs_ref, out_qs_ref)
    three.step(1, (0,), relay)

    for j in range(1, reach + 1):

        @pl.when(d - j >= 0)
        def _():
            slot = 2 * reach - 2 * j + f
            arrived(kv_ref.at[:, slot], kv_recv.at[slot])
            kv_pass(j).start()

    arrived(kv_ref.at[:, 2 * reach + other], kv_recv.at[2 * reach + other])
    for j in range(1, reach + 1):

        @pl.when(d - j >= 0)
        def _():
            slot = 2 * reach - 2 * j + other
            arrived(kv_ref.at[:, slot], kv_recv.at[slot])

    score_scale = HEAD ** (-0.5)
    chunks = [slice(i, i + 64) for i in range(0, span, 64)]

    def attend(hm):
        h, m = hm // 2, hm % 2
        keys = kv_ref[m, h : h + 2 * reach + 1, :, 0:HEAD].reshape(span, HEAD)
        values_t = kv_ref[m, h : h + 2 * reach + 1, :, HEAD:].reshape(span, HEAD).T

        def pair_step(pair, carry):
            start = pl.multiple_of(pair * 2 * micro, 2 * micro)
            band = pl.ds(start, 2 * micro)
            scores_ref[...] = mm_nt(keys, qs_ref[hm, band, :])
            top = jnp.full((8, 2 * micro), NEGATIVE, F32)
            for at in chunks:
                bias = bias_ref[hm, at, :]
                scores = scores_ref[at, :] * score_scale + jnp.concatenate([bias, bias], axis=1)
                scores_ref[at, :] = scores
                top = jnp.maximum(top, fold(scores, jnp.maximum))
            top = jnp.max(top, axis=0, keepdims=True)
            total = jnp.zeros((8, 2 * micro), F32)
            for at in chunks:
                exp_scores = jnp.exp(scores_ref[at, :] - top)
                scores_ref[at, :] = exp_scores
                total = total + fold(exp_scores, jnp.add)
            share_of = 1.0 / jnp.sum(total, axis=0, keepdims=True)
            for at in chunks:
                probs_ref[hm, at, band] = (scores_ref[at, :] * share_of).astype(BF16)
            out_t = mm(values_t, probs_ref[hm, :, band])
            mixed_ref[hm, :, band] = jnp.concatenate(
                [out_t[:, i * micro : (i + 1) * micro].T for i in range(2)], axis=1
            ).astype(BF16)
            return carry

        lax.fori_loop(0, heads // 2, pair_step, 0)

    save(kv_ref, out_kv_ref)
    attend(0)
    save(probs_ref.at[0], out_probs_ref.at[0])
    three.step(1, (1,), relay)
    attend(1)
    save(probs_ref.at[1], out_probs_ref.at[1])
    pass_all(2)
    pg_all[place.p] = take_rows(1).astype(BF16)
    cotangents.start()
    attend(2)
    save(probs_ref.at[2], out_probs_ref.at[2])
    three.step(2, (0,), relay)
    attend(3)
    save(probs_ref.at[3], out_probs_ref.at[3])

    def branch(h):
        return mm_nt(mixed_ref[pl.ds(2 * h, 2)].reshape(rows, heads * HEAD), full_ot[...])

    save(mixed_ref, out_mixed_ref)
    attn_wait(2)
    save(full_ot, out_full_ot)
    branch_out[...] = branch(other).astype(BF16)
    sent.remote(branch_out, branch_in, branch_sems.at[0], branch_sems.at[1], (d, other))
    own = branch(f)
    cotangents.pass_on()
    arrived(branch_in, branch_sems.at[1])
    middle = rows_out[...].astype(F32) + own + branch_in[...].astype(F32)
    middle_ref[...] = middle
    gain_two = gain_row(full_kvg, 1, chips, width, share)
    gain_two_ref[...] = gain_two
    n2_ref[...] = (middle * rms_scale(middle) * gain_two).astype(BF16)
    three.step(2, (1,), relay)
    three_start(2)
    for k in range(3, groups):
        three.step(k, (0, 1), relay)

    def relayed(a, k, use):
        pl.when(place.g >= k)(functools.partial(use, a, place.g - k))
        if k > 0:
            pl.when(place.g + k < groups)(functools.partial(use, a, place.g + k))

    def relay_wait(a, g):
        arrived(full_three.at[a, pl.ds(g * PLANE, PLANE), other], relay_recv.at[a, g])

    def relay_sent(a, g):
        relay_copy(a, g).wait_send()

    for a in range(3):
        for k in range(groups if a < 2 else 1):
            relayed(a, k, relay_wait)
            relayed(a, k, relay_sent)
    cotangents.wait()
    cotangents.finish()

    attn.finish()
    three.finish()
    for g in range(groups):
        for a in range(3):
            for j in range(1, PLANE if a == 0 else PLANE - 1):
                fan_copy(a, g, j).wait_send()
            if a > 0:
                pass_copy(a, g).wait_send()
    for a in range(3):
        for core in range(2):
            stage_copy(a, 1, core).wait_send()

        @pl.when(place.y != f)
        def _():
            for core in range(2):
                stage_copy(a, 0, core).wait_send()

        @pl.when(place.y == f)
        def _():
            pair_copy(a).wait_send()

    for j in range(1, reach + 1):
        pl.when(d + j < chips)(kv_copy(j).wait_send)
        pl.when(d - j >= 0)(kv_pass(j).wait_send)

    for copy in saves:
        copy.wait()
    sent.finish()


def forward(
    chips, reach, first_len, deal, key_t, value_t, gains, cosine, sine, tokens, cotangent, wq, wot, gate, up, down
):
    rows, width = tokens.shape
    share = wq.shape[0]
    groups = chips // PLANE
    part = gate.shape[1] // 2
    micro = rows // MICRO
    heads = wq.shape[1] // HEAD
    slots = 2 * reach + 2
    span = (2 * reach + 1) * micro
    dma = pltpu.SemaphoreType.DMA
    shape = jax.ShapeDtypeStruct
    small = (share + 16, HEAD)
    return pl.pallas_call(
        functools.partial(forward_kernel, chips, reach),
        out_shape=(
            shape((3, chips, 2, share // 2, part), BF16),
            shape((width, wq.shape[1]), BF16),
            shape((width, wq.shape[1]), BF16),
            shape((2, chips) + small, BF16),
            shape((rows, width), BF16),
            shape((PLANE, rows, width), BF16),
            shape((rows, rows), BF16),
            shape((rows, rows), BF16),
            shape((2, rows, width), BF16),
            shape((4, heads * micro, HEAD), BF16),
            shape((MICRO, slots, micro, 2 * HEAD), BF16),
            shape((4, span, heads * micro), BF16),
            shape((4, micro, heads * HEAD), BF16),
            shape((rows, width), F32),
            shape((rows, width), BF16),
            shape((1, width), F32),
        ),
        in_specs=[SM] + [VM] * 8 + [ANY] * 5,
        out_specs=(ANY,) * 4 + (VM,) * 4 + (ANY,) * 5 + (VM,) * 3,
        scratch_shapes=[
            pltpu.VMEM((HEAD, HEAD), F32),
            pltpu.VMEM(small, BF16),
            pltpu.VMEM((chips, 8, rows), jnp.int32),
            pltpu.VMEM((2, rows, width), BF16),
            pltpu.VMEM((2, rows, width), BF16),
            pltpu.VMEM((4, span, micro), F32),
            pltpu.VMEM((rows, width), BF16),
            pltpu.VMEM((rows, width), BF16),
            pltpu.VMEM((span, 2 * micro), F32),
            dma((chips,)),
            dma((chips,)),
            dma((2, chips)),
            dma((2, chips)),
            dma((3, groups)),
            dma((3, groups)),
            dma((3, groups)),
            dma((3, groups, PLANE)),
            dma((3, chips)),
            dma((2,)),
            dma((3, 2, 2)),
            dma((3, PLANE)),
            dma((3, groups)),
            dma((3, groups)),
            dma((3, groups)),
            dma((3, groups)),
            dma((3, groups)),
            dma((6,)),
            dma((PLANE, 2)),
            dma((2,)),
            dma((reach + 1, 2)),
            dma((slots,)),
            dma((2,)),
            dma((3,)),
            pltpu.VMEM((width, wq.shape[1]), BF16),
            pltpu.VMEM((width, wq.shape[1]), BF16),
            pltpu.VMEM((2, chips) + small, BF16),
            pltpu.VMEM((2, rows, width), BF16),
            pltpu.VMEM((4, heads * micro, HEAD), BF16),
            pltpu.VMEM((MICRO, slots, micro, 2 * HEAD), BF16),
            pltpu.VMEM((4, span, heads * micro), BF16),
            pltpu.VMEM((4, micro, heads * HEAD), BF16),
            dma((16,)),
        ],
        compiler_params=pltpu.CompilerParams(
            collective_id=0, has_side_effects=True, vmem_limit_bytes=VMEM_ASK
        ),
        name="gather_and_attention",
    )(
        first_len, deal.reshape(1, rows), key_t, value_t, gains, cosine, sine, tokens, cotangent, wq, wot, gate, up, down
    )


def norm_back(values, gain, grad):
    scale = rms_scale(values)
    unit = values * scale
    lifted = grad * gain
    gain_grad = jnp.sum(grad * unit, axis=0, keepdims=True)
    back = scale * (lifted - unit * jnp.mean(lifted * unit, axis=-1, keepdims=True))
    return back, gain_grad


class ChainSum:
    def __init__(
        self, place, value, got, last, give, up_sems, down_sems, recv_sems, last_sems, early=None
    ):
        self.place, self.value, self.got, self.last, self.give = place, value, got, last, give
        self.early = early or {}
        self.top = place.groups - 1
        self.up_sems, self.down_sems = up_sems, down_sems
        self.recv_sems, self.last_sems = recv_sems, last_sems
        self.has_up = place.g + 1 < place.groups
        self.has_down = place.g >= 1

    def hop(self, a, g, k, up):
        to_last = k == 1 and not up
        place = self.place
        return pltpu.make_async_remote_copy(
            src_ref=self.give(a, g),
            dst_ref=self.last(a) if to_last else self.got(a, g),
            send_sem=(self.up_sems if up else self.down_sems).at[a, g],
            recv_sem=self.last_sems.at[a] if to_last else self.recv_sems.at[a, g],
            device_id=(place.d + PLANE if up else place.d - PLANE, place.f),
            device_id_type=MESH,
        )

    def step(self, a, k):
        place = self.place

        def toward(up):
            g = place.g + k if up else place.g - k
            total = self.value(a, k, up)
            from_behind = self.has_down if up else self.has_up

            @pl.when(from_behind)
            def _():
                if a in self.early and k == self.top - 1:
                    behind = self.early[a]
                else:
                    behind = self.got(a, g)
                    arrived(behind, self.recv_sems.at[a, g])
                self.give(a, g)[...] = (total + behind[...].astype(F32)).astype(BF16)

            @pl.when(jnp.logical_not(from_behind))
            def _():
                self.give(a, g)[...] = total.astype(BF16)

            self.hop(a, g, k, up).start()

        pl.when(place.g + k < place.groups)(functools.partial(toward, True))
        pl.when(place.g >= k)(functools.partial(toward, False))

    def final(self, a):
        place = self.place
        got, last = self.got(a, place.g), self.last(a)

        @pl.when(self.has_down)
        def _():
            arrived(got, self.recv_sems.at[a, place.g])

        @pl.when(jnp.logical_not(self.has_down))
        def _():
            got[...] = jnp.zeros(got.shape, BF16)

        @pl.when(self.has_up)
        def _():
            arrived(last, self.last_sems.at[a])

        @pl.when(jnp.logical_not(self.has_up))
        def _():
            last[...] = jnp.zeros(last.shape, BF16)

        return self.value(a, 0, True) + got[...].astype(F32) + last[...].astype(F32)

    def finish(self, count):
        place = self.place
        for a in range(count):
            for k in range(1, self.top if a in self.early else self.top + 1):

                @pl.when(place.g + k < place.groups)
                def _():
                    self.hop(a, place.g + k, k, True).wait_send()

                @pl.when(place.g >= k)
                def _():
                    self.hop(a, place.g - k, k, False).wait_send()


class PlaneReduce:
    def __init__(self, place, give, got, relay, send_sems, recv_sems, relay_sems):
        self.place, self.give, self.got, self.relay = place, give, got, relay
        self.send_sems, self.recv_sems, self.relay_sems = send_sems, recv_sems, relay_sems
        self.half = give.shape[1] // 2

    def copy(self, which):
        place = self.place
        slot, side, over_x = ((2, 0, 1), (2, 1, 0), (0, 0, 1), (1, 1, 0), (0, 1, 1), (1, 0, 0))[which]
        band = pl.ds(side * self.half, self.half)
        if which < 2:
            dst, recv = self.relay.at[side], self.relay_sems.at[side]
        else:
            dst, recv = self.got.at[slot, band], self.recv_sems.at[slot, side]
        return pltpu.make_async_remote_copy(
            src_ref=self.give.at[slot, band] if which < 4 else self.relay.at[side],
            dst_ref=dst,
            send_sem=self.send_sems.at[which],
            recv_sem=recv,
            device_id=(place.plane_chip(1 if over_x else 2), place.f),
            device_id_type=MESH,
        )

    def start(self, turn):
        @pl.when(turn == 0)
        def _():
            self.copy(0).start()
            self.copy(1).start()

        @pl.when(turn == 1)
        def _():
            self.copy(2).start()

        @pl.when(turn == 2)
        def _():
            self.copy(3).start()

    def pass_on(self):
        for side, slot, which in ((0, 1, 5), (1, 0, 4)):
            arrived(self.relay.at[side], self.relay_sems.at[side])
            mine = self.give[slot, side * self.half : (side + 1) * self.half]
            self.relay[side] = (mine.astype(F32) + self.relay[side].astype(F32)).astype(BF16)
            self.copy(which).start()

    def total(self):
        for slot in range(2):
            for side in range(2):
                band = pl.ds(side * self.half, self.half)
                arrived(self.got.at[slot, band], self.recv_sems.at[slot, side])
        return self.got[0].astype(F32) + self.got[1].astype(F32)

    def finish(self):
        for which in range(6):
            self.copy(which).wait_send()


def mlp_kernel(
    chips,
    n2_own,
    middle_ref,
    pg_ref,
    gain_ref,
    three_hbm,
    out_total,
    out_give,
    two_ref,
    gain_grad_ref,
    half_ref,
    early_ref,
    down_sum,
    three_ref,
    hidden_ref,
    gate_rows_ref,
    up_rows_ref,
    two_give,
    two_got,
    two_relay,
    pair_got,
    down_grad,
    down_half,
    down_got,
    down_last,
    gate_ref,
    upward_ref,
    n2_all,
    n2_send,
    n2_recv,
    load_sems,
    rest_up,
    rest_down,
    rest_recv,
    rest_relay,
    rest_relayed,
    two_send,
    two_recv,
    two_relays,
    pair_send,
    pair_recv,
    down_up,
    down_down,
    down_recv,
    down_last_sems,
    early_send,
    early_recv,
):
    place = Place(chips)
    d, f, other = place.d, place.f, place.other
    groups = place.groups
    rows, width = middle_ref.shape
    wide = PLANE * rows
    part = three_ref.shape[-1]
    plane_width = width // groups
    loads = [
        pltpu.make_async_copy(three_hbm.at[a], three_ref.at[a], load_sems.at[0, a])
        for a in range(2)
    ]
    for load in loads:
        load.start()

    def planes(ref, g):
        return ref.at[2, pl.ds(g * PLANE, PLANE)]

    down_load = pltpu.make_async_copy(
        planes(three_hbm, place.g), planes(three_ref, place.g), load_sems.at[0, 2]
    )
    down_load.start()
    greet_all(place)

    def rest_hop(g, up, k):
        src = three_hbm if k == 0 else three_ref
        return pltpu.make_async_remote_copy(
            src_ref=src.at[2, pl.ds(g * PLANE, PLANE), f],
            dst_ref=three_ref.at[2, pl.ds(g * PLANE, PLANE), f],
            send_sem=(rest_up if up else rest_down).at[g],
            recv_sem=rest_recv.at[g],
            device_id=(d + PLANE if up else d - PLANE, f),
            device_id_type=MESH,
        )

    def rest_pass(g):
        ref = three_ref.at[2, pl.ds(g * PLANE, PLANE), f]
        return pltpu.make_async_remote_copy(
            src_ref=ref,
            dst_ref=ref,
            send_sem=rest_relay.at[g],
            recv_sem=rest_relayed.at[g],
            device_id=(d, other),
            device_id_type=MESH,
        )

    has_up, has_down = place.g + 1 < groups, place.g >= 1

    def rest_each(k, use):
        pl.when(place.g >= k)(lambda: use(place.g - k, True, has_up))
        pl.when(place.g + k < groups)(lambda: use(place.g + k, False, has_down))

    def rest_step(k):
        def use(g, up, more):
            arrived(three_ref.at[2, pl.ds(g * PLANE, PLANE), f], rest_recv.at[g])
            if k + 1 < groups:
                pl.when(more)(rest_hop(g, up, k).start)
            rest_pass(g).start()

        rest_each(k, use)

    def rest_hops(k, act):
        if k + 1 < groups:
            up, down = (rest_hop(place.g - k, True, k), rest_hop(place.g + k, False, k))
            pl.when((place.g >= k) & (place.g < groups - 1))(getattr(up, act))
            pl.when((place.g < groups - k) & (place.g >= 1))(getattr(down, act))

    def rest_finish(k):
        def use(g, up, more):
            rest_pass(g).wait_send()
            arrived(three_ref.at[2, pl.ds(g * PLANE, PLANE), other], rest_relayed.at[g])

        rest_hops(k, "wait_send")
        if k > 0:
            rest_each(k, use)

    n2 = PlaneSpread(place, n2_all, n2_send, n2_recv)
    n2_all[place.p] = n2_own[...]
    n2.start()
    rest_hops(0, "start")

    two = PlaneReduce(place, two_give, two_got, two_relay, two_send, two_recv, two_relays)
    curve = 0.7978845608028654
    cubic = 0.044715
    step_width = 2 * HEAD

    def weight(a, band):
        return three_ref[a, :, :, :, band].reshape(width, -1)

    def chunks(count):
        return range(0, count, 32)

    def forward_units(j, band, size):
        pos = place.plane_pos(j)
        x = n2_all[pos]
        gate_ref[:rows, :size] = mm(x, weight(0, band))
        upward_ref[:rows, :size] = mm(x, weight(1, band))
        for i in chunks(rows):
            gate = gate_ref[i : i + 32, :size]
            upward = upward_ref[i : i + 32, :size]
            square = gate * gate
            tanh = jnp.tanh(gate * (curve + (curve * cubic) * square))
            above = 0.5 * (1.0 + tanh)
            activated = gate * above
            slope = above + activated * (1.0 - tanh) * (curve + (3.0 * curve * cubic) * square)
            at = pl.ds(pl.multiple_of(pos * rows + i, 32), 32)
            hidden_ref[at, band] = (activated * upward).astype(BF16)
            gate_rows_ref[at, band] = (upward * slope).astype(BF16)
            up_rows_ref[at, band] = activated.astype(BF16)

    def backward_units(band, size):
        gate_ref[:, :size] = mm(pg_ref[...].reshape(wide, width), weight(2, band))
        for i in chunks(wide):
            at = slice(i, i + 32)
            grad_hidden = gate_ref[at, :size]
            gate_rows_ref[at, band] = (
                grad_hidden * gate_rows_ref[at, band].astype(F32)
            ).astype(BF16)
            up_rows_ref[at, band] = (grad_hidden * up_rows_ref[at, band].astype(F32)).astype(BF16)

    def over_units(body):
        full = part // step_width

        def step(i, carry):
            body(pl.ds(pl.multiple_of(i * step_width, step_width), step_width), step_width)
            return carry

        lax.fori_loop(0, full, step, 0)
        if part % step_width:
            body(pl.ds(full * step_width, part % step_width), part % step_width)

    def at_turn(i):
        return ((i + 2) % 3 + 1) * (1 - i // 3)

    def band_of(pos):
        return pl.ds(pl.multiple_of(pos * rows, rows), rows)

    def whole(a):
        return three_ref[a].reshape(width, part)

    def back_block(i, carry):
        band = band_of(place.plane_pos(at_turn(i)))
        back = mm_nt(gate_rows_ref[band, :], whole(0)) + mm_nt(up_rows_ref[band, :], whole(1))

        @pl.when(i < PLANE - 1)
        def _():
            two_give[(i + 2) % 3] = back.astype(BF16)

        @pl.when(i == PLANE - 1)
        def _():
            two_ref[...] = back

        two.start(i)
        return carry

    def out_block(i, carry):
        piece = mm_nt(hidden_ref[band_of(place.plane_pos(at_turn(i))), :], whole(2))

        @pl.when(i < PLANE - 1)
        def _():
            out_give[(i + 2) % 3] = piece.astype(BF16)

        @pl.when(i == PLANE - 1)
        def _():
            out_total[...] = (middle_ref[...] + piece).astype(BF16)

        return carry

    def grad_at(a, g, core):
        if a == 2:
            return down_grad.at[pl.ds(g * PLANE, PLANE), core]
        return three_ref.at[a, pl.ds(g * PLANE, PLANE), core]

    def pair_copy(a, g):
        return pltpu.make_async_remote_copy(
            src_ref=grad_at(a, g, other),
            dst_ref=pair_got.at[a, g],
            send_sem=pair_send.at[a, g],
            recv_sem=pair_recv.at[a, g],
            device_id=(d, other),
            device_id_type=MESH,
        )

    def weight_grad(a, left, right):
        def step(g, carry):
            at = pl.ds(pl.multiple_of(g * plane_width, 128), plane_width)
            piece = mm_tn(left[:, :, at].reshape(wide, plane_width), right[...]).astype(BF16)
            pieces = piece.reshape(PLANE, 2, plane_width // (2 * PLANE), part)
            for core in range(2):
                grad_at(a, g, core)[...] = pieces[:, core]
            pair_copy(a, g).start()
            return carry

        lax.fori_loop(0, groups, step, 0)

    def pair_sum(a, into):
        def step(g, carry):
            arrived(pair_got.at[a, g], pair_recv.at[a, g])
            into[g] = (grad_at(a, g, f)[...].astype(F32) + pair_got[a, g].astype(F32)).astype(BF16)
            return carry

        lax.fori_loop(0, groups, step, 0)

    down = ChainSum(
        place,
        lambda a, k, up: down_half[place.g + k if up else place.g - k].astype(F32),
        lambda a, g: down_got.at[g],
        lambda a: down_last.at[0],
        lambda a, g: down_got.at[g],
        down_up,
        down_down,
        down_recv,
        down_last_sems,
    )
    loads[0].wait()
    loads[1].wait()
    over_units(functools.partial(forward_units, 0))
    n2.pass_on()
    rest_step(1)
    for j in range(1, PLANE):
        n2.wait((j,))
        over_units(functools.partial(forward_units, j))
        if j == 2:
            for k in range(2, min(3, groups)):
                rest_step(k)
    weight_grad(2, pg_ref, hidden_ref)
    for k in range(3, groups):
        rest_step(k)
    for k in range(groups):
        rest_finish(k)
    down_load.wait()
    over_units(backward_units)
    pair_sum(2, down_half)
    for k in range(groups - 1, 2, -1):
        down.step(0, k)
    lax.fori_loop(0, PLANE, back_block, 0)
    for k in range(min(2, groups - 1), 1, -1):
        down.step(0, k)
    def early_copy(a, bottom):
        return pltpu.make_async_remote_copy(
            src_ref=half_ref.at[a, groups - 1 if bottom else 0],
            dst_ref=early_ref,
            send_sem=early_send.at[a],
            recv_sem=early_recv.at[a],
            device_id=(d + PLANE if bottom else d - PLANE, f),
            device_id_type=MESH,
        )

    def early_start(a):
        pl.when(place.g == 0)(early_copy(a, True).start)
        pl.when(place.g == groups - 1)(early_copy(a, False).start)

    weight_grad(0, n2_all, gate_rows_ref)
    two.pass_on()
    pair_sum(0, half_ref.at[0])
    early_start(0)
    lax.fori_loop(0, PLANE, out_block, 0)
    down.step(0, 1)
    weight_grad(1, n2_all, up_rows_ref)
    pair_sum(1, half_ref.at[1])
    grad_two = two_ref[...] + two.total()
    back, gain_grad_ref[...] = norm_back(middle_ref[...], gain_ref[...], grad_two)
    two_ref[...] = pg_ref[place.p].astype(F32) + back
    down_sum[...] = down.final(0).astype(BF16)
    two.finish()
    n2.finish()
    for a in range(3):
        for g in range(groups):
            pair_copy(a, g).wait_send()
    down.finish(1)
    pl.when(place.g == 0)(early_copy(0, True).wait_send)
    pl.when(place.g == groups - 1)(early_copy(0, False).wait_send)

    @pl.when((place.g == 1) | (place.g == groups - 2))
    def _():
        arrived(early_ref, early_recv.at[0])


def mlp(chips, n2, middle, pg, gain_two, three):
    rows, width = middle.shape
    part = three.shape[-1]
    groups = chips // PLANE
    dma = pltpu.SemaphoreType.DMA
    shape = jax.ShapeDtypeStruct
    wide = PLANE * rows
    column = (groups, PLANE) + three.shape[3:]
    return pl.pallas_call(
        functools.partial(mlp_kernel, chips),
        out_shape=(
            shape((rows, width), BF16),
            shape((PLANE - 1, rows, width), BF16),
            shape((rows, width), F32),
            shape((1, width), F32),
            shape((2,) + column, BF16),
            shape(column[1:], BF16),
            shape(column[1:], BF16),
        ),
        in_specs=[VM] * 4 + [ANY],
        out_specs=(VM,) * 5 + (ANY, VM),
        scratch_shapes=[
            pltpu.VMEM(three.shape, BF16),
            pltpu.VMEM((wide, part), BF16),
            pltpu.VMEM((wide, part), BF16),
            pltpu.VMEM((wide, part), BF16),
        ]
        + [
            pltpu.VMEM((PLANE - 1, rows, width), BF16),
            pltpu.VMEM((2, rows, width), BF16),
            pltpu.VMEM((2, rows // 2, width), BF16),
            pltpu.VMEM((3,) + column, BF16),
            pltpu.VMEM(three.shape[1:], BF16),
            pltpu.VMEM(column, BF16),
            pltpu.VMEM(column, BF16),
            pltpu.VMEM((1,) + column[1:], BF16),
            pltpu.VMEM((wide, 2 * HEAD), F32),
            pltpu.VMEM((wide, 2 * HEAD), F32),
            pltpu.VMEM((PLANE, rows, width), BF16),
            dma((6,)),
            dma((PLANE, 2)),
            dma((2, max(3, groups))),
        ]
        + [dma((groups,))] * 5
        + [
            dma((6,)),
            dma((2, 2)),
            dma((2,)),
            dma((3, groups)),
            dma((3, groups)),
            dma((1, groups)),
            dma((1, groups)),
            dma((1, groups)),
            dma((1,)),
            dma((1,)),
            dma((1,)),
        ],
        compiler_params=pltpu.CompilerParams(
            collective_id=1, has_side_effects=True, vmem_limit_bytes=VMEM_ASK
        ),
        name="mlp_both_ways",
    )(n2, middle, pg, gain_two, three)


def backward_kernel(
    chips,
    reach,
    hbm_out_own,
    out_give,
    down_sum,
    early_ref,
    hbm_rows_ref,
    grad_middle_ref,
    gain_two_grad_ref,
    hbm_n1_ref,
    hbm_qs_ref,
    hbm_kv_ref,
    hbm_mixed_ref,
    hbm_wq_ref,
    wot_ref,
    hbm_kvg_ref,
    cos_ref,
    sin_ref,
    hbm_take_ref,
    place_ref,
    probs_hbm,
    half_hbm,
    three_end,
    q_out,
    ot_out,
    kvg_out,
    output_ref,
    input_grad_ref,
    probs_ref,
    low_ref,
    mixed_rows,
    grad_mixed,
    grad_q,
    kv_total,
    kv_give,
    kv_pair,
    kv_got,
    one_out,
    one_in,
    three_got,
    three_last,
    three_stage,
    heads_ref,
    plane_relay,
    plane_got,
    column_got,
    column_last,
    column_give,
    gkvg_ref,
    gkvg_pair,
    small_got,
    small_give,
    small_column,
    give,
    got,
    probs_sems,
    stage_sems,
    low_sems,
    kv_send,
    kv_recv,
    one_sems,
    three_up,
    three_down,
    three_recv,
    three_last_sems,
    end_send,
    end_recv,
    direct_send,
    relay_send,
    relay_recv,
    plane_recv,
    small_send,
    small_recv,
    column_up,
    column_down,
    column_recv,
    column_last_sems,
    row_send,
    row_recv,
    grad_probs_ref,
    grad_scores_ref,
    out_got,
    out_relay,
    out_send,
    out_recv,
    out_relays,
    mixed_ref,
    qs_ref,
    kv_ref,
    out_own,
    n1_ref,
    wq_ref,
    kvg_ref,
    rows_ref,
    take_ref,
    late_sems,
):
    place = Place(chips)
    d, f, other = place.d, place.f, place.other
    groups = place.groups
    rows, width = grad_middle_ref.shape
    micro = rows // MICRO
    heads = wq_ref.shape[1] // HEAD
    share = width // chips
    half = share // 2
    part = half_hbm.shape[-1]
    per = rows // chips
    span = (2 * reach + 1) * micro
    by_x, by_y, far = (place.plane_pos(j) for j in range(1, PLANE))
    to_x, to_y = place.plane_chip(1), place.plane_chip(2)
    sent = Sent()

    pairs = heads // 2

    def probs_copy(n):
        band = pl.ds(pl.multiple_of((n % pairs) * 2 * micro, 2 * micro), 2 * micro)
        return pltpu.make_async_copy(
            probs_hbm.at[n // pairs, :, band], probs_ref.at[n % 2], probs_sems.at[n % 2]
        )

    probs_copy(0).start()
    late = {}
    for n, (name, src, dst) in enumerate(
        (
            ("mixed", hbm_mixed_ref, mixed_ref),
            ("qs", hbm_qs_ref, qs_ref),
            ("kv", hbm_kv_ref, kv_ref),
            ("out_own", hbm_out_own, out_own),
            ("n1", hbm_n1_ref, n1_ref),
            ("wq", hbm_wq_ref, wq_ref),
            ("kvg", hbm_kvg_ref, kvg_ref),
            ("rows", hbm_rows_ref, rows_ref),
            ("take", hbm_take_ref, take_ref),
        )
    ):
        late[name] = pltpu.make_async_copy(src, dst, late_sems.at[n])
        late[name].start()
    greet_all(place)

    events = [(1, groups - 1)] + [(a, k) for k in range(groups - 2, -1, -1) for a in range(2)]

    def stage_copy(n, up):
        a, k = events[n]
        slot = 0 if up else 1
        return pltpu.make_async_copy(
            half_hbm.at[a, place.g + k if up else place.g - k],
            three_stage.at[n % 2, slot],
            stage_sems.at[n % 2, slot],
        )

    def fetch(n):
        k = events[n][1]
        pl.when(place.g + k < groups)(stage_copy(n, True).start)
        if k > 0:
            pl.when(place.g >= k)(stage_copy(n, False).start)

    def three_value(a, k, up):
        n = events.index((a, k))
        stage_copy(n, up).wait()
        return three_stage[n % 2, 0 if up else 1].astype(F32)

    out = PlaneReduce(place, out_give, out_got, out_relay, out_send, out_recv, out_relays)
    for which in range(4):
        out.copy(which).start()
    fetch(0)
    three = ChainSum(
        place,
        three_value,
        lambda a, g: three_got.at[a, g],
        lambda a: three_last.at[a],
        lambda a, g: three_got.at[a, g],
        three_up,
        three_down,
        three_recv,
        three_last_sems,
        early={0: early_ref},
    )

    def three_steps(k, arrays=(0, 1)):
        for a in arrays:
            fetch(events.index((a, k)) + 1)
            three.step(a, k)

    three_steps(groups - 1, (1,))
    three_steps(groups - 2, (0,))

    low_ref[f] = grad_middle_ref[...].astype(BF16)
    sent.remote(low_ref.at[f], low_ref.at[f], low_sems.at[0], low_sems.at[1], (d, other))
    kv_total[...] = jnp.zeros_like(kv_total)

    def block(k):
        return pl.ds(pl.multiple_of(k * per, per), per)

    home = (Sent(), Sent())

    def rows_home(i, source_ref):
        if i > 0:
            home[i - 1].finish()
        give[...] = mm_tn(place_ref[...], source_ref[...]).astype(BF16)
        for k in range(1, chips):
            to = (d + k) % chips
            home[i].remote(
                give.at[block(to)],
                got.at[i, block(d)],
                row_send.at[i, k],
                row_recv.at[i, d],
                (to, f),
            )
        got[i, block(d), :] = give[block(d), :]

    def rows_back(i):
        for k in range(1, chips):
            s = (d + k) % chips
            arrived(got.at[i, block(s)], row_recv.at[i, s])
        return mm_tn(take_ref[...], got[i]).astype(BF16)

    def mix_back(h):
        grads = mm(low_ref[h], wot_ref[...])
        for m in range(MICRO):
            for i in range(heads):
                grad_mixed[2 * h + m, i * micro : (i + 1) * micro, :] = grads[
                    m * micro : (m + 1) * micro, i * HEAD : (i + 1) * HEAD
                ].astype(BF16)

    mix_back(f)
    arrived(low_ref.at[other], low_sems.at[1])
    mix_back(other)

    def whole(g, pos):
        return pl.ds(pl.multiple_of((g * PLANE + pos) * share, 16), share)

    def term(a, g, pos):
        return heads_ref.at[a, whole(g, pos)]

    def plane_copy(kind, a, g):
        even = g % 2 == 0
        near_pos, near_to, near_side = (by_x, to_x, 0) if even else (by_y, to_y, 1)
        if kind == 0:
            src, dst, to = term(a, g, near_pos), plane_got.at[a, near_side, g], near_to
            send, recv = direct_send.at[a, 0, g], plane_recv.at[a, near_side, g]
        elif kind == 1:
            src, dst, to = term(a, g, far), plane_relay.at[a, g], near_to
            send, recv = direct_send.at[a, 1, g], relay_recv.at[a, g]
        else:
            side = 1 - near_side
            src, dst, to = plane_relay.at[a, g], plane_got.at[a, side, g], to_y if even else to_x
            send, recv = relay_send.at[a, g], plane_recv.at[a, side, g]
        return pltpu.make_async_remote_copy(
            src_ref=src,
            dst_ref=dst,
            send_sem=send,
            recv_sem=recv,
            device_id=(to, f),
            device_id_type=MESH,
        )

    def plane_start(a):
        for g in range(groups):
            plane_copy(1, a, g).start()
            plane_copy(0, a, g).start()

    def plane_pass(a):
        for g in range(groups):
            arrived(plane_relay.at[a, g], relay_recv.at[a, g])
            mine = term(a, g, by_y if g % 2 == 0 else by_x)
            plane_relay[a, g] = (plane_relay[a, g].astype(F32) + mine[...].astype(F32)).astype(BF16)
            plane_copy(2, a, g).start()

    def plane_total(a, k, up):
        g = place.g + k if up else place.g - k
        total = term(a, g, place.p)[...].astype(F32)
        for side in range(2):
            arrived(plane_got.at[a, side, g], plane_recv.at[a, side, g])
            total = total + plane_got[a, side, g].astype(F32)
        return total

    column = ChainSum(
        place,
        plane_total,
        lambda a, g: column_got.at[a, g],
        lambda a: column_last.at[a],
        lambda a, g: column_give.at[a, g],
        column_up,
        column_down,
        column_recv,
        column_last_sems,
    )

    tile = 2 * HEAD

    def head_grads(a, left_ref):
        def step(i, carry):
            at = pl.ds(pl.multiple_of(i * tile, tile), tile)
            left = left_ref[:, :, at].reshape(2 * rows, tile)
            heads_ref[a, at, :] = mm_tn(left, mixed_rows[...]).astype(BF16)
            return carry

        lax.fori_loop(0, width // tile, step, 0)

    late["mixed"].wait()
    for hm in range(4):
        mixed_rows[hm * micro : (hm + 1) * micro, :] = mixed_ref[hm]
    head_grads(0, low_ref)
    plane_start(0)
    out.pass_on()

    score_scale = HEAD ** (-0.5)
    chunks = [slice(i, i + 64) for i in range(0, span, 64)]

    def attend_back(hm):
        h, m = hm // 2, hm % 2
        at = slice(h, h + 2 * reach + 1)
        keys = kv_ref[m, at, :, 0:HEAD].reshape(span, HEAD)
        values = kv_ref[m, at, :, HEAD:].reshape(span, HEAD)
        keys_t = keys.T

        def pair_step(pair, carry):
            band = pl.ds(pl.multiple_of(pair * 2 * micro, 2 * micro), 2 * micro)
            n = hm * pairs + pair
            probs_copy(n).wait()
            pl.when(n + 1 < 4 * pairs)(lambda: probs_copy(n + 1).start())
            grads = grad_mixed[hm, band, :]
            queries = qs_ref[hm, band, :]
            grad_probs_ref[...] = mm_nt(values, grads)
            delta = jnp.zeros((8, 2 * micro), F32)
            for part_at in chunks:
                wide = probs_ref[n % 2, part_at, :].astype(F32)
                delta = delta + fold(grad_probs_ref[part_at, :] * wide, jnp.add)
            delta = jnp.sum(delta, axis=0, keepdims=True)
            for part_at in chunks:
                wide = probs_ref[n % 2, part_at, :].astype(F32)
                grad_scores_ref[part_at, :] = (
                    wide * (grad_probs_ref[part_at, :] - delta)
                ).astype(BF16)
            grad_scores = grad_scores_ref[...]
            value_total = mm(probs_ref[n % 2], grads).reshape(2 * reach + 1, micro, HEAD)
            kv_total[m, at, :, HEAD:] = kv_total[m, at, :, HEAD:] + value_total
            key_total = mm(grad_scores, queries).reshape(2 * reach + 1, micro, HEAD)
            kv_total[m, at, :, 0:HEAD] = kv_total[m, at, :, 0:HEAD] + key_total
            query_t = mm(keys_t, grad_scores) * score_scale
            grad_q[hm, :, band] = jnp.concatenate(
                [
                    turned(
                        query_t[:, i * micro : (i + 1) * micro].T, cos_ref[hm], -sin_ref[hm]
                    )
                    for i in range(2)
                ],
                axis=1,
            ).astype(BF16)
            return carry

        lax.fori_loop(0, heads // 2, pair_step, 0)

    middle_steps = [(k, (a,)) for a, k in events[2:-2]]
    turns = iter(middle_steps)

    def next_step():
        for step in turns:
            three_steps(*step)
            break

    late["qs"].wait()
    late["kv"].wait()
    attend_back(0)
    next_step()
    attend_back(1)
    plane_pass(0)
    next_step()
    attend_back(2)
    late["out_own"].wait()
    one_out[...] = (out_own[...].astype(F32) + out.total()).astype(BF16)
    rows_home(0, one_out)
    next_step()
    attend_back(3)

    for m in range(MICRO):
        for slot in range(2 * reach + 2):
            kv_total[m, slot, :, 0:HEAD] = kv_total[m, slot, :, 0:HEAD] * score_scale
            kv_give[m, slot] = kv_total[m, slot].astype(BF16)
    own_slots = [2 * j + f for j in range(reach + 1)]
    other_slots = [2 * j + other for j in range(reach + 1)]
    for j in range(reach + 1):
        sent.remote(
            kv_give.at[:, other_slots[j]],
            kv_pair.at[:, j],
            kv_send.at[0, j],
            kv_recv.at[0, j],
            (d, other),
        )

    def kv_copy(j):
        return pltpu.make_async_remote_copy(
            src_ref=kv_give.at[:, own_slots[reach - j]],
            dst_ref=kv_got.at[j],
            send_sem=kv_send.at[1, j],
            recv_sem=kv_recv.at[1, j],
            device_id=(d - j, f),
            device_id_type=MESH,
        )

    for hm in range(4):
        mixed_rows[hm * micro : (hm + 1) * micro, :] = grad_q[hm]
    late["n1"].wait()
    head_grads(1, n1_ref)
    plane_start(1)
    for j in range(reach, -1, -1):
        s = reach - j
        arrived(kv_pair.at[:, s], kv_recv.at[0, s])
        total = kv_total[:, own_slots[s]] + kv_pair[:, s].astype(F32)
        kv_total[:, own_slots[s]] = total
        if j > 0:
            kv_give[:, own_slots[s]] = total.astype(BF16)

            @pl.when(d - j >= 0)
            def _():
                kv_copy(j).start()

    def one_back(h):
        at = pl.ds(pl.multiple_of(h * rows, rows), rows)
        return mm_nt(mixed_rows[at, :], wq_ref[...])

    for _ in middle_steps[3:]:
        next_step()
    column_steps = [k for k in range(groups - 1, 0, -1)]
    column.step(0, column_steps[0])
    late["wq"].wait()
    one_out[...] = one_back(other).astype(BF16)
    sent.remote(one_out, one_in, one_sems.at[0], one_sems.at[1], (d, other))
    grad_one = one_back(f)
    for k in column_steps[1:2]:
        column.step(0, k)
    plane_pass(1)
    for k in column_steps[2:]:
        column.step(0, k)

    sums = [kv_total[m, 2 * reach + f] for m in range(MICRO)]
    for j in range(1, reach + 1):

        @pl.when(d + j < chips)
        def _():
            arrived(kv_got.at[j], kv_recv.at[1, j])

        @pl.when(d + j >= chips)
        def _():
            kv_got[j] = jnp.zeros((MICRO, micro, 2 * HEAD), BF16)

        sums = [sums[m] + kv_got[j, m].astype(F32) for m in range(MICRO)]
    key_rows = jnp.concatenate(
        [
            turned(sums[m][:, 0:HEAD], cos_ref[2 * f + m], -sin_ref[2 * f + m])
            for m in range(MICRO)
        ],
        axis=0,
    )
    value_rows = jnp.concatenate([sums[m][:, HEAD:] for m in range(MICRO)], axis=0)
    pieces = halves_in(key_rows, value_rows)
    late["kvg"].wait()
    late["rows"].wait()
    row_values = rows_ref[...].astype(F32)
    for i in range(2):
        piece = pieces[i].astype(BF16)
        gkvg_ref[i, :, 0:share, :] = mm_tn(n1_ref[f], piece).astype(BF16).reshape(chips, share, HEAD)
        grad_one = grad_one + mm_nt(piece, kvg_ref[i, :, 0:share, :].reshape(width, HEAD))
    arrived(one_in, one_sems.at[1])
    grad_one = grad_one + one_in[...].astype(F32)
    gain_one = gain_row(kvg_ref, 0, chips, width, share)
    back_one, gain_one_grad = norm_back(row_values, gain_one, grad_one)
    one_in[...] = (grad_middle_ref[...] + back_one).astype(BF16)
    column.step(1, column_steps[0])
    rows_home(1, one_in)
    spread = gain_spread(width, share)
    stretch = own_stretch(chips, width, share)
    for i, grad in enumerate((gain_one_grad, gain_two_grad_ref[...])):
        piece = mm_nt(jnp.where(stretch, grad, 0.0).astype(BF16), spread)
        row = iota((chips, 16, HEAD), 1)
        gkvg_ref[i, :, share : share + 16, :] = jnp.where(
            row == 0, piece[:, None, :], 0.0
        ).astype(BF16)
    sent.remote(gkvg_ref.at[other], gkvg_pair, small_send.at[0], small_recv.at[0], (d, other))
    arrived(gkvg_pair, small_recv.at[0])

    def small_sum(s):
        return gkvg_ref[f, s].astype(F32) + gkvg_pair[s].astype(F32)

    for j in range(1, PLANE):
        pos = place.plane_pos(j)
        for g in range(groups):
            small_give[j, g] = small_sum(g * PLANE + pos).astype(BF16)
        sent.remote(
            small_give.at[j],
            small_got.at[j],
            small_send.at[j],
            small_recv.at[j],
            (place.plane_chip(j), f),
        )

    for k in column_steps[1:]:
        column.step(1, k)
    for j in range(1, PLANE):
        arrived(small_got.at[j], small_recv.at[j])
    for k in range(1, groups):
        g = (place.g + k) % groups
        s = g * PLANE + place.p
        total = small_sum(s)
        for j in range(1, PLANE):
            total = total + small_got[j, g].astype(F32)
        small_give[0, g] = total.astype(BF16)
        sent.remote(
            small_give.at[0, g],
            small_column.at[place.g],
            small_send.at[PLANE + k],
            small_recv.at[PLANE + place.g],
            (s, f),
        )
    total = small_sum(d)
    for j in range(1, PLANE):
        total = total + small_got[j, place.g].astype(F32)
    kvg_out[...] = total

    def end_copy(a, j):
        pos = place.plane_pos(j)
        src = down_sum.at[pos] if a == 2 else three_got.at[a, place.g, pos]
        return pltpu.make_async_remote_copy(
            src_ref=src,
            dst_ref=three_end.at[a, place.x, f],
            send_sem=end_send.at[a, j],
            recv_sem=end_recv.at[a, place.x, f],
            device_id=(place.plane_chip(j), place.y),
            device_id_type=MESH,
        )

    def end_local(a):
        src = down_sum.at[place.p] if a == 2 else three_got.at[a, place.g, place.p]
        return pltpu.make_async_copy(src, three_end.at[a, place.x, f], end_send.at[a, 0])

    for a in (2, 0, 1):
        if a == 0:
            fetch(events.index((1, 0)))
        if a < 2:
            three_got[a, place.g] = three.final(a).astype(BF16)
        for j in range(1, PLANE):
            end_copy(a, j).start()
        pl.when(place.y == f)(end_local(a).start)
        pl.when(place.y != f)(end_copy(a, 0).start)

    late["take"].wait()
    output_ref[...] = rows_back(0)
    for a in range(2):
        (ot_out, q_out)[a][...] = column.final(a)
    for k in range(1, groups):
        g = (place.g + k) % groups
        arrived(small_column.at[g], small_recv.at[PLANE + g])
        kvg_out[...] = kvg_out[...] + small_column[g].astype(F32)
    input_grad_ref[...] = rows_back(1)
    for a in (2, 0, 1):
        for cx in range(2):
            for core in range(2):
                own = (place.y == f) & (place.x == cx) & (core == f)

                @pl.when(own)
                def _():
                    end_local(a).wait()

                @pl.when(jnp.logical_not(own))
                def _():
                    arrived(three_end.at[a, cx, core], end_recv.at[a, cx, core])

    out.finish()
    three.finish(2)
    column.finish(2)
    for a in range(3):
        for j in range(1, PLANE):
            end_copy(a, j).wait_send()
        pl.when(place.y != f)(end_copy(a, 0).wait_send)
    for a in range(2):
        for g in range(groups):
            for kind in range(3):
                plane_copy(kind, a, g).wait_send()
    for j in range(1, reach + 1):

        @pl.when(d - j >= 0)
        def _():
            kv_copy(j).wait_send()

    home[1].finish()
    sent.finish()


def backward(chips, reach, out_own, out_give, down_sum, early, rows_in, grad_middle, gain_two_grad, n1, qs, kv, mixed, wq, wot, kvg, cosine, sine, take, placing, probs, halves):
    rows, width = rows_in.shape
    micro = rows // MICRO
    heads_wide = wq.shape[1]
    heads = heads_wide // HEAD
    groups = chips // PLANE
    share = width // chips
    half, part = halves.shape[3:]
    slots = 2 * reach + 2
    small = kvg.shape[2:]
    dma = pltpu.SemaphoreType.DMA
    shape = jax.ShapeDtypeStruct
    vm = pltpu.VMEM
    kv_shape = (MICRO, slots, micro, 2 * HEAD)
    return pl.pallas_call(
        functools.partial(backward_kernel, chips, reach),
        out_shape=(
            shape((3, 2, 2, half, part), BF16),
            shape((share, heads_wide), F32),
            shape((share, heads_wide), F32),
            shape(small, F32),
            shape((rows, width), BF16),
            shape((rows, width), BF16),
        ),
        in_specs=[
            ANY, VM, VM, VM, ANY, VM, VM, ANY, ANY, ANY, ANY, ANY, VM, ANY, VM, VM, ANY, VM, ANY, ANY,
        ],
        out_specs=(ANY,) + (VM,) * 5,
        scratch_shapes=[
            vm((2, probs.shape[1], 2 * micro), BF16),
            vm((2, rows, width), BF16),
            vm((2 * rows, heads_wide), BF16),
            vm((4, heads * micro, HEAD), BF16),
            vm((4, micro, heads_wide), BF16),
            vm(kv_shape, F32),
            vm(kv_shape, BF16),
            vm((MICRO, reach + 1, micro, 2 * HEAD), BF16),
            vm((reach + 1, MICRO, micro, 2 * HEAD), BF16),
            vm((rows, width), BF16),
            vm((rows, width), BF16),
            vm((2, groups, PLANE, half, part), BF16),
            vm((2, PLANE, half, part), BF16),
            vm((2, 2, PLANE, half, part), BF16),
            vm((2, width, heads_wide), BF16),
            vm((2, groups, share, heads_wide), BF16),
            vm((2, 2, groups, share, heads_wide), BF16),
            vm((2, groups, share, heads_wide), BF16),
            vm((2, share, heads_wide), BF16),
            vm((2, groups, share, heads_wide), BF16),
            vm((2, chips) + small, BF16),
            vm((chips,) + small, BF16),
            vm((PLANE, groups) + small, BF16),
            vm((PLANE, groups) + small, BF16),
            vm((groups,) + small, BF16),
            vm((rows, width), BF16),
            vm((2, rows, width), BF16),
            dma((2,)),
            dma((2, 2)),
            dma((2,)),
            dma((2, reach + 1)),
            dma((2, reach + 1)),
            dma((2,)),
            dma((2, groups)),
            dma((2, groups)),
            dma((2, groups)),
            dma((2,)),
            dma((3, PLANE)),
            dma((3, 2, 2)),
            dma((2, 2, groups)),
            dma((2, groups)),
            dma((2, groups)),
            dma((2, 2, groups)),
            dma((PLANE + groups,)),
            dma((PLANE + groups,)),
            dma((2, groups)),
            dma((2, groups)),
            dma((2, groups)),
            dma((2,)),
            dma((2, chips)),
            dma((2, chips)),
            vm((probs.shape[1], 2 * micro), F32),
            vm((probs.shape[1], 2 * micro), BF16),
            vm((2, rows, width), BF16),
            vm((2, rows // 2, width), BF16),
            dma((6,)),
            dma((2, 2)),
            dma((2,)),
        ]
        + [
            vm(one.shape, one.dtype)
            for one in (mixed, qs, kv, out_own, n1, wq, kvg, rows_in, take)
        ]
        + [dma((9,))],
        compiler_params=pltpu.CompilerParams(
            collective_id=2, has_side_effects=True, vmem_limit_bytes=VMEM_ASK
        ),
        name="attention_backward_and_scatter",
    )(out_own, out_give, down_sum, early, rows_in, grad_middle, gain_two_grad, n1, qs, kv, mixed, wq, wot, kvg, cosine, sine, take, placing, probs, halves)


def hand_over_kernel(
    three_ref,
    q_ref,
    ot_ref,
    kvg_ref,
    rows_ref,
    rows_grad_ref,
    output_ref,
    input_grad_ref,
    q_out,
    key_out,
    value_out,
    ot_out,
    gate_out,
    up_out,
    down_out,
    gains_out,
):
    half, part = three_ref.shape[3:]
    share = 2 * half
    key_columns = key_out.shape[0]
    output_ref[...] = rows_ref[...]
    input_grad_ref[...] = rows_grad_ref[...]
    q_out[...] = q_ref[...]
    ot_out[...] = ot_ref[...]
    square = jnp.concatenate(
        [kvg_ref[...], jnp.zeros((HEAD - kvg_ref.shape[0], HEAD), F32)], axis=0
    ).T
    key_out[...] = square[0:key_columns, 0:share]
    value_out[...] = square[key_columns : 2 * key_columns, 0:share]
    gains_out[...] = kvg_ref[share : share + 1, 0:share]
    for a, out in enumerate((gate_out, up_out, down_out)):
        for cx in range(2):
            for core in range(2):
                out[half * core : half * (core + 1), cx * part : (cx + 1) * part] = three_ref[
                    a, cx, core
                ].astype(F32)


def hand_over(key_columns, three, q, ot, kvg, rows, rows_grad):
    half, part = three.shape[3:]
    share = 2 * half
    shape = jax.ShapeDtypeStruct
    return pl.pallas_call(
        hand_over_kernel,
        out_shape=(
            shape(rows.shape, BF16),
            shape(rows.shape, BF16),
            shape(q.shape, F32),
            shape((key_columns, share), F32),
            shape((key_columns, share), F32),
            shape(ot.shape, F32),
            shape((share, 2 * part), F32),
            shape((share, 2 * part), F32),
            shape((share, 2 * part), F32),
            shape((1, share), F32),
        ),
        in_specs=[VM] * 6,
        out_specs=(VM,) * 10,
        compiler_params=pltpu.CompilerParams(vmem_limit_bytes=VMEM_ASK),
        name="hand_over",
    )(three, q, ot, kvg, rows, rows_grad)


def planned(
    tokens,
    cotangent,
    deal,
    first_len,
    w_query,
    w_key,
    w_value,
    w_out,
    w_gate,
    w_up,
    w_down,
    norm_gains,
):
    chips = lax.axis_size("dp")
    rows, width = tokens.shape
    micro = rows // MICRO
    share = w_query.shape[0]
    back_blocks = min(2 * chips - 1, (WINDOW + micro - 2) // micro)
    reach = (back_blocks + 1) // 2
    d = lax.axis_index("dp")
    inside = jnp.arange(micro, dtype=jnp.int32)
    positions = (2 * d + jnp.arange(2, dtype=jnp.int32))[:, None, None] * micro + inside
    second = positions >= first_len[None, :, None]
    within = positions - jnp.where(second, first_len[None, :, None], 0)
    cosine, sine = angles(within.reshape(-1))
    cosine = jnp.concatenate([cosine, cosine], axis=1).reshape(4, micro, HEAD)
    sine = jnp.concatenate([-sine, sine], axis=1).reshape(4, micro, HEAD)
    (
        three, wq, wot, kvg_all, rows_in, pg, take, placing, n1, qs, kv, probs, mixed, middle, n2, gain_two
    ) = forward(
        chips, reach, first_len, deal, w_key.T, w_value.T, norm_gains, cosine, sine, tokens, cotangent,
        w_query, w_out.T, w_gate, w_up, w_down.T,
    )
    out_own, out_give, grad_middle, gain_two_grad, halves, early, down_sum = mlp(
        chips, n2, middle, pg, gain_two, three
    )
    three_out, q_out, ot_out, kvg_out, output, input_grad = backward(
        chips, reach, out_own, out_give, down_sum, early, rows_in, grad_middle, gain_two_grad, n1, qs, kv, mixed, wq, wot,
        kvg_all, cosine, sine, take, placing, probs, halves,
    )
    output, input_grad, q_out, key_out, value_out, ot_out, gate_out, up_out, down_out, gains_out = hand_over(
        w_key.shape[1], three_out, q_out, ot_out, kvg_out, output, input_grad
    )
    return (
        output,
        input_grad,
        q_out,
        key_out.T,
        value_out.T,
        ot_out.T,
        gate_out,
        up_out,
        down_out.T,
        gains_out,
    )


def fits_plan(mesh, share):
    chips = mesh.shape["dp"]
    whole = share % 32 == 0 and share < HEAD
    return mesh.shape["fsdp"] == 2 and chips % PLANE == 0 and chips // PLANE >= 4 and whole


def solution(mesh):
    in_specs = (
        P(("dp", "fsdp"), None),
        P(("dp", "fsdp"), None),
        P(("dp", "fsdp")),
        P(),
        P("dp", "fsdp"),
        P("dp", "fsdp"),
        P("dp", "fsdp"),
        P("fsdp", "dp"),
        P("dp", "fsdp"),
        P("dp", "fsdp"),
        P("fsdp", "dp"),
        P("fsdp", "dp"),
    )
    out_specs = (
        P(("dp", "fsdp"), None),
        P(("dp", "fsdp"), None),
        P("dp", "fsdp"),
        P("dp", "fsdp"),
        P("dp", "fsdp"),
        P("fsdp", "dp"),
        P("dp", "fsdp"),
        P("dp", "fsdp"),
        P("fsdp", "dp"),
        P("fsdp", "dp"),
    )
    def placed(*arrays):
        share = arrays[4].shape[0] // mesh.shape["dp"]
        program = planned if fits_plan(mesh, share) else per_device
        return jax.shard_map(
            program, mesh=mesh, in_specs=in_specs, out_specs=out_specs, check_vma=False
        )(*arrays)

    return placed
```

```python
import functools

import jax
import jax.numpy as jnp
from jax import lax
from jax.experimental import pallas as pl
from jax.experimental.pallas import tpu as pltpu
from jax.sharding import PartitionSpec as P

HEADS = 12
HEAD = 128
WINDOW = 1024
MICRO = 2


EPSILON = 1e-06
NEGATIVE = -1e30
VMEM_ASK = 62 * 2**20


def passed_along(x, axis, by):
    count = lax.axis_size(axis)
    pairs = [(i, i + by) for i in range(count) if 0 <= i + by < count]
    return lax.ppermute(x, axis, pairs)


def normed(row_values, gain_row):
    return (
        row_values
        * lax.rsqrt(jnp.mean(row_values * row_values, axis=-1, keepdims=True) + EPSILON)
        * gain_row
    )


def rotate(values, cosine, sine_table):
    half_width = values.shape[-1] // 2
    front_half = values[..., :half_width]
    back_half = values[..., half_width:]
    return jnp.concatenate(
        [
            front_half * cosine - back_half * sine_table,
            back_half * cosine + front_half * sine_table,
        ],
        axis=-1,
    )


def angles(places):
    half_width = HEAD // 2
    frequency = 10000.0 ** (-jnp.arange(half_width, dtype=jnp.float32) * 2.0 / HEAD)
    angle_rows = places.astype(jnp.float32)[:, None] * frequency[None, :]
    return (jnp.cos(angle_rows), jnp.sin(angle_rows))


def contract_rows(left, right):
    return lax.dot_general(
        left, right, (((0,), (0,)), ((), ())), preferred_element_type=jnp.float32
    )


def against(left, right):
    return lax.dot_general(
        left, right, (((1,), (1,)), ((), ())), preferred_element_type=jnp.float32
    )


def gelu_tanh(inputs):
    return jax.nn.gelu(inputs, approximate=True)


def per_device(
    tokens,
    cotangent,
    deal,
    first_len,
    w_query,
    w_key,
    w_value,
    w_out,
    w_gate,
    w_up,
    w_down,
    norm_gains,
):
    peer_count = lax.axis_size("dp")
    core_count = lax.axis_size("fsdp")
    device_total = peer_count * core_count
    row_count = tokens.shape[0]
    model_width = tokens.shape[1]
    per_peer = row_count // peer_count
    micro_rows = row_count // MICRO
    reach_steps = min(device_total - 1, (WINDOW + micro_rows - 2) // micro_rows)
    linear = lax.axis_index("dp") * core_count + lax.axis_index("fsdp")
    source_peer = deal // (row_count * core_count)
    offsets = deal % row_count
    bucket_order = jnp.argsort(source_peer, stable=True)
    inverse = jnp.argsort(bucket_order)
    wanted = offsets[bucket_order].reshape(peer_count, per_peer)
    requested = lax.all_to_all(wanted, "dp", split_axis=0, concat_axis=0, tiled=True)
    picked = requested.reshape(-1)
    fetched = (
        lax.all_to_all(
            tokens[picked].reshape(peer_count, per_peer, model_width),
            "dp",
            split_axis=0,
            concat_axis=0,
            tiled=True,
        ),
        lax.all_to_all(
            cotangent[picked].reshape(peer_count, per_peer, model_width),
            "dp",
            split_axis=0,
            concat_axis=0,
            tiled=True,
        ),
    )
    rows_in = fetched[0].reshape(row_count, model_width)[inverse]
    grad_in = fetched[1].reshape(row_count, model_width)[inverse]
    halves = (
        lax.all_gather(w_query, "dp", axis=0, tiled=True),
        lax.all_gather(w_key, "dp", axis=0, tiled=True),
        lax.all_gather(w_value, "dp", axis=0, tiled=True),
        lax.all_gather(w_out, "dp", axis=1, tiled=True),
        lax.all_gather(w_gate, "dp", axis=0, tiled=True),
        lax.all_gather(w_up, "dp", axis=0, tiled=True),
        lax.all_gather(w_down, "dp", axis=1, tiled=True),
        lax.all_gather(norm_gains, "dp", axis=1, tiled=True),
    )
    gathered = (
        lax.all_gather(halves[0], "fsdp", axis=1, tiled=True),
        lax.all_gather(halves[1], "fsdp", axis=1, tiled=True),
        lax.all_gather(halves[2], "fsdp", axis=1, tiled=True),
        lax.all_gather(halves[3], "fsdp", axis=0, tiled=True),
        lax.all_gather(halves[4], "fsdp", axis=1, tiled=True),
        lax.all_gather(halves[5], "fsdp", axis=1, tiled=True),
        lax.all_gather(halves[6], "fsdp", axis=0, tiled=True),
        lax.all_gather(halves[7], "fsdp", axis=0, tiled=True),
    )
    full_query, full_key, full_value, full_out, full_gate, full_up, full_down, full_gains = gathered
    gain_one = full_gains[0].astype(jnp.float32)
    gain_two = full_gains[1].astype(jnp.float32)
    inside = jnp.arange(micro_rows, dtype=jnp.int32)
    query_place = linear * micro_rows + inside
    query_later = query_place[None, :] >= first_len[:, None]
    query_within = query_place[None, :] - jnp.where(query_later, first_len[:, None], 0)
    distance = jnp.arange(reach_steps, -1, -1, dtype=jnp.int32)
    key_place = ((linear - distance)[:, None] * micro_rows + inside[None, :]).reshape(-1)
    key_later = key_place[None, :] >= first_len[:, None]
    allowed = (
        (query_later[:, :, None] == key_later[:, None, :])
        & (key_place[None, None, :] >= 0)
        & (key_place[None, None, :] <= query_place[None, :, None])
        & (query_place[None, :, None] - key_place[None, None, :] < WINDOW)
    )
    rows_float = rows_in.astype(jnp.float32)
    cosine, sine_table = angles(query_within.reshape(-1))
    score_scale = HEAD ** (-0.5)
    normal_one = normed(rows_float, gain_one).astype(jnp.bfloat16)
    query_raw = jnp.dot(normal_one, full_query, preferred_element_type=jnp.float32).reshape(
        row_count, HEADS, HEAD
    )
    query_rows = rotate(query_raw, cosine[:, None, :], sine_table[:, None, :]).astype(jnp.bfloat16)
    key_rows = rotate(
        jnp.dot(normal_one, full_key, preferred_element_type=jnp.float32), cosine, sine_table
    ).astype(jnp.bfloat16)
    value_rows = jnp.dot(normal_one, full_value, preferred_element_type=jnp.float32).astype(
        jnp.bfloat16
    )
    earlier = []
    for distance_step in range(1, reach_steps + 1):
        earlier.append(passed_along((key_rows, value_rows), ("dp", "fsdp"), distance_step))
    ordered = earlier[::-1] + [(key_rows, value_rows)]
    all_keys = jnp.concatenate(
        [member[0].reshape(MICRO, micro_rows, HEAD) for member in ordered], axis=1
    )
    all_values = jnp.concatenate(
        [member[1].reshape(MICRO, micro_rows, HEAD) for member in ordered], axis=1
    )
    by_head = jnp.transpose(query_rows.reshape(MICRO, micro_rows, HEADS, HEAD), (2, 0, 1, 3))

    def attend(query_head):
        scores = jnp.where(
            allowed,
            jnp.einsum("mqd,mkd->mqk", query_head, all_keys, preferred_element_type=jnp.float32)
            * score_scale,
            NEGATIVE,
        )
        row_top = jnp.max(scores, axis=2, keepdims=True)
        exp_scores = jnp.exp(scores - row_top)
        row_total = jnp.sum(exp_scores, axis=2, keepdims=True)
        soft_weights = (exp_scores / row_total).astype(jnp.bfloat16)
        attended_head = jnp.einsum(
            "mqk,mkd->mqd", soft_weights, all_values, preferred_element_type=jnp.float32
        )
        return (attended_head, row_top[..., 0] + jnp.log(row_total[..., 0]))

    attended, log_total = lax.map(attend, by_head)
    mixed_heads = (
        jnp.transpose(attended, (1, 2, 0, 3)).reshape(row_count, HEADS * HEAD).astype(jnp.bfloat16)
    )
    middle = rows_float + jnp.dot(mixed_heads, full_out, preferred_element_type=jnp.float32)
    normal_two = normed(middle, gain_two).astype(jnp.bfloat16)
    gate_rows = jnp.dot(normal_two, full_gate, preferred_element_type=jnp.float32)
    upward = jnp.dot(normal_two, full_up, preferred_element_type=jnp.float32)
    activated = gelu_tanh(gate_rows)
    hidden = (activated * upward).astype(jnp.bfloat16)
    result = (middle + jnp.dot(hidden, full_down, preferred_element_type=jnp.float32)).astype(
        jnp.bfloat16
    )
    grad_float = grad_in.astype(jnp.float32)
    grad_down = contract_rows(hidden, grad_in)
    grad_hidden = against(grad_in, full_down)
    gelu_value, gelu_pull = jax.vjp(gelu_tanh, gate_rows)
    grad_gate_rows = gelu_pull(grad_hidden * upward)[0].astype(jnp.bfloat16)
    grad_up_rows = (grad_hidden * activated).astype(jnp.bfloat16)
    grad_gate = contract_rows(normal_two, grad_gate_rows)
    grad_up = contract_rows(normal_two, grad_up_rows)
    grad_two = against(grad_gate_rows, full_gate) + against(grad_up_rows, full_up)
    norm_value, norm_pull = jax.vjp(normed, middle, gain_two)
    grad_middle_norm, gain_two_grad = norm_pull(grad_two)
    grad_middle = grad_float + grad_middle_norm
    grad_middle_low = grad_middle.astype(jnp.bfloat16)
    grad_out = contract_rows(mixed_heads, grad_middle_low)
    grad_mixed = against(grad_middle_low, full_out).astype(jnp.bfloat16)
    grad_by_head = jnp.transpose(grad_mixed.reshape(MICRO, micro_rows, HEADS, HEAD), (2, 0, 1, 3))

    def attend_back(running, pieces):
        key_total, value_total = running
        query_head, grad_head, total_head = pieces
        scores = (
            jnp.einsum("mqd,mkd->mqk", query_head, all_keys, preferred_element_type=jnp.float32)
            * score_scale
        )
        soft_weights = jnp.where(allowed, jnp.exp(scores - total_head[..., None]), 0.0)
        value_total = value_total + jnp.einsum(
            "mqk,mqd->mkd",
            soft_weights.astype(jnp.bfloat16),
            grad_head,
            preferred_element_type=jnp.float32,
        )
        grad_soft = jnp.einsum(
            "mqd,mkd->mqk", grad_head, all_values, preferred_element_type=jnp.float32
        )
        row_delta = jnp.sum(grad_soft * soft_weights, axis=2, keepdims=True)
        grad_scores = (soft_weights * (grad_soft - row_delta)).astype(jnp.bfloat16)
        grad_query_head = (
            jnp.einsum("mqk,mkd->mqd", grad_scores, all_keys, preferred_element_type=jnp.float32)
            * score_scale
        )
        key_total = (
            key_total
            + jnp.einsum(
                "mqk,mqd->mkd", grad_scores, query_head, preferred_element_type=jnp.float32
            )
            * score_scale
        )
        return ((key_total, value_total), grad_query_head)

    zero_block = jnp.zeros((MICRO, (reach_steps + 1) * micro_rows, HEAD), jnp.float32)
    totals, grad_query_heads = lax.scan(
        attend_back, (zero_block, zero_block), (by_head, grad_by_head, log_total)
    )
    key_total, value_total = totals

    def piece_of(total, distance_step):
        begin_row = (reach_steps - distance_step) * micro_rows
        return total[:, begin_row : begin_row + micro_rows].reshape(row_count, HEAD)

    own_key = piece_of(key_total, 0)
    own_value = piece_of(value_total, 0)
    for distance_step in range(1, reach_steps + 1):
        returned_pair = (
            passed_along(
                piece_of(key_total, distance_step).astype(jnp.bfloat16),
                ("dp", "fsdp"),
                -distance_step,
            ).astype(jnp.float32),
            passed_along(
                piece_of(value_total, distance_step).astype(jnp.bfloat16),
                ("dp", "fsdp"),
                -distance_step,
            ).astype(jnp.float32),
        )
        own_key = own_key + returned_pair[0]
        own_value = own_value + returned_pair[1]
    grad_value_rows = own_value.astype(jnp.bfloat16)
    grad_query_rot = jnp.transpose(grad_query_heads, (1, 2, 0, 3)).reshape(row_count, HEADS, HEAD)
    grad_query_raw = (
        rotate(grad_query_rot, cosine[:, None, :], -sine_table[:, None, :])
        .reshape(row_count, HEADS * HEAD)
        .astype(jnp.bfloat16)
    )
    grad_key_raw = rotate(own_key, cosine, -sine_table).astype(jnp.bfloat16)
    grad_query = contract_rows(normal_one, grad_query_raw)
    grad_key = contract_rows(normal_one, grad_key_raw)
    grad_value = contract_rows(normal_one, grad_value_rows)
    grad_one = (
        against(grad_query_raw, full_query)
        + against(grad_key_raw, full_key)
        + against(grad_value_rows, full_value)
    )
    first_value, first_pull = jax.vjp(normed, rows_float, gain_one)
    grad_rows_norm, gain_one_grad = first_pull(grad_one)
    grad_rows = (grad_middle + grad_rows_norm).astype(jnp.bfloat16)
    grad_gains = jnp.stack([gain_one_grad, gain_two_grad])
    sectioned = (
        lax.psum_scatter(
            grad_query.astype(jnp.bfloat16), "fsdp", scatter_dimension=1, tiled=True
        ).astype(jnp.float32),
        lax.psum_scatter(
            grad_key.astype(jnp.bfloat16), "fsdp", scatter_dimension=1, tiled=True
        ).astype(jnp.float32),
        lax.psum_scatter(
            grad_value.astype(jnp.bfloat16), "fsdp", scatter_dimension=1, tiled=True
        ).astype(jnp.float32),
        lax.psum_scatter(
            grad_out.astype(jnp.bfloat16), "fsdp", scatter_dimension=0, tiled=True
        ).astype(jnp.float32),
        lax.psum_scatter(
            grad_gate.astype(jnp.bfloat16), "fsdp", scatter_dimension=1, tiled=True
        ).astype(jnp.float32),
        lax.psum_scatter(
            grad_up.astype(jnp.bfloat16), "fsdp", scatter_dimension=1, tiled=True
        ).astype(jnp.float32),
        lax.psum_scatter(
            grad_down.astype(jnp.bfloat16), "fsdp", scatter_dimension=0, tiled=True
        ).astype(jnp.float32),
        lax.psum_scatter(
            grad_gains.astype(jnp.bfloat16), "fsdp", scatter_dimension=0, tiled=True
        ).astype(jnp.float32),
    )
    reduced = (
        lax.psum_scatter(sectioned[0], "dp", scatter_dimension=0, tiled=True),
        lax.psum_scatter(sectioned[1], "dp", scatter_dimension=0, tiled=True),
        lax.psum_scatter(sectioned[2], "dp", scatter_dimension=0, tiled=True),
        lax.psum_scatter(sectioned[3], "dp", scatter_dimension=1, tiled=True),
        lax.psum_scatter(sectioned[4], "dp", scatter_dimension=0, tiled=True),
        lax.psum_scatter(sectioned[5], "dp", scatter_dimension=0, tiled=True),
        lax.psum_scatter(sectioned[6], "dp", scatter_dimension=1, tiled=True),
        lax.psum_scatter(sectioned[7], "dp", scatter_dimension=1, tiled=True),
    )
    returned = (
        lax.all_to_all(
            result[bucket_order].reshape(peer_count, per_peer, model_width),
            "dp",
            split_axis=0,
            concat_axis=0,
            tiled=True,
        ),
        lax.all_to_all(
            grad_rows[bucket_order].reshape(peer_count, per_peer, model_width),
            "dp",
            split_axis=0,
            concat_axis=0,
            tiled=True,
        ),
    )
    output = jnp.zeros_like(tokens).at[picked].set(returned[0].reshape(row_count, model_width))
    input_grad = jnp.zeros_like(tokens).at[picked].set(returned[1].reshape(row_count, model_width))
    return (
        output,
        input_grad,
        reduced[0],
        reduced[1],
        reduced[2],
        reduced[3],
        reduced[4],
        reduced[5],
        reduced[6],
        reduced[7],
    )


MESH = pl.DeviceIdType.MESH
BF16 = jnp.bfloat16
F32 = jnp.float32
PLANE = 4
ANY = pl.BlockSpec(memory_space=pl.ANY)
VM = pl.BlockSpec(memory_space=pltpu.VMEM)
SM = pl.BlockSpec(memory_space=pltpu.SMEM)


def mm(left, right):
    return jnp.dot(left, right, preferred_element_type=F32)


def mm_nt(left, right):
    return lax.dot_general(left, right, (((1,), (1,)), ((), ())), preferred_element_type=F32)


def mm_tn(left, right):
    return lax.dot_general(left, right, (((0,), (0,)), ((), ())), preferred_element_type=F32)


class Place:
    def __init__(self, chips):
        self.chips = chips
        self.groups = chips // PLANE
        self.d = lax.axis_index("dp")
        self.f = lax.axis_index("fsdp")
        self.other = 1 - self.f
        self.g = self.d // PLANE
        self.p = self.d % PLANE
        self.x = self.p % 2
        self.y = self.p // 2

    def plane_pos(self, j):
        return ((self.y + j // 2) % 2) * 2 + (self.x + j % 2) % 2

    def plane_chip(self, j):
        return self.g * PLANE + self.plane_pos(j)

    def column_chip(self, k):
        return ((self.g + k) % self.groups) * PLANE + self.p


def greet(barrier, device):
    pl.semaphore_signal(barrier, inc=1, device_id=device, device_id_type=MESH)


def greet_wide(place):
    barrier = pltpu.get_barrier_semaphore()

    def signal(k, carry):
        greet(barrier, ((place.d + k) % place.chips, place.f))
        return carry

    lax.fori_loop(1, place.chips, signal, 0)
    for j in range(PLANE):
        greet(barrier, (place.plane_chip(j), place.other))
    pl.semaphore_wait(barrier, place.chips - 1 + PLANE)


def greet_near(place):
    barrier = pltpu.get_barrier_semaphore()
    for j in (1, 2):
        greet(barrier, (place.plane_chip(j), place.f))
    greet(barrier, (place.d, place.other))

    @pl.when(place.g + 1 < place.groups)
    def _():
        greet(barrier, (place.d + PLANE, place.f))

    @pl.when(place.g >= 1)
    def _():
        greet(barrier, (place.d - PLANE, place.f))

    top = place.groups - 1
    pl.semaphore_wait(barrier, 5 - place.g // top - (top - place.g) // top)


class Sent:
    def __init__(self):
        self.copies = []

    def remote(self, src, dst, send_sem, recv_sem, device):
        copy = pltpu.make_async_remote_copy(
            src_ref=src,
            dst_ref=dst,
            send_sem=send_sem,
            recv_sem=recv_sem,
            device_id=device,
            device_id_type=MESH,
        )
        copy.start()
        self.copies.append(copy)

    def finish(self):
        for copy in self.copies:
            copy.wait_send()
        self.copies = []


def arrived(ref, sem):
    pltpu.make_async_copy(ref, ref, sem).wait()


def iota(shape, dim):
    return lax.broadcasted_iota(jnp.int32, shape, dim)


def fold(values, combine):
    parts = values.reshape(values.shape[0] // 8, 8, values.shape[1])
    total = parts[0]
    for i in range(1, parts.shape[0]):
        total = combine(total, parts[i])
    return total


def gain_spread(width, share):
    column = iota((128, width), 1).astype(F32)
    inside = column - jnp.floor((column + 0.5) * (1.0 / share)) * share
    row = iota((128, width), 0).astype(F32)
    return (inside == row).astype(BF16)


def own_stretch(chips, width, share):
    row = iota((chips, width), 0)
    column = iota((chips, width), 1)
    return (column >= row * share) & (column < row * share + share)


def gain_row(kvg_ref, which, chips, width, share):
    block = kvg_ref[which, :, share : share + 16, :].astype(F32)[:, 0, :].astype(BF16)
    spread = mm(block, gain_spread(width, share))
    return jnp.sum(jnp.where(own_stretch(chips, width, share), spread, 0.0), axis=0, keepdims=True)


def rms_scale(values):
    return lax.rsqrt(jnp.mean(values * values, axis=-1, keepdims=True) + EPSILON)


def turned(values, cosine, sine):
    return values * cosine + pltpu.roll(values, HEAD // 2, 1) * sine


def halves_in(first, second):
    front = iota(first.shape, 1) < HEAD // 2
    return (
        jnp.where(front, first, pltpu.roll(second, HEAD // 2, 1)),
        jnp.where(front, pltpu.roll(first, HEAD // 2, 1), second),
    )


class PlaneSpread:
    def __init__(self, place, blocks, send_sems, recv_sems):
        self.place, self.blocks, self.send_sems, self.recv_sems = place, blocks, send_sems, recv_sems
        self.half = blocks.shape[1] // 2
        self.by_x, self.by_y, self.far = (place.plane_pos(j) for j in range(1, PLANE))

    def piece(self, pos, side):
        return self.blocks.at[pos, pl.ds(side * self.half, self.half)]

    def copy(self, slot):
        place = self.place
        pos, side, over_x = (
            (place.p, 0, 1),
            (place.p, 1, 0),
            (place.p, 1, 1),
            (place.p, 0, 0),
            (self.by_x, 0, 0),
            (self.by_y, 1, 1),
        )[slot]
        return pltpu.make_async_remote_copy(
            src_ref=self.piece(pos, side),
            dst_ref=self.piece(pos, side),
            send_sem=self.send_sems.at[slot],
            recv_sem=self.recv_sems.at[pos, side],
            device_id=(place.plane_chip(1 if over_x else 2), place.f),
            device_id_type=MESH,
        )

    def start(self):
        for slot in range(4):
            self.copy(slot).start()

    def pass_on(self):
        for slot, pos, side in ((4, self.by_x, 0), (5, self.by_y, 1)):
            arrived(self.piece(pos, side), self.recv_sems.at[pos, side])
            self.copy(slot).start()

    def wait(self, blocks=(1, 2, 3)):
        left = ((1, self.by_x, 1), (2, self.by_y, 0), (3, self.far, 0), (3, self.far, 1))
        for block, pos, side in left:
            if block in blocks:
                arrived(self.piece(pos, side), self.recv_sems.at[pos, side])

    def finish(self):
        for slot in range(6):
            self.copy(slot).wait_send()


class Chain:
    def __init__(self, place, piece, hops, up_sems, down_sems, recv_sems):
        self.place, self.piece, self.hops = place, piece, hops
        self.up_sems, self.down_sems, self.recv_sems = up_sems, down_sems, recv_sems
        self.has_up = place.g + 1 < place.groups
        self.has_down = place.g >= 1

    def hop(self, a, origin, up):
        place = self.place
        ref = self.piece(a, origin)
        to = place.d + PLANE if up else place.d - PLANE
        sems = self.up_sems if up else self.down_sems
        return pltpu.make_async_remote_copy(
            src_ref=ref,
            dst_ref=ref,
            send_sem=sems.at[a, origin],
            recv_sem=self.recv_sems.at[a, origin],
            device_id=(to, place.f),
            device_id_type=MESH,
        )

    def start(self, a):
        def one(up):
            self.hop(a, self.place.g, up).start()

        pl.when(self.has_up)(functools.partial(one, True))
        pl.when(self.has_down)(functools.partial(one, False))

    def step(self, k, arrays, then):
        place = self.place

        def from_below():
            origin = place.g - k
            for a in arrays:
                arrived(self.piece(a, origin), self.recv_sems.at[a, origin])

                if k < self.hops[a]:
                    pl.when(self.has_up)(self.hop(a, origin, True).start)
                then(a, origin)

        def from_above():
            origin = place.g + k
            for a in arrays:
                arrived(self.piece(a, origin), self.recv_sems.at[a, origin])

                if k < self.hops[a]:
                    pl.when(self.has_down)(self.hop(a, origin, False).start)
                then(a, origin)

        pl.when(place.g >= k)(from_below)
        pl.when(place.g + k < place.groups)(from_above)

    def finish(self):
        place = self.place
        for a, hops in enumerate(self.hops):
            for k in range(hops):

                @pl.when((place.g >= k) & self.has_up)
                def _():
                    self.hop(a, place.g - k, True).wait_send()

                @pl.when((place.g + k < place.groups) & self.has_down)
                def _():
                    self.hop(a, place.g + k, False).wait_send()


def forward_kernel(
    chips,
    reach,
    first_ref,
    deal_ref,
    key_ref,
    value_ref,
    gains_ref,
    cos_ref,
    sin_ref,
    tokens_ref,
    cot_ref,
    wq_ref,
    wot_ref,
    gate_ref,
    up_ref,
    down_ref,
    full_three,
    out_full_q,
    out_full_ot,
    out_full_kvg,
    rows_out,
    pg_all,
    take_ref,
    place_ref,
    out_n1_ref,
    out_qs_ref,
    out_kv_ref,
    out_probs_ref,
    out_mixed_ref,
    middle_ref,
    n2_ref,
    gain_two_ref,
    square_ref,
    kvg_ref,
    deal_all,
    give,
    got,
    bias_ref,
    branch_out,
    branch_in,
    scores_ref,
    deal_send,
    deal_recv,
    row_send,
    row_recv,
    attn_up,
    attn_down,
    attn_recv,
    fan_send,
    fan_recv,
    kvg_sems,
    stage_send,
    stage_recv,
    three_up,
    three_down,
    three_recv,
    relay_send,
    relay_recv,
    plane_send,
    plane_recv,
    n1_sems,
    kv_send,
    kv_recv,
    branch_sems,
    local_sems,
    full_q,
    full_ot,
    full_kvg,
    n1_ref,
    qs_ref,
    kv_ref,
    probs_ref,
    mixed_ref,
    save_sems,
):
    place = Place(chips)
    d, f, other = place.d, place.f, place.other
    groups = place.groups
    rows, width = tokens_ref.shape
    share = wq_ref.shape[0]
    half = share // 2
    per = rows // chips
    part = gate_ref.shape[1] // 2
    micro = rows // MICRO
    heads = wq_ref.shape[1] // HEAD
    span = (2 * reach + 1) * micro
    sent = Sent()
    greet_wide(place)
    saves = []

    def save(src, dst):
        copy = pltpu.make_async_copy(src, dst, save_sems.at[len(saves)])
        copy.start()
        saves.append(copy)


    deal_all[d] = jnp.broadcast_to(deal_ref[...], (8, rows))
    for k in range(1, chips):
        to = (d + k) % chips
        sent.remote(deal_all.at[d], deal_all.at[d], deal_send.at[k], deal_recv.at[d], (to, f))

    key_columns = key_ref.shape[0]
    square_ref[...] = jnp.zeros_like(square_ref)
    square_ref[0:key_columns, 0:share] = key_ref[...].astype(F32)
    square_ref[key_columns : 2 * key_columns, 0:share] = value_ref[...].astype(F32)
    kvg_ref[0:share] = square_ref[...].T[0:share].astype(BF16)
    square_ref[0:1, 0:share] = gains_ref[...].astype(F32)
    kvg_ref[share : share + 16] = jnp.where(
        iota((16, HEAD), 0) + iota((16, HEAD), 1) // share == 0, square_ref[0:16], 0.0
    ).astype(BF16)

    def attn_piece(a, s):
        if a == 0:
            return full_kvg.at[f, s]
        band = pl.ds(pl.multiple_of(s * share, 16), share)
        return (full_q if a == 1 else full_ot).at[band]

    own_attn = (kvg_ref, wq_ref, wot_ref)
    copies = [
        pltpu.make_async_copy(own_attn[a], attn_piece(a, d), local_sems.at[a]) for a in range(3)
    ]
    for copy in copies:
        copy.start()
    for copy in copies:
        copy.wait()
    attn = Chain(
        place,
        lambda a, g: attn_piece(a, g * PLANE + place.p),
        (groups - 1,) * 3,
        attn_up,
        attn_down,
        attn_recv,
    )

    def fan(a, g):
        for j in range(1, PLANE if a == 0 else PLANE - 1):
            fan_copy(a, g, j).start()

    def fan_copy(a, g, j):
        s = g * PLANE + place.p
        return pltpu.make_async_remote_copy(
            src_ref=attn_piece(a, s),
            dst_ref=attn_piece(a, s),
            send_sem=fan_send.at[a, g, j],
            recv_sem=fan_recv.at[a, s],
            device_id=(place.plane_chip(j), f),
            device_id_type=MESH,
        )

    def pass_copy(a, g):
        by_x = place.plane_pos(1)
        by_y = place.plane_pos(2)
        even = g % 2 == 0
        s = g * PLANE + jnp.where(even, by_x, by_y)
        to = jnp.where(even, place.plane_chip(2), place.plane_chip(1))
        return pltpu.make_async_remote_copy(
            src_ref=attn_piece(a, s),
            dst_ref=attn_piece(a, s),
            send_sem=fan_send.at[a, g, PLANE - 1],
            recv_sem=fan_recv.at[a, s],
            device_id=(to, f),
            device_id_type=MESH,
        )

    def pass_on(a, g):
        s = g * PLANE + jnp.where(g % 2 == 0, place.plane_pos(1), place.plane_pos(2))
        arrived(attn_piece(a, s), fan_recv.at[a, s])
        pass_copy(a, g).start()

    def pass_all(a):
        pass_on(a, place.g)
        for k in range(1, groups):
            pl.when(place.g >= k)(functools.partial(pass_on, a, place.g - k))
            pl.when(place.g + k < groups)(functools.partial(pass_on, a, place.g + k))

    for a in range(2):
        attn.start(a)
        fan(a, place.g)
    attn.start(2)

    def soon(a, g):
        if a < 2:
            fan(a, g)

    mats = (gate_ref, up_ref, down_ref)

    def stage_src(a, to_x, core):
        return mats[a].at[pl.ds(half * core, half), pl.ds(pl.multiple_of(part * to_x, 128), part)]

    def stage_copy(a, b, core):
        to_x = (place.x + b) % 2
        return pltpu.make_async_remote_copy(
            src_ref=stage_src(a, to_x, core),
            dst_ref=full_three.at[a, d, core],
            send_sem=stage_send.at[a, b, core],
            recv_sem=stage_recv.at[a, place.p],
            device_id=(place.g * PLANE + 2 * f + to_x, core),
            device_id_type=MESH,
        )

    def own_copy(a):
        return pltpu.make_async_copy(
            mats[a].at[pl.ds(pl.multiple_of(half * f, 16), half), pl.ds(pl.multiple_of(part * place.x, 128), part)],
            full_three.at[a, d, f],
            local_sems.at[a],
        )

    def pair_copy(a):
        return pltpu.make_async_remote_copy(
            src_ref=mats[a].at[
                pl.ds(pl.multiple_of(half * other, 16), half),
                pl.ds(pl.multiple_of(part * place.x, 128), part),
            ],
            dst_ref=full_three.at[a, d, other],
            send_sem=stage_send.at[a, 0, 0],
            recv_sem=stage_recv.at[a, place.p],
            device_id=(d, other),
            device_id_type=MESH,
        )

    def stage_start(a):
        for core in range(2):
            stage_copy(a, 1, core).start()

        @pl.when(place.y != f)
        def _():
            for core in range(2):
                stage_copy(a, 0, core).start()

        @pl.when(place.y == f)
        def _():
            own_copy(a).start()
            pair_copy(a).start()

    stage_start(0)

    for k in range(1, chips):
        s = (d + k) % chips
        arrived(deal_all.at[s], deal_recv.at[s])
    chip_bits = (2 * rows).bit_length() - 1
    deals = deal_all[:, 0, :]
    wants = lax.shift_right_logical(deals, chip_bits) == d
    offset = deals & (rows - 1)
    earlier = (iota((rows, rows), 0) < iota((rows, rows), 1)).astype(BF16)
    rank = mm(wants.astype(F32).astype(BF16), earlier)
    for j in range(chips):
        hit = wants[j : j + 1, :] & (rank[j : j + 1, :] == iota((per, rows), 0).astype(F32))
        index = jnp.sum(jnp.where(hit, offset[j : j + 1, :], 0), axis=1, keepdims=True)
        take_ref[j * per : (j + 1) * per, :] = (
            (index == iota((per, rows), 1)).astype(F32).astype(BF16)
        )

    def block(k):
        return pl.ds(pl.multiple_of(k * per, per), per)

    def give_rows(i, source_ref):
        give[i] = mm(take_ref[...], source_ref[...]).astype(BF16)
        got[i, block(d), :] = give[i, block(d), :]

    def send_rows(i):
        for k in range(1, chips):
            to = (d + k) % chips
            sent.remote(
                give.at[i, block(to)],
                got.at[i, block(d)],
                row_send.at[i, k],
                row_recv.at[i, d],
                (to, f),
            )

    def take_rows(i):
        for k in range(1, chips):
            s = (d + k) % chips
            arrived(got.at[i, block(s)], row_recv.at[i, s])
        return mm(place_ref[...], got[i])

    give_rows(0, tokens_ref)
    def column_pass(k, a):
        pl.when(place.g >= k)(functools.partial(pass_on, a, place.g - k))
        pl.when(place.g + k < groups)(functools.partial(pass_on, a, place.g + k))

    attn.step(1, (0, 1, 2), soon)
    pass_on(1, place.g)
    three = Chain(
        place,
        lambda a, g: full_three.at[a, pl.ds(g * PLANE, PLANE), f],
        (groups - 1, groups - 1, 0),
        three_up,
        three_down,
        three_recv,
    )

    def relay_copy(a, g):
        ref = full_three.at[a, pl.ds(g * PLANE, PLANE), f]
        return pltpu.make_async_remote_copy(
            src_ref=ref,
            dst_ref=ref,
            send_sem=relay_send.at[a, g],
            recv_sem=relay_recv.at[a, g],
            device_id=(d, other),
            device_id_type=MESH,
        )

    def relay(a, g):
        relay_copy(a, g).start()

    def three_start(a):
        for j in range(1, PLANE):
            pos = place.plane_pos(j)
            arrived(full_three.at[a, place.g * PLANE + pos, f], stage_recv.at[a, pos])

        @pl.when(place.y == f)
        def _():
            own_copy(a).wait()

        @pl.when(place.y != f)
        def _():
            arrived(full_three.at[a, d, f], stage_recv.at[a, place.p])

        if a < 2:
            three.start(a)
        relay(a, place.g)

    def meanwhile():
        source_row = lax.shift_right_logical(deal_ref[...], chip_bits)
        source_wide = jnp.broadcast_to(source_row.astype(F32), (rows, rows))
        source_col = source_wide.T.astype(jnp.int32)
        same = (source_col == source_row) & (iota((rows, rows), 1) < iota((rows, rows), 0))
        order = jnp.sum(same.astype(F32), axis=1, keepdims=True).astype(jnp.int32)
        where_from = source_col * per + order
        place_ref[...] = (where_from == iota((rows, rows), 1)).astype(F32).astype(BF16)

        def make_bias(hm, carry):
            h, m = hm // 2, hm % 2
            first = first_ref[m]
            query = (2 * d + h) * micro + iota((span, micro), 1)
            key = (2 * d + h - 2 * reach) * micro + iota((span, micro), 0)
            allowed = (
                (jnp.where(query >= first, 1, 0) == jnp.where(key >= first, 1, 0))
                & (key >= 0)
                & (key <= query)
                & (query - key < WINDOW)
            )
            bias_ref[hm] = jnp.where(allowed, 0.0, NEGATIVE)
            return carry

        lax.fori_loop(0, 4, make_bias, 0)

    for k in range(2, groups):
        attn.step(k, (0, 1, 2), soon)
        column_pass(k - 1, 1)
        if k == 2:
            send_rows(0)
            three_start(0)
            stage_start(1)
            stage_start(2)
            meanwhile()
    row_values = take_rows(0)
    column_pass(groups - 1, 1)
    rows_out[...] = row_values.astype(BF16)

    def attn_wait(a):
        for g in range(groups):
            if a == 0:
                left = range(1, PLANE)
            else:
                left = (2 - g % 2, 3)
            for j in left:
                s = g * PLANE + place.plane_pos(j)
                arrived(attn_piece(a, s), fan_recv.at[a, s])

    cotangents = PlaneSpread(place, pg_all, plane_send, plane_recv)

    attn_wait(0)
    sent.remote(full_kvg.at[f], full_kvg.at[f], kvg_sems.at[0], kvg_sems.at[1], (d, other))
    arrived(full_kvg.at[other], kvg_sems.at[1])
    save(full_kvg, out_full_kvg)

    gain_one = gain_row(full_kvg, 0, chips, width, share)
    n1_ref[f] = (row_values * rms_scale(row_values) * gain_one).astype(BF16)
    sent.remote(n1_ref.at[f], n1_ref.at[f], n1_sems.at[0], n1_sems.at[1], (d, other))

    kvw = [full_kvg[i, :, 0:share, :].reshape(width, HEAD) for i in range(2)]
    raw = [mm(n1_ref[f], kvw[i]) for i in range(2)]
    key_raw, value_raw = halves_in(raw[0], raw[1])
    for m in range(MICRO):
        hm = 2 * f + m
        band = slice(m * micro, (m + 1) * micro)
        key = turned(key_raw[band], cos_ref[hm], sin_ref[hm])
        kv_ref[m, 2 * reach + f, :, 0:HEAD] = key.astype(BF16)
        kv_ref[m, 2 * reach + f, :, HEAD:] = value_raw[band].astype(BF16)
    own_kv = kv_ref.at[:, 2 * reach + f]

    def kv_copy(j):
        return pltpu.make_async_remote_copy(
            src_ref=own_kv,
            dst_ref=kv_ref.at[:, 2 * reach + f - 2 * j],
            send_sem=kv_send.at[j, 0],
            recv_sem=kv_recv.at[2 * reach + f - 2 * j],
            device_id=(d + j, f),
            device_id_type=MESH,
        )

    def kv_pass(j):
        slot = 2 * reach + f - 2 * j
        return pltpu.make_async_remote_copy(
            src_ref=kv_ref.at[:, slot],
            dst_ref=kv_ref.at[:, slot],
            send_sem=kv_send.at[j, 1],
            recv_sem=kv_recv.at[slot],
            device_id=(d, other),
            device_id_type=MESH,
        )

    sent.remote(own_kv, own_kv, kv_send.at[0, 0], kv_recv.at[2 * reach + f], (d, other))
    for j in range(reach, 0, -1):
        pl.when(d + j < chips)(kv_copy(j).start)
    for j in range(1, reach + 1):

        @pl.when(d - j < 0)
        def _():
            for core in range(2):
                kv_ref[:, 2 * reach - 2 * j + core] = jnp.zeros((MICRO, micro, 2 * HEAD), BF16)

    give_rows(1, cot_ref)
    send_rows(1)
    for g in range(groups):
        fan(2, g)
    three_start(1)

    def project(h):
        raw_q = mm(n1_ref[h], full_q[...])
        for m in range(MICRO):
            hm = 2 * h + m
            cosine, sine = cos_ref[hm], sin_ref[hm]
            for i in range(heads):
                one = raw_q[m * micro : (m + 1) * micro, i * HEAD : (i + 1) * HEAD]
                qs_ref[hm, i * micro : (i + 1) * micro, :] = turned(one, cosine, sine).astype(BF16)

    attn_wait(1)
    save(full_q, out_full_q)
    project(f)
    arrived(n1_ref.at[other], n1_sems.at[1])
    project(other)
    save(n1_ref, out_n1_ref)
    save(qs_ref, out_qs_ref)
    three.step(1, (0,), relay)

    for j in range(1, reach + 1):

        @pl.when(d - j >= 0)
        def _():
            slot = 2 * reach - 2 * j + f
            arrived(kv_ref.at[:, slot], kv_recv.at[slot])
            kv_pass(j).start()

    arrived(kv_ref.at[:, 2 * reach + other], kv_recv.at[2 * reach + other])
    for j in range(1, reach + 1):

        @pl.when(d - j >= 0)
        def _():
            slot = 2 * reach - 2 * j + other
            arrived(kv_ref.at[:, slot], kv_recv.at[slot])

    score_scale = HEAD ** (-0.5)
    chunks = [slice(i, i + 64) for i in range(0, span, 64)]

    def attend(hm):
        h, m = hm // 2, hm % 2
        keys = kv_ref[m, h : h + 2 * reach + 1, :, 0:HEAD].reshape(span, HEAD)
        values_t = kv_ref[m, h : h + 2 * reach + 1, :, HEAD:].reshape(span, HEAD).T

        def pair_step(pair, carry):
            start = pl.multiple_of(pair * 2 * micro, 2 * micro)
            band = pl.ds(start, 2 * micro)
            scores_ref[...] = mm_nt(keys, qs_ref[hm, band, :])
            top = jnp.full((8, 2 * micro), NEGATIVE, F32)
            for at in chunks:
                bias = bias_ref[hm, at, :]
                scores = scores_ref[at, :] * score_scale + jnp.concatenate([bias, bias], axis=1)
                scores_ref[at, :] = scores
                top = jnp.maximum(top, fold(scores, jnp.maximum))
            top = jnp.max(top, axis=0, keepdims=True)
            total = jnp.zeros((8, 2 * micro), F32)
            for at in chunks:
                exp_scores = jnp.exp(scores_ref[at, :] - top)
                scores_ref[at, :] = exp_scores
                total = total + fold(exp_scores, jnp.add)
            share_of = 1.0 / jnp.sum(total, axis=0, keepdims=True)
            for at in chunks:
                probs_ref[hm, at, band] = (scores_ref[at, :] * share_of).astype(BF16)
            out_t = mm(values_t, probs_ref[hm, :, band])
            mixed_ref[hm, :, band] = jnp.concatenate(
                [out_t[:, i * micro : (i + 1) * micro].T for i in range(2)], axis=1
            ).astype(BF16)
            return carry

        lax.fori_loop(0, heads // 2, pair_step, 0)

    save(kv_ref, out_kv_ref)
    attend(0)
    save(probs_ref.at[0], out_probs_ref.at[0])
    three.step(1, (1,), relay)
    attend(1)
    save(probs_ref.at[1], out_probs_ref.at[1])
    pass_all(2)
    pg_all[place.p] = take_rows(1).astype(BF16)
    cotangents.start()
    attend(2)
    save(probs_ref.at[2], out_probs_ref.at[2])
    three.step(2, (0,), relay)
    attend(3)
    save(probs_ref.at[3], out_probs_ref.at[3])

    def branch(h):
        return mm_nt(mixed_ref[pl.ds(2 * h, 2)].reshape(rows, heads * HEAD), full_ot[...])

    save(mixed_ref, out_mixed_ref)
    attn_wait(2)
    save(full_ot, out_full_ot)
    branch_out[...] = branch(other).astype(BF16)
    sent.remote(branch_out, branch_in, branch_sems.at[0], branch_sems.at[1], (d, other))
    own = branch(f)
    cotangents.pass_on()
    arrived(branch_in, branch_sems.at[1])
    middle = rows_out[...].astype(F32) + own + branch_in[...].astype(F32)
    middle_ref[...] = middle
    gain_two = gain_row(full_kvg, 1, chips, width, share)
    gain_two_ref[...] = gain_two
    n2_ref[...] = (middle * rms_scale(middle) * gain_two).astype(BF16)
    three.step(2, (1,), relay)
    three_start(2)
    for k in range(3, groups):
        three.step(k, (0, 1), relay)

    def relayed(a, k, use):
        pl.when(place.g >= k)(functools.partial(use, a, place.g - k))
        if k > 0:
            pl.when(place.g + k < groups)(functools.partial(use, a, place.g + k))

    def relay_wait(a, g):
        arrived(full_three.at[a, pl.ds(g * PLANE, PLANE), other], relay_recv.at[a, g])

    def relay_sent(a, g):
        relay_copy(a, g).wait_send()

    for a in range(3):
        for k in range(groups if a < 2 else 1):
            relayed(a, k, relay_wait)
            relayed(a, k, relay_sent)
    cotangents.wait()
    cotangents.finish()

    attn.finish()
    three.finish()
    for g in range(groups):
        for a in range(3):
            for j in range(1, PLANE if a == 0 else PLANE - 1):
                fan_copy(a, g, j).wait_send()
            if a > 0:
                pass_copy(a, g).wait_send()
    for a in range(3):
        for core in range(2):
            stage_copy(a, 1, core).wait_send()

        @pl.when(place.y != f)
        def _():
            for core in range(2):
                stage_copy(a, 0, core).wait_send()

        @pl.when(place.y == f)
        def _():
            pair_copy(a).wait_send()

    for j in range(1, reach + 1):
        pl.when(d + j < chips)(kv_copy(j).wait_send)
        pl.when(d - j >= 0)(kv_pass(j).wait_send)

    for copy in saves:
        copy.wait()
    sent.finish()


def forward(
    chips, reach, first_len, deal, key_t, value_t, gains, cosine, sine, tokens, cotangent, wq, wot, gate, up, down
):
    rows, width = tokens.shape
    share = wq.shape[0]
    groups = chips // PLANE
    part = gate.shape[1] // 2
    micro = rows // MICRO
    heads = wq.shape[1] // HEAD
    slots = 2 * reach + 2
    span = (2 * reach + 1) * micro
    dma = pltpu.SemaphoreType.DMA
    shape = jax.ShapeDtypeStruct
    small = (share + 16, HEAD)
    return pl.pallas_call(
        functools.partial(forward_kernel, chips, reach),
        out_shape=(
            shape((3, chips, 2, share // 2, part), BF16),
            shape((width, wq.shape[1]), BF16),
            shape((width, wq.shape[1]), BF16),
            shape((2, chips) + small, BF16),
            shape((rows, width), BF16),
            shape((PLANE, rows, width), BF16),
            shape((rows, rows), BF16),
            shape((rows, rows), BF16),
            shape((2, rows, width), BF16),
            shape((4, heads * micro, HEAD), BF16),
            shape((MICRO, slots, micro, 2 * HEAD), BF16),
            shape((4, span, heads * micro), BF16),
            shape((4, micro, heads * HEAD), BF16),
            shape((rows, width), F32),
            shape((rows, width), BF16),
            shape((1, width), F32),
        ),
        in_specs=[SM] + [VM] * 8 + [ANY] * 5,
        out_specs=(ANY,) * 4 + (VM,) * 4 + (ANY,) * 5 + (VM,) * 3,
        scratch_shapes=[
            pltpu.VMEM((HEAD, HEAD), F32),
            pltpu.VMEM(small, BF16),
            pltpu.VMEM((chips, 8, rows), jnp.int32),
            pltpu.VMEM((2, rows, width), BF16),
            pltpu.VMEM((2, rows, width), BF16),
            pltpu.VMEM((4, span, micro), F32),
            pltpu.VMEM((rows, width), BF16),
            pltpu.VMEM((rows, width), BF16),
            pltpu.VMEM((span, 2 * micro), F32),
            dma((chips,)),
            dma((chips,)),
            dma((2, chips)),
            dma((2, chips)),
            dma((3, groups)),
            dma((3, groups)),
            dma((3, groups)),
            dma((3, groups, PLANE)),
            dma((3, chips)),
            dma((2,)),
            dma((3, 2, 2)),
            dma((3, PLANE)),
            dma((3, groups)),
            dma((3, groups)),
            dma((3, groups)),
            dma((3, groups)),
            dma((3, groups)),
            dma((6,)),
            dma((PLANE, 2)),
            dma((2,)),
            dma((reach + 1, 2)),
            dma((slots,)),
            dma((2,)),
            dma((3,)),
            pltpu.VMEM((width, wq.shape[1]), BF16),
            pltpu.VMEM((width, wq.shape[1]), BF16),
            pltpu.VMEM((2, chips) + small, BF16),
            pltpu.VMEM((2, rows, width), BF16),
            pltpu.VMEM((4, heads * micro, HEAD), BF16),
            pltpu.VMEM((MICRO, slots, micro, 2 * HEAD), BF16),
            pltpu.VMEM((4, span, heads * micro), BF16),
            pltpu.VMEM((4, micro, heads * HEAD), BF16),
            dma((16,)),
        ],
        compiler_params=pltpu.CompilerParams(
            collective_id=0, has_side_effects=True, vmem_limit_bytes=VMEM_ASK
        ),
        name="gather_and_attention",
    )(
        first_len, deal.reshape(1, rows), key_t, value_t, gains, cosine, sine, tokens, cotangent, wq, wot, gate, up, down
    )


def norm_back(values, gain, grad):
    scale = rms_scale(values)
    unit = values * scale
    lifted = grad * gain
    gain_grad = jnp.sum(grad * unit, axis=0, keepdims=True)
    back = scale * (lifted - unit * jnp.mean(lifted * unit, axis=-1, keepdims=True))
    return back, gain_grad


class ChainSum:
    def __init__(
        self, place, value, got, last, give, up_sems, down_sems, recv_sems, last_sems, early=None
    ):
        self.place, self.value, self.got, self.last, self.give = place, value, got, last, give
        self.early = early or {}
        self.top = place.groups - 1
        self.up_sems, self.down_sems = up_sems, down_sems
        self.recv_sems, self.last_sems = recv_sems, last_sems
        self.has_up = place.g + 1 < place.groups
        self.has_down = place.g >= 1

    def hop(self, a, g, k, up):
        to_last = k == 1 and not up
        place = self.place
        return pltpu.make_async_remote_copy(
            src_ref=self.give(a, g),
            dst_ref=self.last(a) if to_last else self.got(a, g),
            send_sem=(self.up_sems if up else self.down_sems).at[a, g],
            recv_sem=self.last_sems.at[a] if to_last else self.recv_sems.at[a, g],
            device_id=(place.d + PLANE if up else place.d - PLANE, place.f),
            device_id_type=MESH,
        )

    def step(self, a, k):
        place = self.place

        def toward(up):
            g = place.g + k if up else place.g - k
            total = self.value(a, k, up)
            from_behind = self.has_down if up else self.has_up

            @pl.when(from_behind)
            def _():
                if a in self.early and k == self.top - 1:
                    behind = self.early[a]
                else:
                    behind = self.got(a, g)
                    arrived(behind, self.recv_sems.at[a, g])
                self.give(a, g)[...] = (total + behind[...].astype(F32)).astype(BF16)

            @pl.when(jnp.logical_not(from_behind))
            def _():
                self.give(a, g)[...] = total.astype(BF16)

            self.hop(a, g, k, up).start()

        pl.when(place.g + k < place.groups)(functools.partial(toward, True))
        pl.when(place.g >= k)(functools.partial(toward, False))

    def final(self, a):
        place = self.place
        got, last = self.got(a, place.g), self.last(a)

        @pl.when(self.has_down)
        def _():
            arrived(got, self.recv_sems.at[a, place.g])

        @pl.when(jnp.logical_not(self.has_down))
        def _():
            got[...] = jnp.zeros(got.shape, BF16)

        @pl.when(self.has_up)
        def _():
            arrived(last, self.last_sems.at[a])

        @pl.when(jnp.logical_not(self.has_up))
        def _():
            last[...] = jnp.zeros(last.shape, BF16)

        return self.value(a, 0, True) + got[...].astype(F32) + last[...].astype(F32)

    def finish(self, count):
        place = self.place
        for a in range(count):
            for k in range(1, self.top if a in self.early else self.top + 1):

                @pl.when(place.g + k < place.groups)
                def _():
                    self.hop(a, place.g + k, k, True).wait_send()

                @pl.when(place.g >= k)
                def _():
                    self.hop(a, place.g - k, k, False).wait_send()


class PlaneReduce:
    def __init__(self, place, give, got, relay, send_sems, recv_sems, relay_sems):
        self.place, self.give, self.got, self.relay = place, give, got, relay
        self.send_sems, self.recv_sems, self.relay_sems = send_sems, recv_sems, relay_sems
        self.half = give.shape[1] // 2

    def copy(self, which):
        place = self.place
        slot, side, over_x = ((2, 0, 1), (2, 1, 0), (0, 0, 1), (1, 1, 0), (0, 1, 1), (1, 0, 0))[which]
        band = pl.ds(side * self.half, self.half)
        if which < 2:
            dst, recv = self.relay.at[side], self.relay_sems.at[side]
        else:
            dst, recv = self.got.at[slot, band], self.recv_sems.at[slot, side]
        return pltpu.make_async_remote_copy(
            src_ref=self.give.at[slot, band] if which < 4 else self.relay.at[side],
            dst_ref=dst,
            send_sem=self.send_sems.at[which],
            recv_sem=recv,
            device_id=(place.plane_chip(1 if over_x else 2), place.f),
            device_id_type=MESH,
        )

    def start(self, turn):
        @pl.when(turn == 0)
        def _():
            self.copy(0).start()
            self.copy(1).start()

        @pl.when(turn == 1)
        def _():
            self.copy(2).start()

        @pl.when(turn == 2)
        def _():
            self.copy(3).start()

    def pass_on(self):
        for side, slot, which in ((0, 1, 5), (1, 0, 4)):
            arrived(self.relay.at[side], self.relay_sems.at[side])
            mine = self.give[slot, side * self.half : (side + 1) * self.half]
            self.relay[side] = (mine.astype(F32) + self.relay[side].astype(F32)).astype(BF16)
            self.copy(which).start()

    def total(self):
        for slot in range(2):
            for side in range(2):
                band = pl.ds(side * self.half, self.half)
                arrived(self.got.at[slot, band], self.recv_sems.at[slot, side])
        return self.got[0].astype(F32) + self.got[1].astype(F32)

    def finish(self):
        for which in range(6):
            self.copy(which).wait_send()


def mlp_kernel(
    chips,
    n2_own,
    middle_ref,
    pg_ref,
    gain_ref,
    three_hbm,
    out_total,
    out_give,
    two_ref,
    gain_grad_ref,
    half_ref,
    early_ref,
    down_sum,
    three_ref,
    hidden_ref,
    gate_rows_ref,
    up_rows_ref,
    two_give,
    two_got,
    two_relay,
    pair_got,
    down_grad,
    down_half,
    down_got,
    down_last,
    gate_ref,
    upward_ref,
    n2_all,
    n2_send,
    n2_recv,
    load_sems,
    rest_up,
    rest_down,
    rest_recv,
    rest_relay,
    rest_relayed,
    two_send,
    two_recv,
    two_relays,
    pair_send,
    pair_recv,
    down_up,
    down_down,
    down_recv,
    down_last_sems,
    early_send,
    early_recv,
):
    place = Place(chips)
    d, f, other = place.d, place.f, place.other
    groups = place.groups
    rows, width = middle_ref.shape
    wide = PLANE * rows
    part = three_ref.shape[-1]
    plane_width = width // groups
    loads = [
        pltpu.make_async_copy(three_hbm.at[a], three_ref.at[a], load_sems.at[0, a])
        for a in range(2)
    ]
    for load in loads:
        load.start()

    def planes(ref, g):
        return ref.at[2, pl.ds(g * PLANE, PLANE)]

    down_load = pltpu.make_async_copy(
        planes(three_hbm, place.g), planes(three_ref, place.g), load_sems.at[0, 2]
    )
    down_load.start()
    greet_near(place)

    def rest_hop(g, up, k):
        src = three_hbm if k == 0 else three_ref
        return pltpu.make_async_remote_copy(
            src_ref=src.at[2, pl.ds(g * PLANE, PLANE), f],
            dst_ref=three_ref.at[2, pl.ds(g * PLANE, PLANE), f],
            send_sem=(rest_up if up else rest_down).at[g],
            recv_sem=rest_recv.at[g],
            device_id=(d + PLANE if up else d - PLANE, f),
            device_id_type=MESH,
        )

    def rest_pass(g):
        ref = three_ref.at[2, pl.ds(g * PLANE, PLANE), f]
        return pltpu.make_async_remote_copy(
            src_ref=ref,
            dst_ref=ref,
            send_sem=rest_relay.at[g],
            recv_sem=rest_relayed.at[g],
            device_id=(d, other),
            device_id_type=MESH,
        )

    has_up, has_down = place.g + 1 < groups, place.g >= 1

    def rest_each(k, use):
        pl.when(place.g >= k)(lambda: use(place.g - k, True, has_up))
        pl.when(place.g + k < groups)(lambda: use(place.g + k, False, has_down))

    def rest_step(k):
        def use(g, up, more):
            arrived(three_ref.at[2, pl.ds(g * PLANE, PLANE), f], rest_recv.at[g])
            if k + 1 < groups:
                pl.when(more)(rest_hop(g, up, k).start)
            rest_pass(g).start()

        rest_each(k, use)

    def rest_hops(k, act):
        if k + 1 < groups:
            up, down = (rest_hop(place.g - k, True, k), rest_hop(place.g + k, False, k))
            pl.when((place.g >= k) & (place.g < groups - 1))(getattr(up, act))
            pl.when((place.g < groups - k) & (place.g >= 1))(getattr(down, act))

    def rest_finish(k):
        def use(g, up, more):
            rest_pass(g).wait_send()
            arrived(three_ref.at[2, pl.ds(g * PLANE, PLANE), other], rest_relayed.at[g])

        rest_hops(k, "wait_send")
        if k > 0:
            rest_each(k, use)

    n2 = PlaneSpread(place, n2_all, n2_send, n2_recv)
    n2_all[place.p] = n2_own[...]
    n2.start()
    rest_hops(0, "start")

    two = PlaneReduce(place, two_give, two_got, two_relay, two_send, two_recv, two_relays)
    curve = 0.7978845608028654
    cubic = 0.044715
    step_width = 2 * HEAD

    def weight(a, band):
        return three_ref[a, :, :, :, band].reshape(width, -1)

    def chunks(count):
        return range(0, count, 32)

    def forward_units(j, band, size):
        pos = place.plane_pos(j)
        x = n2_all[pos]
        gate_ref[:rows, :size] = mm(x, weight(0, band))
        upward_ref[:rows, :size] = mm(x, weight(1, band))
        for i in chunks(rows):
            gate = gate_ref[i : i + 32, :size]
            upward = upward_ref[i : i + 32, :size]
            square = gate * gate
            tanh = jnp.tanh(gate * (curve + (curve * cubic) * square))
            above = 0.5 * (1.0 + tanh)
            activated = gate * above
            slope = above + activated * (1.0 - tanh) * (curve + (3.0 * curve * cubic) * square)
            at = pl.ds(pl.multiple_of(pos * rows + i, 32), 32)
            hidden_ref[at, band] = (activated * upward).astype(BF16)
            gate_rows_ref[at, band] = (upward * slope).astype(BF16)
            up_rows_ref[at, band] = activated.astype(BF16)

    def backward_units(band, size):
        gate_ref[:, :size] = mm(pg_ref[...].reshape(wide, width), weight(2, band))
        for i in chunks(wide):
            at = slice(i, i + 32)
            grad_hidden = gate_ref[at, :size]
            gate_rows_ref[at, band] = (
                grad_hidden * gate_rows_ref[at, band].astype(F32)
            ).astype(BF16)
            up_rows_ref[at, band] = (grad_hidden * up_rows_ref[at, band].astype(F32)).astype(BF16)

    def over_units(body):
        full = part // step_width

        def step(i, carry):
            body(pl.ds(pl.multiple_of(i * step_width, step_width), step_width), step_width)
            return carry

        lax.fori_loop(0, full, step, 0)
        if part % step_width:
            body(pl.ds(full * step_width, part % step_width), part % step_width)

    def at_turn(i):
        return ((i + 2) % 3 + 1) * (1 - i // 3)

    def band_of(pos):
        return pl.ds(pl.multiple_of(pos * rows, rows), rows)

    def whole(a):
        return three_ref[a].reshape(width, part)

    def back_block(i, carry):
        band = band_of(place.plane_pos(at_turn(i)))
        back = mm_nt(gate_rows_ref[band, :], whole(0)) + mm_nt(up_rows_ref[band, :], whole(1))

        @pl.when(i < PLANE - 1)
        def _():
            two_give[(i + 2) % 3] = back.astype(BF16)

        @pl.when(i == PLANE - 1)
        def _():
            two_ref[...] = back

        two.start(i)
        return carry

    def out_block(i, carry):
        piece = mm_nt(hidden_ref[band_of(place.plane_pos(at_turn(i))), :], whole(2))

        @pl.when(i < PLANE - 1)
        def _():
            out_give[(i + 2) % 3] = piece.astype(BF16)

        @pl.when(i == PLANE - 1)
        def _():
            out_total[...] = (middle_ref[...] + piece).astype(BF16)

        return carry

    def grad_at(a, g, core):
        if a == 2:
            return down_grad.at[pl.ds(g * PLANE, PLANE), core]
        return three_ref.at[a, pl.ds(g * PLANE, PLANE), core]

    def pair_copy(a, g):
        return pltpu.make_async_remote_copy(
            src_ref=grad_at(a, g, other),
            dst_ref=pair_got.at[a, g],
            send_sem=pair_send.at[a, g],
            recv_sem=pair_recv.at[a, g],
            device_id=(d, other),
            device_id_type=MESH,
        )

    def weight_grad(a, left, right):
        def step(g, carry):
            at = pl.ds(pl.multiple_of(g * plane_width, 128), plane_width)
            piece = mm_tn(left[:, :, at].reshape(wide, plane_width), right[...]).astype(BF16)
            pieces = piece.reshape(PLANE, 2, plane_width // (2 * PLANE), part)
            for core in range(2):
                grad_at(a, g, core)[...] = pieces[:, core]
            pair_copy(a, g).start()
            return carry

        lax.fori_loop(0, groups, step, 0)

    def pair_sum(a, into):
        def step(g, carry):
            arrived(pair_got.at[a, g], pair_recv.at[a, g])
            into[g] = (grad_at(a, g, f)[...].astype(F32) + pair_got[a, g].astype(F32)).astype(BF16)
            return carry

        lax.fori_loop(0, groups, step, 0)

    down = ChainSum(
        place,
        lambda a, k, up: down_half[place.g + k if up else place.g - k].astype(F32),
        lambda a, g: down_got.at[g],
        lambda a: down_last.at[0],
        lambda a, g: down_got.at[g],
        down_up,
        down_down,
        down_recv,
        down_last_sems,
    )
    loads[0].wait()
    loads[1].wait()
    over_units(functools.partial(forward_units, 0))
    n2.pass_on()
    rest_step(1)
    for j in range(1, PLANE):
        n2.wait((j,))
        over_units(functools.partial(forward_units, j))
        if j == 2:
            for k in range(2, min(3, groups)):
                rest_step(k)
    weight_grad(2, pg_ref, hidden_ref)
    for k in range(3, groups):
        rest_step(k)
    for k in range(groups):
        rest_finish(k)
    down_load.wait()
    over_units(backward_units)
    pair_sum(2, down_half)
    for k in range(groups - 1, 2, -1):
        down.step(0, k)
    lax.fori_loop(0, PLANE, back_block, 0)
    for k in range(min(2, groups - 1), 1, -1):
        down.step(0, k)
    def early_copy(a, bottom):
        return pltpu.make_async_remote_copy(
            src_ref=half_ref.at[a, groups - 1 if bottom else 0],
            dst_ref=early_ref,
            send_sem=early_send.at[a],
            recv_sem=early_recv.at[a],
            device_id=(d + PLANE if bottom else d - PLANE, f),
            device_id_type=MESH,
        )

    def early_start(a):
        pl.when(place.g == 0)(early_copy(a, True).start)
        pl.when(place.g == groups - 1)(early_copy(a, False).start)

    weight_grad(0, n2_all, gate_rows_ref)
    two.pass_on()
    pair_sum(0, half_ref.at[0])
    early_start(0)
    lax.fori_loop(0, PLANE, out_block, 0)
    down.step(0, 1)
    weight_grad(1, n2_all, up_rows_ref)
    pair_sum(1, half_ref.at[1])
    grad_two = two_ref[...] + two.total()
    back, gain_grad_ref[...] = norm_back(middle_ref[...], gain_ref[...], grad_two)
    two_ref[...] = pg_ref[place.p].astype(F32) + back
    down_sum[...] = down.final(0).astype(BF16)
    two.finish()
    n2.finish()
    for a in range(3):
        for g in range(groups):
            pair_copy(a, g).wait_send()
    down.finish(1)
    pl.when(place.g == 0)(early_copy(0, True).wait_send)
    pl.when(place.g == groups - 1)(early_copy(0, False).wait_send)

    @pl.when((place.g == 1) | (place.g == groups - 2))
    def _():
        arrived(early_ref, early_recv.at[0])


def mlp(chips, n2, middle, pg, gain_two, three):
    rows, width = middle.shape
    part = three.shape[-1]
    groups = chips // PLANE
    dma = pltpu.SemaphoreType.DMA
    shape = jax.ShapeDtypeStruct
    wide = PLANE * rows
    column = (groups, PLANE) + three.shape[3:]
    return pl.pallas_call(
        functools.partial(mlp_kernel, chips),
        out_shape=(
            shape((rows, width), BF16),
            shape((PLANE - 1, rows, width), BF16),
            shape((rows, width), F32),
            shape((1, width), F32),
            shape((2,) + column, BF16),
            shape(column[1:], BF16),
            shape(column[1:], BF16),
        ),
        in_specs=[VM] * 4 + [ANY],
        out_specs=(VM,) * 5 + (ANY, VM),
        scratch_shapes=[
            pltpu.VMEM(three.shape, BF16),
            pltpu.VMEM((wide, part), BF16),
            pltpu.VMEM((wide, part), BF16),
            pltpu.VMEM((wide, part), BF16),
        ]
        + [
            pltpu.VMEM((PLANE - 1, rows, width), BF16),
            pltpu.VMEM((2, rows, width), BF16),
            pltpu.VMEM((2, rows // 2, width), BF16),
            pltpu.VMEM((3,) + column, BF16),
            pltpu.VMEM(three.shape[1:], BF16),
            pltpu.VMEM(column, BF16),
            pltpu.VMEM(column, BF16),
            pltpu.VMEM((1,) + column[1:], BF16),
            pltpu.VMEM((wide, 2 * HEAD), F32),
            pltpu.VMEM((wide, 2 * HEAD), F32),
            pltpu.VMEM((PLANE, rows, width), BF16),
            dma((6,)),
            dma((PLANE, 2)),
            dma((2, max(3, groups))),
        ]
        + [dma((groups,))] * 5
        + [
            dma((6,)),
            dma((2, 2)),
            dma((2,)),
            dma((3, groups)),
            dma((3, groups)),
            dma((1, groups)),
            dma((1, groups)),
            dma((1, groups)),
            dma((1,)),
            dma((1,)),
            dma((1,)),
        ],
        compiler_params=pltpu.CompilerParams(
            collective_id=1, has_side_effects=True, vmem_limit_bytes=VMEM_ASK
        ),
        name="mlp_both_ways",
    )(n2, middle, pg, gain_two, three)


def backward_kernel(
    chips,
    reach,
    hbm_out_own,
    out_give,
    down_sum,
    early_ref,
    hbm_rows_ref,
    grad_middle_ref,
    gain_two_grad_ref,
    hbm_n1_ref,
    hbm_qs_ref,
    hbm_kv_ref,
    hbm_mixed_ref,
    hbm_wq_ref,
    wot_ref,
    hbm_kvg_ref,
    cos_ref,
    sin_ref,
    hbm_take_ref,
    place_ref,
    probs_hbm,
    half_hbm,
    three_end,
    q_out,
    ot_out,
    kvg_out,
    output_ref,
    input_grad_ref,
    probs_ref,
    low_ref,
    mixed_rows,
    grad_mixed,
    grad_q,
    kv_total,
    kv_give,
    kv_pair,
    kv_got,
    one_out,
    one_in,
    three_got,
    three_last,
    three_stage,
    heads_ref,
    plane_relay,
    plane_got,
    column_got,
    column_last,
    column_give,
    gkvg_ref,
    gkvg_pair,
    small_got,
    small_give,
    small_column,
    give,
    got,
    probs_sems,
    stage_sems,
    low_sems,
    kv_send,
    kv_recv,
    one_sems,
    three_up,
    three_down,
    three_recv,
    three_last_sems,
    end_send,
    end_recv,
    direct_send,
    relay_send,
    relay_recv,
    plane_recv,
    small_send,
    small_recv,
    column_up,
    column_down,
    column_recv,
    column_last_sems,
    row_send,
    row_recv,
    grad_probs_ref,
    grad_scores_ref,
    out_got,
    out_relay,
    out_send,
    out_recv,
    out_relays,
    mixed_ref,
    qs_ref,
    kv_ref,
    out_own,
    n1_ref,
    wq_ref,
    kvg_ref,
    rows_ref,
    take_ref,
    late_sems,
):
    place = Place(chips)
    d, f, other = place.d, place.f, place.other
    groups = place.groups
    rows, width = grad_middle_ref.shape
    micro = rows // MICRO
    heads = wq_ref.shape[1] // HEAD
    share = width // chips
    half = share // 2
    part = half_hbm.shape[-1]
    per = rows // chips
    span = (2 * reach + 1) * micro
    by_x, by_y, far = (place.plane_pos(j) for j in range(1, PLANE))
    to_x, to_y = place.plane_chip(1), place.plane_chip(2)
    sent = Sent()

    pairs = heads // 2

    def probs_copy(n):
        band = pl.ds(pl.multiple_of((n % pairs) * 2 * micro, 2 * micro), 2 * micro)
        return pltpu.make_async_copy(
            probs_hbm.at[n // pairs, :, band], probs_ref.at[n % 2], probs_sems.at[n % 2]
        )

    probs_copy(0).start()
    late = {}
    for n, (name, src, dst) in enumerate(
        (
            ("mixed", hbm_mixed_ref, mixed_ref),
            ("qs", hbm_qs_ref, qs_ref),
            ("kv", hbm_kv_ref, kv_ref),
            ("out_own", hbm_out_own, out_own),
            ("n1", hbm_n1_ref, n1_ref),
            ("wq", hbm_wq_ref, wq_ref),
            ("kvg", hbm_kvg_ref, kvg_ref),
            ("rows", hbm_rows_ref, rows_ref),
            ("take", hbm_take_ref, take_ref),
        )
    ):
        late[name] = pltpu.make_async_copy(src, dst, late_sems.at[n])
        late[name].start()
    greet_wide(place)

    events = [(1, groups - 1)] + [(a, k) for k in range(groups - 2, -1, -1) for a in range(2)]

    def stage_copy(n, up):
        a, k = events[n]
        slot = 0 if up else 1
        return pltpu.make_async_copy(
            half_hbm.at[a, place.g + k if up else place.g - k],
            three_stage.at[n % 2, slot],
            stage_sems.at[n % 2, slot],
        )

    def fetch(n):
        k = events[n][1]
        pl.when(place.g + k < groups)(stage_copy(n, True).start)
        if k > 0:
            pl.when(place.g >= k)(stage_copy(n, False).start)

    def three_value(a, k, up):
        n = events.index((a, k))
        stage_copy(n, up).wait()
        return three_stage[n % 2, 0 if up else 1].astype(F32)

    out = PlaneReduce(place, out_give, out_got, out_relay, out_send, out_recv, out_relays)
    for which in range(4):
        out.copy(which).start()
    fetch(0)
    three = ChainSum(
        place,
        three_value,
        lambda a, g: three_got.at[a, g],
        lambda a: three_last.at[a],
        lambda a, g: three_got.at[a, g],
        three_up,
        three_down,
        three_recv,
        three_last_sems,
        early={0: early_ref},
    )

    def three_steps(k, arrays=(0, 1)):
        for a in arrays:
            fetch(events.index((a, k)) + 1)
            three.step(a, k)

    three_steps(groups - 1, (1,))
    three_steps(groups - 2, (0,))
    middle_steps = [(k, (a,)) for a, k in events[2:-2]]

    outermost = (place.g == 0) | (place.g == groups - 1)

    @pl.when(outermost)
    def _():
        for step in middle_steps:
            three_steps(*step)


    low_ref[f] = grad_middle_ref[...].astype(BF16)
    sent.remote(low_ref.at[f], low_ref.at[f], low_sems.at[0], low_sems.at[1], (d, other))
    kv_total[...] = jnp.zeros_like(kv_total)

    def block(k):
        return pl.ds(pl.multiple_of(k * per, per), per)

    home = (Sent(), Sent())

    def rows_home(i, values):
        if i > 0:
            home[i - 1].finish()
        give[...] = mm_tn(place_ref[...], values).astype(BF16)
        for k in range(1, chips):
            to = (d + k) % chips
            home[i].remote(
                give.at[block(to)],
                got.at[i, block(d)],
                row_send.at[i, k],
                row_recv.at[i, d],
                (to, f),
            )
        got[i, block(d), :] = give[block(d), :]

    def rows_back(i):
        for k in range(1, chips):
            s = (d + k) % chips
            arrived(got.at[i, block(s)], row_recv.at[i, s])
        return mm_tn(take_ref[...], got[i]).astype(BF16)

    def mix_back(h):
        grads = mm(low_ref[h], wot_ref[...])
        for m in range(MICRO):
            for i in range(heads):
                grad_mixed[2 * h + m, i * micro : (i + 1) * micro, :] = grads[
                    m * micro : (m + 1) * micro, i * HEAD : (i + 1) * HEAD
                ].astype(BF16)

    mix_back(f)
    arrived(low_ref.at[other], low_sems.at[1])
    mix_back(other)

    def end_copy(a, j):
        pos = place.plane_pos(j)
        src = down_sum.at[pos] if a == 2 else three_got.at[a, place.g, pos]
        return pltpu.make_async_remote_copy(
            src_ref=src,
            dst_ref=three_end.at[a, place.x, f],
            send_sem=end_send.at[a, j],
            recv_sem=end_recv.at[a, place.x, f],
            device_id=(place.plane_chip(j), place.y),
            device_id_type=MESH,
        )

    def end_local(a):
        src = down_sum.at[place.p] if a == 2 else three_got.at[a, place.g, place.p]
        return pltpu.make_async_copy(src, three_end.at[a, place.x, f], end_send.at[a, 0])

    def end_start(a):
        for j in range(1, PLANE):
            end_copy(a, j).start()
        pl.when(place.y == f)(end_local(a).start)
        pl.when(place.y != f)(end_copy(a, 0).start)

    def whole(g, pos):
        return pl.ds(pl.multiple_of((g * PLANE + pos) * share, 16), share)

    def term(a, g, pos):
        return heads_ref.at[a, whole(g, pos)]

    def plane_copy(kind, a, g):
        even = g % 2 == 0
        near_pos, near_to, near_side = (by_x, to_x, 0) if even else (by_y, to_y, 1)
        if kind == 0:
            src, dst, to = term(a, g, near_pos), plane_got.at[a, near_side, g], near_to
            send, recv = direct_send.at[a, 0, g], plane_recv.at[a, near_side, g]
        elif kind == 1:
            src, dst, to = term(a, g, far), plane_relay.at[a, g], near_to
            send, recv = direct_send.at[a, 1, g], relay_recv.at[a, g]
        else:
            side = 1 - near_side
            src, dst, to = plane_relay.at[a, g], plane_got.at[a, side, g], to_y if even else to_x
            send, recv = relay_send.at[a, g], plane_recv.at[a, side, g]
        return pltpu.make_async_remote_copy(
            src_ref=src,
            dst_ref=dst,
            send_sem=send,
            recv_sem=recv,
            device_id=(to, f),
            device_id_type=MESH,
        )

    def plane_start(a):
        for g in range(groups):
            plane_copy(1, a, g).start()
            plane_copy(0, a, g).start()

    def plane_pass(a):
        for g in range(groups):
            arrived(plane_relay.at[a, g], relay_recv.at[a, g])
            mine = term(a, g, by_y if g % 2 == 0 else by_x)
            plane_relay[a, g] = (plane_relay[a, g].astype(F32) + mine[...].astype(F32)).astype(BF16)
            plane_copy(2, a, g).start()

    def plane_total(a, k, up):
        g = place.g + k if up else place.g - k
        total = term(a, g, place.p)[...].astype(F32)
        for side in range(2):
            arrived(plane_got.at[a, side, g], plane_recv.at[a, side, g])
            total = total + plane_got[a, side, g].astype(F32)
        return total

    column = ChainSum(
        place,
        plane_total,
        lambda a, g: column_got.at[a, g],
        lambda a: column_last.at[a],
        lambda a, g: column_give.at[a, g],
        column_up,
        column_down,
        column_recv,
        column_last_sems,
    )

    tile = 2 * HEAD

    def head_grads(a, left_ref):
        def step(i, carry):
            at = pl.ds(pl.multiple_of(i * tile, tile), tile)
            left = left_ref[:, :, at].reshape(2 * rows, tile)
            heads_ref[a, at, :] = mm_tn(left, mixed_rows[...]).astype(BF16)
            return carry

        lax.fori_loop(0, width // tile, step, 0)

    late["mixed"].wait()
    for hm in range(4):
        mixed_rows[hm * micro : (hm + 1) * micro, :] = mixed_ref[hm]
    head_grads(0, low_ref)
    plane_start(0)
    end_start(2)
    out.pass_on()

    score_scale = HEAD ** (-0.5)
    chunks = [slice(i, i + 64) for i in range(0, span, 64)]

    def attend_back(hm):
        h, m = hm // 2, hm % 2
        at = slice(h, h + 2 * reach + 1)
        keys = kv_ref[m, at, :, 0:HEAD].reshape(span, HEAD)
        values = kv_ref[m, at, :, HEAD:].reshape(span, HEAD)
        keys_t = keys.T

        def pair_step(pair, carry):
            band = pl.ds(pl.multiple_of(pair * 2 * micro, 2 * micro), 2 * micro)
            n = hm * pairs + pair
            probs_copy(n).wait()
            pl.when(n + 1 < 4 * pairs)(lambda: probs_copy(n + 1).start())
            grads = grad_mixed[hm, band, :]
            queries = qs_ref[hm, band, :]
            grad_probs_ref[...] = mm_nt(values, grads)
            delta = jnp.zeros((8, 2 * micro), F32)
            for part_at in chunks:
                wide = probs_ref[n % 2, part_at, :].astype(F32)
                delta = delta + fold(grad_probs_ref[part_at, :] * wide, jnp.add)
            delta = jnp.sum(delta, axis=0, keepdims=True)
            for part_at in chunks:
                wide = probs_ref[n % 2, part_at, :].astype(F32)
                grad_scores_ref[part_at, :] = (
                    wide * (grad_probs_ref[part_at, :] - delta)
                ).astype(BF16)
            grad_scores = grad_scores_ref[...]
            value_total = mm(probs_ref[n % 2], grads).reshape(2 * reach + 1, micro, HEAD)
            kv_total[m, at, :, HEAD:] = kv_total[m, at, :, HEAD:] + value_total
            key_total = mm(grad_scores, queries).reshape(2 * reach + 1, micro, HEAD)
            kv_total[m, at, :, 0:HEAD] = kv_total[m, at, :, 0:HEAD] + key_total
            query_t = mm(keys_t, grad_scores) * score_scale
            grad_q[hm, :, band] = jnp.concatenate(
                [
                    turned(
                        query_t[:, i * micro : (i + 1) * micro].T, cos_ref[hm], -sin_ref[hm]
                    )
                    for i in range(2)
                ],
                axis=1,
            ).astype(BF16)
            return carry

        lax.fori_loop(0, heads // 2, pair_step, 0)

    turns = iter(middle_steps)

    def next_step():
        for step in turns:

            @pl.when(jnp.logical_not(outermost))
            def _():
                three_steps(*step)

            break

    late["qs"].wait()
    late["kv"].wait()
    attend_back(0)
    next_step()
    attend_back(1)
    next_step()
    attend_back(2)
    plane_pass(0)
    next_step()
    attend_back(3)

    for m in range(MICRO):
        for slot in range(2 * reach + 2):
            kv_total[m, slot, :, 0:HEAD] = kv_total[m, slot, :, 0:HEAD] * score_scale
            kv_give[m, slot] = kv_total[m, slot].astype(BF16)
    own_slots = [2 * j + f for j in range(reach + 1)]
    other_slots = [2 * j + other for j in range(reach + 1)]
    for j in range(reach + 1):
        sent.remote(
            kv_give.at[:, other_slots[j]],
            kv_pair.at[:, j],
            kv_send.at[0, j],
            kv_recv.at[0, j],
            (d, other),
        )

    def kv_copy(j):
        return pltpu.make_async_remote_copy(
            src_ref=kv_give.at[:, own_slots[reach - j]],
            dst_ref=kv_got.at[j],
            send_sem=kv_send.at[1, j],
            recv_sem=kv_recv.at[1, j],
            device_id=(d - j, f),
            device_id_type=MESH,
        )

    for hm in range(4):
        mixed_rows[hm * micro : (hm + 1) * micro, :] = grad_q[hm]
    column_steps = [k for k in range(groups - 1, 0, -1)]
    late["n1"].wait()
    head_grads(1, n1_ref)
    plane_start(1)
    column.step(0, column_steps[0])
    for j in range(reach, -1, -1):
        s = reach - j
        arrived(kv_pair.at[:, s], kv_recv.at[0, s])
        total = kv_total[:, own_slots[s]] + kv_pair[:, s].astype(F32)
        kv_total[:, own_slots[s]] = total
        if j > 0:
            kv_give[:, own_slots[s]] = total.astype(BF16)

            @pl.when(d - j >= 0)
            def _():
                kv_copy(j).start()

    def one_back(h):
        at = pl.ds(pl.multiple_of(h * rows, rows), rows)
        return mm_nt(mixed_rows[at, :], wq_ref[...])

    for k in column_steps[1:2]:
        column.step(0, k)
    for _ in middle_steps[3:]:
        next_step()
    late["wq"].wait()
    one_out[...] = one_back(other).astype(BF16)
    sent.remote(one_out, one_in, one_sems.at[0], one_sems.at[1], (d, other))
    grad_one = one_back(f)
    for k in column_steps[2:]:
        column.step(0, k)
    plane_pass(1)
    late["out_own"].wait()
    rows_home(0, (out_own[...].astype(F32) + out.total()).astype(BF16))

    sums = [kv_total[m, 2 * reach + f] for m in range(MICRO)]
    for j in range(1, reach + 1):

        @pl.when(d + j < chips)
        def _():
            arrived(kv_got.at[j], kv_recv.at[1, j])

        @pl.when(d + j >= chips)
        def _():
            kv_got[j] = jnp.zeros((MICRO, micro, 2 * HEAD), BF16)

        sums = [sums[m] + kv_got[j, m].astype(F32) for m in range(MICRO)]
    key_rows = jnp.concatenate(
        [
            turned(sums[m][:, 0:HEAD], cos_ref[2 * f + m], -sin_ref[2 * f + m])
            for m in range(MICRO)
        ],
        axis=0,
    )
    value_rows = jnp.concatenate([sums[m][:, HEAD:] for m in range(MICRO)], axis=0)
    pieces = halves_in(key_rows, value_rows)
    late["kvg"].wait()
    late["rows"].wait()
    row_values = rows_ref[...].astype(F32)
    for i in range(2):
        piece = pieces[i].astype(BF16)
        gkvg_ref[i, :, 0:share, :] = mm_tn(n1_ref[f], piece).astype(BF16).reshape(chips, share, HEAD)
        grad_one = grad_one + mm_nt(piece, kvg_ref[i, :, 0:share, :].reshape(width, HEAD))
    arrived(one_in, one_sems.at[1])
    grad_one = grad_one + one_in[...].astype(F32)
    gain_one = gain_row(kvg_ref, 0, chips, width, share)
    back_one, gain_one_grad = norm_back(row_values, gain_one, grad_one)
    one_in[...] = (grad_middle_ref[...] + back_one).astype(BF16)
    spread = gain_spread(width, share)
    stretch = own_stretch(chips, width, share)
    for i, grad in enumerate((gain_one_grad, gain_two_grad_ref[...])):
        piece = mm_nt(jnp.where(stretch, grad, 0.0).astype(BF16), spread)
        row = iota((chips, 16, HEAD), 1)
        gkvg_ref[i, :, share : share + 16, :] = jnp.where(
            row == 0, piece[:, None, :], 0.0
        ).astype(BF16)
    sent.remote(gkvg_ref.at[other], gkvg_pair, small_send.at[0], small_recv.at[0], (d, other))
    arrived(gkvg_pair, small_recv.at[0])

    def small_sum(s):
        return gkvg_ref[f, s].astype(F32) + gkvg_pair[s].astype(F32)

    for j in range(1, PLANE):
        pos = place.plane_pos(j)
        for g in range(groups):
            small_give[j, g] = small_sum(g * PLANE + pos).astype(BF16)
        sent.remote(
            small_give.at[j],
            small_got.at[j],
            small_send.at[j],
            small_recv.at[j],
            (place.plane_chip(j), f),
        )

    column.step(1, column_steps[0])
    rows_home(1, one_in[...])
    for a in range(2):
        if a == 0:
            fetch(events.index((1, 0)))
        three_got[a, place.g] = three.final(a).astype(BF16)
        end_start(a)
    for k in column_steps[1:]:
        column.step(1, k)
    for j in range(1, PLANE):
        arrived(small_got.at[j], small_recv.at[j])
    for k in range(1, groups):
        g = (place.g + k) % groups
        s = g * PLANE + place.p
        total = small_sum(s)
        for j in range(1, PLANE):
            total = total + small_got[j, g].astype(F32)
        small_give[0, g] = total.astype(BF16)
        sent.remote(
            small_give.at[0, g],
            small_column.at[place.g],
            small_send.at[PLANE + k],
            small_recv.at[PLANE + place.g],
            (s, f),
        )
    total = small_sum(d)
    for j in range(1, PLANE):
        total = total + small_got[j, place.g].astype(F32)
    kvg_out[...] = total

    late["take"].wait()
    output_ref[...] = rows_back(0)
    for a in range(2):
        (ot_out, q_out)[a][...] = column.final(a)
    for k in range(1, groups):
        g = (place.g + k) % groups
        arrived(small_column.at[g], small_recv.at[PLANE + g])
        kvg_out[...] = kvg_out[...] + small_column[g].astype(F32)
    input_grad_ref[...] = rows_back(1)
    for a in (2, 0, 1):
        for cx in range(2):
            for core in range(2):
                own = (place.y == f) & (place.x == cx) & (core == f)

                @pl.when(own)
                def _():
                    end_local(a).wait()

                @pl.when(jnp.logical_not(own))
                def _():
                    arrived(three_end.at[a, cx, core], end_recv.at[a, cx, core])

    out.finish()
    three.finish(2)
    column.finish(2)
    for a in range(3):
        for j in range(1, PLANE):
            end_copy(a, j).wait_send()
        pl.when(place.y != f)(end_copy(a, 0).wait_send)
    for a in range(2):
        for g in range(groups):
            for kind in range(3):
                plane_copy(kind, a, g).wait_send()
    for j in range(1, reach + 1):

        @pl.when(d - j >= 0)
        def _():
            kv_copy(j).wait_send()

    home[1].finish()
    sent.finish()


def backward(chips, reach, out_own, out_give, down_sum, early, rows_in, grad_middle, gain_two_grad, n1, qs, kv, mixed, wq, wot, kvg, cosine, sine, take, placing, probs, halves):
    rows, width = rows_in.shape
    micro = rows // MICRO
    heads_wide = wq.shape[1]
    heads = heads_wide // HEAD
    groups = chips // PLANE
    share = width // chips
    half, part = halves.shape[3:]
    slots = 2 * reach + 2
    small = kvg.shape[2:]
    dma = pltpu.SemaphoreType.DMA
    shape = jax.ShapeDtypeStruct
    vm = pltpu.VMEM
    kv_shape = (MICRO, slots, micro, 2 * HEAD)
    return pl.pallas_call(
        functools.partial(backward_kernel, chips, reach),
        out_shape=(
            shape((3, 2, 2, half, part), BF16),
            shape((share, heads_wide), F32),
            shape((share, heads_wide), F32),
            shape(small, F32),
            shape((rows, width), BF16),
            shape((rows, width), BF16),
        ),
        in_specs=[
            ANY, VM, VM, VM, ANY, VM, VM, ANY, ANY, ANY, ANY, ANY, VM, ANY, VM, VM, ANY, VM, ANY, ANY,
        ],
        out_specs=(ANY,) + (VM,) * 5,
        scratch_shapes=[
            vm((2, probs.shape[1], 2 * micro), BF16),
            vm((2, rows, width), BF16),
            vm((2 * rows, heads_wide), BF16),
            vm((4, heads * micro, HEAD), BF16),
            vm((4, micro, heads_wide), BF16),
            vm(kv_shape, F32),
            vm(kv_shape, BF16),
            vm((MICRO, reach + 1, micro, 2 * HEAD), BF16),
            vm((reach + 1, MICRO, micro, 2 * HEAD), BF16),
            vm((rows, width), BF16),
            vm((rows, width), BF16),
            vm((2, groups, PLANE, half, part), BF16),
            vm((2, PLANE, half, part), BF16),
            vm((2, 2, PLANE, half, part), BF16),
            vm((2, width, heads_wide), BF16),
            vm((2, groups, share, heads_wide), BF16),
            vm((2, 2, groups, share, heads_wide), BF16),
            vm((2, groups, share, heads_wide), BF16),
            vm((2, share, heads_wide), BF16),
            vm((2, groups, share, heads_wide), BF16),
            vm((2, chips) + small, BF16),
            vm((chips,) + small, BF16),
            vm((PLANE, groups) + small, BF16),
            vm((PLANE, groups) + small, BF16),
            vm((groups,) + small, BF16),
            vm((rows, width), BF16),
            vm((2, rows, width), BF16),
            dma((2,)),
            dma((2, 2)),
            dma((2,)),
            dma((2, reach + 1)),
            dma((2, reach + 1)),
            dma((2,)),
            dma((2, groups)),
            dma((2, groups)),
            dma((2, groups)),
            dma((2,)),
            dma((3, PLANE)),
            dma((3, 2, 2)),
            dma((2, 2, groups)),
            dma((2, groups)),
            dma((2, groups)),
            dma((2, 2, groups)),
            dma((PLANE + groups,)),
            dma((PLANE + groups,)),
            dma((2, groups)),
            dma((2, groups)),
            dma((2, groups)),
            dma((2,)),
            dma((2, chips)),
            dma((2, chips)),
            vm((probs.shape[1], 2 * micro), F32),
            vm((probs.shape[1], 2 * micro), BF16),
            vm((2, rows, width), BF16),
            vm((2, rows // 2, width), BF16),
            dma((6,)),
            dma((2, 2)),
            dma((2,)),
        ]
        + [
            vm(one.shape, one.dtype)
            for one in (mixed, qs, kv, out_own, n1, wq, kvg, rows_in, take)
        ]
        + [dma((9,))],
        compiler_params=pltpu.CompilerParams(
            collective_id=2, has_side_effects=True, vmem_limit_bytes=VMEM_ASK
        ),
        name="attention_backward_and_scatter",
    )(out_own, out_give, down_sum, early, rows_in, grad_middle, gain_two_grad, n1, qs, kv, mixed, wq, wot, kvg, cosine, sine, take, placing, probs, halves)


def hand_over_kernel(
    three_ref,
    q_ref,
    ot_ref,
    kvg_ref,
    rows_ref,
    rows_grad_ref,
    output_ref,
    input_grad_ref,
    q_out,
    key_out,
    value_out,
    ot_out,
    gate_out,
    up_out,
    down_out,
    gains_out,
):
    half, part = three_ref.shape[3:]
    share = 2 * half
    key_columns = key_out.shape[0]
    output_ref[...] = rows_ref[...]
    input_grad_ref[...] = rows_grad_ref[...]
    q_out[...] = q_ref[...]
    ot_out[...] = ot_ref[...]
    square = jnp.concatenate(
        [kvg_ref[...], jnp.zeros((HEAD - kvg_ref.shape[0], HEAD), F32)], axis=0
    ).T
    key_out[...] = square[0:key_columns, 0:share]
    value_out[...] = square[key_columns : 2 * key_columns, 0:share]
    gains_out[...] = kvg_ref[share : share + 1, 0:share]
    for a, out in enumerate((gate_out, up_out, down_out)):
        for cx in range(2):
            for core in range(2):
                out[half * core : half * (core + 1), cx * part : (cx + 1) * part] = three_ref[
                    a, cx, core
                ].astype(F32)


def hand_over(key_columns, three, q, ot, kvg, rows, rows_grad):
    half, part = three.shape[3:]
    share = 2 * half
    shape = jax.ShapeDtypeStruct
    return pl.pallas_call(
        hand_over_kernel,
        out_shape=(
            shape(rows.shape, BF16),
            shape(rows.shape, BF16),
            shape(q.shape, F32),
            shape((key_columns, share), F32),
            shape((key_columns, share), F32),
            shape(ot.shape, F32),
            shape((share, 2 * part), F32),
            shape((share, 2 * part), F32),
            shape((share, 2 * part), F32),
            shape((1, share), F32),
        ),
        in_specs=[VM] * 6,
        out_specs=(VM,) * 10,
        compiler_params=pltpu.CompilerParams(vmem_limit_bytes=VMEM_ASK),
        name="hand_over",
    )(three, q, ot, kvg, rows, rows_grad)


def planned(
    tokens,
    cotangent,
    deal,
    first_len,
    w_query,
    w_key,
    w_value,
    w_out,
    w_gate,
    w_up,
    w_down,
    norm_gains,
):
    chips = lax.axis_size("dp")
    rows, width = tokens.shape
    micro = rows // MICRO
    share = w_query.shape[0]
    back_blocks = min(2 * chips - 1, (WINDOW + micro - 2) // micro)
    reach = (back_blocks + 1) // 2
    d = lax.axis_index("dp")
    inside = jnp.arange(micro, dtype=jnp.int32)
    positions = (2 * d + jnp.arange(2, dtype=jnp.int32))[:, None, None] * micro + inside
    second = positions >= first_len[None, :, None]
    within = positions - jnp.where(second, first_len[None, :, None], 0)
    cosine, sine = angles(within.reshape(-1))
    cosine = jnp.concatenate([cosine, cosine], axis=1).reshape(4, micro, HEAD)
    sine = jnp.concatenate([-sine, sine], axis=1).reshape(4, micro, HEAD)
    (
        three, wq, wot, kvg_all, rows_in, pg, take, placing, n1, qs, kv, probs, mixed, middle, n2, gain_two
    ) = forward(
        chips, reach, first_len, deal, w_key.T, w_value.T, norm_gains, cosine, sine, tokens, cotangent,
        w_query, w_out.T, w_gate, w_up, w_down.T,
    )
    out_own, out_give, grad_middle, gain_two_grad, halves, early, down_sum = mlp(
        chips, n2, middle, pg, gain_two, three
    )
    three_out, q_out, ot_out, kvg_out, output, input_grad = backward(
        chips, reach, out_own, out_give, down_sum, early, rows_in, grad_middle, gain_two_grad, n1, qs, kv, mixed, wq, wot,
        kvg_all, cosine, sine, take, placing, probs, halves,
    )
    output, input_grad, q_out, key_out, value_out, ot_out, gate_out, up_out, down_out, gains_out = hand_over(
        w_key.shape[1], three_out, q_out, ot_out, kvg_out, output, input_grad
    )
    return (
        output,
        input_grad,
        q_out,
        key_out.T,
        value_out.T,
        ot_out.T,
        gate_out,
        up_out,
        down_out.T,
        gains_out,
    )


def fits_plan(mesh, share):
    chips = mesh.shape["dp"]
    whole = share % 32 == 0 and share < HEAD
    return mesh.shape["fsdp"] == 2 and chips % PLANE == 0 and chips // PLANE >= 4 and whole


def solution(mesh):
    in_specs = (
        P(("dp", "fsdp"), None),
        P(("dp", "fsdp"), None),
        P(("dp", "fsdp")),
        P(),
        P("dp", "fsdp"),
        P("dp", "fsdp"),
        P("dp", "fsdp"),
        P("fsdp", "dp"),
        P("dp", "fsdp"),
        P("dp", "fsdp"),
        P("fsdp", "dp"),
        P("fsdp", "dp"),
    )
    out_specs = (
        P(("dp", "fsdp"), None),
        P(("dp", "fsdp"), None),
        P("dp", "fsdp"),
        P("dp", "fsdp"),
        P("dp", "fsdp"),
        P("fsdp", "dp"),
        P("dp", "fsdp"),
        P("dp", "fsdp"),
        P("fsdp", "dp"),
        P("fsdp", "dp"),
    )
    def placed(*arrays):
        share = arrays[4].shape[0] // mesh.shape["dp"]
        program = planned if fits_plan(mesh, share) else per_device
        return jax.shard_map(
            program, mesh=mesh, in_specs=in_specs, out_specs=out_specs, check_vma=False
        )(*arrays)

    return placed
```
